32 devices in a mesh: gx: 4 (over y, core), gy: 8 (over z, x).
Axes of the slice: x: 2, y: 2, z: 4, core: 2. Of those that a mesh axis runs over, the one named last changes fastest.
Arguments:
- inputs: bfloat16 [64, 4, 2304], P('gy', None, 'gx'), may hold values from -8 to 8
- cache_pool: bfloat16 [2, 40, 1024, 1024], P(None, 'gx', 'gy'), may hold values from -6 to 6
- lengths: int32 [8], P('gy'), may hold values from 1 to 32768, as said below
- block_table: int32 [8, 33], P('gy'), may hold values from -1 to 39, as said below
- parents: int32 [3, 64], P(None, 'gy'), may hold values from 0 to 7
- norm_gains: float32 [4, 2304], P(None, 'gx'), may hold values from -0.5 to 1
- w_query: bfloat16 [2304, 2048], P('gx', 'gy'), may hold values from -0.125 to 0.125
- w_key: bfloat16 [2304, 1024], P('gx', 'gy'), may hold values from -0.125 to 0.125
- w_value: bfloat16 [2304, 1024], P('gx', 'gy'), may hold values from -0.125 to 0.125
- w_out: bfloat16 [2048, 2304], P('gy', 'gx'), may hold values from -1 to 1
- w_gate: bfloat16 [2304, 9216], P('gx', 'gy'), may hold values from -0.125 to 0.125
- w_up: bfloat16 [2304, 9216], P('gx', 'gy'), may hold values from -0.125 to 0.125
- w_down: bfloat16 [9216, 2304], P('gy', 'gx'), may hold values from -1 to 1
Outputs:
- outputs: bfloat16 [64, 4, 2304], P('gy', None, 'gx')
The draws below stay inside these ranges and needn't reach their ends.
Inputs may be any that keep to these rules, and one draw needn't show every extreme that they name: `lengths`: a group's beams share its prompt length. block_table[g, j] is the slot, numbered over the index of gy that holds group g as gx index times 10 plus the device's slot, of page first(g) + j of the group, for j up to (lengths[g] - 1) // 128 - first(g), and -1 beyond; no slot is named twice; a device holds at most 10 pages, and some device holds 10. Beam b at step s + 1 continues beam parents[s, b] of its own group, numbered within the group.
All inputs are finite; a program needn't handle non-finite values.
Results may differ from the reference program's by a relative error of at most 0.015.
Values may be sent and summed in bfloat16 or wider, within the bound.
No kernel may reach another device: no remote copies, remote signals or barrier semaphores. Data moves between devices by JAX's collectives and lax.ppermute only.
A program may use at most 64 MiB of HBM per device.

```python
import math
import jax
import jax.numpy as jnp
from jax import lax

D = 2304
FF = 9216
HEADS = 8
KV_HEADS = 4
HEAD_DIM = 256
WINDOW = 4096
MAXLEN = 32768
PAGE = 128
BEAM = 8
STEPS = 4
GROUPS_DEV = 1
GROUPS = 8
BEAMS = 64
PAGES_MAX = 33
SLOTS = 10
POOL_SLOTS = 40
Q_WIDTH = 2048
KV_WIDTH = 1024
N_GY = 8


def permute_slots(key_item):
    return jax.random.permutation(key_item, POOL_SLOTS)


def group_layout(key):
    key_one = jax.random.fold_in(key, 101)
    key_two = jax.random.fold_in(key, 102)
    key_three = jax.random.fold_in(key, 103)
    key_four = jax.random.fold_in(key, 104)
    key_five = jax.random.fold_in(key, 105)
    key_six = jax.random.fold_in(key, 106)
    shifts = jax.random.randint(key_one, (GROUPS,), 0, 8)
    top_lengths = jnp.right_shift(jnp.full((GROUPS,), MAXLEN, jnp.int32), shifts)
    half_tops = top_lengths // 2
    offsets = jax.random.randint(key_two, (GROUPS,), 0, half_tops)
    group_lengths = half_tops + offsets
    longest = jax.random.randint(key_three, (), 0, GROUPS)
    second = (longest + 1 + jax.random.randint(key_four, (), 0, GROUPS - 1)) % GROUPS
    group_ids = jnp.arange(GROUPS, dtype=jnp.int32)
    group_lengths = jnp.where(group_ids == longest, MAXLEN, group_lengths)
    group_lengths = jnp.where(group_ids == second, MAXLEN - PAGE // 2, group_lengths)
    first_page = jnp.maximum(group_lengths - WINDOW + 1, 0) // PAGE
    last_page = (group_lengths - 1) // PAGE
    page_counts = last_page - first_page + 1
    column_count = GROUPS // GROUPS_DEV
    per_column = page_counts.reshape(column_count, GROUPS_DEV)
    first_flat = jnp.cumsum(per_column, axis=1) - per_column
    rank_rows = jax.vmap(permute_slots)(jax.random.split(key_five, column_count)).astype(jnp.int32)
    hot_device = jax.random.randint(key_six, (column_count, 1), 0, POOL_SLOTS // SLOTS)
    owner_dev = jnp.arange(POOL_SLOTS, dtype=jnp.int32) // SLOTS
    slot_scores = rank_rows + POOL_SLOTS * (owner_dev[None, :] != hot_device).astype(jnp.int32)
    slot_order = jnp.argsort(slot_scores, axis=1, stable=True).astype(jnp.int32)
    flat_index = first_flat.reshape(GROUPS, 1) + jnp.arange(PAGES_MAX, dtype=jnp.int32)[None, :]
    column_ids = group_ids // GROUPS_DEV
    picked = slot_order[column_ids[:, None], jnp.minimum(flat_index, POOL_SLOTS - 1)]
    block_rows = jnp.where(jnp.arange(PAGES_MAX, dtype=jnp.int32)[None, :] < page_counts[:, None], picked, -1)
    return (group_lengths.astype(jnp.int32), block_rows.astype(jnp.int32))


def draw_lengths(key, part):
    return group_layout(key)[0]


def draw_block_table(key, part):
    return group_layout(key)[1]


def common_direction(key):
    return jax.random.normal(jax.random.fold_in(key, 301), (D,), jnp.float32)


def draw_inputs(key, part):
    column_frac = jnp.arange(D, dtype=jnp.float32) / D
    direction = common_direction(key)
    loadings = jax.random.normal(jax.random.fold_in(key, 10), (BEAMS, STEPS, 1), jnp.float32)
    base_draw = jax.random.normal(jax.random.fold_in(key, 9), (BEAMS, STEPS, D), jnp.float32)
    mixed_draw = base_draw * math.sqrt(0.7) + loadings * direction * math.sqrt(0.3)
    values = mixed_draw * jnp.exp(column_frac * math.log(3.0)) / 1.7
    return jnp.clip(values, -8.0, 8.0).astype(jnp.bfloat16)


def draw_w_out(key, part):
    column_frac = jnp.arange(D, dtype=jnp.float32) / D
    direction = common_direction(key)
    loadings = jax.random.normal(jax.random.fold_in(key, 23), (Q_WIDTH, 1), jnp.float32)
    base_draw = jax.random.normal(jax.random.fold_in(key, 22), (Q_WIDTH, D), jnp.float32)
    mixed_draw = base_draw * math.sqrt(0.7) + loadings * direction * math.sqrt(0.3)
    values = mixed_draw * jnp.exp(column_frac * math.log(3.0)) / 1.9
    return jnp.clip(values * (1.0 / math.sqrt(Q_WIDTH)), -1.0, 1.0).astype(jnp.bfloat16)


def draw_w_down(key, part):
    column_frac = jnp.arange(D, dtype=jnp.float32) / D
    direction = jax.random.normal(jax.random.fold_in(key, 302), (D,), jnp.float32)
    loadings = jax.random.normal(jax.random.fold_in(key, 33), (FF, 1), jnp.float32)
    base_draw = jax.random.normal(jax.random.fold_in(key, 32), (FF, D), jnp.float32)
    mixed_draw = base_draw * math.sqrt(0.7) + loadings * direction * math.sqrt(0.3)
    values = mixed_draw * jnp.exp(column_frac * math.log(3.0)) / 1.9
    return jnp.clip(values * (1.0 / math.sqrt(FF)), -1.0, 1.0).astype(jnp.bfloat16)


def with_ends(entries, stream_key, least, high):
    place = [jax.random.randint(jax.random.fold_in(stream_key, axis), (), 0, length) for axis, length in enumerate(entries.shape)]
    widest = entries.shape.index(max(entries.shape))
    next_to = place[:widest] + [(place[widest] + 1) % entries.shape[widest]] + place[widest + 1:]
    return entries.at[tuple(place)].set(least).at[tuple(next_to)].set(high)


def block_levels(key, dims, pieces, least, largest):
    def one(dim, parts):
        heights = jax.random.uniform(jax.random.fold_in(jax.random.fold_in(key, 6), dim), (parts,), jnp.float32, least / len(pieces), largest / len(pieces))
        return jnp.repeat(jnp.exp(heights), dims[dim] // parts).reshape((-1,) + (1,) * (len(dims) - dim - 1))

    loudness = one(*pieces[0])
    for cut in pieces[1:]:
        loudness = loudness * one(*cut)
    return loudness


def noise(rng, dims, scale, most, cuts=(), held_as=jnp.bfloat16):
    entries = scale * jax.random.normal(rng, dims, jnp.float32)
    if cuts:
        entries = entries * block_levels(rng, dims, cuts, -0.22, 0.18)
    return jnp.clip(entries, -most, most).astype(held_as)


def setup_inputs(seed: int = 0) -> dict:
    key_of = jax.random.split(jax.random.key(seed), 14)
    return {
        "inputs": draw_inputs(jax.random.fold_in(key_of[13], 71), 0),
        "cache_pool": noise(key_of[1], (2, POOL_SLOTS, N_GY * PAGE, KV_WIDTH), 1.0, 6.0, ((1, 4), (2, 8))),
        "lengths": draw_lengths(jax.random.fold_in(key_of[13], 71), 0),
        "block_table": draw_block_table(jax.random.fold_in(key_of[13], 71), 0),
        "parents": with_ends(jax.random.randint(key_of[4], (STEPS - 1, BEAMS), 0, BEAM), jax.random.fold_in(key_of[4], 1), 0, BEAM - 1).astype(jnp.int32),
        "norm_gains": jnp.clip(-0.5 + 1.5 * jax.random.uniform(key_of[5], (4, D), jnp.float32) ** block_levels(key_of[5], (4, D), ((1, 4),), -0.2, 0.2), -0.5, 1.0),
        "w_query": noise(key_of[6], (D, Q_WIDTH), D ** -0.5, 0.125, ((0, 4), (1, 8))),
        "w_key": noise(key_of[7], (D, KV_WIDTH), D ** -0.5, 0.125, ((0, 4), (1, 8))),
        "w_value": noise(key_of[8], (D, KV_WIDTH), D ** -0.5, 0.125, ((0, 4), (1, 8))),
        "w_out": draw_w_out(jax.random.fold_in(key_of[13], 71), 0),
        "w_gate": noise(key_of[10], (D, FF), D ** -0.5, 0.125, ((0, 4), (1, 8))),
        "w_up": noise(key_of[11], (D, FF), D ** -0.5, 0.125, ((0, 4), (1, 8))),
        "w_down": draw_w_down(jax.random.fold_in(key_of[13], 71), 0),
    }


EPSILON = 1e-06
SOFT_CAP = 50.0
ROPE_BASE = 10000.0

def row_scale(values):
    return lax.rsqrt(lax.optimization_barrier(jnp.mean(values * values, axis=-1, keepdims=True)) + EPSILON)

def rotate(values, positions):
    half_width = values.shape[-1] // 2
    inverse_freq = ROPE_BASE ** (-jnp.arange(half_width, dtype=jnp.float32) * 2.0 / values.shape[-1])
    angles = positions[..., None].astype(jnp.float32) * inverse_freq
    cosine = jnp.cos(angles)[..., None, :]
    sine_part = jnp.sin(angles)[..., None, :]
    first_half = values[..., :half_width]
    second_half = values[..., half_width:]
    return jnp.concatenate([first_half * cosine - second_half * sine_part, second_half * cosine + first_half * sine_part], axis=-1)

def ancestry(parents, beam_count, group_size, steps_count):
    beam_ids = jnp.arange(beam_count, dtype=jnp.int32)
    group_base = beam_ids // group_size * group_size
    table_rows = []
    for moment in range(steps_count):
        current = beam_ids
        chain_list = [beam_ids] * steps_count
        for earlier in range(moment, 0, -1):
            current = group_base + jnp.take(parents[earlier - 1], current)
            chain_list[earlier - 1] = current
        table_rows.append(jnp.stack(chain_list))
    return jnp.stack(table_rows)

def tail_terms(grouped, key_steps, value_steps, ancestors):
    steps_count = grouped.shape[1]
    step_ids = jnp.arange(steps_count, dtype=jnp.int32)
    tail_keys = key_steps[ancestors, step_ids[None, :, None]]
    tail_values = value_steps[ancestors, step_ids[None, :, None]]
    scores = jnp.einsum('bskgd,sjbkd->bskgj', grouped.astype(jnp.float32), tail_keys.astype(jnp.float32))
    allowed = step_ids[None, :] <= step_ids[:, None]
    weights = jnp.where(allowed[None, :, None, None, :], jnp.exp(SOFT_CAP * jnp.tanh(scores / SOFT_CAP)), 0.0)
    rounded = lax.optimization_barrier(weights.astype(jnp.bfloat16)).astype(jnp.float32)
    numerator = jnp.einsum('bskgj,sjbkd->bskgd', rounded, tail_values.astype(jnp.float32))
    return (numerator, lax.optimization_barrier(jnp.sum(weights, axis=-1)))

def reference(inputs, cache_pool, lengths, block_table, parents, norm_gains, w_query, w_key, w_value, w_out, w_gate, w_up, w_down):
    x_wide = inputs.astype(jnp.float32)
    gain_rows = 1.0 + norm_gains.astype(jnp.float32)
    normed = (x_wide * row_scale(x_wide) * gain_rows[0]).astype(jnp.bfloat16)
    matrix_rows = normed.reshape(BEAMS * STEPS, D)
    query_raw = jnp.dot(matrix_rows, w_query, preferred_element_type=jnp.float32).reshape(BEAMS, STEPS, HEADS, HEAD_DIM)
    key_raw = jnp.dot(matrix_rows, w_key, preferred_element_type=jnp.float32).reshape(BEAMS, STEPS, KV_HEADS, HEAD_DIM)
    value_raw = jnp.dot(matrix_rows, w_value, preferred_element_type=jnp.float32).reshape(BEAMS, STEPS, KV_HEADS, HEAD_DIM)
    beam_lengths = jnp.repeat(lengths, BEAM)
    positions = beam_lengths[:, None] + jnp.arange(STEPS, dtype=jnp.int32)[None, :]
    queries = (rotate(query_raw, positions) * HEAD_DIM ** (-0.5)).astype(jnp.bfloat16)
    key_steps = rotate(key_raw, positions).astype(jnp.bfloat16)
    value_steps = value_raw.astype(jnp.bfloat16)
    grouped = queries.reshape(BEAMS, STEPS, KV_HEADS, HEADS // KV_HEADS, HEAD_DIM)
    ancestors = ancestry(parents, BEAMS, BEAM, STEPS)
    tail_num, tail_den = tail_terms(grouped, key_steps, value_steps, ancestors)
    group_queries = grouped.reshape(GROUPS, BEAM, STEPS, KV_HEADS, HEADS // KV_HEADS, HEAD_DIM)

    def one_group(operands):
        group_query, length, slot_list, column = operands
        column_pool = lax.dynamic_slice_in_dim(cache_pool, (column * PAGE).astype(jnp.int32), PAGE, 2)
        valid_page = slot_list >= 0
        page_rows = jnp.take(column_pool, jnp.maximum(slot_list, 0), axis=1)
        key_rows = page_rows[0].reshape(PAGES_MAX * PAGE, KV_HEADS, HEAD_DIM)
        value_rows = page_rows[1].reshape(PAGES_MAX * PAGE, KV_HEADS, HEAD_DIM)
        first_page = jnp.maximum(length - WINDOW + 1, 0) // PAGE
        key_positions = ((first_page + jnp.arange(PAGES_MAX, dtype=jnp.int32))[:, None] * PAGE + jnp.arange(PAGE, dtype=jnp.int32)[None, :]).reshape(-1)
        page_valid = jnp.repeat(valid_page, PAGE)
        lower_bound = length + jnp.arange(STEPS, dtype=jnp.int32) - WINDOW + 1
        visible = page_valid[None, :] & (key_positions[None, :] < length) & (key_positions[None, :] >= lower_bound[:, None])
        scores = jnp.einsum('bskgd,tkd->bskgt', group_query.astype(jnp.float32), key_rows.astype(jnp.float32))
        weights = jnp.where(visible[None, :, None, None, :], jnp.exp(SOFT_CAP * jnp.tanh(scores / SOFT_CAP)), 0.0)
        rounded = lax.optimization_barrier(weights.astype(jnp.bfloat16)).astype(jnp.float32)
        numerator = jnp.einsum('bskgt,tkd->bskgd', rounded, value_rows.astype(jnp.float32))
        return (numerator, lax.optimization_barrier(jnp.sum(weights, axis=-1)))
    columns = jnp.arange(GROUPS, dtype=jnp.int32) // GROUPS_DEV
    prefix_num, prefix_den = lax.map(one_group, (group_queries, lengths, block_table, columns))
    numerator = prefix_num.reshape(BEAMS, STEPS, KV_HEADS, HEADS // KV_HEADS, HEAD_DIM) + tail_num
    denominator = prefix_den.reshape(BEAMS, STEPS, KV_HEADS, HEADS // KV_HEADS) + tail_den
    attended = (numerator / denominator[..., None]).astype(jnp.bfloat16).reshape(BEAMS * STEPS, HEADS * HEAD_DIM)
    attn_full = jnp.dot(attended, w_out, preferred_element_type=jnp.float32).reshape(BEAMS, STEPS, D)
    mixed_full = x_wide + attn_full * row_scale(attn_full) * gain_rows[1]
    ff_input = (mixed_full * row_scale(mixed_full) * gain_rows[2]).astype(jnp.bfloat16).reshape(BEAMS * STEPS, D)
    gate_part = jnp.dot(ff_input, w_gate, preferred_element_type=jnp.float32)
    up_part = jnp.dot(ff_input, w_up, preferred_element_type=jnp.float32)
    hidden = (jax.nn.gelu(gate_part, approximate=True) * up_part).astype(jnp.bfloat16)
    down_full = jnp.dot(hidden, w_down, preferred_element_type=jnp.float32).reshape(BEAMS, STEPS, D)
    return (mixed_full + down_full * row_scale(down_full) * gain_rows[3]).astype(jnp.bfloat16)
```

```python
import jax
import jax.numpy as jnp
from jax import lax
from jax.experimental import pallas as pl
from jax.experimental.pallas import tpu as pltpu
from jax.sharding import PartitionSpec as P

D = 2304
HEADS = 8
KV_HEADS = 4
HEAD_DIM = 256
HALF = HEAD_DIM // 2
WINDOW = 4096
PAGE = 128
BEAM = 8
EPSILON = 1e-06
SOFT_CAP = 50.0
ROPE_BASE = 10000.0
BF = jnp.bfloat16
F32 = jnp.float32
MIB = 1024 * 1024
GAIN_ROWS = 16


def stage(fast, name, f, outs, *args, limit=16):
    if not fast:
        return f(*args)

    def kernel(*refs):
        results = f(*[r[...] for r in refs[: len(args)]])
        for ref, result in zip(refs[len(args) :], results):
            ref[...] = result.astype(ref.dtype)

    return pl.pallas_call(
        kernel,
        out_shape=[jax.ShapeDtypeStruct(s, d) for s, d in outs],
        compiler_params=pltpu.CompilerParams(vmem_limit_bytes=limit * MIB),
        name=name,
    )(*args)


def exchange(values, axes):
    return lax.all_to_all(values, axes, split_axis=0, concat_axis=0, tiled=True)


def exchange_all(values):
    nx, ny = values.shape[:2]
    flat = values.reshape((nx * ny,) + values.shape[2:])
    return exchange(flat, ("gx", "gy")).reshape(values.shape)


def weight_of(scores):
    return jnp.exp(SOFT_CAP * jnp.tanh(scores * (1.0 / SOFT_CAP)))


def attention_kernel(
    table_ref, length_ref, parents_ref, g_ref, x_ref, cos_ref, sin_ref, pool_ref, out_ref, page_ref
):
    parts, reps, part_rows = out_ref.shape[:3]
    rows = parts * part_rows
    steps = rows // BEAM
    slots = pool_ref.shape[1]
    first_owner = lax.axis_index("gx") * slots
    length = length_ref[0]
    first_page = jnp.maximum(length - WINDOW + 1, 0) // PAGE
    x = x_ref[...].astype(F32)
    square = jnp.sum(jnp.sum(x * x, axis=0), axis=-1, keepdims=True)
    scale = lax.rsqrt(square / D + EPSILON)
    cos, sin = cos_ref[...], sin_ref[...]

    def rotated(u, w):
        u, w = u.astype(F32) * scale, w.astype(F32) * scale
        return u * cos - w * sin, w * cos + u * sin

    query = []
    for rep in range(reps):
        u, w = rotated(g_ref[0, rep], g_ref[1, rep])
        query.append(jnp.concatenate([u, w], axis=1) * HEAD_DIM ** (-0.5))
    query = jnp.concatenate(query, axis=0).astype(BF)
    key_step = jnp.concatenate(rotated(g_ref[2, 0], g_ref[2, 1]), axis=1).astype(BF)
    value_step = jnp.concatenate(
        [g_ref[3, 0].astype(F32) * scale, g_ref[3, 1].astype(F32) * scale], axis=1
    ).astype(BF)

    for slot in range(slots):
        page_ref[slot] = -1

    def place(j, carry):
        slot = table_ref[0, j] - first_owner

        @pl.when((slot >= 0) & (slot < slots))
        def _():
            page_ref[slot] = j

        return carry

    lax.fori_loop(0, table_ref.shape[1], place, 0)
    lane = lax.broadcasted_iota(jnp.int32, (1, PAGE), 1)
    far = jnp.int32(2**30)
    position = jnp.concatenate(
        [
            lane + jnp.where(page_ref[s] >= 0, (first_page + page_ref[s]) * PAGE, far)
            for s in range(slots)
        ],
        axis=1,
    )
    step_of = lax.broadcasted_iota(jnp.int32, (reps * rows, 1), 0) % steps
    lower = length + step_of - (WINDOW - 1)
    seen = (position < length) & (position >= lower)
    keys = pool_ref[0].reshape(slots * PAGE, HEAD_DIM)
    values = pool_ref[1].reshape(slots * PAGE, HEAD_DIM)
    contract_last = (((1,), (1,)), ((), ()))
    scores = lax.dot_general(query, keys, contract_last, preferred_element_type=F32)
    weights = jnp.where(seen, weight_of(scores), 0.0)
    den = jnp.sum(weights, axis=-1, keepdims=True)
    num = jnp.dot(weights.astype(BF), values, preferred_element_type=F32)

    shape = (reps * rows, rows)
    row = lax.broadcasted_iota(jnp.int32, shape, 0) % rows
    column = lax.broadcasted_iota(jnp.int32, shape, 1)
    row_step, column_step, column_beam = row % steps, column % steps, column // steps
    current = row // steps
    visible = jnp.zeros(shape, jnp.bool_)
    for j in range(steps - 1, -1, -1):
        if j < steps - 1:
            parent = jnp.zeros(shape, jnp.int32)
            for beam in range(BEAM):
                parent = jnp.where(current == beam, parents_ref[j, beam], parent)
            current = jnp.where(row_step > j, parent, current)
        visible = visible | ((column_step == j) & (row_step >= j) & (column_beam == current))
    visible = visible & (lax.axis_index("gx") == 0)
    scores = lax.dot_general(query, key_step, contract_last, preferred_element_type=F32)
    weights = jnp.where(visible, weight_of(scores), 0.0)
    den = den + jnp.sum(weights, axis=-1, keepdims=True)
    num = num + jnp.dot(weights.astype(BF), value_step, preferred_element_type=F32)

    high = den.astype(BF).astype(F32)
    wide = lax.broadcasted_iota(jnp.int32, (reps * rows, PAGE), 1)
    den_lanes = jnp.where(wide < PAGE // 2, high, den - high)
    for part in range(parts):
        for rep in range(reps):
            here = slice(rep * rows + part * part_rows, rep * rows + (part + 1) * part_rows)
            out_ref[part, rep, :, 0:HEAD_DIM] = num[here].astype(BF)
            out_ref[part, rep, :, HEAD_DIM:] = den_lanes[here].astype(BF)


def attention(parts, table, lengths, parents, g, wide, x_block, cos, sin, pool):
    rows = g.shape[2]
    reps = HEADS // KV_HEADS
    nx, _, width = wide.shape
    slots = pool.shape[1]
    smem = pl.BlockSpec(memory_space=pltpu.SMEM)
    return pl.pallas_call(
        attention_kernel,
        grid=(KV_HEADS,),
        in_specs=[
            smem,
            smem,
            smem,
            pl.BlockSpec((4, 2, rows, HALF), lambda h: (0, h, 0, 0)),
            pl.BlockSpec((nx, rows, width), lambda h: (0, x_block, 0)),
            pl.BlockSpec((rows, HALF), lambda h: (0, 0)),
            pl.BlockSpec((rows, HALF), lambda h: (0, 0)),
            pl.BlockSpec((2, slots, PAGE, HEAD_DIM), lambda h: (0, 0, 0, h)),
        ],
        out_specs=pl.BlockSpec(
            (parts, reps, rows // parts, HEAD_DIM + PAGE), lambda h: (0, h, 0, 0)
        ),
        out_shape=jax.ShapeDtypeStruct((parts, HEADS, rows // parts, HEAD_DIM + PAGE), BF),
        scratch_shapes=[pltpu.SMEM((slots,), jnp.int32)],
        compiler_params=pltpu.CompilerParams(vmem_limit_bytes=24 * MIB),
        name="attention",
    )(table, lengths, parents, g, wide, cos, sin, pool)


def body(
    inputs,
    cache_pool,
    lengths,
    block_table,
    parents,
    norm_gains,
    w_query,
    w_key,
    w_value,
    w_out,
    w_gate,
    w_up,
    w_down,
):
    beams, steps, width = inputs.shape
    nx, ny = lax.axis_size("gx"), lax.axis_size("gy")
    rows = beams * steps
    part = rows // nx
    head_part = w_out.shape[0]
    hidden_part = w_gate.shape[1]
    query_part, key_part = w_query.shape[1], w_key.shape[1]
    columns = query_part + 2 * key_part
    share = columns // nx
    fast = part % 8 == 0 and share == HALF and head_part == HEAD_DIM and query_part == 2 * share
    x_own = inputs.reshape(rows, width)

    def rounded(v):
        return lax.reduce_precision(v, 8, 7)

    gain_high = rounded(norm_gains)
    gain_mid = rounded(norm_gains - gain_high)
    gain_low = norm_gains - gain_high - gain_mid
    gain_pad = jnp.zeros((GAIN_ROWS - 12, width), F32)
    gain_block = jnp.concatenate([gain_high, gain_mid, gain_low, gain_pad], axis=0).astype(BF)
    wide = lax.all_gather(jnp.concatenate([w_out, x_own, gain_block], axis=0), "gx", axis=0)

    x_all = exchange(jnp.broadcast_to(x_own[None], (ny, rows, width)), "gy")

    def project(x, gains, wq, wk, wv):
        flat = (x.astype(F32) * (1.0 + gains[0:1])).astype(BF).reshape(ny * rows, width)
        sums = [jnp.dot(flat, w, preferred_element_type=F32) for w in (wq, wk, wv)]
        if fast:
            sums = [sums[0][:, :share], sums[0][:, share:], sums[1], sums[2]]
            return [jnp.stack([s.reshape(ny, rows, share) for s in sums]).astype(BF)]
        both = jnp.concatenate(sums, axis=1).reshape(ny, rows, nx, share)
        return [both.transpose(2, 0, 1, 3).astype(BF)]

    (send,) = stage(
        fast,
        "project",
        project,
        [((nx, ny, rows, share), BF)],
        x_all,
        norm_gains,
        w_query,
        w_key,
        w_value,
    )
    received = exchange_all(send)
    (shares,) = stage(
        fast,
        "sum_shares",
        lambda v: [jnp.sum(v.astype(F32), axis=0).astype(BF)],
        [((ny, rows, share), BF)],
        received,
    )
    g = lax.all_gather(shares, "gx", axis=0)
    if not fast:
        every = g.transpose(2, 1, 0, 3).reshape(rows, ny, columns)
        q = every[..., :query_part].reshape(rows, HEADS, 2, HALF).transpose(2, 1, 0, 3)
        k, v = (
            every[..., start : start + key_part].reshape(rows, 2 * KV_HEADS, HALF).transpose(1, 0, 2)
            for start in (query_part, query_part + key_part)
        )
        g = jnp.concatenate([q, k[None], v[None]], axis=0)

    positions = lengths[0] + jnp.arange(rows, dtype=jnp.int32) % steps
    inverse_freq = ROPE_BASE ** (-jnp.arange(HALF, dtype=F32) * 2.0 / HEAD_DIM)
    angles = positions[:, None].astype(F32) * inverse_freq
    terms = attention(
        nx if fast else 1,
        block_table,
        lengths,
        parents,
        g,
        wide,
        head_part // rows,
        jnp.cos(angles),
        jnp.sin(angles),
        cache_pool,
    )
    if not fast:
        terms = terms.reshape(HEADS, rows, HEAD_DIM + PAGE)
        num = terms[..., :HEAD_DIM].transpose(1, 0, 2).reshape(nx, part, ny, head_part)
        den = terms[..., HEAD_DIM :: PAGE // 2].transpose(1, 0, 2)
        den = jnp.repeat(den, ny // HEADS, axis=1).reshape(nx, part, ny, 2)
        terms = jnp.concatenate([num, den], axis=-1).transpose(0, 2, 1, 3)
    terms = exchange_all(terms)

    def project_out(t, w_wide):
        t = jnp.sum(t.astype(F32), axis=0)
        den = t[..., head_part : head_part + 1] + t[..., -1:]
        attended = (t[..., :head_part] / den).reshape(ny * part, head_part).astype(BF)
        return [
            jnp.stack(
                [
                    jnp.dot(attended, w_wide[k, :head_part], preferred_element_type=F32).reshape(
                        ny, part, width
                    )
                    for k in range(nx)
                ],
                axis=1,
            ).astype(BF)
        ]

    (attn_parts,) = stage(
        fast, "project_out", project_out, [((ny, nx, part, width), BF)], terms, wide
    )
    attn_parts = exchange(attn_parts, "gy")
    x_rows = lax.dynamic_slice_in_dim(wide, head_part + lax.axis_index("gx") * part, part, 1)
    gains_wide = wide[:, head_part + rows :]

    def gain_of(gains, index):
        gains = gains.astype(F32)
        high, mid, low = (gains[:, 4 * t + index : 4 * t + index + 1] for t in range(3))
        return 1.0 + (high + (mid + low))

    def row_scale(v):
        square = jnp.sum(jnp.sum(v * v, axis=0), axis=-1, keepdims=True)
        return lax.rsqrt(square / D + EPSILON)[None]

    def mix(parts, x, gains):
        attn = jnp.sum(parts.astype(F32), axis=0)
        mixed = x.astype(F32) + attn * row_scale(attn) * gain_of(gains, 1)
        ff_input = (mixed * row_scale(mixed) * gain_of(gains, 2)).astype(BF)
        return [mixed, jnp.broadcast_to(ff_input[:, None], (nx, ny, part, width))]

    mixed, ff_input = stage(
        fast,
        "mix",
        mix,
        [((nx, part, width), F32), ((nx, ny, part, width), BF)],
        attn_parts,
        x_rows,
        gains_wide,
    )
    ff_input = exchange_all(ff_input)

    def gate_up(ff, wg, wu):
        flat = ff.astype(F32).reshape(nx * ny * part, width).astype(BF)
        both = [jnp.dot(flat, w, preferred_element_type=F32).astype(BF) for w in (wg, wu)]
        return [jnp.concatenate(both, axis=1).reshape(nx, ny * part, 2 * hidden_part)]

    (both,) = stage(
        fast,
        "gate_up",
        gate_up,
        [((nx, ny * part, 2 * hidden_part), BF)],
        ff_input,
        w_gate,
        w_up,
        limit=24,
    )
    both = exchange(both, "gx")

    def activate(v):
        v = jnp.sum(v.astype(F32), axis=0)
        gate, up = v[:, :hidden_part], v[:, hidden_part:]
        return [(jax.nn.gelu(gate, approximate=True) * up).astype(BF)]

    (hidden,) = stage(fast, "activate", activate, [((ny * part, hidden_part), BF)], both)
    hidden = lax.all_gather(hidden, "gx", axis=0)

    def project_down(h, w):
        down = jnp.dot(
            h.reshape(nx * ny * part, hidden_part), w, preferred_element_type=F32
        )
        return [down.reshape(nx, ny, part, width).astype(BF)]

    (down,) = stage(
        fast, "project_down", project_down, [((nx, ny, part, width), BF)], hidden, w_down
    )
    down = exchange_all(down)

    def finish(parts, mixed_rows, gains):
        total = jnp.sum(parts.astype(F32), axis=1)
        return [(mixed_rows + total * row_scale(total) * gain_of(gains, 3)).astype(BF)]

    (out,) = stage(fast, "finish", finish, [((nx, part, width), BF)], down, mixed, gains_wide)
    return exchange(out, "gx").reshape(beams, steps, width)


def solution(mesh):
    return jax.shard_map(
        body,
        mesh=mesh,
        in_specs=(
            P("gy", None, "gx"),
            P(None, "gx", "gy", None),
            P("gy"),
            P("gy", None),
            P(None, "gy"),
            P(None, "gx"),
            P("gx", "gy"),
            P("gx", "gy"),
            P("gx", "gy"),
            P("gy", "gx"),
            P("gx", "gy"),
            P("gx", "gy"),
            P("gy", "gx"),
        ),
        out_specs=P("gy", None, "gx"),
        check_vma=False,
    )
```

```python
import jax
import jax.numpy as jnp
from jax import lax
from jax.experimental import pallas as pl
from jax.experimental.pallas import tpu as pltpu
from jax.sharding import PartitionSpec as P

D = 2304
HEADS = 8
KV_HEADS = 4
HEAD_DIM = 256
HALF = HEAD_DIM // 2
WINDOW = 4096
PAGE = 128
BEAM = 8
EPSILON = 1e-06
SOFT_CAP = 50.0
ROPE_BASE = 10000.0
BF = jnp.bfloat16
F32 = jnp.float32
MIB = 1024 * 1024
GAIN_ROWS = 16


def stage(fast, name, f, outs, *args, limit=16, specs=None):
    if not fast:
        return f(*args)

    def kernel(*refs):
        results = f(*[r[...] for r in refs[: len(args)]])
        for ref, result in zip(refs[len(args) :], results):
            ref[...] = result.astype(ref.dtype)

    return run(kernel, name, outs, args, limit, specs)


def run(kernel, name, outs, args, limit=16, specs=None, scratch=()):
    more = {}
    if specs is not None:
        whole = pl.BlockSpec(memory_space=pltpu.VMEM)
        more = {"in_specs": [whole if s is None else s for s in specs], "grid": (1,)}
    return pl.pallas_call(
        kernel,
        out_shape=[jax.ShapeDtypeStruct(s, d) for s, d in outs],
        scratch_shapes=scratch,
        compiler_params=pltpu.CompilerParams(vmem_limit_bytes=limit * MIB),
        name=name,
        **more,
    )(*args)


def exchange(values, axes):
    return lax.all_to_all(values, axes, split_axis=0, concat_axis=0, tiled=True)


def exchange_all(values):
    nx, ny = values.shape[:2]
    flat = values.reshape((nx * ny,) + values.shape[2:])
    return exchange(flat, ("gx", "gy")).reshape(values.shape)


def weight_of(scores):
    return jnp.exp(SOFT_CAP * jnp.tanh(scores * (1.0 / SOFT_CAP)))


def attention_kernel(
    table_ref,
    length_ref,
    parents_ref,
    g_ref,
    square_ref,
    cos_ref,
    sin_ref,
    pool_ref,
    out_ref,
    page_ref,
):
    parts, reps, part_rows = out_ref.shape[:3]
    rows = parts * part_rows
    steps = rows // BEAM
    slots = pool_ref.shape[1]
    first_owner = lax.axis_index("gx") * slots
    length = length_ref[0]
    first_page = jnp.maximum(length - WINDOW + 1, 0) // PAGE
    square = jnp.sum(square_ref[:, 0].astype(F32), axis=0)
    square = square[:, 0:1] + square[:, HALF // 2 : HALF // 2 + 1]
    scale = lax.rsqrt(square / D + EPSILON)
    cos, sin = cos_ref[...], sin_ref[...]

    def rotated(u, w):
        u, w = u.astype(F32) * scale, w.astype(F32) * scale
        return u * cos - w * sin, w * cos + u * sin

    query = []
    for rep in range(reps):
        u, w = rotated(g_ref[0, rep], g_ref[1, rep])
        query.append(jnp.concatenate([u, w], axis=1) * HEAD_DIM ** (-0.5))
    query = jnp.concatenate(query, axis=0).astype(BF)
    key_step = jnp.concatenate(rotated(g_ref[2, 0], g_ref[2, 1]), axis=1).astype(BF)
    value_step = jnp.concatenate(
        [g_ref[3, 0].astype(F32) * scale, g_ref[3, 1].astype(F32) * scale], axis=1
    ).astype(BF)

    for slot in range(slots):
        page_ref[slot] = -1

    def place(j, carry):
        slot = table_ref[0, j] - first_owner

        @pl.when((slot >= 0) & (slot < slots))
        def _():
            page_ref[slot] = j

        return carry

    lax.fori_loop(0, table_ref.shape[1], place, 0)
    lane = lax.broadcasted_iota(jnp.int32, (1, PAGE), 1)
    far = jnp.int32(2**30)
    position = jnp.concatenate(
        [
            lane + jnp.where(page_ref[s] >= 0, (first_page + page_ref[s]) * PAGE, far)
            for s in range(slots)
        ],
        axis=1,
    )
    step_of = lax.broadcasted_iota(jnp.int32, (reps * rows, 1), 0) % steps
    lower = length + step_of - (WINDOW - 1)
    seen = (position < length) & (position >= lower)
    keys = pool_ref[0].reshape(slots * PAGE, HEAD_DIM)
    values = pool_ref[1].reshape(slots * PAGE, HEAD_DIM)
    contract_last = (((1,), (1,)), ((), ()))
    scores = lax.dot_general(query, keys, contract_last, preferred_element_type=F32)
    weights = jnp.where(seen, weight_of(scores), 0.0)
    den = jnp.sum(weights, axis=-1, keepdims=True)
    num = jnp.dot(weights.astype(BF), values, preferred_element_type=F32)

    shape = (reps * rows, rows)
    row = lax.broadcasted_iota(jnp.int32, shape, 0) % rows
    column = lax.broadcasted_iota(jnp.int32, shape, 1)
    row_step, column_step, column_beam = row % steps, column % steps, column // steps
    current = row // steps
    visible = jnp.zeros(shape, jnp.bool_)
    for j in range(steps - 1, -1, -1):
        if j < steps - 1:
            parent = jnp.zeros(shape, jnp.int32)
            for beam in range(BEAM):
                parent = jnp.where(current == beam, parents_ref[j, beam], parent)
            current = jnp.where(row_step > j, parent, current)
        visible = visible | ((column_step == j) & (row_step >= j) & (column_beam == current))
    visible = visible & (lax.axis_index("gx") == 0)
    scores = lax.dot_general(query, key_step, contract_last, preferred_element_type=F32)
    weights = jnp.where(visible, weight_of(scores), 0.0)
    den = den + jnp.sum(weights, axis=-1, keepdims=True)
    num = num + jnp.dot(weights.astype(BF), value_step, preferred_element_type=F32)

    den_lanes = high_low(den, PAGE)
    for part in range(parts):
        for rep in range(reps):
            here = slice(rep * rows + part * part_rows, rep * rows + (part + 1) * part_rows)
            out_ref[part, rep, :, 0:HEAD_DIM] = num[here].astype(BF)
            out_ref[part, rep, :, HEAD_DIM:] = den_lanes[here].astype(BF)


def attention(parts, table, lengths, parents, g, cos, sin, pool):
    rows = g.shape[2]
    reps = HEADS // KV_HEADS
    slots = pool.shape[1]
    smem = pl.BlockSpec(memory_space=pltpu.SMEM)
    return pl.pallas_call(
        attention_kernel,
        grid=(KV_HEADS,),
        in_specs=[
            smem,
            smem,
            smem,
            pl.BlockSpec((4, 2, rows, HALF), lambda h: (0, h, 0, 0)),
            pl.BlockSpec((4, 1, rows, HALF), lambda h: (0, 2 * KV_HEADS, 0, 0)),
            pl.BlockSpec((rows, HALF), lambda h: (0, 0)),
            pl.BlockSpec((rows, HALF), lambda h: (0, 0)),
            pl.BlockSpec((2, slots, PAGE, HEAD_DIM), lambda h: (0, 0, 0, h)),
        ],
        out_specs=pl.BlockSpec(
            (parts, reps, rows // parts, HEAD_DIM + PAGE), lambda h: (0, h, 0, 0)
        ),
        out_shape=jax.ShapeDtypeStruct((parts, HEADS, rows // parts, HEAD_DIM + PAGE), BF),
        scratch_shapes=[pltpu.SMEM((slots,), jnp.int32)],
        compiler_params=pltpu.CompilerParams(vmem_limit_bytes=60 * MIB),
        name="attention",
    )(table, lengths, parents, g, g, cos, sin, pool)


def rounded(v):
    return lax.reduce_precision(v, 8, 7)


def high_low(column, lanes):
    shape = (column.shape[0], lanes)
    high = column.astype(BF).astype(F32)
    lane = lax.broadcasted_iota(jnp.int32, shape, 1)
    return jnp.where(lane < lanes // 2, high, column - high)


def partner_send(blocks):
    count = len(blocks)
    return [blocks[0]] + [
        lax.ppermute(blocks[m], "gx", [(i, i ^ m) for i in range(count)]) for m in range(1, count)
    ]


def body(
    inputs,
    cache_pool,
    lengths,
    block_table,
    parents,
    norm_gains,
    w_query,
    w_key,
    w_value,
    w_out,
    w_gate,
    w_up,
    w_down,
):
    beams, steps, width = inputs.shape
    nx, ny = lax.axis_size("gx"), lax.axis_size("gy")
    rows = beams * steps
    part = rows // nx
    head_part = w_out.shape[0]
    hidden_part = w_gate.shape[1]
    query_part, key_part = w_query.shape[1], w_key.shape[1]
    columns = query_part + 2 * key_part
    share = columns // nx
    fast = part % 8 == 0 and share == HALF and head_part == HEAD_DIM and query_part == 2 * share
    x_own = inputs.reshape(rows, width)
    me = lax.axis_index("gx")
    x_all = exchange(jnp.broadcast_to(x_own[None], (ny, rows, width)), "gy")

    def project(x, gains, wq, wk, wv):
        flat = (x.astype(F32) * (1.0 + gains[0:1])).astype(BF).reshape(ny * rows, width)
        sums = [jnp.dot(flat, w, preferred_element_type=F32) for w in (wq, wk, wv)]
        if fast:
            sums = [sums[0][:, :share], sums[0][:, share:], sums[1], sums[2]]
            return [jnp.stack([s.reshape(ny, rows, share) for s in sums]).astype(BF)]
        both = jnp.concatenate(sums, axis=1).reshape(ny, rows, nx, share)
        return [both.transpose(2, 0, 1, 3).astype(BF)]

    (send,) = stage(
        fast,
        "project",
        project,
        [((nx, ny, rows, share), BF)],
        x_all,
        norm_gains,
        w_query,
        w_key,
        w_value,
    )
    received = exchange_all(send)

    x_late, _ = lax.optimization_barrier((x_own, x_all))
    chunks = [(c, min(c + head_part, width)) for c in range(0, width, head_part)]
    if fast:
        side_rows = len(chunks) * (rows + GAIN_ROWS)

        def prepare(w_ref, x_ref, gain_ref, out_ref):
            out_ref[0:width] = w_ref[...]
            x = x_ref[...]
            gains = gain_ref[...]
            high = gains.astype(BF).astype(F32)
            mid = (gains - high).astype(BF).astype(F32)
            row = lax.broadcasted_iota(jnp.int32, gains.shape, 0)
            split = jnp.where(row < 4, high, jnp.where(row < 8, mid, gains - high - mid))
            split = jnp.where(row < 12, split, 0.0).astype(BF)
            out_ref[width:] = jnp.zeros((side_rows, head_part), BF)
            for n, (start, end) in enumerate(chunks):
                at = width + n * rows
                out_ref[at : at + rows, 0 : end - start] = x[:, start:end]
                at = width + len(chunks) * rows + n * GAIN_ROWS
                out_ref[at : at + GAIN_ROWS, 0 : end - start] = split[:, start:end]

        (side,) = run(
            prepare,
            "prepare",
            [((width + side_rows, head_part), BF)],
            (w_out.T, x_late, jnp.tile(norm_gains, (GAIN_ROWS // 4, 1))),
        )
        side = lax.all_gather(side, "gx", axis=0)
        out_spec = pl.BlockSpec((nx, width, head_part), lambda i: (0, 0, 0))
        side_spec = pl.BlockSpec((nx, side_rows, head_part), lambda i: (0, width // side_rows, 0))
        w_wide, x_and_gains = side, side
    else:
        w_wide = lax.all_gather(w_out.T, "gx", axis=0)
        x_and_gains = (lax.all_gather(x_late, "gx", axis=0), lax.all_gather(norm_gains, "gx"))
        out_spec = side_spec = None

    def rows_and_gain(values, index=None):
        if not fast:
            if index is not None:
                return 1.0 + values[1][:, index : index + 1]
            return lax.dynamic_slice_in_dim(values[0], me * part, part, 1).astype(F32)
        values = values.astype(F32)
        pieces = []
        for n, (start, end) in enumerate(chunks):
            if index is None:
                at = n * rows
                mine = lax.axis_index("gx")
                piece = sum(
                    jnp.where(mine == p, values[:, at + p * part : at + (p + 1) * part], 0.0)
                    for p in range(nx)
                )
            else:
                at = len(chunks) * rows + n * GAIN_ROWS + index
                high, mid, low = (values[:, at + 4 * t : at + 4 * t + 1] for t in range(3))
                piece = 1.0 + (high + (mid + low))
            pieces.append(piece[..., : end - start])
        return jnp.concatenate(pieces, axis=-1)

    def sum_shares(parts, x):
        x = x.astype(F32)
        squares = high_low(jnp.sum(x * x, axis=-1, keepdims=True), HALF)
        return [jnp.concatenate([jnp.sum(parts.astype(F32), axis=0), squares[None]], axis=0)]

    if fast:
        (shares,) = stage(
            fast, "sum_shares", sum_shares, [((ny + 1, rows, share), BF)], received, x_own
        )
        g = lax.all_gather(shares, "gx", axis=0)
    else:
        shares = jnp.sum(received.astype(F32), axis=0).astype(BF)
        every = lax.all_gather(shares, "gx", axis=0)
        every = every.transpose(2, 1, 0, 3).reshape(rows, ny, columns)
        q = every[..., :query_part].reshape(rows, HEADS, 2, HALF).transpose(2, 1, 0, 3)
        k, v = (
            every[..., start : start + key_part].reshape(rows, 2 * KV_HEADS, HALF).transpose(1, 0, 2)
            for start in (query_part, query_part + key_part)
        )
        g = jnp.concatenate([q, k[None], v[None]], axis=0)
        square = lax.psum(jnp.sum(jnp.square(x_own.astype(F32)), axis=-1, keepdims=True), "gx")
        lane = jnp.arange(HALF)
        square = jnp.where(lane < HALF // 2, rounded(square), square - rounded(square)).astype(BF)
        square = jnp.concatenate([square[None], jnp.zeros((3, rows, HALF), BF)], axis=0)
        g = jnp.concatenate([g, square[:, None]], axis=1)

    positions = lengths[0] + jnp.arange(rows, dtype=jnp.int32) % steps
    inverse_freq = ROPE_BASE ** (-jnp.arange(HALF, dtype=F32) * 2.0 / HEAD_DIM)
    angles = positions[:, None].astype(F32) * inverse_freq
    terms = attention(
        nx if fast else 1,
        block_table,
        lengths,
        parents,
        g,
        jnp.cos(angles),
        jnp.sin(angles),
        cache_pool,
    )
    if not fast:
        terms = terms.reshape(HEADS, rows, HEAD_DIM + PAGE)
        num = terms[..., :HEAD_DIM].transpose(1, 0, 2).reshape(nx, part, ny, head_part)
        den = terms[..., HEAD_DIM :: PAGE // 2].transpose(1, 0, 2)
        den = jnp.repeat(den, ny // HEADS, axis=1).reshape(nx, part, ny, 2)
        terms = jnp.concatenate([num, den], axis=-1).transpose(0, 2, 1, 3)
    terms = exchange_all(terms)

    contract_last = (((1,), (1,)), ((), ()))

    def project_out(t, w):
        t = jnp.sum(t.astype(F32), axis=0)
        den = t[..., head_part : head_part + 1] + t[..., -1:]
        attended = (t[..., :head_part] / den).reshape(ny * part, head_part).astype(BF)
        slices = [
            lax.dot_general(attended, w[k], contract_last, preferred_element_type=F32)
            for k in range(nx)
        ]
        return [jnp.stack([v.reshape(ny, part, width) for v in slices], axis=1).astype(BF)]

    (attn_parts,) = stage(
        fast,
        "project_out",
        project_out,
        [((ny, nx, part, width), BF)],
        terms,
        w_wide,
        specs=(None, out_spec),
    )
    attn_parts = exchange(attn_parts, "gy")

    def row_scale(v):
        square = jnp.sum(jnp.sum(v * v, axis=0), axis=-1, keepdims=True)
        return lax.rsqrt(square / D + EPSILON)[None]

    def mix(parts, others):
        attn = jnp.sum(parts.astype(F32), axis=0)
        mixed = rows_and_gain(others) + attn * row_scale(attn) * rows_and_gain(others, 1)
        ff_input = mixed * row_scale(mixed) * rows_and_gain(others, 2)
        ff_input = jnp.broadcast_to(ff_input[:, None], (nx, ny, part, width))
        last_gain = jnp.broadcast_to(rows_and_gain(others, 3), (nx, 8, width))
        return [mixed, last_gain, ff_input.astype(BF)]

    mixed, last_gain, ff_input = stage(
        fast,
        "mix",
        mix,
        [((nx, part, width), F32), ((nx, 8, width), F32), ((nx, ny, part, width), BF)],
        attn_parts,
        x_and_gains,
        specs=(None, side_spec),
    )
    ff_input = exchange_all(ff_input)

    block_shape = (ny * part, 2 * hidden_part)
    if fast:

        def gate_up(ff_ref, gate_ref, up_ref, *out_refs):
            mine = lax.axis_index("gx")
            blocks = [ff_ref[mine ^ m].astype(F32).reshape(ny * part, width) for m in range(nx)]
            flat = jnp.concatenate(blocks, axis=0).astype(BF)
            for n, w_ref in enumerate((gate_ref, up_ref)):
                sums = jnp.dot(flat, w_ref[...], preferred_element_type=F32).astype(BF)
                for m, out_ref in enumerate(out_refs):
                    out_ref[:, n * hidden_part : (n + 1) * hidden_part] = sums[
                        m * ny * part : (m + 1) * ny * part
                    ]

        blocks = run(
            gate_up, "gate_up", [(block_shape, BF)] * nx, (ff_input, w_gate, w_up), limit=24
        )
    else:
        flat = ff_input.reshape(-1, width)
        both = [jnp.dot(flat, w, preferred_element_type=F32).astype(BF) for w in (w_gate, w_up)]
        both = jnp.concatenate(both, axis=1).reshape((nx,) + block_shape)
        blocks = [lax.dynamic_index_in_dim(both, me ^ m, 0, False) for m in range(nx)]
    blocks = partner_send(blocks)

    def activate(*parts):
        total = sum(v.astype(F32) for v in parts)
        gate, up = total[:, :hidden_part], total[:, hidden_part:]
        return [(jax.nn.gelu(gate, approximate=True) * up).astype(BF)]

    (hidden,) = stage(fast, "activate", activate, [((ny * part, hidden_part), BF)], *blocks)
    hidden = lax.all_gather(hidden, "gx", axis=0)

    def project_down(h, w):
        flat = h.reshape(nx * ny * part, hidden_part)
        down = lax.dot_general(flat, w, contract_last, preferred_element_type=F32)
        return [down.reshape(nx, ny, part, width).astype(BF)]

    (down,) = stage(
        fast, "project_down", project_down, [((nx, ny, part, width), BF)], hidden, w_down.T
    )
    down = exchange_all(down)

    def finish(parts, mixed_rows, gain):
        total = jnp.sum(parts.astype(F32), axis=1)
        return mixed_rows + total * row_scale(total) * gain[:, 0:1]

    if fast:

        def finish_kernel(parts_ref, mixed_ref, gain_ref, *refs):
            mine = lax.axis_index("gx")
            whole_ref = refs[-1]
            whole_ref[...] = finish(parts_ref[...], mixed_ref[...], gain_ref[...])
            for m in range(nx):
                refs[m][...] = whole_ref[mine ^ m].astype(BF)

        blocks = run(
            finish_kernel,
            "finish",
            [((part, width), BF)] * nx,
            (down, mixed, last_gain),
            scratch=[pltpu.VMEM((nx, part, width), F32)],
        )

        def gather_rows(*refs):
            mine = lax.axis_index("gx")
            for m in range(nx):
                refs[-1][mine ^ m] = refs[m][...]

        (out,) = run(gather_rows, "gather_rows", [((nx, part, width), BF)], partner_send(blocks))
    else:
        out = exchange(finish(down, mixed, last_gain).astype(BF), "gx")
    return out.reshape(beams, steps, width)


def solution(mesh):
    return jax.shard_map(
        body,
        mesh=mesh,
        in_specs=(
            P("gy", None, "gx"),
            P(None, "gx", "gy", None),
            P("gy"),
            P("gy", None),
            P(None, "gy"),
            P(None, "gx"),
            P("gx", "gy"),
            P("gx", "gy"),
            P("gx", "gy"),
            P("gy", "gx"),
            P("gx", "gy"),
            P("gx", "gy"),
            P("gy", "gx"),
        ),
        out_specs=P("gy", None, "gx"),
        check_vma=False,
    )
```

```python
import jax
import jax.numpy as jnp
from jax import lax
from jax.experimental import pallas as pl
from jax.experimental.pallas import tpu as pltpu
from jax.sharding import PartitionSpec as P

D = 2304
HEADS = 8
KV_HEADS = 4
HEAD_DIM = 256
HALF = HEAD_DIM // 2
WINDOW = 4096
PAGE = 128
BEAM = 8
EPSILON = 1e-06
SOFT_CAP = 50.0
ROPE_BASE = 10000.0
REPS = HEADS // KV_HEADS
WIDE = HEAD_DIM + PAGE
BF = jnp.bfloat16
F32 = jnp.float32
MIB = 1024 * 1024
NT = (((1,), (1,)), ((), ()))


def run(name, kernel, outs, args, scratch=(), limit=16):
    return pl.pallas_call(
        kernel,
        out_shape=[jax.ShapeDtypeStruct(s, d) for s, d in outs],
        scratch_shapes=scratch,
        compiler_params=pltpu.CompilerParams(vmem_limit_bytes=limit * MIB),
        name=name,
    )(*args)


def exchange(values, axes):
    return lax.all_to_all(values, axes, split_axis=0, concat_axis=0, tiled=True)


def exchange_all(values):
    nx, ny = values.shape[:2]
    flat = values.reshape((nx * ny,) + values.shape[2:])
    return exchange(flat, ("gx", "gy")).reshape(values.shape)


def permute(values, axis, m):
    count = lax.axis_size(axis)
    return lax.ppermute(values, axis, [(i, i ^ m) for i in range(count)])


def trade(blocks, axis):
    return [blocks[0]] + [permute(blocks[m], axis, m) for m in range(1, len(blocks))]


def gather_gx(values):
    across = permute(values, "gx", 2)
    return [values, permute(values, "gx", 1), across, permute(across, "gx", 1)]


def weight_of(scores):
    return jnp.exp(SOFT_CAP * jnp.tanh(scores * (1.0 / SOFT_CAP)))


def high_low(column, lanes):
    shape = column.shape[:-1] + (lanes,)
    high = column.astype(BF).astype(F32)
    lane = lax.broadcasted_iota(jnp.int32, shape, len(shape) - 1)
    return jnp.where(lane < lanes // 2, high, column - high)


def row_sum(v):
    return jnp.sum(v, axis=-1, keepdims=True)


def attend(shares, squares, refs):
    table_ref, length_ref, parents_ref, cos_ref, sin_ref, pool_ref, page_ref = refs
    first_owner = lax.axis_index("gx") * pool_ref.shape[1]
    length = length_ref[0]
    first_page = jnp.maximum(length - WINDOW + 1, 0) // PAGE
    square = jnp.sum(squares.astype(F32), axis=0)
    square = square[:, 0:1] + square[:, HALF // 2 : HALF // 2 + 1]
    scale = lax.rsqrt(square / D + EPSILON)
    cos, sin = cos_ref[...], sin_ref[...]
    rows = cos.shape[0]
    reps = REPS
    steps = rows // BEAM
    slots = pool_ref.shape[1]

    def rotated(u, w):
        u, w = u.astype(F32) * scale, w.astype(F32) * scale
        return u * cos - w * sin, w * cos + u * sin

    query = []
    for rep in range(reps):
        u, w = rotated(shares(0, rep), shares(1, rep))
        query.append(jnp.concatenate([u, w], axis=1) * HEAD_DIM ** (-0.5))
    query = jnp.concatenate(query, axis=0).astype(BF)
    key_step = jnp.concatenate(rotated(shares(2, 0), shares(2, 1)), axis=1).astype(BF)
    value_step = jnp.concatenate(
        [shares(3, 0).astype(F32) * scale, shares(3, 1).astype(F32) * scale], axis=1
    ).astype(BF)

    for slot in range(slots):
        page_ref[slot] = -1

    def place(j, carry):
        slot = table_ref[0, j] - first_owner

        @pl.when((slot >= 0) & (slot < slots))
        def _():
            page_ref[slot] = j

        return carry

    lax.fori_loop(0, table_ref.shape[1], place, 0)
    lane = lax.broadcasted_iota(jnp.int32, (1, PAGE), 1)
    far = jnp.int32(2**30)
    position = jnp.concatenate(
        [
            lane + jnp.where(page_ref[s] >= 0, (first_page + page_ref[s]) * PAGE, far)
            for s in range(slots)
        ],
        axis=1,
    )
    step_of = lax.broadcasted_iota(jnp.int32, (reps * rows, 1), 0) % steps
    lower = length + step_of - (WINDOW - 1)
    seen = (position < length) & (position >= lower)
    keys = pool_ref[0].reshape(slots * PAGE, HEAD_DIM)
    values = pool_ref[1].reshape(slots * PAGE, HEAD_DIM)
    scores = lax.dot_general(query, keys, NT, preferred_element_type=F32)
    weights = jnp.where(seen, weight_of(scores), 0.0)
    den = jnp.sum(weights, axis=-1, keepdims=True)
    num = jnp.dot(weights.astype(BF), values, preferred_element_type=F32)

    shape = (reps * rows, rows)
    row = lax.broadcasted_iota(jnp.int32, shape, 0) % rows
    column = lax.broadcasted_iota(jnp.int32, shape, 1)
    row_step, column_step, column_beam = row % steps, column % steps, column // steps
    current = row // steps
    visible = jnp.zeros(shape, jnp.bool_)
    for j in range(steps - 1, -1, -1):
        if j < steps - 1:
            parent = jnp.zeros(shape, jnp.int32)
            for beam in range(BEAM):
                parent = jnp.where(current == beam, parents_ref[j, beam], parent)
            current = jnp.where(row_step > j, parent, current)
        visible = visible | ((column_step == j) & (row_step >= j) & (column_beam == current))
    visible = visible & (lax.axis_index("gx") == 0)
    scores = lax.dot_general(query, key_step, NT, preferred_element_type=F32)
    weights = jnp.where(visible, weight_of(scores), 0.0)
    den = den + jnp.sum(weights, axis=-1, keepdims=True)
    num = num + jnp.dot(weights.astype(BF), value_step, preferred_element_type=F32)

    return num, den


def attention_call(kernel, scalars, blocks, block_specs, pool, outs, out_specs, scratch):
    slots = pool.shape[1]
    smem = pl.BlockSpec(memory_space=pltpu.SMEM)
    return pl.pallas_call(
        kernel,
        grid=(KV_HEADS,),
        in_specs=[smem] * len(scalars)
        + block_specs
        + [pl.BlockSpec((2, slots, PAGE, HEAD_DIM), lambda h: (0, 0, 0, h))],
        out_specs=out_specs,
        out_shape=[jax.ShapeDtypeStruct(s, BF) for s in outs],
        scratch_shapes=[pltpu.SMEM((slots,), jnp.int32)] + scratch,
        compiler_params=pltpu.CompilerParams(vmem_limit_bytes=60 * MIB),
        name="attention",
    )(*scalars, *blocks, pool)


def whole_block(shape):
    return pl.BlockSpec(shape, lambda h: (0,) * len(shape))


def rope_tables(lengths, rows, steps):
    positions = lengths[0] + jnp.arange(rows, dtype=jnp.int32) % steps
    inverse_freq = ROPE_BASE ** (-jnp.arange(HALF, dtype=F32) * 2.0 / HEAD_DIM)
    angles = positions[:, None].astype(F32) * inverse_freq
    return jnp.cos(angles), jnp.sin(angles)


def body_permutes(
    inputs,
    cache_pool,
    lengths,
    block_table,
    parents,
    norm_gains,
    w_query,
    w_key,
    w_value,
    w_out,
    w_gate,
    w_up,
    w_down,
):
    beams, steps, width = inputs.shape
    nx, ny = lax.axis_size("gx"), lax.axis_size("gy")
    rows = beams * steps
    part = rows // nx
    all_rows = ny * rows
    share_rows = all_rows // nx
    hidden = w_gate.shape[1]
    x_own = inputs.reshape(rows, width)
    cos, sin = rope_tables(lengths, rows, steps)

    def my(axis):
        return lax.axis_index(axis)

    def project(*refs):
        x_refs, (gain_ref, q_ref, k_ref, v_ref, z0_ref, z2_ref, z13_ref, held) = refs[:ny], refs[ny:]
        gain = 1.0 + gain_ref[0:1]
        flat = jnp.concatenate([(r[...].astype(F32) * gain).astype(BF) for r in x_refs], axis=0)
        query = jnp.dot(flat, q_ref[...], preferred_element_type=F32).astype(BF)
        held[0], held[1] = query[:, :HALF], query[:, HALF:]
        held[2] = jnp.dot(flat, k_ref[...], preferred_element_type=F32).astype(BF)
        held[3] = jnp.dot(flat, v_ref[...], preferred_element_type=F32).astype(BF)
        me = my("gx")
        z0_ref[...], z2_ref[...] = held[me], held[me ^ 2]
        z13_ref[0], z13_ref[1] = held[me ^ 1], held[me ^ 3]

    x_blocks = trade([x_own] * ny, "gy")
    shape = (all_rows, HALF)
    z0, z2, z13 = run(
        "project",
        project,
        [(shape, BF), (shape, BF), ((2,) + shape, BF)],
        (*x_blocks, norm_gains, w_query, w_key, w_value),
        scratch=[pltpu.VMEM((nx,) + shape, BF)],
    )
    z13 = permute(z13, "gx", 1)

    def pair_sum(z_ref, from_pair_ref, out_ref):
        total = z_ref[...].astype(F32) + from_pair_ref[1].astype(F32)
        out_ref[...] = total.astype(BF)

    (z2,) = run("pair_sum", pair_sum, [(shape, BF)], (z2, z13))
    z2 = permute(z2, "gx", 2)

    def share_sum(z0_ref, z13_ref, z2_ref, *out_refs):
        total = z0_ref[...].astype(F32) + z13_ref[0].astype(F32) + z2_ref[...].astype(F32)
        for m, out_ref in enumerate(out_refs):
            out_ref[...] = total[m * rows : (m + 1) * rows].astype(BF)

    blocks = run("share_sum", share_sum, [((rows, HALF), BF)] * ny, (z0, z13, z2))
    blocks = trade(blocks, "gy")

    def pack_shares(*refs):
        x = refs[ny][...].astype(F32)
        me = my("gy")
        for m in range(ny):
            refs[-1][me ^ m] = refs[m][...]
        refs[-1][ny] = high_low(row_sum(x * x), HALF).astype(BF)

    (shares,) = run(
        "pack_shares", pack_shares, [((ny + 1, rows, HALF), BF)], (*blocks, x_own)
    )
    shares = gather_gx(shares)

    def attention(*refs):
        table, length, parent, a0, a1, a2, a3, cos_ref, sin_ref, pool_ref = refs[:10]
        z0_ref, z2_ref, z13_ref, page_ref, held, num_held, den_held = refs[10:]
        me = my("gx")
        h = pl.program_id(0)

        @pl.when(h == 0)
        def _():
            for n, ref in enumerate((a0, a1, a2, a3)):
                held[me ^ n] = ref[...]

        num, den = attend(
            lambda share, which: held[share, 2 * h + which],
            held[:, ny],
            (table, length, parent, cos_ref, sin_ref, pool_ref, page_ref),
        )
        num_held[...] = num.reshape(REPS, nx, part, HEAD_DIM)
        den_held[...] = high_low(den, PAGE).reshape(REPS, nx, part, PAGE)
        for rep in range(REPS):
            for n, out in enumerate((z0_ref, z13_ref.at[0], z2_ref, z13_ref.at[1])):
                out[rep, :, 0:HEAD_DIM] = num_held[rep, me ^ n].astype(BF)
                out[rep, :, HEAD_DIM:] = den_held[rep, me ^ n].astype(BF)

    shape = (HEADS, part, WIDE)
    half_spec = pl.BlockSpec((REPS, part, WIDE), lambda h: (h, 0, 0))
    z0, z2, z13 = attention_call(
        attention,
        (block_table, lengths, parents),
        (*shares, cos, sin),
        [whole_block(shares[0].shape)] * nx + [whole_block(cos.shape)] * 2,
        cache_pool,
        [shape, shape, (2,) + shape],
        [
            half_spec,
            half_spec,
            pl.BlockSpec((2, REPS, part, WIDE), lambda h: (0, h, 0, 0)),
        ],
        [
            pltpu.VMEM((nx,) + shares[0].shape, BF),
            pltpu.VMEM((REPS, nx, part, HEAD_DIM), F32),
            pltpu.VMEM((REPS, nx, part, PAGE), F32),
        ],
    )
    z13 = permute(z13, "gx", 1)

    def pair_terms(z_ref, from_pair_ref, out_ref):
        total = z_ref[...].astype(F32) + from_pair_ref[1].astype(F32)
        den = total[..., HEAD_DIM : HEAD_DIM + 1] + total[..., WIDE - 1 :]
        out_ref[..., 0:HEAD_DIM] = total[..., 0:HEAD_DIM].astype(BF)
        out_ref[..., HEAD_DIM:] = high_low(den, PAGE).astype(BF)

    (z2,) = run("pair_terms", pair_terms, [(shape, BF)], (z2, z13))
    z2 = permute(z2, "gx", 2)

    def divide(z0_ref, z13_ref, z2_ref, *refs):
        total = z0_ref[...].astype(F32) + z13_ref[0].astype(F32) + z2_ref[...].astype(F32)
        den = total[..., HEAD_DIM : HEAD_DIM + 1] + total[..., WIDE - 1 :]
        held = refs[ny]
        held[...] = total[..., 0:HEAD_DIM] / den
        me = my("gy")
        for m in range(ny):
            refs[m][...] = held[me ^ m].astype(BF)

    blocks = run(
        "divide",
        divide,
        [((part, HEAD_DIM), BF)] * ny,
        (z0, z13, z2),
        scratch=[pltpu.VMEM((HEADS, part, HEAD_DIM), F32)],
    )
    blocks = trade(blocks, "gy")

    def pack_heads(*refs):
        for m in range(ny):
            refs[ny][m] = refs[m][...]

    (attended,) = run("pack_heads", pack_heads, [((ny, part, HEAD_DIM), BF)], blocks)
    attended = gather_gx(attended)

    def project_out(*refs):
        w_ref, held = refs[nx], refs[-1]
        me = my("gx")
        for n in range(nx):
            held[:, me ^ n] = refs[n][...].astype(F32)
        flat = held[...].reshape(all_rows, HEAD_DIM).astype(BF)
        sums = lax.dot_general(flat, w_ref[...], NT, preferred_element_type=F32).astype(BF)
        for m in range(ny):
            refs[nx + 1 + m][...] = sums[m * rows : (m + 1) * rows]

    blocks = run(
        "project_out",
        project_out,
        [((rows, width), BF)] * ny,
        (*attended, w_out.T),
        scratch=[pltpu.VMEM((ny, nx, part, HEAD_DIM), F32)],
    )
    blocks = trade(blocks, "gy")

    def attn_sum(*refs):
        x_ref, gain_ref, attn_ref, sums_ref = refs[ny:]
        attn = sum(r[...].astype(F32) for r in refs[:ny])
        attn_ref[...] = attn
        x = x_ref[...].astype(F32)
        scaled = attn * (1.0 + gain_ref[1:2])
        lane = lax.broadcasted_iota(jnp.int32, (rows, PAGE), 1)
        sums = jnp.zeros((rows, PAGE), F32)
        for n, terms in enumerate((attn * attn, scaled * scaled, x * scaled, x * x)):
            sums = jnp.where(lane == n, row_sum(terms), sums)
        sums_ref[...] = sums

    attn, sums = run(
        "attn_sum",
        attn_sum,
        [((rows, width), F32), ((rows, PAGE), F32)],
        (*blocks, x_own, norm_gains),
    )
    sums = trade([sums] * nx, "gx")

    def mix(*refs):
        attn_ref, x_ref, gain_ref, mixed_ref, ff_ref = refs[nx:]
        total = sum(r[...] for r in refs[:nx])
        plain, scaled, cross, square = (total[:, n : n + 1] for n in range(4))
        scale = lax.rsqrt(plain / D + EPSILON)
        mixed = x_ref[...].astype(F32) + attn_ref[...] * scale * (1.0 + gain_ref[1:2])
        square = jnp.maximum(square + 2.0 * scale * cross + scale * scale * scaled, 0.0)
        mixed_ref[...] = mixed
        scale = lax.rsqrt(square / D + EPSILON)
        ff_ref[...] = (mixed * scale * (1.0 + gain_ref[2:3])).astype(BF)

    mixed, ff_input = run(
        "mix",
        mix,
        [((rows, width), F32), ((rows, width), BF)],
        (*sums, attn, x_own, norm_gains),
    )
    blocks = trade([ff_input] * ny, "gy")

    def gate_up(*refs):
        w_refs, z0_ref, z2_ref, z13_ref, held = refs[ny : ny + 2], *refs[ny + 2 :]
        me = my("gx")
        for m in range(ny):
            held[m // 2, m % 2 * rows : (m % 2 + 1) * rows] = refs[m][...]
        flat = jnp.concatenate([held[me ^ n] for n in range(nx)], axis=0)
        for n, w_ref in enumerate(w_refs):
            sums = jnp.dot(flat, w_ref[...], preferred_element_type=F32).astype(BF)
            here = pl.ds(n * hidden, hidden)
            for p, out in enumerate((z0_ref, z13_ref.at[0], z2_ref, z13_ref.at[1])):
                out[:, here] = sums[p * share_rows : (p + 1) * share_rows]

    shape = (share_rows, 2 * hidden)
    z0, z2, z13 = run(
        "gate_up",
        gate_up,
        [(shape, BF), (shape, BF), ((2,) + shape, BF)],
        (*blocks, w_gate, w_up),
        scratch=[pltpu.VMEM((nx, share_rows, width), BF)],
        limit=24,
    )
    z13 = permute(z13, "gx", 1)
    (z2,) = run("pair_sum_ff", pair_sum, [(shape, BF)], (z2, z13))
    z2 = permute(z2, "gx", 2)

    def activate(z0_ref, z13_ref, z2_ref, out_ref):
        total = z0_ref[...].astype(F32) + z13_ref[0].astype(F32) + z2_ref[...].astype(F32)
        gate, up = total[:, :hidden], total[:, hidden:]
        out_ref[...] = (jax.nn.gelu(gate, approximate=True) * up).astype(BF)

    (blocks,) = run("activate", activate, [((share_rows, hidden), BF)], (z0, z13, z2))
    blocks = gather_gx(blocks)

    def project_down(*refs):
        w_ref, held = refs[nx], refs[-1]
        me = my("gx")
        flat = jnp.concatenate([r[...] for r in refs[:nx]], axis=0)
        sums = lax.dot_general(flat, w_ref[...], NT, preferred_element_type=F32)
        held[...] = sums.reshape(nx, share_rows, width).astype(BF)
        for m in range(ny):
            refs[nx + 1 + m][...] = held[me ^ (m // 2), m % 2 * rows : (m % 2 + 1) * rows]

    blocks = run(
        "project_down",
        project_down,
        [((rows, width), BF)] * ny,
        (*blocks, w_down.T),
        scratch=[pltpu.VMEM((nx, share_rows, width), BF)],
    )
    blocks = trade(blocks, "gy")

    def down_sum(*refs):
        down = sum(r[...].astype(F32) for r in refs[:ny])
        refs[ny][...] = down
        refs[ny + 1][...] = jnp.broadcast_to(row_sum(down * down), (rows, PAGE))

    down, sums = run(
        "down_sum", down_sum, [((rows, width), F32), ((rows, PAGE), F32)], blocks
    )
    sums = trade([sums] * nx, "gx")

    def finish(*refs):
        down_ref, mixed_ref, gain_ref, out_ref = refs[nx:]
        square = sum(r[...] for r in refs[:nx])[:, 0:1]
        scale = lax.rsqrt(square / D + EPSILON)
        out = mixed_ref[...] + down_ref[...] * scale * (1.0 + gain_ref[3:4])
        out_ref[...] = out.astype(BF)

    (out,) = run(
        "finish", finish, [((rows, width), BF)], (*sums, down, mixed, norm_gains)
    )
    return out.reshape(beams, steps, width)


def body_general(
    inputs,
    cache_pool,
    lengths,
    block_table,
    parents,
    norm_gains,
    w_query,
    w_key,
    w_value,
    w_out,
    w_gate,
    w_up,
    w_down,
):
    beams, steps, width = inputs.shape
    nx, ny = lax.axis_size("gx"), lax.axis_size("gy")
    rows = beams * steps
    part = rows // nx
    head_part = w_out.shape[0]
    hidden_part = w_gate.shape[1]
    query_part, key_part = w_query.shape[1], w_key.shape[1]
    columns = query_part + 2 * key_part
    share = columns // nx
    x_own = inputs.reshape(rows, width)
    me = lax.axis_index("gx")

    x_all = exchange(jnp.broadcast_to(x_own[None], (ny, rows, width)), "gy")
    flat = (x_all.astype(F32) * (1.0 + norm_gains[0:1])).astype(BF).reshape(ny * rows, width)
    sums = [jnp.dot(flat, w, preferred_element_type=F32) for w in (w_query, w_key, w_value)]
    sums = jnp.concatenate(sums, axis=1).reshape(ny, rows, nx, share)
    received = exchange_all(sums.transpose(2, 0, 1, 3).astype(BF))
    shares = jnp.sum(received.astype(F32), axis=0).astype(BF)
    every = lax.all_gather(shares, "gx", axis=0)
    every = every.transpose(2, 1, 0, 3).reshape(rows, ny, columns)
    q = every[..., :query_part].reshape(rows, HEADS, 2, HALF).transpose(2, 1, 0, 3)
    k, v = (
        every[..., start : start + key_part].reshape(rows, 2 * KV_HEADS, HALF).transpose(1, 0, 2)
        for start in (query_part, query_part + key_part)
    )
    shares = jnp.concatenate([q, k[None], v[None]], axis=0)
    square = lax.psum(row_sum(jnp.square(x_own.astype(F32))), "gx")
    high = lax.reduce_precision(square, 8, 7)
    squares = jnp.where(jnp.arange(HALF) < HALF // 2, high, square - high).astype(BF)[None]
    cos, sin = rope_tables(lengths, rows, steps)

    def attention(*refs):
        table, length, parent, g_ref, square_ref, cos_ref, sin_ref, pool_ref = refs[:8]
        out_ref, page_ref = refs[8:]
        num, den = attend(
            lambda share, which: g_ref[share, which],
            square_ref[...],
            (table, length, parent, cos_ref, sin_ref, pool_ref, page_ref),
        )
        den = high_low(den, PAGE)
        for rep in range(REPS):
            here = slice(rep * rows, (rep + 1) * rows)
            out_ref[rep, :, 0:HEAD_DIM] = num[here].astype(BF)
            out_ref[rep, :, HEAD_DIM:] = den[here].astype(BF)

    (terms,) = attention_call(
        attention,
        (block_table, lengths, parents),
        (shares, squares, cos, sin),
        [
            pl.BlockSpec((4, 2, rows, HALF), lambda h: (0, h, 0, 0)),
            whole_block(squares.shape),
            whole_block(cos.shape),
            whole_block(sin.shape),
        ],
        cache_pool,
        [(HEADS, rows, WIDE)],
        [pl.BlockSpec((REPS, rows, WIDE), lambda h: (h, 0, 0))],
        [],
    )
    num = terms[..., :HEAD_DIM].transpose(1, 0, 2).reshape(nx, part, ny, head_part)
    den = terms[..., HEAD_DIM :: PAGE // 2].transpose(1, 0, 2)
    den = jnp.repeat(den, ny // HEADS, axis=1).reshape(nx, part, ny, 2)
    terms = exchange_all(jnp.concatenate([num, den], axis=-1).transpose(0, 2, 1, 3))

    w_wide = lax.all_gather(w_out, "gx", axis=1, tiled=True)
    x_wide = lax.all_gather(x_own, "gx", axis=1, tiled=True)
    x_rows = lax.dynamic_slice_in_dim(x_wide, me * part, part, 0).astype(F32)
    gains = 1.0 + lax.all_gather(norm_gains, "gx", axis=1, tiled=True)

    def scaled(v, gain):
        return v * lax.rsqrt(row_sum(v * v) / D + EPSILON) * gain

    terms = jnp.sum(terms.astype(F32), axis=0)
    den = terms[..., head_part : head_part + 1] + terms[..., -1:]
    attended = (terms[..., :head_part] / den).reshape(ny * part, head_part).astype(BF)
    attn = jnp.dot(attended, w_wide, preferred_element_type=F32).astype(BF)
    attn = exchange(attn.reshape(ny, part, D), "gy").astype(F32).sum(axis=0)
    mixed = x_rows + scaled(attn, gains[1])
    ff_input = scaled(mixed, gains[2]).astype(BF)
    ff_input = ff_input.reshape(part, nx, width).transpose(1, 0, 2)[:, None]
    ff_input = exchange_all(jnp.broadcast_to(ff_input, (nx, ny, part, width)))

    flat = ff_input.reshape(-1, width)
    both = [jnp.dot(flat, w, preferred_element_type=F32).astype(BF) for w in (w_gate, w_up)]
    both = jnp.stack(both, axis=1).reshape(nx, ny * part, 2, hidden_part)
    both = jnp.sum(exchange(both, "gx").astype(F32), axis=0)
    hidden = (jax.nn.gelu(both[:, 0], approximate=True) * both[:, 1]).astype(BF)
    hidden = lax.all_gather(hidden, "gx", axis=0, tiled=True)
    down = jnp.dot(hidden, w_down, preferred_element_type=F32).astype(BF)
    down = exchange_all(down.reshape(nx, ny, part, width)).astype(F32).sum(axis=1)
    down = down.transpose(1, 0, 2).reshape(part, D)
    out = (mixed + scaled(down, gains[3])).astype(BF)
    out = exchange(out.reshape(part, nx, width).transpose(1, 0, 2), "gx")
    return out.reshape(beams, steps, width)


def solution(mesh):
    sizes = dict(mesh.shape)
    fits = sizes["gx"] == 4 and sizes["gy"] == HEADS
    return jax.shard_map(
        body_permutes if fits else body_general,
        mesh=mesh,
        in_specs=(
            P("gy", None, "gx"),
            P(None, "gx", "gy", None),
            P("gy"),
            P("gy", None),
            P(None, "gy"),
            P(None, "gx"),
            P("gx", "gy"),
            P("gx", "gy"),
            P("gx", "gy"),
            P("gy", "gx"),
            P("gx", "gy"),
            P("gx", "gy"),
            P("gy", "gx"),
        ),
        out_specs=P("gy", None, "gx"),
        check_vma=False,
    )
```

```python
import jax
import jax.numpy as jnp
from jax import lax
from jax.experimental import pallas as pl
from jax.experimental.pallas import tpu as pltpu
from jax.sharding import PartitionSpec as P

D = 2304
HEADS = 8
KV_HEADS = 4
HEAD_DIM = 256
HALF = HEAD_DIM // 2
WINDOW = 4096
PAGE = 128
BEAM = 8
EPSILON = 1e-06
SOFT_CAP = 50.0
ROPE_BASE = 10000.0
REPS = HEADS // KV_HEADS
WIDE = HEAD_DIM + PAGE
BF = jnp.bfloat16
F32 = jnp.float32
MIB = 1024 * 1024
NT = (((1,), (1,)), ((), ()))


def run(name, kernel, outs, args, scratch=(), limit=16):
    return pl.pallas_call(
        kernel,
        out_shape=[jax.ShapeDtypeStruct(s, d) for s, d in outs],
        scratch_shapes=scratch,
        compiler_params=pltpu.CompilerParams(vmem_limit_bytes=limit * MIB),
        name=name,
    )(*args)


def exchange(values, axes):
    return lax.all_to_all(values, axes, split_axis=0, concat_axis=0, tiled=True)


def exchange_all(values):
    nx, ny = values.shape[:2]
    flat = values.reshape((nx * ny,) + values.shape[2:])
    return exchange(flat, ("gx", "gy")).reshape(values.shape)


def permute(values, axis, m):
    count = lax.axis_size(axis)
    return lax.ppermute(values, axis, [(i, i ^ m) for i in range(count)])


def trade(blocks, axis):
    return [blocks[0]] + [permute(blocks[m], axis, m) for m in range(1, len(blocks))]


def gather_gx(values):
    across = permute(values, "gx", 2)
    return [values, permute(values, "gx", 1), across, permute(across, "gx", 1)]


def weight_of(scores):
    return jnp.exp(SOFT_CAP * jnp.tanh(scores * (1.0 / SOFT_CAP)))


def high_low(column, lanes):
    shape = column.shape[:-1] + (lanes,)
    high = column.astype(BF).astype(F32)
    lane = lax.broadcasted_iota(jnp.int32, shape, len(shape) - 1)
    return jnp.where(lane < lanes // 2, high, column - high)


def row_sum(v):
    return jnp.sum(v, axis=-1, keepdims=True)


def attend(shares, squares, refs):
    table_ref, length_ref, parents_ref, cos_ref, sin_ref, pool_ref, page_ref = refs
    first_owner = lax.axis_index("gx") * pool_ref.shape[1]
    length = length_ref[0]
    first_page = jnp.maximum(length - WINDOW + 1, 0) // PAGE
    square = jnp.sum(squares.astype(F32), axis=0)
    square = square[:, 0:1] + square[:, HALF // 2 : HALF // 2 + 1]
    scale = lax.rsqrt(square / D + EPSILON)
    cos, sin = cos_ref[...], sin_ref[...]
    rows = cos.shape[0]
    reps = REPS
    steps = rows // BEAM
    slots = pool_ref.shape[1]

    def rotated(u, w):
        u, w = u.astype(F32) * scale, w.astype(F32) * scale
        return u * cos - w * sin, w * cos + u * sin

    query = []
    for rep in range(reps):
        u, w = rotated(shares(0, rep), shares(1, rep))
        query.append(jnp.concatenate([u, w], axis=1) * HEAD_DIM ** (-0.5))
    query = jnp.concatenate(query, axis=0).astype(BF)
    key_step = jnp.concatenate(rotated(shares(2, 0), shares(2, 1)), axis=1).astype(BF)
    value_step = jnp.concatenate(
        [shares(3, 0).astype(F32) * scale, shares(3, 1).astype(F32) * scale], axis=1
    ).astype(BF)

    for slot in range(slots):
        page_ref[slot] = -1

    def place(j, carry):
        slot = table_ref[0, j] - first_owner

        @pl.when((slot >= 0) & (slot < slots))
        def _():
            page_ref[slot] = j

        return carry

    lax.fori_loop(0, table_ref.shape[1], place, 0)
    lane = lax.broadcasted_iota(jnp.int32, (1, PAGE), 1)
    far = jnp.int32(2**30)
    position = jnp.concatenate(
        [
            lane + jnp.where(page_ref[s] >= 0, (first_page + page_ref[s]) * PAGE, far)
            for s in range(slots)
        ],
        axis=1,
    )
    step_of = lax.broadcasted_iota(jnp.int32, (reps * rows, 1), 0) % steps
    lower = length + step_of - (WINDOW - 1)
    seen = (position < length) & (position >= lower)
    keys = pool_ref[0].reshape(slots * PAGE, HEAD_DIM)
    values = pool_ref[1].reshape(slots * PAGE, HEAD_DIM)
    scores = lax.dot_general(query, keys, NT, preferred_element_type=F32)
    weights = jnp.where(seen, weight_of(scores), 0.0)
    den = jnp.sum(weights, axis=-1, keepdims=True)
    num = jnp.dot(weights.astype(BF), values, preferred_element_type=F32)

    shape = (reps * rows, rows)
    row = lax.broadcasted_iota(jnp.int32, shape, 0) % rows
    column = lax.broadcasted_iota(jnp.int32, shape, 1)
    row_step, column_step, column_beam = row % steps, column % steps, column // steps
    current = row // steps
    visible = jnp.zeros(shape, jnp.bool_)
    for j in range(steps - 1, -1, -1):
        if j < steps - 1:
            parent = jnp.zeros(shape, jnp.int32)
            for beam in range(BEAM):
                parent = jnp.where(current == beam, parents_ref[j, beam], parent)
            current = jnp.where(row_step > j, parent, current)
        visible = visible | ((column_step == j) & (row_step >= j) & (column_beam == current))
    visible = visible & (lax.axis_index("gx") == 0)
    scores = lax.dot_general(query, key_step, NT, preferred_element_type=F32)
    weights = jnp.where(visible, weight_of(scores), 0.0)
    den = den + jnp.sum(weights, axis=-1, keepdims=True)
    num = num + jnp.dot(weights.astype(BF), value_step, preferred_element_type=F32)

    return num, den


def attention_call(kernel, scalars, blocks, block_specs, pool, outs, out_specs, scratch):
    slots = pool.shape[1]
    smem = pl.BlockSpec(memory_space=pltpu.SMEM)
    return pl.pallas_call(
        kernel,
        grid=(KV_HEADS,),
        in_specs=[smem] * len(scalars)
        + block_specs
        + [pl.BlockSpec((2, slots, PAGE, HEAD_DIM), lambda h: (0, 0, 0, h))],
        out_specs=out_specs,
        out_shape=[jax.ShapeDtypeStruct(s, BF) for s in outs],
        scratch_shapes=[pltpu.SMEM((slots,), jnp.int32)] + scratch,
        compiler_params=pltpu.CompilerParams(vmem_limit_bytes=58 * MIB),
        name="attention",
    )(*scalars, *blocks, pool)


def whole_block(shape):
    return pl.BlockSpec(shape, lambda h: (0,) * len(shape))


def rope_tables(lengths, rows, steps):
    positions = lengths[0] + jnp.arange(rows, dtype=jnp.int32) % steps
    inverse_freq = ROPE_BASE ** (-jnp.arange(HALF, dtype=F32) * 2.0 / HEAD_DIM)
    angles = positions[:, None].astype(F32) * inverse_freq
    return jnp.cos(angles), jnp.sin(angles)


def body_permutes(
    inputs,
    cache_pool,
    lengths,
    block_table,
    parents,
    norm_gains,
    w_query,
    w_key,
    w_value,
    w_out,
    w_gate,
    w_up,
    w_down,
):
    beams, steps, width = inputs.shape
    nx, ny = lax.axis_size("gx"), lax.axis_size("gy")
    rows = beams * steps
    half = rows // 2
    all_rows = ny * rows
    share_rows = all_rows // nx
    hidden = w_gate.shape[1]
    cos, sin = rope_tables(lengths, rows, steps)
    w_wide = lax.all_gather(w_out.T, "gy", axis=0)

    def my(axis):
        return lax.axis_index(axis)

    def spread(x_ref, own_ref, out_ref):
        own = x_ref[...].astype(F32).reshape(rows, width).astype(BF)
        own_ref[...] = own
        for m in range(ny):
            out_ref[m] = own

    x_own, x_all = run(
        "spread", spread, [((rows, width), BF), ((ny, rows, width), BF)], (inputs,)
    )
    x_all = exchange(x_all, "gy")

    def project(x_ref, gain_ref, q_ref, k_ref, v_ref, z0_ref, z2_ref, z13_ref, held):
        x = x_ref[...].reshape(all_rows, width).astype(F32)
        flat = (x * (1.0 + gain_ref[0:1])).astype(BF)
        query = jnp.dot(flat, q_ref[...], preferred_element_type=F32).astype(BF)
        held[0], held[1] = query[:, :HALF], query[:, HALF:]
        held[2] = jnp.dot(flat, k_ref[...], preferred_element_type=F32).astype(BF)
        held[3] = jnp.dot(flat, v_ref[...], preferred_element_type=F32).astype(BF)
        me = my("gx")
        z0_ref[...], z2_ref[...] = held[me], held[me ^ 2]
        z13_ref[0], z13_ref[1] = held[me ^ 1], held[me ^ 3]

    shape = (all_rows, HALF)
    z0, z2, z13 = run(
        "project",
        project,
        [(shape, BF), (shape, BF), ((2,) + shape, BF)],
        (x_all, norm_gains, w_query, w_key, w_value),
        scratch=[pltpu.VMEM((nx,) + shape, BF)],
    )
    z13 = permute(z13, "gx", 1)

    def pair_sum(z_ref, from_pair_ref, out_ref):
        total = z_ref[...].astype(F32) + from_pair_ref[1].astype(F32)
        out_ref[...] = total.astype(BF)

    (z2,) = run("pair_sum", pair_sum, [(shape, BF)], (z2, z13))
    z2 = permute(z2, "gx", 2)

    def share_sum(z0_ref, z13_ref, z2_ref, out_ref):
        total = z0_ref[...].astype(F32) + z13_ref[0].astype(F32) + z2_ref[...].astype(F32)
        out_ref[...] = total.reshape(ny, rows, HALF).astype(BF)

    (shares,) = run("share_sum", share_sum, [((ny, rows, HALF), BF)], (z0, z13, z2))
    shares = exchange(shares, "gy")

    def pack_shares(share_ref, x_ref, out_ref):
        x = x_ref[...].astype(F32)
        out_ref[0:ny] = share_ref[...]
        out_ref[ny] = high_low(row_sum(x * x), HALF).astype(BF)

    (shares,) = run("pack_shares", pack_shares, [((ny + 1, rows, HALF), BF)], (shares, x_own))
    shares = gather_gx(shares)

    def attention(*refs):
        table, length, parent, a0, a1, a2, a3, cos_ref, sin_ref, pool_ref = refs[:10]
        own_ref, pair_ref, page_ref, held, num_held, den_held = refs[10:]
        me = my("gx")
        h = pl.program_id(0)

        @pl.when(h == 0)
        def _():
            for n, ref in enumerate((a0, a1, a2, a3)):
                held[me ^ n] = ref[...]

        num, den = attend(
            lambda share, which: held[share, 2 * h + which],
            held[:, ny],
            (table, length, parent, cos_ref, sin_ref, pool_ref, page_ref),
        )
        num_held[...] = num.reshape(REPS, 2, half, HEAD_DIM)
        den_held[...] = high_low(den, PAGE).reshape(REPS, 2, half, PAGE)
        core = me & 1
        for rep in range(REPS):
            for n, out in enumerate((own_ref, pair_ref)):
                out[rep, :, 0:HEAD_DIM] = num_held[rep, core ^ n].astype(BF)
                out[rep, :, HEAD_DIM:] = den_held[rep, core ^ n].astype(BF)

    shape = (HEADS, half, WIDE)
    half_spec = pl.BlockSpec((REPS, half, WIDE), lambda h: (h, 0, 0))
    own, pair = attention_call(
        attention,
        (block_table, lengths, parents),
        (*shares, cos, sin),
        [whole_block(shares[0].shape)] * nx + [whole_block(cos.shape)] * 2,
        cache_pool,
        [shape, shape],
        [half_spec, half_spec],
        [
            pltpu.VMEM((nx,) + shares[0].shape, BF),
            pltpu.VMEM((REPS, 2, half, HEAD_DIM), F32),
            pltpu.VMEM((REPS, 2, half, PAGE), F32),
        ],
    )
    pair = permute(pair, "gx", 1)

    def pair_terms(own_ref, pair_ref, out_ref):
        total = own_ref[...].astype(F32) + pair_ref[...].astype(F32)
        den = total[..., HEAD_DIM : HEAD_DIM + 1] + total[..., WIDE - 1 :]
        out_ref[..., 0:HEAD_DIM] = total[..., 0:HEAD_DIM].astype(BF)
        out_ref[..., HEAD_DIM:] = high_low(den, PAGE).astype(BF)

    (own,) = run("pair_terms", pair_terms, [(shape, BF)], (own, pair))
    across = permute(own, "gx", 2)

    def divide(own_ref, across_ref, out_ref):
        total = own_ref[...].astype(F32) + across_ref[...].astype(F32)
        den = total[..., HEAD_DIM : HEAD_DIM + 1] + total[..., WIDE - 1 :]
        out_ref[...] = (total[..., 0:HEAD_DIM] / den).astype(BF)

    (attended,) = run("divide", divide, [((HEADS, half, HEAD_DIM), BF)], (own, across))
    others = permute(attended, "gx", 1)

    def project_out(own_ref, other_ref, w_ref, x_ref, gain_ref, attn_ref, sums_ref, held):
        core = my("gx") & 1
        held[core], held[1 - core] = own_ref[...], other_ref[...]
        attn = jnp.zeros((rows, width), F32)
        for head in range(HEADS):
            flat = jnp.concatenate([held[0, head], held[1, head]], axis=0)
            attn = attn + lax.dot_general(flat, w_ref[head], NT, preferred_element_type=F32)
        attn_ref[...] = attn
        x = x_ref[...].astype(F32)
        scaled = attn * (1.0 + gain_ref[1:2])
        lane = lax.broadcasted_iota(jnp.int32, (rows, PAGE), 1)
        sums = jnp.zeros((rows, PAGE), F32)
        for n, terms in enumerate((attn * attn, scaled * scaled, x * scaled, x * x)):
            sums = jnp.where(lane == n, row_sum(terms), sums)
        sums_ref[...] = sums

    attn, sums = run(
        "project_out",
        project_out,
        [((rows, width), F32), ((rows, PAGE), F32)],
        (attended, others, w_wide, x_own, norm_gains),
        scratch=[pltpu.VMEM((2, HEADS, half, HEAD_DIM), BF)],
    )
    sums = trade([sums] * nx, "gx")

    def mix(*refs):
        attn_ref, x_ref, gain_ref, mixed_ref, ff_ref = refs[nx:]
        total = sum(r[...] for r in refs[:nx])
        plain, scaled, cross, square = (total[:, n : n + 1] for n in range(4))
        scale = lax.rsqrt(plain / D + EPSILON)
        mixed = x_ref[...].astype(F32) + attn_ref[...] * scale * (1.0 + gain_ref[1:2])
        square = jnp.maximum(square + 2.0 * scale * cross + scale * scale * scaled, 0.0)
        mixed_ref[...] = mixed
        scale = lax.rsqrt(square / D + EPSILON)
        ff_input = (mixed * scale * (1.0 + gain_ref[2:3])).astype(BF)
        for m in range(ny):
            ff_ref[m] = ff_input

    mixed, ff_input = run(
        "mix",
        mix,
        [((rows, width), F32), ((ny, rows, width), BF)],
        (*sums, attn, x_own, norm_gains),
    )
    ff_input = exchange(ff_input, "gy")

    groups = ny // nx

    def gate_up(ff_ref, gate_ref, up_ref, z0_ref, z2_ref, z13_ref):
        me = my("gx")
        flat = [
            ff_ref[pl.ds((me ^ n) * groups, groups)].reshape(share_rows, width) for n in range(nx)
        ]
        flat = jnp.concatenate(flat, axis=0)
        w_refs = gate_ref, up_ref
        for n, w_ref in enumerate(w_refs):
            sums = jnp.dot(flat, w_ref[...], preferred_element_type=F32).astype(BF)
            here = pl.ds(n * hidden, hidden)
            for p, out in enumerate((z0_ref, z13_ref.at[0], z2_ref, z13_ref.at[1])):
                out[:, here] = sums[p * share_rows : (p + 1) * share_rows]

    shape = (share_rows, 2 * hidden)
    z0, z2, z13 = run(
        "gate_up",
        gate_up,
        [(shape, BF), (shape, BF), ((2,) + shape, BF)],
        (ff_input, w_gate, w_up),
        limit=24,
    )
    z13 = permute(z13, "gx", 1)
    (z2,) = run("pair_sum_ff", pair_sum, [(shape, BF)], (z2, z13))
    z2 = permute(z2, "gx", 2)

    def activate(z0_ref, z13_ref, z2_ref, out_ref):
        total = z0_ref[...].astype(F32) + z13_ref[0].astype(F32) + z2_ref[...].astype(F32)
        gate, up = total[:, :hidden], total[:, hidden:]
        out_ref[...] = (jax.nn.gelu(gate, approximate=True) * up).astype(BF)

    (blocks,) = run("activate", activate, [((share_rows, hidden), BF)], (z0, z13, z2))
    blocks = gather_gx(blocks)

    def project_down(*refs):
        w_ref, out_ref = refs[nx:]
        me = my("gx")
        flat = jnp.concatenate([r[...] for r in refs[:nx]], axis=0)
        sums = lax.dot_general(flat, w_ref[...], NT, preferred_element_type=F32)
        sums = sums.reshape(nx, groups, rows, width).astype(BF)
        for n in range(nx):
            out_ref[pl.ds((me ^ n) * groups, groups)] = sums[n]

    (down,) = run(
        "project_down", project_down, [((ny, rows, width), BF)], (*blocks, w_down.T)
    )
    down = exchange(down, "gy")

    def down_sum(parts_ref, down_ref, sums_ref):
        down = jnp.sum(parts_ref[...].astype(F32), axis=0)
        down_ref[...] = down
        sums_ref[...] = jnp.broadcast_to(row_sum(down * down), (rows, PAGE))

    down, sums = run(
        "down_sum", down_sum, [((rows, width), F32), ((rows, PAGE), F32)], (down,)
    )
    sums = trade([sums] * nx, "gx")

    def finish(*refs):
        down_ref, mixed_ref, gain_ref, out_ref = refs[nx:]
        square = sum(r[...] for r in refs[:nx])[:, 0:1]
        scale = lax.rsqrt(square / D + EPSILON)
        out = mixed_ref[...] + down_ref[...] * scale * (1.0 + gain_ref[3:4])
        out_ref[...] = out.reshape(beams, steps, width).astype(BF)

    (out,) = run("finish", finish, [(inputs.shape, BF)], (*sums, down, mixed, norm_gains))
    return out


def body_general(
    inputs,
    cache_pool,
    lengths,
    block_table,
    parents,
    norm_gains,
    w_query,
    w_key,
    w_value,
    w_out,
    w_gate,
    w_up,
    w_down,
):
    beams, steps, width = inputs.shape
    nx, ny = lax.axis_size("gx"), lax.axis_size("gy")
    rows = beams * steps
    part = rows // nx
    head_part = w_out.shape[0]
    hidden_part = w_gate.shape[1]
    query_part, key_part = w_query.shape[1], w_key.shape[1]
    columns = query_part + 2 * key_part
    share = columns // nx
    x_own = inputs.reshape(rows, width)
    me = lax.axis_index("gx")

    x_all = exchange(jnp.broadcast_to(x_own[None], (ny, rows, width)), "gy")
    flat = (x_all.astype(F32) * (1.0 + norm_gains[0:1])).astype(BF).reshape(ny * rows, width)
    sums = [jnp.dot(flat, w, preferred_element_type=F32) for w in (w_query, w_key, w_value)]
    sums = jnp.concatenate(sums, axis=1).reshape(ny, rows, nx, share)
    received = exchange_all(sums.transpose(2, 0, 1, 3).astype(BF))
    shares = jnp.sum(received.astype(F32), axis=0).astype(BF)
    every = lax.all_gather(shares, "gx", axis=0)
    every = every.transpose(2, 1, 0, 3).reshape(rows, ny, columns)
    q = every[..., :query_part].reshape(rows, HEADS, 2, HALF).transpose(2, 1, 0, 3)
    k, v = (
        every[..., start : start + key_part].reshape(rows, 2 * KV_HEADS, HALF).transpose(1, 0, 2)
        for start in (query_part, query_part + key_part)
    )
    shares = jnp.concatenate([q, k[None], v[None]], axis=0)
    square = lax.psum(row_sum(jnp.square(x_own.astype(F32))), "gx")
    high = lax.reduce_precision(square, 8, 7)
    squares = jnp.where(jnp.arange(HALF) < HALF // 2, high, square - high).astype(BF)[None]
    cos, sin = rope_tables(lengths, rows, steps)

    def attention(*refs):
        table, length, parent, g_ref, square_ref, cos_ref, sin_ref, pool_ref = refs[:8]
        out_ref, page_ref = refs[8:]
        num, den = attend(
            lambda share, which: g_ref[share, which],
            square_ref[...],
            (table, length, parent, cos_ref, sin_ref, pool_ref, page_ref),
        )
        den = high_low(den, PAGE)
        for rep in range(REPS):
            here = slice(rep * rows, (rep + 1) * rows)
            out_ref[rep, :, 0:HEAD_DIM] = num[here].astype(BF)
            out_ref[rep, :, HEAD_DIM:] = den[here].astype(BF)

    (terms,) = attention_call(
        attention,
        (block_table, lengths, parents),
        (shares, squares, cos, sin),
        [
            pl.BlockSpec((4, 2, rows, HALF), lambda h: (0, h, 0, 0)),
            whole_block(squares.shape),
            whole_block(cos.shape),
            whole_block(sin.shape),
        ],
        cache_pool,
        [(HEADS, rows, WIDE)],
        [pl.BlockSpec((REPS, rows, WIDE), lambda h: (h, 0, 0))],
        [],
    )
    num = terms[..., :HEAD_DIM].transpose(1, 0, 2).reshape(nx, part, ny, head_part)
    den = terms[..., HEAD_DIM :: PAGE // 2].transpose(1, 0, 2)
    den = jnp.repeat(den, ny // HEADS, axis=1).reshape(nx, part, ny, 2)
    terms = exchange_all(jnp.concatenate([num, den], axis=-1).transpose(0, 2, 1, 3))

    w_wide = lax.all_gather(w_out, "gx", axis=1, tiled=True)
    x_wide = lax.all_gather(x_own, "gx", axis=1, tiled=True)
    x_rows = lax.dynamic_slice_in_dim(x_wide, me * part, part, 0).astype(F32)
    gains = 1.0 + lax.all_gather(norm_gains, "gx", axis=1, tiled=True)

    def scaled(v, gain):
        return v * lax.rsqrt(row_sum(v * v) / D + EPSILON) * gain

    terms = jnp.sum(terms.astype(F32), axis=0)
    den = terms[..., head_part : head_part + 1] + terms[..., -1:]
    attended = (terms[..., :head_part] / den).reshape(ny * part, head_part).astype(BF)
    attn = jnp.dot(attended, w_wide, preferred_element_type=F32).astype(BF)
    attn = exchange(attn.reshape(ny, part, D), "gy").astype(F32).sum(axis=0)
    mixed = x_rows + scaled(attn, gains[1])
    ff_input = scaled(mixed, gains[2]).astype(BF)
    ff_input = ff_input.reshape(part, nx, width).transpose(1, 0, 2)[:, None]
    ff_input = exchange_all(jnp.broadcast_to(ff_input, (nx, ny, part, width)))

    flat = ff_input.reshape(-1, width)
    both = [jnp.dot(flat, w, preferred_element_type=F32).astype(BF) for w in (w_gate, w_up)]
    both = jnp.stack(both, axis=1).reshape(nx, ny * part, 2, hidden_part)
    both = jnp.sum(exchange(both, "gx").astype(F32), axis=0)
    hidden = (jax.nn.gelu(both[:, 0], approximate=True) * both[:, 1]).astype(BF)
    hidden = lax.all_gather(hidden, "gx", axis=0, tiled=True)
    down = jnp.dot(hidden, w_down, preferred_element_type=F32).astype(BF)
    down = exchange_all(down.reshape(nx, ny, part, width)).astype(F32).sum(axis=1)
    down = down.transpose(1, 0, 2).reshape(part, D)
    out = (mixed + scaled(down, gains[3])).astype(BF)
    out = exchange(out.reshape(part, nx, width).transpose(1, 0, 2), "gx")
    return out.reshape(beams, steps, width)


def solution(mesh):
    sizes = dict(mesh.shape)
    fits = sizes["gx"] == 4 and sizes["gy"] == HEADS
    return jax.shard_map(
        body_permutes if fits else body_general,
        mesh=mesh,
        in_specs=(
            P("gy", None, "gx"),
            P(None, "gx", "gy", None),
            P("gy"),
            P("gy", None),
            P(None, "gy"),
            P(None, "gx"),
            P("gx", "gy"),
            P("gx", "gy"),
            P("gx", "gy"),
            P("gy", "gx"),
            P("gx", "gy"),
            P("gx", "gy"),
            P("gy", "gx"),
        ),
        out_specs=P("gy", None, "gx"),
        check_vma=False,
    )
```

```python
import jax
import jax.numpy as jnp
from jax import lax
from jax.experimental import pallas as pl
from jax.experimental.pallas import tpu as pltpu
from jax.sharding import PartitionSpec as P

D = 2304
HEADS = 8
KV_HEADS = 4
HEAD_DIM = 256
HALF = HEAD_DIM // 2
WINDOW = 4096
PAGE = 128
BEAM = 8
EPSILON = 1e-06
SOFT_CAP = 50.0
ROPE_BASE = 10000.0
REPS = HEADS // KV_HEADS
WIDE = HEAD_DIM + PAGE
BF = jnp.bfloat16
F32 = jnp.float32
MIB = 1024 * 1024
NT = (((1,), (1,)), ((), ()))
IN_HBM = pl.BlockSpec(memory_space=pltpu.HBM)
IN_SMEM = pl.BlockSpec(memory_space=pltpu.SMEM)


def run(name, kernel, outs, args, scratch=(), limit=16, specs=None):
    specs = specs or {}
    vmem = pl.BlockSpec(memory_space=pltpu.VMEM)
    return pl.pallas_call(
        kernel,
        out_shape=[jax.ShapeDtypeStruct(s, d) for s, d in outs],
        in_specs=[specs.get(n, vmem) for n in range(len(args))],
        scratch_shapes=scratch,
        compiler_params=pltpu.CompilerParams(vmem_limit_bytes=limit * MIB),
        name=name,
    )(*args)


def exchange(values, axes):
    return lax.all_to_all(values, axes, split_axis=0, concat_axis=0, tiled=True)


def exchange_all(values):
    nx, ny = values.shape[:2]
    flat = values.reshape((nx * ny,) + values.shape[2:])
    return exchange(flat, ("gx", "gy")).reshape(values.shape)


def permute(values, axis, m):
    count = lax.axis_size(axis)
    return lax.ppermute(values, axis, [(i, i ^ m) for i in range(count)])


def trade(blocks, axis):
    return [blocks[0]] + [permute(blocks[m], axis, m) for m in range(1, len(blocks))]


def gather_gx(values):
    across = permute(values, "gx", 2)
    return [values, permute(values, "gx", 1), across, permute(across, "gx", 1)]


def weight_of(scores):
    return jnp.exp(SOFT_CAP * jnp.tanh(scores * (1.0 / SOFT_CAP)))


def high_low(column, lanes):
    shape = column.shape[:-1] + (lanes,)
    high = column.astype(BF).astype(F32)
    lane = lax.broadcasted_iota(jnp.int32, shape, len(shape) - 1)
    return jnp.where(lane < lanes // 2, high, column - high)


def row_sum(v):
    return jnp.sum(v, axis=-1, keepdims=True)


def make_tables(table, lengths, parents, slots, rows, steps):
    def tables(table_ref, length_ref, parents_ref, cached_ref, own_ref, page_ref):
        first_owner = lax.axis_index("gx") * slots
        length = length_ref[0]
        first_page = jnp.maximum(length - WINDOW + 1, 0) // PAGE
        for slot in range(slots + 1):
            page_ref[slot] = -1
        for j in range(table_ref.shape[1]):
            slot = table_ref[0, j] - first_owner
            page_ref[jnp.where((slot >= 0) & (slot < slots), slot, slots)] = j
        step = lax.broadcasted_iota(jnp.int32, (8, PAGE), 0) % steps
        lane = lax.broadcasted_iota(jnp.int32, (8, PAGE), 1)
        for slot in range(slots):
            page = page_ref[slot]
            position = lane + jnp.where(page >= 0, (first_page + page) * PAGE, 2**30)
            seen = (position < length) & (position >= length + step - (WINDOW - 1))
            cached_ref[:, slot * PAGE : (slot + 1) * PAGE] = jnp.where(seen, 1.0, 0.0)

        shape = (REPS * rows, rows)
        row = lax.broadcasted_iota(jnp.int32, shape, 0) % rows
        column = lax.broadcasted_iota(jnp.int32, shape, 1)
        row_step, column_step, column_beam = row % steps, column % steps, column // steps
        current = row // steps
        visible = jnp.zeros(shape, jnp.bool_)
        for j in range(steps - 1, -1, -1):
            if j < steps - 1:
                parent = jnp.zeros(shape, jnp.int32)
                for beam in range(BEAM):
                    parent = jnp.where(current == beam, parents_ref[j, beam], parent)
                current = jnp.where(row_step > j, parent, current)
            visible = visible | ((column_step == j) & (row_step >= j) & (column_beam == current))
        visible = visible & (lax.axis_index("gx") == 0)
        own_ref[...] = jnp.where(visible, 1.0, 0.0)

    return run(
        "tables",
        tables,
        [((8, slots * PAGE), F32), ((REPS * rows, rows), F32)],
        (table, lengths, parents),
        scratch=[pltpu.SMEM((slots + 1,), jnp.int32)],
        specs={0: IN_SMEM, 1: IN_SMEM, 2: IN_SMEM},
    )


def attend(shares, squares, tables, pool_ref, kept, store):
    cos_ref, sin_ref, cached_ref, own_ref = tables
    keys_ref, sems = kept
    slots = pool_ref.shape[1]
    rows = cos_ref.shape[0]
    copies = []
    for head in range(KV_HEADS):
        here = pool_ref.at[:, :, :, head * HEAD_DIM : (head + 1) * HEAD_DIM]
        copies.append(pltpu.make_async_copy(here, keys_ref.at[head], sems.at[head]))
        copies[-1].start()
    square = jnp.sum(squares.astype(F32), axis=0)
    square = square[:, 0:1] + square[:, HALF // 2 : HALF // 2 + 1]
    scale = lax.rsqrt(square / D + EPSILON)
    cos, sin = cos_ref[...] * scale, sin_ref[...] * scale
    cached, own = cached_ref[...], own_ref[...]

    def rotated(u, w):
        u, w = u.astype(F32), w.astype(F32)
        return u * cos - w * sin, w * cos + u * sin

    for head in range(KV_HEADS):
        query = []
        for rep in range(REPS):
            u, w = rotated(shares(0, REPS * head + rep), shares(1, REPS * head + rep))
            query.append(jnp.concatenate([u, w], axis=1) * HEAD_DIM ** (-0.5))
        query = jnp.concatenate(query, axis=0).astype(BF)
        first, second = 2 * head, 2 * head + 1
        key_step = rotated(shares(2, first), shares(2, second))
        key_step = jnp.concatenate(key_step, axis=1).astype(BF)
        value_step = [shares(3, n).astype(F32) * scale for n in (first, second)]
        value_step = jnp.concatenate(value_step, axis=1).astype(BF)

        scores = lax.dot_general(query, key_step, NT, preferred_element_type=F32)
        weights = weight_of(scores) * own
        den = row_sum(weights)
        num = jnp.dot(weights.astype(BF), value_step, preferred_element_type=F32)

        copies[head].wait()
        keys = keys_ref[head, 0].reshape(slots * PAGE, HEAD_DIM)
        values = keys_ref[head, 1].reshape(slots * PAGE, HEAD_DIM)
        scores = lax.dot_general(query, keys, NT, preferred_element_type=F32)
        weights = weight_of(scores).reshape(REPS * rows // 8, 8, slots * PAGE) * cached[None]
        weights = weights.reshape(REPS * rows, slots * PAGE)
        den = den + row_sum(weights)
        num = num + jnp.dot(weights.astype(BF), values, preferred_element_type=F32)
        store(head, num, den)


def key_scratch(pool):
    return [
        pltpu.VMEM((KV_HEADS, 2) + pool.shape[1:3] + (HEAD_DIM,), BF),
        pltpu.SemaphoreType.DMA((KV_HEADS,)),
    ]


def rope_tables(lengths, rows, steps):
    positions = lengths[0] + jnp.arange(rows, dtype=jnp.int32) % steps
    inverse_freq = ROPE_BASE ** (-jnp.arange(HALF, dtype=F32) * 2.0 / HEAD_DIM)
    angles = positions[:, None].astype(F32) * inverse_freq
    return jnp.cos(angles), jnp.sin(angles)


def body_permutes(
    inputs,
    cache_pool,
    lengths,
    block_table,
    parents,
    norm_gains,
    w_query,
    w_key,
    w_value,
    w_out,
    w_gate,
    w_up,
    w_down,
):
    beams, steps, width = inputs.shape
    nx, ny = lax.axis_size("gx"), lax.axis_size("gy")
    rows = beams * steps
    half = rows // 2
    all_rows = ny * rows
    share_rows = all_rows // nx
    hidden = w_gate.shape[1]
    cos, sin = rope_tables(lengths, rows, steps)
    tables = make_tables(block_table, lengths, parents, cache_pool.shape[1], rows, steps)

    def my(axis):
        return lax.axis_index(axis)

    def spread(x_ref, own_ref, out_ref):
        own = x_ref[...].astype(F32).reshape(rows, width).astype(BF)
        own_ref[...] = own
        for m in range(ny):
            out_ref[m] = own

    x_own, x_all = run(
        "spread", spread, [((rows, width), BF), ((ny, rows, width), BF)], (inputs,)
    )
    x_all = exchange(x_all, "gy")

    w_blocks = [None] * ny
    w_blocks[0], _ = lax.optimization_barrier((w_out.T, x_all))
    for m in (4, 2, 1):
        w_blocks[m] = permute(w_blocks[0], "gy", m)

    def project(x_ref, gain_hbm, q_hbm, k_hbm, v_hbm, z0_ref, z2_ref, z13_ref, *kept):
        held, gain_ref, q_ref, k_ref, v_ref, sems = kept
        pairs = (gain_hbm, gain_ref), (q_hbm, q_ref), (k_hbm, k_ref), (v_hbm, v_ref)
        copies = [
            pltpu.make_async_copy(src, dst, sems.at[n]) for n, (src, dst) in enumerate(pairs)
        ]
        for copy in copies:
            copy.start()
        x = x_ref[...].reshape(all_rows, width).astype(F32)
        copies[0].wait()
        flat = (x * (1.0 + gain_ref[0:1])).astype(BF)
        copies[1].wait()
        query = jnp.dot(flat, q_ref[...], preferred_element_type=F32).astype(BF)
        held[0], held[1] = query[:, :HALF], query[:, HALF:]
        copies[2].wait()
        held[2] = jnp.dot(flat, k_ref[...], preferred_element_type=F32).astype(BF)
        copies[3].wait()
        held[3] = jnp.dot(flat, v_ref[...], preferred_element_type=F32).astype(BF)
        me = my("gx")
        z0_ref[...], z2_ref[...] = held[me], held[me ^ 2]
        z13_ref[0], z13_ref[1] = held[me ^ 1], held[me ^ 3]

    shape = (all_rows, HALF)
    z0, z2, z13 = run(
        "project",
        project,
        [(shape, BF), (shape, BF), ((2,) + shape, BF)],
        (x_all, norm_gains, w_query, w_key, w_value),
        scratch=[
            pltpu.VMEM((nx,) + shape, BF),
            pltpu.VMEM(norm_gains.shape, F32),
            *[pltpu.VMEM(w.shape, BF) for w in (w_query, w_key, w_value)],
            pltpu.SemaphoreType.DMA((4,)),
        ],
        specs={n: IN_HBM for n in range(1, 5)},
    )
    z13 = permute(z13, "gx", 1)

    def pair_sum(z_ref, from_pair_ref, out_ref):
        total = z_ref[...].astype(F32) + from_pair_ref[1].astype(F32)
        out_ref[...] = total.astype(BF)

    (z2,) = run("pair_sum", pair_sum, [(shape, BF)], (z2, z13))
    z2 = permute(z2, "gx", 2)

    def share_sum(z0_ref, z13_ref, z2_ref, out_ref):
        total = z0_ref[...].astype(F32) + z13_ref[0].astype(F32) + z2_ref[...].astype(F32)
        out_ref[...] = total.reshape(ny, rows, HALF).astype(BF)

    (shares,) = run("share_sum", share_sum, [((ny, rows, HALF), BF)], (z0, z13, z2))
    shares = exchange(shares, "gy")
    _, (w_late, w_later) = lax.optimization_barrier((shares, (w_blocks[4], w_blocks[2])))
    w_blocks[6] = permute(w_late, "gy", 2)
    w_blocks[5] = permute(w_late, "gy", 1)
    w_blocks[3] = permute(w_later, "gy", 1)

    def pack_shares(share_ref, x_ref, out_ref):
        x = x_ref[...].astype(F32)
        out_ref[0:ny] = share_ref[...]
        out_ref[ny] = high_low(row_sum(x * x), HALF).astype(BF)

    (shares,) = run("pack_shares", pack_shares, [((ny + 1, rows, HALF), BF)], (shares, x_own))
    shares = gather_gx(shares)

    def attention(*refs):
        a_refs, tables, pool_ref, outs = refs[:nx], refs[nx : nx + 4], refs[nx + 4], refs[nx + 5 :]
        own_ref, pair_ref, keys_ref, sems, held, num_held, den_held = outs
        me = my("gx")
        core = me & 1
        for n, ref in enumerate(a_refs):
            held[me ^ n] = ref[...]

        def store(head, num, den):
            num_held[head] = num.reshape(REPS, 2, half, HEAD_DIM)
            den_held[head] = high_low(den, PAGE).reshape(REPS, 2, half, PAGE)
            for rep in range(REPS):
                for n, out in enumerate((own_ref, pair_ref)):
                    at = REPS * head + rep
                    out[at, :, 0:HEAD_DIM] = num_held[head, rep, core ^ n].astype(BF)
                    out[at, :, HEAD_DIM:] = den_held[head, rep, core ^ n].astype(BF)

        attend(
            lambda share, which: held[share, which],
            held[:, ny],
            tables,
            pool_ref,
            (keys_ref, sems),
            store,
        )

    shape = (HEADS, half, WIDE)
    own, pair = run(
        "attention",
        attention,
        [(shape, BF), (shape, BF)],
        (*shares, cos, sin, *tables, cache_pool),
        scratch=key_scratch(cache_pool)
        + [
            pltpu.VMEM((nx,) + shares[0].shape, BF),
            pltpu.VMEM((KV_HEADS, REPS, 2, half, HEAD_DIM), F32),
            pltpu.VMEM((KV_HEADS, REPS, 2, half, PAGE), F32),
        ],
        limit=24,
        specs={nx + 4: IN_HBM},
    )
    _, w_last = lax.optimization_barrier((own, w_blocks[6]))
    w_blocks[7] = permute(w_last, "gy", 1)
    pair = permute(pair, "gx", 1)

    def pair_terms(own_ref, pair_ref, out_ref):
        total = own_ref[...].astype(F32) + pair_ref[...].astype(F32)
        den = total[..., HEAD_DIM : HEAD_DIM + 1] + total[..., WIDE - 1 :]
        out_ref[..., 0:HEAD_DIM] = total[..., 0:HEAD_DIM].astype(BF)
        out_ref[..., HEAD_DIM:] = high_low(den, PAGE).astype(BF)

    (own,) = run("pair_terms", pair_terms, [(shape, BF)], (own, pair))
    across = permute(own, "gx", 2)

    def divide(own_ref, across_ref, out_ref):
        total = own_ref[...].astype(F32) + across_ref[...].astype(F32)
        den = total[..., HEAD_DIM : HEAD_DIM + 1] + total[..., WIDE - 1 :]
        out_ref[...] = (total[..., 0:HEAD_DIM] / den).astype(BF)

    (attended,) = run("divide", divide, [((HEADS, half, HEAD_DIM), BF)], (own, across))
    others = permute(attended, "gx", 1)

    def project_out(own_ref, other_ref, x_ref, gain_ref, *refs):
        w_refs, (attn_ref, sums_ref, held) = refs[:ny], refs[ny:]
        core = my("gx") & 1
        held[core], held[1 - core] = own_ref[...], other_ref[...]
        me = my("gy")
        attn = jnp.zeros((rows, width), F32)
        for m, w_ref in enumerate(w_refs):
            flat = jnp.concatenate([held[0, me ^ m], held[1, me ^ m]], axis=0)
            attn = attn + lax.dot_general(flat, w_ref[...], NT, preferred_element_type=F32)
        attn_ref[...] = attn
        x = x_ref[...].astype(F32)
        scaled = attn * (1.0 + gain_ref[1:2])
        lane = lax.broadcasted_iota(jnp.int32, (rows, PAGE), 1)
        sums = jnp.zeros((rows, PAGE), F32)
        for n, terms in enumerate((attn * attn, scaled * scaled, x * scaled, x * x)):
            sums = jnp.where(lane == n, row_sum(terms), sums)
        sums_ref[...] = sums

    attn, sums = run(
        "project_out",
        project_out,
        [((rows, width), F32), ((rows, PAGE), F32)],
        (attended, others, x_own, norm_gains, *w_blocks),
        scratch=[pltpu.VMEM((2, HEADS, half, HEAD_DIM), BF)],
    )
    sums = trade([sums] * nx, "gx")

    def mix(*refs):
        attn_ref, x_ref, gain_ref, mixed_ref, ff_ref = refs[nx:]
        total = sum(r[...] for r in refs[:nx])
        plain, scaled, cross, square = (total[:, n : n + 1] for n in range(4))
        scale = lax.rsqrt(plain / D + EPSILON)
        mixed = x_ref[...].astype(F32) + attn_ref[...] * scale * (1.0 + gain_ref[1:2])
        square = jnp.maximum(square + 2.0 * scale * cross + scale * scale * scaled, 0.0)
        mixed_ref[...] = mixed
        scale = lax.rsqrt(square / D + EPSILON)
        ff_input = (mixed * scale * (1.0 + gain_ref[2:3])).astype(BF)
        for m in range(ny):
            ff_ref[m] = ff_input

    mixed, ff_input = run(
        "mix",
        mix,
        [((rows, width), F32), ((ny, rows, width), BF)],
        (*sums, attn, x_own, norm_gains),
    )
    ff_input = exchange(ff_input, "gy")

    groups = ny // nx

    def gate_up(ff_ref, gate_ref, up_ref, z0_ref, z2_ref, z13_ref):
        me = my("gx")
        flat = [
            ff_ref[pl.ds((me ^ n) * groups, groups)].reshape(share_rows, width) for n in range(nx)
        ]
        flat = jnp.concatenate(flat, axis=0)
        w_refs = gate_ref, up_ref
        for n, w_ref in enumerate(w_refs):
            sums = jnp.dot(flat, w_ref[...], preferred_element_type=F32).astype(BF)
            here = pl.ds(n * hidden, hidden)
            for p, out in enumerate((z0_ref, z13_ref.at[0], z2_ref, z13_ref.at[1])):
                out[:, here] = sums[p * share_rows : (p + 1) * share_rows]

    shape = (share_rows, 2 * hidden)
    z0, z2, z13 = run(
        "gate_up",
        gate_up,
        [(shape, BF), (shape, BF), ((2,) + shape, BF)],
        (ff_input, w_gate, w_up),
        limit=24,
    )
    z13 = permute(z13, "gx", 1)
    (z2,) = run("pair_sum_ff", pair_sum, [(shape, BF)], (z2, z13))
    z2 = permute(z2, "gx", 2)

    def activate(z0_ref, z13_ref, z2_ref, out_ref):
        total = z0_ref[...].astype(F32) + z13_ref[0].astype(F32) + z2_ref[...].astype(F32)
        gate, up = total[:, :hidden], total[:, hidden:]
        out_ref[...] = (jax.nn.gelu(gate, approximate=True) * up).astype(BF)

    (blocks,) = run("activate", activate, [((share_rows, hidden), BF)], (z0, z13, z2))
    blocks = gather_gx(blocks)

    def project_down(*refs):
        w_ref, out_ref = refs[nx:]
        me = my("gx")
        flat = jnp.concatenate([r[...] for r in refs[:nx]], axis=0)
        sums = lax.dot_general(flat, w_ref[...], NT, preferred_element_type=F32)
        sums = sums.reshape(nx, groups, rows, width).astype(BF)
        for n in range(nx):
            out_ref[pl.ds((me ^ n) * groups, groups)] = sums[n]

    (down,) = run(
        "project_down", project_down, [((ny, rows, width), BF)], (*blocks, w_down.T)
    )
    down = exchange(down, "gy")

    def down_sum(parts_ref, down_ref, sums_ref):
        down = jnp.sum(parts_ref[...].astype(F32), axis=0)
        down_ref[...] = down
        sums_ref[...] = jnp.broadcast_to(row_sum(down * down), (rows, PAGE))

    down, sums = run(
        "down_sum", down_sum, [((rows, width), F32), ((rows, PAGE), F32)], (down,)
    )
    sums = trade([sums] * nx, "gx")

    def finish(*refs):
        down_ref, mixed_ref, gain_ref, out_ref = refs[nx:]
        square = sum(r[...] for r in refs[:nx])[:, 0:1]
        scale = lax.rsqrt(square / D + EPSILON)
        out = mixed_ref[...] + down_ref[...] * scale * (1.0 + gain_ref[3:4])
        out_ref[...] = out.reshape(beams, steps, width).astype(BF)

    (out,) = run("finish", finish, [(inputs.shape, BF)], (*sums, down, mixed, norm_gains))
    return out


def body_general(
    inputs,
    cache_pool,
    lengths,
    block_table,
    parents,
    norm_gains,
    w_query,
    w_key,
    w_value,
    w_out,
    w_gate,
    w_up,
    w_down,
):
    beams, steps, width = inputs.shape
    nx, ny = lax.axis_size("gx"), lax.axis_size("gy")
    rows = beams * steps
    part = rows // nx
    head_part = w_out.shape[0]
    hidden_part = w_gate.shape[1]
    query_part, key_part = w_query.shape[1], w_key.shape[1]
    columns = query_part + 2 * key_part
    share = columns // nx
    x_own = inputs.reshape(rows, width)
    me = lax.axis_index("gx")

    x_all = exchange(jnp.broadcast_to(x_own[None], (ny, rows, width)), "gy")
    flat = (x_all.astype(F32) * (1.0 + norm_gains[0:1])).astype(BF).reshape(ny * rows, width)
    sums = [jnp.dot(flat, w, preferred_element_type=F32) for w in (w_query, w_key, w_value)]
    sums = jnp.concatenate(sums, axis=1).reshape(ny, rows, nx, share)
    received = exchange_all(sums.transpose(2, 0, 1, 3).astype(BF))
    shares = jnp.sum(received.astype(F32), axis=0).astype(BF)
    every = lax.all_gather(shares, "gx", axis=0)
    every = every.transpose(2, 1, 0, 3).reshape(rows, ny, columns)
    q = every[..., :query_part].reshape(rows, HEADS, 2, HALF).transpose(2, 1, 0, 3)
    k, v = (
        every[..., start : start + key_part].reshape(rows, 2 * KV_HEADS, HALF).transpose(1, 0, 2)
        for start in (query_part, query_part + key_part)
    )
    shares = jnp.concatenate([q, k[None], v[None]], axis=0)
    square = lax.psum(row_sum(jnp.square(x_own.astype(F32))), "gx")
    high = lax.reduce_precision(square, 8, 7)
    squares = jnp.where(jnp.arange(HALF) < HALF // 2, high, square - high).astype(BF)[None]
    cos, sin = rope_tables(lengths, rows, steps)

    def attention(*refs):
        g_ref, square_ref, tables, pool_ref = refs[0], refs[1], refs[2:6], refs[6]
        out_ref, keys_ref, sems = refs[7:]

        def store(head, num, den):
            den = high_low(den, PAGE)
            for rep in range(REPS):
                here = slice(rep * rows, (rep + 1) * rows)
                out_ref[REPS * head + rep, :, 0:HEAD_DIM] = num[here].astype(BF)
                out_ref[REPS * head + rep, :, HEAD_DIM:] = den[here].astype(BF)

        attend(
            lambda share, which: g_ref[share, which],
            square_ref[...],
            tables,
            pool_ref,
            (keys_ref, sems),
            store,
        )

    tables = make_tables(block_table, lengths, parents, cache_pool.shape[1], rows, steps)
    (terms,) = run(
        "attention",
        attention,
        [((HEADS, rows, WIDE), BF)],
        (shares, squares, cos, sin, *tables, cache_pool),
        scratch=key_scratch(cache_pool),
        limit=24,
        specs={6: IN_HBM},
    )
    num = terms[..., :HEAD_DIM].transpose(1, 0, 2).reshape(nx, part, ny, head_part)
    den = terms[..., HEAD_DIM :: PAGE // 2].transpose(1, 0, 2)
    den = jnp.repeat(den, ny // HEADS, axis=1).reshape(nx, part, ny, 2)
    terms = exchange_all(jnp.concatenate([num, den], axis=-1).transpose(0, 2, 1, 3))

    w_wide = lax.all_gather(w_out, "gx", axis=1, tiled=True)
    x_wide = lax.all_gather(x_own, "gx", axis=1, tiled=True)
    x_rows = lax.dynamic_slice_in_dim(x_wide, me * part, part, 0).astype(F32)
    gains = 1.0 + lax.all_gather(norm_gains, "gx", axis=1, tiled=True)

    def scaled(v, gain):
        return v * lax.rsqrt(row_sum(v * v) / D + EPSILON) * gain

    terms = jnp.sum(terms.astype(F32), axis=0)
    den = terms[..., head_part : head_part + 1] + terms[..., -1:]
    attended = (terms[..., :head_part] / den).reshape(ny * part, head_part).astype(BF)
    attn = jnp.dot(attended, w_wide, preferred_element_type=F32).astype(BF)
    attn = exchange(attn.reshape(ny, part, D), "gy").astype(F32).sum(axis=0)
    mixed = x_rows + scaled(attn, gains[1])
    ff_input = scaled(mixed, gains[2]).astype(BF)
    ff_input = ff_input.reshape(part, nx, width).transpose(1, 0, 2)[:, None]
    ff_input = exchange_all(jnp.broadcast_to(ff_input, (nx, ny, part, width)))

    flat = ff_input.reshape(-1, width)
    both = [jnp.dot(flat, w, preferred_element_type=F32).astype(BF) for w in (w_gate, w_up)]
    both = jnp.stack(both, axis=1).reshape(nx, ny * part, 2, hidden_part)
    both = jnp.sum(exchange(both, "gx").astype(F32), axis=0)
    hidden = (jax.nn.gelu(both[:, 0], approximate=True) * both[:, 1]).astype(BF)
    hidden = lax.all_gather(hidden, "gx", axis=0, tiled=True)
    down = jnp.dot(hidden, w_down, preferred_element_type=F32).astype(BF)
    down = exchange_all(down.reshape(nx, ny, part, width)).astype(F32).sum(axis=1)
    down = down.transpose(1, 0, 2).reshape(part, D)
    out = (mixed + scaled(down, gains[3])).astype(BF)
    out = exchange(out.reshape(part, nx, width).transpose(1, 0, 2), "gx")
    return out.reshape(beams, steps, width)


def solution(mesh):
    sizes = dict(mesh.shape)
    fits = sizes["gx"] == 4 and sizes["gy"] == HEADS
    return jax.shard_map(
        body_permutes if fits else body_general,
        mesh=mesh,
        in_specs=(
            P("gy", None, "gx"),
            P(None, "gx", "gy", None),
            P("gy"),
            P("gy", None),
            P(None, "gy"),
            P(None, "gx"),
            P("gx", "gy"),
            P("gx", "gy"),
            P("gx", "gy"),
            P("gy", "gx"),
            P("gx", "gy"),
            P("gx", "gy"),
            P("gy", "gx"),
        ),
        out_specs=P("gy", None, "gx"),
        check_vma=False,
    )
```

```python
import jax
import jax.numpy as jnp
from jax import lax
from jax.experimental import pallas as pl
from jax.experimental.pallas import tpu as pltpu
from jax.sharding import PartitionSpec as P

D = 2304
HEADS = 8
KV_HEADS = 4
HEAD_DIM = 256
HALF = HEAD_DIM // 2
WINDOW = 4096
PAGE = 128
BEAM = 8
EPSILON = 1e-06
SOFT_CAP = 50.0
ROPE_BASE = 10000.0
REPS = HEADS // KV_HEADS
WIDE = HEAD_DIM + PAGE
BF = jnp.bfloat16
F32 = jnp.float32
MIB = 1024 * 1024
NT = (((1,), (1,)), ((), ()))
IN_HBM = pl.BlockSpec(memory_space=pltpu.HBM)
IN_SMEM = pl.BlockSpec(memory_space=pltpu.SMEM)


def run(name, kernel, outs, args, scratch=(), limit=16, specs=None, micros=0):
    cost = pl.CostEstimate(flops=micros * 10**9, bytes_accessed=0, transcendentals=0)
    specs = specs or {}
    vmem = pl.BlockSpec(memory_space=pltpu.VMEM)
    return pl.pallas_call(
        kernel,
        out_shape=[jax.ShapeDtypeStruct(s, d) for s, d in outs],
        in_specs=[specs.get(n, vmem) for n in range(len(args))],
        scratch_shapes=scratch,
        compiler_params=pltpu.CompilerParams(vmem_limit_bytes=limit * MIB),
        cost_estimate=cost if micros else None,
        name=name,
    )(*args)


def exchange(values, axes):
    return lax.all_to_all(values, axes, split_axis=0, concat_axis=0, tiled=True)


def exchange_all(values):
    nx, ny = values.shape[:2]
    flat = values.reshape((nx * ny,) + values.shape[2:])
    return exchange(flat, ("gx", "gy")).reshape(values.shape)


def permute(values, axis, m):
    count = lax.axis_size(axis)
    return lax.ppermute(values, axis, [(i, i ^ m) for i in range(count)])


def trade(blocks, axis):
    return [blocks[0]] + [permute(blocks[m], axis, m) for m in range(1, len(blocks))]


def gather_gx(values):
    across = permute(values, "gx", 2)
    return [values, permute(values, "gx", 1), across, permute(across, "gx", 1)]


def weight_of(scores):
    return jnp.exp(SOFT_CAP * jnp.tanh(scores * (1.0 / SOFT_CAP)))


def high_low(column, lanes):
    shape = column.shape[:-1] + (lanes,)
    high = column.astype(BF).astype(F32)
    lane = lax.broadcasted_iota(jnp.int32, shape, len(shape) - 1)
    return jnp.where(lane < lanes // 2, high, column - high)


def pack_lanes(v):
    rows, width = v.shape
    whole = width // 128 * 128
    tiles = [v[:, c : c + 128] for c in range(0, whole, 128)]
    last = jnp.concatenate([v[: rows // 2, whole:], v[rows // 2 :, whole:]], axis=1)
    return jnp.concatenate(tiles + [last], axis=0)


def unpack_lanes(v, rows):
    whole = v.shape[0] // rows * rows
    tiles = [v[r : r + rows] for r in range(0, whole, rows)]
    last = jnp.concatenate([v[whole:, :64], v[whole:, 64:]], axis=0)
    return jnp.concatenate(tiles + [last], axis=1)


def row_sum(v):
    return jnp.sum(v, axis=-1, keepdims=True)


def make_tables(table, lengths, parents, slots, rows, steps):
    def tables(table_ref, length_ref, parents_ref, cached_ref, own_ref, page_ref):
        first_owner = lax.axis_index("gx") * slots
        length = length_ref[0]
        first_page = jnp.maximum(length - WINDOW + 1, 0) // PAGE
        for slot in range(slots + 1):
            page_ref[slot] = -1
        for j in range(table_ref.shape[1]):
            slot = table_ref[0, j] - first_owner
            page_ref[jnp.where((slot >= 0) & (slot < slots), slot, slots)] = j
        step = lax.broadcasted_iota(jnp.int32, (8, PAGE), 0) % steps
        lane = lax.broadcasted_iota(jnp.int32, (8, PAGE), 1)
        for slot in range(slots):
            page = page_ref[slot]
            position = lane + jnp.where(page >= 0, (first_page + page) * PAGE, 2**30)
            seen = (position < length) & (position >= length + step - (WINDOW - 1))
            cached_ref[:, slot * PAGE : (slot + 1) * PAGE] = jnp.where(seen, 1.0, 0.0)

        shape = (REPS * rows, rows)
        row = lax.broadcasted_iota(jnp.int32, shape, 0) % rows
        column = lax.broadcasted_iota(jnp.int32, shape, 1)
        row_step, column_step, column_beam = row % steps, column % steps, column // steps
        current = row // steps
        visible = jnp.zeros(shape, jnp.bool_)
        for j in range(steps - 1, -1, -1):
            if j < steps - 1:
                parent = jnp.zeros(shape, jnp.int32)
                for beam in range(BEAM):
                    parent = jnp.where(current == beam, parents_ref[j, beam], parent)
                current = jnp.where(row_step > j, parent, current)
            visible = visible | ((column_step == j) & (row_step >= j) & (column_beam == current))
        visible = visible & (lax.axis_index("gx") == 0)
        own_ref[...] = jnp.where(visible, 1.0, 0.0)

    return run(
        "tables",
        tables,
        [((8, slots * PAGE), F32), ((REPS * rows, rows), F32)],
        (table, lengths, parents),
        scratch=[pltpu.SMEM((slots + 1,), jnp.int32)],
        specs={0: IN_SMEM, 1: IN_SMEM, 2: IN_SMEM},
    )


def attend(shares, squares, tables, pool_ref, kept, store):
    cos_ref, sin_ref, cached_ref, own_ref = tables
    keys_ref, sems = kept
    slots = pool_ref.shape[1]
    rows = cos_ref.shape[0]
    copies = []
    for head in range(KV_HEADS):
        here = pool_ref.at[:, :, :, head * HEAD_DIM : (head + 1) * HEAD_DIM]
        copies.append(pltpu.make_async_copy(here, keys_ref.at[head], sems.at[head]))
        copies[-1].start()
    square = jnp.sum(squares.astype(F32), axis=0)
    square = square[:, 0:1] + square[:, HALF // 2 : HALF // 2 + 1]
    scale = lax.rsqrt(square / D + EPSILON)
    cos, sin = cos_ref[...] * scale, sin_ref[...] * scale
    cached, own = cached_ref[...], own_ref[...]

    def rotated(u, w):
        u, w = u.astype(F32), w.astype(F32)
        return u * cos - w * sin, w * cos + u * sin

    for head in range(KV_HEADS):
        query = []
        for rep in range(REPS):
            u, w = rotated(shares(0, REPS * head + rep), shares(1, REPS * head + rep))
            query.append(jnp.concatenate([u, w], axis=1) * HEAD_DIM ** (-0.5))
        query = jnp.concatenate(query, axis=0).astype(BF)
        first, second = 2 * head, 2 * head + 1
        key_step = rotated(shares(2, first), shares(2, second))
        key_step = jnp.concatenate(key_step, axis=1).astype(BF)
        value_step = [shares(3, n).astype(F32) * scale for n in (first, second)]
        value_step = jnp.concatenate(value_step, axis=1).astype(BF)

        scores = lax.dot_general(query, key_step, NT, preferred_element_type=F32)
        weights = weight_of(scores) * own
        den = row_sum(weights)
        num = jnp.dot(weights.astype(BF), value_step, preferred_element_type=F32)

        copies[head].wait()
        keys = keys_ref[head, 0].reshape(slots * PAGE, HEAD_DIM)
        values = keys_ref[head, 1].reshape(slots * PAGE, HEAD_DIM)
        scores = lax.dot_general(query, keys, NT, preferred_element_type=F32)
        weights = weight_of(scores).reshape(REPS * rows // 8, 8, slots * PAGE) * cached[None]
        weights = weights.reshape(REPS * rows, slots * PAGE)
        den = den + row_sum(weights)
        num = num + jnp.dot(weights.astype(BF), values, preferred_element_type=F32)
        store(head, num, den)


def key_scratch(pool):
    return [
        pltpu.VMEM((KV_HEADS, 2) + pool.shape[1:3] + (HEAD_DIM,), BF),
        pltpu.SemaphoreType.DMA((KV_HEADS,)),
    ]


def rope_tables(lengths, rows, steps):
    positions = lengths[0] + jnp.arange(rows, dtype=jnp.int32) % steps
    inverse_freq = ROPE_BASE ** (-jnp.arange(HALF, dtype=F32) * 2.0 / HEAD_DIM)
    angles = positions[:, None].astype(F32) * inverse_freq
    return jnp.cos(angles), jnp.sin(angles)


def body_permutes(
    inputs,
    cache_pool,
    lengths,
    block_table,
    parents,
    norm_gains,
    w_query,
    w_key,
    w_value,
    w_out,
    w_gate,
    w_up,
    w_down,
):
    beams, steps, width = inputs.shape
    nx, ny = lax.axis_size("gx"), lax.axis_size("gy")
    rows = beams * steps
    half = rows // 2
    all_rows = ny * rows
    share_rows = all_rows // nx
    hidden = w_gate.shape[1]
    packed = rows * width // 128

    def my(axis):
        return lax.axis_index(axis)

    def spread(x_ref, own_ref, out_ref):
        own = x_ref[...].astype(F32).reshape(rows, width).astype(BF)
        own_ref[...] = own
        own = pack_lanes(own)
        for m in range(ny):
            out_ref[m] = own

    x_own, x_all = run(
        "spread", spread, [((rows, width), BF), ((ny, packed, 128), BF)], (inputs,), micros=12
    )
    x_all = exchange(x_all, "gy")

    w_own = w_out.T
    w_blocks = [w_own, permute(w_own, "gy", 1), permute(w_own, "gy", 2)] + [None] * (ny - 3)
    (w_late, _, w_later), _ = lax.optimization_barrier((w_blocks[:3], x_all))
    w_blocks[4] = permute(w_late, "gy", 4)
    w_blocks[3] = permute(w_later, "gy", 1)

    def project(x_ref, gain_ref, q_ref, k_ref, v_ref, z0_ref, z2_ref, z13_ref, held):
        gain = 1.0 + gain_ref[0:1]
        flat = [
            (unpack_lanes(x_ref[m], rows).astype(F32) * gain).astype(BF) for m in range(ny)
        ]
        flat = jnp.concatenate(flat, axis=0)
        query = jnp.dot(flat, q_ref[...], preferred_element_type=F32).astype(BF)
        held[0], held[1] = query[:, :HALF], query[:, HALF:]
        held[2] = jnp.dot(flat, k_ref[...], preferred_element_type=F32).astype(BF)
        held[3] = jnp.dot(flat, v_ref[...], preferred_element_type=F32).astype(BF)
        me = my("gx")
        z0_ref[...], z2_ref[...] = held[me], held[me ^ 2]
        z13_ref[0], z13_ref[1] = held[me ^ 1], held[me ^ 3]

    shape = (all_rows, HALF)
    z0, z2, z13 = run(
        "project",
        project,
        [(shape, BF), (shape, BF), ((2,) + shape, BF)],
        (x_all, norm_gains, w_query, w_key, w_value),
        scratch=[
            pltpu.VMEM((nx,) + shape, BF),
        ],
    )
    z13 = permute(z13, "gx", 1)

    def pair_sum(z_ref, from_pair_ref, out_ref):
        total = z_ref[...].astype(F32) + from_pair_ref[1].astype(F32)
        out_ref[...] = total.astype(BF)

    (z2,) = run("pair_sum", pair_sum, [(shape, BF)], (z2, z13))
    z2 = permute(z2, "gx", 2)

    def share_sum(z0_ref, z13_ref, z2_ref, out_ref):
        total = z0_ref[...].astype(F32) + z13_ref[0].astype(F32) + z2_ref[...].astype(F32)
        out_ref[...] = total.reshape(ny, rows, HALF).astype(BF)

    (shares,) = run(
        "share_sum", share_sum, [((ny, rows, HALF), BF)], (z0, z13, z2), micros=6
    )
    cos, sin = rope_tables(lengths, rows, steps)
    tables = make_tables(block_table, lengths, parents, cache_pool.shape[1], rows, steps)
    shares = exchange(shares, "gy")
    shares, _ = lax.optimization_barrier((shares, w_blocks[3]))

    def pack_shares(share_ref, x_ref, out_ref):
        x = x_ref[...].astype(F32)
        out_ref[0:ny] = share_ref[...]
        out_ref[ny] = high_low(row_sum(x * x), HALF).astype(BF)

    (shares,) = run("pack_shares", pack_shares, [((ny + 1, rows, HALF), BF)], (shares, x_own))
    shares = gather_gx(shares)
    _, w_late = lax.optimization_barrier((shares[2], w_blocks[4]))
    w_blocks[6] = permute(w_late, "gy", 2)
    w_blocks[5] = permute(w_late, "gy", 1)

    def attention(*refs):
        a_refs, tables, pool_ref, outs = refs[:nx], refs[nx : nx + 4], refs[nx + 4], refs[nx + 5 :]
        own_ref, pair_ref, keys_ref, sems, held, num_held, den_held = outs
        me = my("gx")
        core = me & 1
        for n, ref in enumerate(a_refs):
            held[me ^ n] = ref[...]

        def store(head, num, den):
            num_held[head] = num.reshape(REPS, 2, half, HEAD_DIM)
            den_held[head] = high_low(den, PAGE).reshape(REPS, 2, half, PAGE)
            for rep in range(REPS):
                for n, out in enumerate((own_ref, pair_ref)):
                    at = REPS * head + rep
                    out[at, :, 0:HEAD_DIM] = num_held[head, rep, core ^ n].astype(BF)
                    out[at, :, HEAD_DIM:] = den_held[head, rep, core ^ n].astype(BF)

        attend(
            lambda share, which: held[share, which],
            held[:, ny],
            tables,
            pool_ref,
            (keys_ref, sems),
            store,
        )

    shape = (HEADS, half, WIDE)
    own, pair = run(
        "attention",
        attention,
        [(shape, BF), (shape, BF)],
        (*shares, cos, sin, *tables, cache_pool),
        scratch=key_scratch(cache_pool)
        + [
            pltpu.VMEM((nx,) + shares[0].shape, BF),
            pltpu.VMEM((KV_HEADS, REPS, 2, half, HEAD_DIM), F32),
            pltpu.VMEM((KV_HEADS, REPS, 2, half, PAGE), F32),
        ],
        limit=24,
        specs={nx + 4: IN_HBM},
    )
    pair = permute(pair, "gx", 1)

    def pair_terms(own_ref, pair_ref, out_ref):
        total = own_ref[...].astype(F32) + pair_ref[...].astype(F32)
        den = total[..., HEAD_DIM : HEAD_DIM + 1] + total[..., WIDE - 1 :]
        out_ref[..., 0:HEAD_DIM] = total[..., 0:HEAD_DIM].astype(BF)
        out_ref[..., HEAD_DIM:] = high_low(den, PAGE).astype(BF)

    (own,) = run("pair_terms", pair_terms, [(shape, BF)], (own, pair))
    across = permute(own, "gx", 2)
    _, w_last, _ = lax.optimization_barrier((own, w_blocks[6], w_blocks[5]))
    w_blocks[7] = permute(w_last, "gy", 1)

    def divide(own_ref, across_ref, out_ref):
        total = own_ref[...].astype(F32) + across_ref[...].astype(F32)
        den = total[..., HEAD_DIM : HEAD_DIM + 1] + total[..., WIDE - 1 :]
        out_ref[...] = (total[..., 0:HEAD_DIM] / den).astype(BF)

    (attended,) = run("divide", divide, [((HEADS, half, HEAD_DIM), BF)], (own, across))
    others = permute(attended, "gx", 1)

    def project_out(own_ref, other_ref, x_ref, gain_ref, *refs):
        w_refs, (attn_ref, sums_ref, held) = refs[:ny], refs[ny:]
        core = my("gx") & 1
        held[core], held[1 - core] = own_ref[...], other_ref[...]
        me = my("gy")
        attn = jnp.zeros((rows, width), F32)
        for m, w_ref in enumerate(w_refs):
            flat = jnp.concatenate([held[0, me ^ m], held[1, me ^ m]], axis=0)
            attn = attn + lax.dot_general(flat, w_ref[...], NT, preferred_element_type=F32)
        attn_ref[...] = attn
        x = x_ref[...].astype(F32)
        scaled = attn * (1.0 + gain_ref[1:2])
        lane = lax.broadcasted_iota(jnp.int32, (rows, PAGE), 1)
        sums = jnp.zeros((rows, PAGE), F32)
        for n, terms in enumerate((attn * attn, scaled * scaled, x * scaled, x * x)):
            sums = jnp.where(lane == n, row_sum(terms), sums)
        sums_ref[...] = sums

    attn, sums = run(
        "project_out",
        project_out,
        [((rows, width), F32), ((rows, PAGE), F32)],
        (attended, others, x_own, norm_gains, *w_blocks),
        scratch=[pltpu.VMEM((2, HEADS, half, HEAD_DIM), BF)],
    )
    sums = trade([sums] * nx, "gx")

    def mix(*refs):
        attn_ref, x_ref, gain_ref, mixed_ref, ff_ref = refs[nx:]
        total = sum(r[...] for r in refs[:nx])
        plain, scaled, cross, square = (total[:, n : n + 1] for n in range(4))
        scale = lax.rsqrt(plain / D + EPSILON)
        mixed = x_ref[...].astype(F32) + attn_ref[...] * scale * (1.0 + gain_ref[1:2])
        square = jnp.maximum(square + 2.0 * scale * cross + scale * scale * scaled, 0.0)
        mixed_ref[...] = mixed
        scale = lax.rsqrt(square / D + EPSILON)
        ff_input = (mixed * scale * (1.0 + gain_ref[2:3])).astype(BF)
        ff_input = pack_lanes(ff_input)
        for m in range(ny):
            ff_ref[m] = ff_input

    mixed, ff_input = run(
        "mix",
        mix,
        [((rows, width), F32), ((ny, packed, 128), BF)],
        (*sums, attn, x_own, norm_gains),
    )
    ff_input = exchange(ff_input, "gy")

    groups = ny // nx

    def gate_up(ff_ref, gate_ref, up_ref, z0_ref, z2_ref, z13_ref):
        me = my("gx")
        flat = [
            unpack_lanes(ff_ref[(me ^ n) * groups + group], rows)
            for n in range(nx)
            for group in range(groups)
        ]
        flat = jnp.concatenate(flat, axis=0)
        w_refs = gate_ref, up_ref
        for n, w_ref in enumerate(w_refs):
            sums = jnp.dot(flat, w_ref[...], preferred_element_type=F32).astype(BF)
            here = pl.ds(n * hidden, hidden)
            for p, out in enumerate((z0_ref, z13_ref.at[0], z2_ref, z13_ref.at[1])):
                out[:, here] = sums[p * share_rows : (p + 1) * share_rows]

    shape = (share_rows, 2 * hidden)
    z0, z2, z13 = run(
        "gate_up",
        gate_up,
        [(shape, BF), (shape, BF), ((2,) + shape, BF)],
        (ff_input, w_gate, w_up),
        limit=24,
    )
    z13 = permute(z13, "gx", 1)
    (z2,) = run("pair_sum_ff", pair_sum, [(shape, BF)], (z2, z13))
    z2 = permute(z2, "gx", 2)

    def activate(z0_ref, z13_ref, z2_ref, out_ref):
        total = z0_ref[...].astype(F32) + z13_ref[0].astype(F32) + z2_ref[...].astype(F32)
        gate, up = total[:, :hidden], total[:, hidden:]
        out_ref[...] = (jax.nn.gelu(gate, approximate=True) * up).astype(BF)

    (blocks,) = run("activate", activate, [((share_rows, hidden), BF)], (z0, z13, z2))
    blocks = gather_gx(blocks)

    def project_down(*refs):
        w_ref, out_ref = refs[nx:]
        me = my("gx")
        flat = jnp.concatenate([r[...] for r in refs[:nx]], axis=0)
        sums = lax.dot_general(flat, w_ref[...], NT, preferred_element_type=F32)
        for n in range(nx):
            for group in range(groups):
                at = (n * groups + group) * rows
                block = pack_lanes(sums[at : at + rows].astype(BF))
                out_ref[(me ^ n) * groups + group] = block

    (down,) = run(
        "project_down", project_down, [((ny, packed, 128), BF)], (*blocks, w_down.T)
    )
    down = exchange(down, "gy")

    def down_sum(parts_ref, down_ref, sums_ref):
        down = unpack_lanes(jnp.sum(parts_ref[...].astype(F32), axis=0), rows)
        down_ref[...] = down
        sums_ref[...] = jnp.broadcast_to(row_sum(down * down), (rows, PAGE))

    down, sums = run(
        "down_sum", down_sum, [((rows, width), F32), ((rows, PAGE), F32)], (down,)
    )
    sums = trade([sums] * nx, "gx")

    def finish(*refs):
        down_ref, mixed_ref, gain_ref, out_ref = refs[nx:]
        square = sum(r[...] for r in refs[:nx])[:, 0:1]
        scale = lax.rsqrt(square / D + EPSILON)
        out = mixed_ref[...] + down_ref[...] * scale * (1.0 + gain_ref[3:4])
        out_ref[...] = out.reshape(beams, steps, width).astype(BF)

    (out,) = run("finish", finish, [(inputs.shape, BF)], (*sums, down, mixed, norm_gains))
    return out


def body_general(
    inputs,
    cache_pool,
    lengths,
    block_table,
    parents,
    norm_gains,
    w_query,
    w_key,
    w_value,
    w_out,
    w_gate,
    w_up,
    w_down,
):
    beams, steps, width = inputs.shape
    nx, ny = lax.axis_size("gx"), lax.axis_size("gy")
    rows = beams * steps
    part = rows // nx
    head_part = w_out.shape[0]
    hidden_part = w_gate.shape[1]
    query_part, key_part = w_query.shape[1], w_key.shape[1]
    columns = query_part + 2 * key_part
    share = columns // nx
    x_own = inputs.reshape(rows, width)
    me = lax.axis_index("gx")

    x_all = exchange(jnp.broadcast_to(x_own[None], (ny, rows, width)), "gy")
    flat = (x_all.astype(F32) * (1.0 + norm_gains[0:1])).astype(BF).reshape(ny * rows, width)
    sums = [jnp.dot(flat, w, preferred_element_type=F32) for w in (w_query, w_key, w_value)]
    sums = jnp.concatenate(sums, axis=1).reshape(ny, rows, nx, share)
    received = exchange_all(sums.transpose(2, 0, 1, 3).astype(BF))
    shares = jnp.sum(received.astype(F32), axis=0).astype(BF)
    every = lax.all_gather(shares, "gx", axis=0)
    every = every.transpose(2, 1, 0, 3).reshape(rows, ny, columns)
    q = every[..., :query_part].reshape(rows, HEADS, 2, HALF).transpose(2, 1, 0, 3)
    k, v = (
        every[..., start : start + key_part].reshape(rows, 2 * KV_HEADS, HALF).transpose(1, 0, 2)
        for start in (query_part, query_part + key_part)
    )
    shares = jnp.concatenate([q, k[None], v[None]], axis=0)
    square = lax.psum(row_sum(jnp.square(x_own.astype(F32))), "gx")
    high = lax.reduce_precision(square, 8, 7)
    squares = jnp.where(jnp.arange(HALF) < HALF // 2, high, square - high).astype(BF)[None]
    cos, sin = rope_tables(lengths, rows, steps)

    def attention(*refs):
        g_ref, square_ref, tables, pool_ref = refs[0], refs[1], refs[2:6], refs[6]
        out_ref, keys_ref, sems = refs[7:]

        def store(head, num, den):
            den = high_low(den, PAGE)
            for rep in range(REPS):
                here = slice(rep * rows, (rep + 1) * rows)
                out_ref[REPS * head + rep, :, 0:HEAD_DIM] = num[here].astype(BF)
                out_ref[REPS * head + rep, :, HEAD_DIM:] = den[here].astype(BF)

        attend(
            lambda share, which: g_ref[share, which],
            square_ref[...],
            tables,
            pool_ref,
            (keys_ref, sems),
            store,
        )

    tables = make_tables(block_table, lengths, parents, cache_pool.shape[1], rows, steps)
    (terms,) = run(
        "attention",
        attention,
        [((HEADS, rows, WIDE), BF)],
        (shares, squares, cos, sin, *tables, cache_pool),
        scratch=key_scratch(cache_pool),
        limit=24,
        specs={6: IN_HBM},
    )
    num = terms[..., :HEAD_DIM].transpose(1, 0, 2).reshape(nx, part, ny, head_part)
    den = terms[..., HEAD_DIM :: PAGE // 2].transpose(1, 0, 2)
    den = jnp.repeat(den, ny // HEADS, axis=1).reshape(nx, part, ny, 2)
    terms = exchange_all(jnp.concatenate([num, den], axis=-1).transpose(0, 2, 1, 3))

    w_wide = lax.all_gather(w_out, "gx", axis=1, tiled=True)
    x_wide = lax.all_gather(x_own, "gx", axis=1, tiled=True)
    x_rows = lax.dynamic_slice_in_dim(x_wide, me * part, part, 0).astype(F32)
    gains = 1.0 + lax.all_gather(norm_gains, "gx", axis=1, tiled=True)

    def scaled(v, gain):
        return v * lax.rsqrt(row_sum(v * v) / D + EPSILON) * gain

    terms = jnp.sum(terms.astype(F32), axis=0)
    den = terms[..., head_part : head_part + 1] + terms[..., -1:]
    attended = (terms[..., :head_part] / den).reshape(ny * part, head_part).astype(BF)
    attn = jnp.dot(attended, w_wide, preferred_element_type=F32).astype(BF)
    attn = exchange(attn.reshape(ny, part, D), "gy").astype(F32).sum(axis=0)
    mixed = x_rows + scaled(attn, gains[1])
    ff_input = scaled(mixed, gains[2]).astype(BF)
    ff_input = ff_input.reshape(part, nx, width).transpose(1, 0, 2)[:, None]
    ff_input = exchange_all(jnp.broadcast_to(ff_input, (nx, ny, part, width)))

    flat = ff_input.reshape(-1, width)
    both = [jnp.dot(flat, w, preferred_element_type=F32).astype(BF) for w in (w_gate, w_up)]
    both = jnp.stack(both, axis=1).reshape(nx, ny * part, 2, hidden_part)
    both = jnp.sum(exchange(both, "gx").astype(F32), axis=0)
    hidden = (jax.nn.gelu(both[:, 0], approximate=True) * both[:, 1]).astype(BF)
    hidden = lax.all_gather(hidden, "gx", axis=0, tiled=True)
    down = jnp.dot(hidden, w_down, preferred_element_type=F32).astype(BF)
    down = exchange_all(down.reshape(nx, ny, part, width)).astype(F32).sum(axis=1)
    down = down.transpose(1, 0, 2).reshape(part, D)
    out = (mixed + scaled(down, gains[3])).astype(BF)
    out = exchange(out.reshape(part, nx, width).transpose(1, 0, 2), "gx")
    return out.reshape(beams, steps, width)


def solution(mesh):
    sizes = dict(mesh.shape)
    fits = sizes["gx"] == 4 and sizes["gy"] == HEADS
    return jax.shard_map(
        body_permutes if fits else body_general,
        mesh=mesh,
        in_specs=(
            P("gy", None, "gx"),
            P(None, "gx", "gy", None),
            P("gy"),
            P("gy", None),
            P(None, "gy"),
            P(None, "gx"),
            P("gx", "gy"),
            P("gx", "gy"),
            P("gx", "gy"),
            P("gy", "gx"),
            P("gx", "gy"),
            P("gx", "gy"),
            P("gy", "gx"),
        ),
        out_specs=P("gy", None, "gx"),
        check_vma=False,
    )
```

```python
import jax
import jax.numpy as jnp
from jax import lax
from jax.experimental import pallas as pl
from jax.experimental.pallas import tpu as pltpu
from jax.sharding import PartitionSpec as P

D = 2304
HEADS = 8
KV_HEADS = 4
HEAD_DIM = 256
HALF = HEAD_DIM // 2
WINDOW = 4096
PAGE = 128
BEAM = 8
EPSILON = 1e-06
SOFT_CAP = 50.0
ROPE_BASE = 10000.0
REPS = HEADS // KV_HEADS
WIDE = HEAD_DIM + PAGE
HALF_PAGE = PAGE // 2
BF = jnp.bfloat16
F32 = jnp.float32
MIB = 1024 * 1024
NT = (((1,), (1,)), ((), ()))
IN_HBM = pl.BlockSpec(memory_space=pltpu.HBM)
IN_SMEM = pl.BlockSpec(memory_space=pltpu.SMEM)


def run(name, kernel, outs, args, scratch=(), limit=16, specs=None, micros=0):
    cost = pl.CostEstimate(flops=micros * 10**9, bytes_accessed=0, transcendentals=0)
    specs = specs or {}
    vmem = pl.BlockSpec(memory_space=pltpu.VMEM)
    return pl.pallas_call(
        kernel,
        out_shape=[jax.ShapeDtypeStruct(s, d) for s, d in outs],
        in_specs=[specs.get(n, vmem) for n in range(len(args))],
        scratch_shapes=scratch,
        compiler_params=pltpu.CompilerParams(vmem_limit_bytes=limit * MIB),
        cost_estimate=cost if micros else None,
        name=name,
    )(*args)


def exchange(values, axes):
    return lax.all_to_all(values, axes, split_axis=0, concat_axis=0, tiled=True)


def exchange_all(values):
    nx, ny = values.shape[:2]
    flat = values.reshape((nx * ny,) + values.shape[2:])
    return exchange(flat, ("gx", "gy")).reshape(values.shape)


def permute(values, axis, m):
    count = lax.axis_size(axis)
    return lax.ppermute(values, axis, [(i, i ^ m) for i in range(count)])


def trade(blocks, axis):
    return [blocks[0]] + [permute(blocks[m], axis, m) for m in range(1, len(blocks))]


def gather_gx(values):
    across = permute(values, "gx", 2)
    return [values, permute(values, "gx", 1), across, permute(across, "gx", 1)]


def weight_of(scores):
    return jnp.exp(SOFT_CAP * jnp.tanh(scores * (1.0 / SOFT_CAP)))


def high_low(column, lanes):
    shape = column.shape[:-1] + (lanes,)
    high = column.astype(BF).astype(F32)
    lane = lax.broadcasted_iota(jnp.int32, shape, len(shape) - 1)
    return jnp.where(lane < lanes // 2, high, column - high)


def pack_lanes(v):
    rows, width = v.shape
    whole = width // 128 * 128
    tiles = [v[:, c : c + 128] for c in range(0, whole, 128)]
    last = jnp.concatenate([v[: rows // 2, whole:], v[rows // 2 :, whole:]], axis=1)
    return jnp.concatenate(tiles + [last], axis=0)


def unpack_lanes(v, rows):
    whole = v.shape[0] // rows * rows
    tiles = [v[r : r + rows] for r in range(0, whole, rows)]
    last = jnp.concatenate([v[whole:, :64], v[whole:, 64:]], axis=0)
    return jnp.concatenate(tiles + [last], axis=1)


def row_sum(v):
    return jnp.sum(v, axis=-1, keepdims=True)


def make_tables(table, lengths, parents, slots, rows, steps):
    def tables(table_ref, length_ref, parents_ref, cached_ref, own_ref, page_ref):
        first_owner = lax.axis_index("gx") * slots
        length = length_ref[0]
        first_page = jnp.maximum(length - WINDOW + 1, 0) // PAGE
        for slot in range(slots + 1):
            page_ref[slot] = -1
        for j in range(table_ref.shape[1]):
            slot = table_ref[0, j] - first_owner
            page_ref[jnp.where((slot >= 0) & (slot < slots), slot, slots)] = j
        step = lax.broadcasted_iota(jnp.int32, (8, PAGE), 0) % steps
        lane = lax.broadcasted_iota(jnp.int32, (8, PAGE), 1)
        for slot in range(slots):
            page = page_ref[slot]
            position = lane + jnp.where(page >= 0, (first_page + page) * PAGE, 2**30)
            seen = (position < length) & (position >= length + step - (WINDOW - 1))
            cached_ref[:, slot * PAGE : (slot + 1) * PAGE] = jnp.where(seen, 1.0, 0.0)

        shape = (REPS * rows, rows)
        row = lax.broadcasted_iota(jnp.int32, shape, 0) % rows
        column = lax.broadcasted_iota(jnp.int32, shape, 1)
        row_step, column_step, column_beam = row % steps, column % steps, column // steps
        current = row // steps
        visible = jnp.zeros(shape, jnp.bool_)
        for j in range(steps - 1, -1, -1):
            if j < steps - 1:
                parent = jnp.zeros(shape, jnp.int32)
                for beam in range(BEAM):
                    parent = jnp.where(current == beam, parents_ref[j, beam], parent)
                current = jnp.where(row_step > j, parent, current)
            visible = visible | ((column_step == j) & (row_step >= j) & (column_beam == current))
        visible = visible & (lax.axis_index("gx") == 0)
        own_ref[...] = jnp.where(visible, 1.0, 0.0)

    return run(
        "tables",
        tables,
        [((8, slots * PAGE), F32), ((REPS * rows, rows), F32)],
        (table, lengths, parents),
        scratch=[pltpu.SMEM((slots + 1,), jnp.int32)],
        specs={0: IN_SMEM, 1: IN_SMEM, 2: IN_SMEM},
    )


def attend(shares, squares, tables, pool_ref, kept, store):
    cos_ref, sin_ref, cached_ref, own_ref = tables
    keys_ref, sems = kept
    slots = pool_ref.shape[1]
    rows = cos_ref.shape[0]
    copies = []
    for head in range(KV_HEADS):
        here = pool_ref.at[:, :, :, head * HEAD_DIM : (head + 1) * HEAD_DIM]
        copies.append(pltpu.make_async_copy(here, keys_ref.at[head], sems.at[head]))
        copies[-1].start()
    square = jnp.sum(squares.astype(F32), axis=0)
    square = square[:, 0:1] + square[:, HALF // 2 : HALF // 2 + 1]
    scale = lax.rsqrt(square / D + EPSILON)
    cos, sin = cos_ref[...] * scale, sin_ref[...] * scale
    cached, own = cached_ref[...], own_ref[...]

    def rotated(u, w):
        u, w = u.astype(F32), w.astype(F32)
        return u * cos - w * sin, w * cos + u * sin

    for head in range(KV_HEADS):
        query = []
        for rep in range(REPS):
            u, w = rotated(shares(0, REPS * head + rep), shares(1, REPS * head + rep))
            query.append(jnp.concatenate([u, w], axis=1) * HEAD_DIM ** (-0.5))
        query = jnp.concatenate(query, axis=0).astype(BF)
        first, second = 2 * head, 2 * head + 1
        key_step = rotated(shares(2, first), shares(2, second))
        key_step = jnp.concatenate(key_step, axis=1).astype(BF)
        value_step = [shares(3, n).astype(F32) * scale for n in (first, second)]
        value_step = jnp.concatenate(value_step, axis=1).astype(BF)

        scores = lax.dot_general(query, key_step, NT, preferred_element_type=F32)
        weights = weight_of(scores) * own
        den = row_sum(weights)
        num = jnp.dot(weights.astype(BF), value_step, preferred_element_type=F32)

        copies[head].wait()
        keys = keys_ref[head, 0].reshape(slots * PAGE, HEAD_DIM)
        values = keys_ref[head, 1].reshape(slots * PAGE, HEAD_DIM)
        scores = lax.dot_general(query, keys, NT, preferred_element_type=F32)
        weights = weight_of(scores).reshape(REPS * rows // 8, 8, slots * PAGE) * cached[None]
        weights = weights.reshape(REPS * rows, slots * PAGE)
        den = den + row_sum(weights)
        num = num + jnp.dot(weights.astype(BF), values, preferred_element_type=F32)
        store(head, num, den)


def key_scratch(pool):
    return [
        pltpu.VMEM((KV_HEADS, 2) + pool.shape[1:3] + (HEAD_DIM,), BF),
        pltpu.SemaphoreType.DMA((KV_HEADS,)),
    ]


def rope_tables(lengths, rows, steps):
    positions = lengths[0] + jnp.arange(rows, dtype=jnp.int32) % steps
    inverse_freq = ROPE_BASE ** (-jnp.arange(HALF, dtype=F32) * 2.0 / HEAD_DIM)
    angles = positions[:, None].astype(F32) * inverse_freq
    return jnp.cos(angles), jnp.sin(angles)


def body_permutes(
    inputs,
    cache_pool,
    lengths,
    block_table,
    parents,
    norm_gains,
    w_query,
    w_key,
    w_value,
    w_out,
    w_gate,
    w_up,
    w_down,
):
    beams, steps, width = inputs.shape
    nx, ny = lax.axis_size("gx"), lax.axis_size("gy")
    rows = beams * steps
    half = rows // 2
    all_rows = ny * rows
    share_rows = all_rows // nx
    hidden = w_gate.shape[1]
    packed = rows * width // 128

    def my(axis):
        return lax.axis_index(axis)

    def spread(x_ref, own_ref, out_ref):
        own = x_ref[...].astype(F32).reshape(rows, width).astype(BF)
        own_ref[...] = own
        own = pack_lanes(own)
        for m in range(ny):
            out_ref[m] = own

    x_own, x_all = run(
        "spread", spread, [((rows, width), BF), ((ny, packed, 128), BF)], (inputs,), micros=12
    )
    x_all = exchange(x_all, "gy")

    w_own = w_out.T
    w_blocks = {0: w_own, 1: permute(w_own, "gy", 1), 4: permute(w_own, "gy", 4)}
    w_late, _ = lax.optimization_barrier((w_blocks, x_all))
    w_blocks[2] = permute(w_late[0], "gy", 2)
    w_blocks[5] = permute(w_late[4], "gy", 1)

    def project(x_ref, gain_ref, q_ref, k_ref, v_ref, z0_ref, z2_ref, z13_ref, held):
        gain = 1.0 + gain_ref[0:1]
        flat = [
            (unpack_lanes(x_ref[m], rows).astype(F32) * gain).astype(BF) for m in range(ny)
        ]
        flat = jnp.concatenate(flat, axis=0)
        query = jnp.dot(flat, q_ref[...], preferred_element_type=F32).astype(BF)
        held[0], held[1] = query[:, :HALF], query[:, HALF:]
        held[2] = jnp.dot(flat, k_ref[...], preferred_element_type=F32).astype(BF)
        held[3] = jnp.dot(flat, v_ref[...], preferred_element_type=F32).astype(BF)
        me = my("gx")
        z0_ref[...], z2_ref[...] = held[me], held[me ^ 2]
        z13_ref[0], z13_ref[1] = held[me ^ 1], held[me ^ 3]

    shape = (all_rows, HALF)
    z0, z2, z13 = run(
        "project",
        project,
        [(shape, BF), (shape, BF), ((2,) + shape, BF)],
        (x_all, norm_gains, w_query, w_key, w_value),
        scratch=[
            pltpu.VMEM((nx,) + shape, BF),
        ],
    )
    z13 = permute(z13, "gx", 1)

    def pair_sum(z_ref, from_pair_ref, out_ref):
        total = z_ref[...].astype(F32) + from_pair_ref[1].astype(F32)
        out_ref[...] = total.astype(BF)

    (z2,) = run("pair_sum", pair_sum, [(shape, BF)], (z2, z13))
    z2 = permute(z2, "gx", 2)

    def share_sum(z0_ref, z13_ref, z2_ref, out_ref):
        total = z0_ref[...].astype(F32) + z13_ref[0].astype(F32) + z2_ref[...].astype(F32)
        out_ref[...] = total.reshape(ny, rows, HALF).astype(BF)

    (shares,) = run("share_sum", share_sum, [((ny, rows, HALF), BF)], (z0, z13, z2))
    shares, *late = lax.optimization_barrier((shares, block_table, lengths, parents))
    cos, sin = rope_tables(late[1], rows, steps)
    tables = make_tables(*late, cache_pool.shape[1], rows, steps)
    shares = exchange(shares, "gy")
    beside = tables, cos, sin, w_blocks[2], w_blocks[5]
    shares, (tables, cos, sin, *_) = lax.optimization_barrier((shares, beside))

    def pack_shares(share_ref, x_ref, out_ref):
        x = x_ref[...].astype(F32)
        out_ref[0:ny] = share_ref[...]
        out_ref[ny] = high_low(row_sum(x * x), HALF).astype(BF)

    (shares,) = run(
        "pack_shares", pack_shares, [((ny + 1, rows, HALF), BF)], (shares, x_own), micros=5
    )
    shares = gather_gx(shares)
    w_late, _ = lax.optimization_barrier((w_blocks, shares[2]))
    w_blocks[6] = permute(w_late[4], "gy", 2)
    w_blocks[3] = permute(w_late[2], "gy", 1)

    def attention(*refs):
        a_refs, tables, pool_ref, outs = refs[:nx], refs[nx : nx + 4], refs[nx + 4], refs[nx + 5 :]
        own_ref, pair_ref, keys_ref, sems, held, num_held, den_held = outs
        me = my("gx")
        core = me & 1
        for n, ref in enumerate(a_refs):
            held[me ^ n] = ref[...]
        den_held[...] = jnp.zeros(den_held.shape, F32)
        lane = lax.broadcasted_iota(jnp.int32, (2, half, PAGE), 2)

        def store(head, num, den):
            num_held[head] = num.reshape(REPS, 2, half, HEAD_DIM)
            den = high_low(den, PAGE).reshape(REPS, 2, half, PAGE)
            for rep in range(REPS):
                at = REPS * head + rep
                den_held[...] = jnp.where(lane % HALF_PAGE == at, den[rep], den_held[...])
                for n, out in enumerate((own_ref, pair_ref)):
                    for tile in range(2):
                        here = num_held[head, rep, core ^ n, :, tile * PAGE : (tile + 1) * PAGE]
                        out[2 * at + tile] = here.astype(BF)

        attend(
            lambda share, which: held[share, which],
            held[:, ny],
            tables,
            pool_ref,
            (keys_ref, sems),
            store,
        )
        for n, out in enumerate((own_ref, pair_ref)):
            out[2 * HEADS] = den_held[core ^ n].astype(BF)

    shape = (2 * HEADS + 1, half, PAGE)
    own, pair = run(
        "attention",
        attention,
        [(shape, BF), (shape, BF)],
        (*shares, cos, sin, *tables, cache_pool),
        scratch=key_scratch(cache_pool)
        + [
            pltpu.VMEM((nx,) + shares[0].shape, BF),
            pltpu.VMEM((KV_HEADS, REPS, 2, half, HEAD_DIM), F32),
            pltpu.VMEM((2, half, PAGE), F32),
        ],
        limit=24,
        specs={nx + 4: IN_HBM},
    )
    w_late, _ = lax.optimization_barrier((w_blocks, own))
    w_blocks[7] = permute(w_late[6], "gy", 1)
    pair = permute(pair, "gx", 1)

    def pair_terms(own_ref, pair_ref, out_ref):
        total = own_ref[...].astype(F32) + pair_ref[...].astype(F32)
        out_ref[0 : 2 * HEADS] = total[0 : 2 * HEADS].astype(BF)
        den = total[2 * HEADS]
        den = den[:, :HALF_PAGE] + den[:, HALF_PAGE:]
        high = den.astype(BF).astype(F32)
        out_ref[2 * HEADS] = jnp.concatenate([high, den - high], axis=1).astype(BF)

    (own,) = run("pair_terms", pair_terms, [(shape, BF)], (own, pair))
    across = permute(own, "gx", 2)

    def divide(own_ref, across_ref, out_ref):
        total = own_ref[...].astype(F32) + across_ref[...].astype(F32)
        den = total[2 * HEADS]
        den = den[:, :HALF_PAGE] + den[:, HALF_PAGE:]
        for head in range(HEADS):
            scale = 1.0 / den[:, head : head + 1]
            for tile in range(2):
                at = 2 * head + tile
                out_ref[at] = (total[at] * scale).astype(BF)

    (attended,) = run("divide", divide, [((2 * HEADS, half, PAGE), BF)], (own, across))
    others = permute(attended, "gx", 1)

    def project_out(own_ref, other_ref, x_ref, gain_ref, *refs):
        w_refs, (attn_ref, sums_ref, held) = refs[:ny], refs[ny:]
        core = my("gx") & 1
        held[core], held[1 - core] = own_ref[...], other_ref[...]
        me = my("gy")
        attn = jnp.zeros((rows, width), F32)
        for m, w_ref in enumerate(w_refs):
            at = 2 * (me ^ m)
            flat = [jnp.concatenate([held[n, at], held[n, at + 1]], axis=1) for n in range(2)]
            flat = jnp.concatenate(flat, axis=0)
            attn = attn + lax.dot_general(flat, w_ref[...], NT, preferred_element_type=F32)
        attn_ref[...] = attn
        x = x_ref[...].astype(F32)
        scaled = attn * (1.0 + gain_ref[1:2])
        lane = lax.broadcasted_iota(jnp.int32, (rows, PAGE), 1)
        sums = jnp.zeros((rows, PAGE), F32)
        for n, terms in enumerate((attn * attn, scaled * scaled, x * scaled, x * x)):
            sums = jnp.where(lane == n, row_sum(terms), sums)
        sums_ref[...] = sums

    attn, sums = run(
        "project_out",
        project_out,
        [((rows, width), F32), ((rows, PAGE), F32)],
        (attended, others, x_own, norm_gains, *[w_blocks[m] for m in range(ny)]),
        scratch=[pltpu.VMEM((2, 2 * HEADS, half, PAGE), BF)],
    )
    sums = trade([sums] * nx, "gx")

    def mix(*refs):
        attn_ref, x_ref, gain_ref, mixed_ref, ff_ref = refs[nx:]
        total = sum(r[...] for r in refs[:nx])
        plain, scaled, cross, square = (total[:, n : n + 1] for n in range(4))
        scale = lax.rsqrt(plain / D + EPSILON)
        mixed = x_ref[...].astype(F32) + attn_ref[...] * scale * (1.0 + gain_ref[1:2])
        square = jnp.maximum(square + 2.0 * scale * cross + scale * scale * scaled, 0.0)
        mixed_ref[...] = mixed
        scale = lax.rsqrt(square / D + EPSILON)
        ff_input = (mixed * scale * (1.0 + gain_ref[2:3])).astype(BF)
        ff_input = pack_lanes(ff_input)
        for m in range(ny):
            ff_ref[m] = ff_input

    mixed, ff_input = run(
        "mix",
        mix,
        [((rows, width), F32), ((ny, packed, 128), BF)],
        (*sums, attn, x_own, norm_gains),
    )
    ff_input = exchange(ff_input, "gy")

    groups = ny // nx

    def gate_up(ff_ref, gate_ref, up_ref, z0_ref, z2_ref, z13_ref):
        me = my("gx")
        flat = [
            unpack_lanes(ff_ref[(me ^ n) * groups + group], rows)
            for n in range(nx)
            for group in range(groups)
        ]
        flat = jnp.concatenate(flat, axis=0)
        w_refs = gate_ref, up_ref
        for n, w_ref in enumerate(w_refs):
            sums = jnp.dot(flat, w_ref[...], preferred_element_type=F32).astype(BF)
            here = pl.ds(n * hidden, hidden)
            for p, out in enumerate((z0_ref, z13_ref.at[0], z2_ref, z13_ref.at[1])):
                out[:, here] = sums[p * share_rows : (p + 1) * share_rows]

    shape = (share_rows, 2 * hidden)
    z0, z2, z13 = run(
        "gate_up",
        gate_up,
        [(shape, BF), (shape, BF), ((2,) + shape, BF)],
        (ff_input, w_gate, w_up),
        limit=24,
    )
    z13 = permute(z13, "gx", 1)
    (z2,) = run("pair_sum_ff", pair_sum, [(shape, BF)], (z2, z13))
    z2 = permute(z2, "gx", 2)

    def activate(z0_ref, z13_ref, z2_ref, out_ref):
        total = z0_ref[...].astype(F32) + z13_ref[0].astype(F32) + z2_ref[...].astype(F32)
        gate, up = total[:, :hidden], total[:, hidden:]
        out_ref[...] = (jax.nn.gelu(gate, approximate=True) * up).astype(BF)

    (blocks,) = run("activate", activate, [((share_rows, hidden), BF)], (z0, z13, z2))
    blocks = gather_gx(blocks)

    def project_down(*refs):
        w_ref, out_ref = refs[nx:]
        me = my("gx")
        flat = jnp.concatenate([r[...] for r in refs[:nx]], axis=0)
        sums = lax.dot_general(flat, w_ref[...], NT, preferred_element_type=F32)
        for n in range(nx):
            for group in range(groups):
                at = (n * groups + group) * rows
                block = pack_lanes(sums[at : at + rows].astype(BF))
                out_ref[(me ^ n) * groups + group] = block

    (down,) = run(
        "project_down", project_down, [((ny, packed, 128), BF)], (*blocks, w_down.T)
    )
    down = exchange(down, "gy")

    def down_sum(parts_ref, down_ref, sums_ref):
        down = unpack_lanes(jnp.sum(parts_ref[...].astype(F32), axis=0), rows)
        down_ref[...] = down
        sums_ref[...] = jnp.broadcast_to(row_sum(down * down), (rows, PAGE))

    down, sums = run(
        "down_sum", down_sum, [((rows, width), F32), ((rows, PAGE), F32)], (down,)
    )
    sums = trade([sums] * nx, "gx")

    def finish(*refs):
        down_ref, mixed_ref, gain_ref, out_ref = refs[nx:]
        square = sum(r[...] for r in refs[:nx])[:, 0:1]
        scale = lax.rsqrt(square / D + EPSILON)
        out = mixed_ref[...] + down_ref[...] * scale * (1.0 + gain_ref[3:4])
        out_ref[...] = out.reshape(beams, steps, width).astype(BF)

    (out,) = run("finish", finish, [(inputs.shape, BF)], (*sums, down, mixed, norm_gains))
    return out


def body_general(
    inputs,
    cache_pool,
    lengths,
    block_table,
    parents,
    norm_gains,
    w_query,
    w_key,
    w_value,
    w_out,
    w_gate,
    w_up,
    w_down,
):
    beams, steps, width = inputs.shape
    nx, ny = lax.axis_size("gx"), lax.axis_size("gy")
    rows = beams * steps
    part = rows // nx
    head_part = w_out.shape[0]
    hidden_part = w_gate.shape[1]
    query_part, key_part = w_query.shape[1], w_key.shape[1]
    columns = query_part + 2 * key_part
    share = columns // nx
    x_own = inputs.reshape(rows, width)
    me = lax.axis_index("gx")

    x_all = exchange(jnp.broadcast_to(x_own[None], (ny, rows, width)), "gy")
    flat = (x_all.astype(F32) * (1.0 + norm_gains[0:1])).astype(BF).reshape(ny * rows, width)
    sums = [jnp.dot(flat, w, preferred_element_type=F32) for w in (w_query, w_key, w_value)]
    sums = jnp.concatenate(sums, axis=1).reshape(ny, rows, nx, share)
    received = exchange_all(sums.transpose(2, 0, 1, 3).astype(BF))
    shares = jnp.sum(received.astype(F32), axis=0).astype(BF)
    every = lax.all_gather(shares, "gx", axis=0)
    every = every.transpose(2, 1, 0, 3).reshape(rows, ny, columns)
    q = every[..., :query_part].reshape(rows, HEADS, 2, HALF).transpose(2, 1, 0, 3)
    k, v = (
        every[..., start : start + key_part].reshape(rows, 2 * KV_HEADS, HALF).transpose(1, 0, 2)
        for start in (query_part, query_part + key_part)
    )
    shares = jnp.concatenate([q, k[None], v[None]], axis=0)
    square = lax.psum(row_sum(jnp.square(x_own.astype(F32))), "gx")
    high = lax.reduce_precision(square, 8, 7)
    squares = jnp.where(jnp.arange(HALF) < HALF // 2, high, square - high).astype(BF)[None]
    cos, sin = rope_tables(lengths, rows, steps)

    def attention(*refs):
        g_ref, square_ref, tables, pool_ref = refs[0], refs[1], refs[2:6], refs[6]
        out_ref, keys_ref, sems = refs[7:]

        def store(head, num, den):
            den = high_low(den, PAGE)
            for rep in range(REPS):
                here = slice(rep * rows, (rep + 1) * rows)
                out_ref[REPS * head + rep, :, 0:HEAD_DIM] = num[here].astype(BF)
                out_ref[REPS * head + rep, :, HEAD_DIM:] = den[here].astype(BF)

        attend(
            lambda share, which: g_ref[share, which],
            square_ref[...],
            tables,
            pool_ref,
            (keys_ref, sems),
            store,
        )

    tables = make_tables(block_table, lengths, parents, cache_pool.shape[1], rows, steps)
    (terms,) = run(
        "attention",
        attention,
        [((HEADS, rows, WIDE), BF)],
        (shares, squares, cos, sin, *tables, cache_pool),
        scratch=key_scratch(cache_pool),
        limit=24,
        specs={6: IN_HBM},
    )
    num = terms[..., :HEAD_DIM].transpose(1, 0, 2).reshape(nx, part, ny, head_part)
    den = terms[..., HEAD_DIM :: PAGE // 2].transpose(1, 0, 2)
    den = jnp.repeat(den, ny // HEADS, axis=1).reshape(nx, part, ny, 2)
    terms = exchange_all(jnp.concatenate([num, den], axis=-1).transpose(0, 2, 1, 3))

    w_wide = lax.all_gather(w_out, "gx", axis=1, tiled=True)
    x_wide = lax.all_gather(x_own, "gx", axis=1, tiled=True)
    x_rows = lax.dynamic_slice_in_dim(x_wide, me * part, part, 0).astype(F32)
    gains = 1.0 + lax.all_gather(norm_gains, "gx", axis=1, tiled=True)

    def scaled(v, gain):
        return v * lax.rsqrt(row_sum(v * v) / D + EPSILON) * gain

    terms = jnp.sum(terms.astype(F32), axis=0)
    den = terms[..., head_part : head_part + 1] + terms[..., -1:]
    attended = (terms[..., :head_part] / den).reshape(ny * part, head_part).astype(BF)
    attn = jnp.dot(attended, w_wide, preferred_element_type=F32).astype(BF)
    attn = exchange(attn.reshape(ny, part, D), "gy").astype(F32).sum(axis=0)
    mixed = x_rows + scaled(attn, gains[1])
    ff_input = scaled(mixed, gains[2]).astype(BF)
    ff_input = ff_input.reshape(part, nx, width).transpose(1, 0, 2)[:, None]
    ff_input = exchange_all(jnp.broadcast_to(ff_input, (nx, ny, part, width)))

    flat = ff_input.reshape(-1, width)
    both = [jnp.dot(flat, w, preferred_element_type=F32).astype(BF) for w in (w_gate, w_up)]
    both = jnp.stack(both, axis=1).reshape(nx, ny * part, 2, hidden_part)
    both = jnp.sum(exchange(both, "gx").astype(F32), axis=0)
    hidden = (jax.nn.gelu(both[:, 0], approximate=True) * both[:, 1]).astype(BF)
    hidden = lax.all_gather(hidden, "gx", axis=0, tiled=True)
    down = jnp.dot(hidden, w_down, preferred_element_type=F32).astype(BF)
    down = exchange_all(down.reshape(nx, ny, part, width)).astype(F32).sum(axis=1)
    down = down.transpose(1, 0, 2).reshape(part, D)
    out = (mixed + scaled(down, gains[3])).astype(BF)
    out = exchange(out.reshape(part, nx, width).transpose(1, 0, 2), "gx")
    return out.reshape(beams, steps, width)


def solution(mesh):
    sizes = dict(mesh.shape)
    fits = sizes["gx"] == 4 and sizes["gy"] == HEADS
    return jax.shard_map(
        body_permutes if fits else body_general,
        mesh=mesh,
        in_specs=(
            P("gy", None, "gx"),
            P(None, "gx", "gy", None),
            P("gy"),
            P("gy", None),
            P(None, "gy"),
            P(None, "gx"),
            P("gx", "gy"),
            P("gx", "gy"),
            P("gx", "gy"),
            P("gy", "gx"),
            P("gx", "gy"),
            P("gx", "gy"),
            P("gy", "gx"),
        ),
        out_specs=P("gy", None, "gx"),
        check_vma=False,
    )
```

```python
import jax
import jax.numpy as jnp
from jax import lax
from jax.experimental import pallas as pl
from jax.experimental.pallas import tpu as pltpu
from jax.sharding import PartitionSpec as P

D = 2304
HEADS = 8
KV_HEADS = 4
HEAD_DIM = 256
HALF = HEAD_DIM // 2
WINDOW = 4096
PAGE = 128
BEAM = 8
EPSILON = 1e-06
SOFT_CAP = 50.0
ROPE_BASE = 10000.0
REPS = HEADS // KV_HEADS
WIDE = HEAD_DIM + PAGE
HALF_PAGE = PAGE // 2
BF = jnp.bfloat16
F32 = jnp.float32
MIB = 1024 * 1024
NT = (((1,), (1,)), ((), ()))
IN_HBM = pl.BlockSpec(memory_space=pltpu.HBM)
IN_SMEM = pl.BlockSpec(memory_space=pltpu.SMEM)


def run(name, kernel, outs, args, scratch=(), limit=16, specs=None, micros=0):
    cost = pl.CostEstimate(flops=micros * 10**9, bytes_accessed=0, transcendentals=0)
    specs = specs or {}
    vmem = pl.BlockSpec(memory_space=pltpu.VMEM)
    return pl.pallas_call(
        kernel,
        out_shape=[jax.ShapeDtypeStruct(s, d) for s, d in outs],
        in_specs=[specs.get(n, vmem) for n in range(len(args))],
        scratch_shapes=scratch,
        compiler_params=pltpu.CompilerParams(vmem_limit_bytes=limit * MIB),
        cost_estimate=cost if micros else None,
        name=name,
    )(*args)


def exchange(values, axes):
    return lax.all_to_all(values, axes, split_axis=0, concat_axis=0, tiled=True)


def exchange_all(values):
    nx, ny = values.shape[:2]
    flat = values.reshape((nx * ny,) + values.shape[2:])
    return exchange(flat, ("gx", "gy")).reshape(values.shape)


def permute(values, axis, m):
    count = lax.axis_size(axis)
    return lax.ppermute(values, axis, [(i, i ^ m) for i in range(count)])


def trade(blocks, axis):
    return [blocks[0]] + [permute(blocks[m], axis, m) for m in range(1, len(blocks))]


def gather_gx(values):
    across = permute(values, "gx", 2)
    return [values, permute(values, "gx", 1), across, permute(across, "gx", 1)]


def weight_of(scores):
    return jnp.exp(SOFT_CAP * jnp.tanh(scores * (1.0 / SOFT_CAP)))


def high_low(column, lanes):
    shape = column.shape[:-1] + (lanes,)
    high = column.astype(BF).astype(F32)
    lane = lax.broadcasted_iota(jnp.int32, shape, len(shape) - 1)
    return jnp.where(lane < lanes // 2, high, column - high)


def pack_lanes(v):
    rows, width = v.shape
    whole = width // 128 * 128
    tiles = [v[:, c : c + 128] for c in range(0, whole, 128)]
    last = jnp.concatenate([v[: rows // 2, whole:], v[rows // 2 :, whole:]], axis=1)
    return jnp.concatenate(tiles + [last], axis=0)


def unpack_lanes(v, rows):
    whole = v.shape[0] // rows * rows
    tiles = [v[r : r + rows] for r in range(0, whole, rows)]
    last = jnp.concatenate([v[whole:, :64], v[whole:, 64:]], axis=0)
    return jnp.concatenate(tiles + [last], axis=1)


def row_sum(v):
    return jnp.sum(v, axis=-1, keepdims=True)


def make_tables(table, lengths, parents, slots, rows, steps):
    def tables(table_ref, length_ref, parents_ref, cached_ref, own_ref, page_ref):
        first_owner = lax.axis_index("gx") * slots
        length = length_ref[0]
        first_page = jnp.maximum(length - WINDOW + 1, 0) // PAGE
        for slot in range(slots + 1):
            page_ref[slot] = -1
        for j in range(table_ref.shape[1]):
            slot = table_ref[0, j] - first_owner
            page_ref[jnp.where((slot >= 0) & (slot < slots), slot, slots)] = j
        step = lax.broadcasted_iota(jnp.int32, (8, PAGE), 0) % steps
        lane = lax.broadcasted_iota(jnp.int32, (8, PAGE), 1)
        for slot in range(slots):
            page = page_ref[slot]
            position = lane + jnp.where(page >= 0, (first_page + page) * PAGE, 2**30)
            seen = (position < length) & (position >= length + step - (WINDOW - 1))
            cached_ref[:, slot * PAGE : (slot + 1) * PAGE] = jnp.where(seen, 1.0, 0.0)

        shape = (REPS * rows, rows)
        row = lax.broadcasted_iota(jnp.int32, shape, 0) % rows
        column = lax.broadcasted_iota(jnp.int32, shape, 1)
        row_step, column_step, column_beam = row % steps, column % steps, column // steps
        current = row // steps
        visible = jnp.zeros(shape, jnp.bool_)
        for j in range(steps - 1, -1, -1):
            if j < steps - 1:
                parent = jnp.zeros(shape, jnp.int32)
                for beam in range(BEAM):
                    parent = jnp.where(current == beam, parents_ref[j, beam], parent)
                current = jnp.where(row_step > j, parent, current)
            visible = visible | ((column_step == j) & (row_step >= j) & (column_beam == current))
        visible = visible & (lax.axis_index("gx") == 0)
        own_ref[...] = jnp.where(visible, 1.0, 0.0)

    return run(
        "tables",
        tables,
        [((8, slots * PAGE), F32), ((REPS * rows, rows), F32)],
        (table, lengths, parents),
        scratch=[pltpu.SMEM((slots + 1,), jnp.int32)],
        specs={0: IN_SMEM, 1: IN_SMEM, 2: IN_SMEM},
    )


def attend(shares, squares, tables, pool_ref, kept, store):
    cos_ref, sin_ref, cached_ref, own_ref = tables
    keys_ref, sems = kept
    slots = pool_ref.shape[1]
    rows = cos_ref.shape[0]
    copies = []
    for head in range(KV_HEADS):
        here = pool_ref.at[:, :, :, head * HEAD_DIM : (head + 1) * HEAD_DIM]
        copies.append(pltpu.make_async_copy(here, keys_ref.at[head], sems.at[head]))
        copies[-1].start()
    square = jnp.sum(squares.astype(F32), axis=0)
    square = square[:, 0:1] + square[:, HALF // 2 : HALF // 2 + 1]
    scale = lax.rsqrt(square / D + EPSILON)
    cos, sin = cos_ref[...] * scale, sin_ref[...] * scale
    cached, own = cached_ref[...], own_ref[...]

    def rotated(u, w):
        u, w = u.astype(F32), w.astype(F32)
        return u * cos - w * sin, w * cos + u * sin

    for head in range(KV_HEADS):
        query = []
        for rep in range(REPS):
            u, w = rotated(shares(0, REPS * head + rep), shares(1, REPS * head + rep))
            query.append(jnp.concatenate([u, w], axis=1) * HEAD_DIM ** (-0.5))
        query = jnp.concatenate(query, axis=0).astype(BF)
        first, second = 2 * head, 2 * head + 1
        key_step = rotated(shares(2, first), shares(2, second))
        key_step = jnp.concatenate(key_step, axis=1).astype(BF)
        value_step = [shares(3, n).astype(F32) * scale for n in (first, second)]
        value_step = jnp.concatenate(value_step, axis=1).astype(BF)

        scores = lax.dot_general(query, key_step, NT, preferred_element_type=F32)
        weights = weight_of(scores) * own
        den = row_sum(weights)
        num = jnp.dot(weights.astype(BF), value_step, preferred_element_type=F32)

        copies[head].wait()
        keys = keys_ref[head, 0].reshape(slots * PAGE, HEAD_DIM)
        values = keys_ref[head, 1].reshape(slots * PAGE, HEAD_DIM)
        scores = lax.dot_general(query, keys, NT, preferred_element_type=F32)
        weights = weight_of(scores).reshape(REPS * rows // 8, 8, slots * PAGE) * cached[None]
        weights = weights.reshape(REPS * rows, slots * PAGE)
        den = den + row_sum(weights)
        num = num + jnp.dot(weights.astype(BF), values, preferred_element_type=F32)
        store(head, num, den)


def key_scratch(pool):
    return [
        pltpu.VMEM((KV_HEADS, 2) + pool.shape[1:3] + (HEAD_DIM,), BF),
        pltpu.SemaphoreType.DMA((KV_HEADS,)),
    ]


def rope_tables(lengths, rows, steps):
    positions = lengths[0] + jnp.arange(rows, dtype=jnp.int32) % steps
    inverse_freq = ROPE_BASE ** (-jnp.arange(HALF, dtype=F32) * 2.0 / HEAD_DIM)
    angles = positions[:, None].astype(F32) * inverse_freq
    return jnp.cos(angles), jnp.sin(angles)


def body_permutes(
    inputs,
    cache_pool,
    lengths,
    block_table,
    parents,
    norm_gains,
    w_query,
    w_key,
    w_value,
    w_out,
    w_gate,
    w_up,
    w_down,
):
    beams, steps, width = inputs.shape
    nx, ny = lax.axis_size("gx"), lax.axis_size("gy")
    rows = beams * steps
    half = rows // 2
    all_rows = ny * rows
    share_rows = all_rows // nx
    hidden = w_gate.shape[1]
    packed = rows * width // 128

    def my(axis):
        return lax.axis_index(axis)

    def spread(x_ref, own_ref, out_ref):
        own = x_ref[...].astype(F32).reshape(rows, width).astype(BF)
        own_ref[...] = own
        own = pack_lanes(own)
        for m in range(ny):
            out_ref[m] = own

    x_own, x_all = run(
        "spread", spread, [((rows, width), BF), ((ny, packed, 128), BF)], (inputs,), micros=12
    )
    w_own = w_out.T
    x_all, w_split = lax.optimization_barrier((x_all, w_own))
    x_all = exchange(x_all, "gy")

    w_blocks = {0: w_own, 1: permute(w_own, "gy", 1), 2: permute(w_own, "gy", 2)}
    w_first = permute(w_split[: width // 2], "gy", 4)
    w_late, _ = lax.optimization_barrier(((w_blocks, w_split[width // 2 :]), x_all))
    w_blocks[3] = permute(w_late[0][2], "gy", 1)
    w_second = permute(w_late[1], "gy", 4)

    def project(x_ref, gain_ref, q_ref, k_ref, v_ref, z0_ref, z2_ref, z13_ref, held):
        gain = 1.0 + gain_ref[0:1]
        flat = [
            (unpack_lanes(x_ref[m], rows).astype(F32) * gain).astype(BF) for m in range(ny)
        ]
        flat = jnp.concatenate(flat, axis=0)
        query = jnp.dot(flat, q_ref[...], preferred_element_type=F32).astype(BF)
        held[0], held[1] = query[:, :HALF], query[:, HALF:]
        held[2] = jnp.dot(flat, k_ref[...], preferred_element_type=F32).astype(BF)
        held[3] = jnp.dot(flat, v_ref[...], preferred_element_type=F32).astype(BF)
        me = my("gx")
        z0_ref[...], z2_ref[...] = held[me], held[me ^ 2]
        z13_ref[0], z13_ref[1] = held[me ^ 1], held[me ^ 3]

    shape = (all_rows, HALF)
    z0, z2, z13 = run(
        "project",
        project,
        [(shape, BF), (shape, BF), ((2,) + shape, BF)],
        (x_all, norm_gains, w_query, w_key, w_value),
        scratch=[
            pltpu.VMEM((nx,) + shape, BF),
        ],
    )
    z13 = permute(z13, "gx", 1)

    def pair_sum(z_ref, from_pair_ref, out_ref):
        total = z_ref[...].astype(F32) + from_pair_ref[1].astype(F32)
        out_ref[...] = total.astype(BF)

    (z2,) = run("pair_sum", pair_sum, [(shape, BF)], (z2, z13))
    z2 = permute(z2, "gx", 2)

    def share_sum(z0_ref, z13_ref, z2_ref, out_ref):
        total = z0_ref[...].astype(F32) + z13_ref[0].astype(F32) + z2_ref[...].astype(F32)
        out_ref[...] = total.reshape(ny, rows, HALF).astype(BF)

    (shares,) = run("share_sum", share_sum, [((ny, rows, HALF), BF)], (z0, z13, z2))
    shares, *late = lax.optimization_barrier((shares, block_table, lengths, parents))
    cos, sin = rope_tables(late[1], rows, steps)
    tables = make_tables(*late, cache_pool.shape[1], rows, steps)
    shares = exchange(shares, "gy")
    beside = tables, cos, sin, w_blocks[3], w_first, w_second
    shares, (tables, cos, sin, *_) = lax.optimization_barrier((shares, beside))

    def pack_shares(share_ref, x_ref, out_ref):
        x = x_ref[...].astype(F32)
        out_ref[0:ny] = share_ref[...]
        out_ref[ny] = high_low(row_sum(x * x), HALF).astype(BF)

    (shares,) = run(
        "pack_shares", pack_shares, [((ny + 1, rows, HALF), BF)], (shares, x_own), micros=5
    )
    shares = gather_gx(shares)
    w_blocks[4] = jnp.concatenate([w_first, w_second], axis=0)
    w_late, _ = lax.optimization_barrier((w_blocks[4], shares[2]))
    w_blocks[6] = permute(w_late, "gy", 2)
    w_blocks[5] = permute(w_late, "gy", 1)

    def attention(*refs):
        a_refs, tables, pool_ref, outs = refs[:nx], refs[nx : nx + 4], refs[nx + 4], refs[nx + 5 :]
        own_ref, pair_ref, keys_ref, sems, held, num_held, den_held = outs
        me = my("gx")
        core = me & 1
        for n, ref in enumerate(a_refs):
            held[me ^ n] = ref[...]
        den_held[...] = jnp.zeros(den_held.shape, F32)
        lane = lax.broadcasted_iota(jnp.int32, (2, half, PAGE), 2)

        def store(head, num, den):
            num_held[head] = num.reshape(REPS, 2, half, HEAD_DIM)
            den = high_low(den, PAGE).reshape(REPS, 2, half, PAGE)
            for rep in range(REPS):
                at = REPS * head + rep
                den_held[...] = jnp.where(lane % HALF_PAGE == at, den[rep], den_held[...])
                for n, out in enumerate((own_ref, pair_ref)):
                    for tile in range(2):
                        here = num_held[head, rep, core ^ n, :, tile * PAGE : (tile + 1) * PAGE]
                        out[2 * at + tile] = here.astype(BF)

        attend(
            lambda share, which: held[share, which],
            held[:, ny],
            tables,
            pool_ref,
            (keys_ref, sems),
            store,
        )
        for n, out in enumerate((own_ref, pair_ref)):
            out[2 * HEADS] = den_held[core ^ n].astype(BF)

    shape = (2 * HEADS + 1, half, PAGE)
    own, pair = run(
        "attention",
        attention,
        [(shape, BF), (shape, BF)],
        (*shares, cos, sin, *tables, cache_pool),
        scratch=key_scratch(cache_pool)
        + [
            pltpu.VMEM((nx,) + shares[0].shape, BF),
            pltpu.VMEM((KV_HEADS, REPS, 2, half, HEAD_DIM), F32),
            pltpu.VMEM((2, half, PAGE), F32),
        ],
        limit=24,
        specs={nx + 4: IN_HBM},
    )
    w_late, _ = lax.optimization_barrier((w_blocks, own))
    w_blocks[7] = permute(w_late[6], "gy", 1)
    pair = permute(pair, "gx", 1)

    def pair_terms(own_ref, pair_ref, out_ref):
        total = own_ref[...].astype(F32) + pair_ref[...].astype(F32)
        out_ref[0 : 2 * HEADS] = total[0 : 2 * HEADS].astype(BF)
        den = total[2 * HEADS]
        den = den[:, :HALF_PAGE] + den[:, HALF_PAGE:]
        high = den.astype(BF).astype(F32)
        out_ref[2 * HEADS] = jnp.concatenate([high, den - high], axis=1).astype(BF)

    (own,) = run("pair_terms", pair_terms, [(shape, BF)], (own, pair))
    across = permute(own, "gx", 2)

    def divide(own_ref, across_ref, out_ref):
        total = own_ref[...].astype(F32) + across_ref[...].astype(F32)
        den = total[2 * HEADS]
        den = den[:, :HALF_PAGE] + den[:, HALF_PAGE:]
        for head in range(HEADS):
            scale = 1.0 / den[:, head : head + 1]
            for tile in range(2):
                at = 2 * head + tile
                out_ref[at] = (total[at] * scale).astype(BF)

    (attended,) = run("divide", divide, [((2 * HEADS, half, PAGE), BF)], (own, across))
    others = permute(attended, "gx", 1)

    def project_out(own_ref, other_ref, x_ref, gain_ref, *refs):
        w_refs, (attn_ref, sums_ref, held) = refs[:ny], refs[ny:]
        core = my("gx") & 1
        held[core], held[1 - core] = own_ref[...], other_ref[...]
        me = my("gy")
        attn = jnp.zeros((rows, width), F32)
        for m, w_ref in enumerate(w_refs):
            at = 2 * (me ^ m)
            flat = [jnp.concatenate([held[n, at], held[n, at + 1]], axis=1) for n in range(2)]
            flat = jnp.concatenate(flat, axis=0)
            attn = attn + lax.dot_general(flat, w_ref[...], NT, preferred_element_type=F32)
        attn_ref[...] = attn
        x = x_ref[...].astype(F32)
        scaled = attn * (1.0 + gain_ref[1:2])
        lane = lax.broadcasted_iota(jnp.int32, (rows, PAGE), 1)
        sums = jnp.zeros((rows, PAGE), F32)
        for n, terms in enumerate((attn * attn, scaled * scaled, x * scaled, x * x)):
            sums = jnp.where(lane == n, row_sum(terms), sums)
        sums_ref[...] = sums

    attn, sums = run(
        "project_out",
        project_out,
        [((rows, width), F32), ((rows, PAGE), F32)],
        (attended, others, x_own, norm_gains, *[w_blocks[m] for m in range(ny)]),
        scratch=[pltpu.VMEM((2, 2 * HEADS, half, PAGE), BF)],
    )
    sums = trade([sums] * nx, "gx")

    def mix(*refs):
        attn_ref, x_ref, gain_ref, mixed_ref, ff_ref = refs[nx:]
        total = sum(r[...] for r in refs[:nx])
        plain, scaled, cross, square = (total[:, n : n + 1] for n in range(4))
        scale = lax.rsqrt(plain / D + EPSILON)
        mixed = x_ref[...].astype(F32) + attn_ref[...] * scale * (1.0 + gain_ref[1:2])
        square = jnp.maximum(square + 2.0 * scale * cross + scale * scale * scaled, 0.0)
        mixed_ref[...] = mixed
        scale = lax.rsqrt(square / D + EPSILON)
        ff_input = (mixed * scale * (1.0 + gain_ref[2:3])).astype(BF)
        ff_input = pack_lanes(ff_input)
        for m in range(ny):
            ff_ref[m] = ff_input

    mixed, ff_input = run(
        "mix",
        mix,
        [((rows, width), F32), ((ny, packed, 128), BF)],
        (*sums, attn, x_own, norm_gains),
    )
    ff_input = exchange(ff_input, "gy")

    groups = ny // nx

    def gate_up(ff_ref, gate_ref, up_ref, z0_ref, z2_ref, z13_ref):
        me = my("gx")
        flat = [
            unpack_lanes(ff_ref[(me ^ n) * groups + group], rows)
            for n in range(nx)
            for group in range(groups)
        ]
        flat = jnp.concatenate(flat, axis=0)
        w_refs = gate_ref, up_ref
        for n, w_ref in enumerate(w_refs):
            sums = jnp.dot(flat, w_ref[...], preferred_element_type=F32).astype(BF)
            here = pl.ds(n * hidden, hidden)
            for p, out in enumerate((z0_ref, z13_ref.at[0], z2_ref, z13_ref.at[1])):
                out[:, here] = sums[p * share_rows : (p + 1) * share_rows]

    shape = (share_rows, 2 * hidden)
    z0, z2, z13 = run(
        "gate_up",
        gate_up,
        [(shape, BF), (shape, BF), ((2,) + shape, BF)],
        (ff_input, w_gate, w_up),
        limit=24,
    )
    z13 = permute(z13, "gx", 1)
    (z2,) = run("pair_sum_ff", pair_sum, [(shape, BF)], (z2, z13))
    z2 = permute(z2, "gx", 2)

    def activate(z0_ref, z13_ref, z2_ref, out_ref):
        total = z0_ref[...].astype(F32) + z13_ref[0].astype(F32) + z2_ref[...].astype(F32)
        gate, up = total[:, :hidden], total[:, hidden:]
        out_ref[...] = (jax.nn.gelu(gate, approximate=True) * up).astype(BF)

    (blocks,) = run("activate", activate, [((share_rows, hidden), BF)], (z0, z13, z2))
    blocks = gather_gx(blocks)

    def project_down(*refs):
        w_ref, out_ref = refs[nx:]
        me = my("gx")
        flat = jnp.concatenate([r[...] for r in refs[:nx]], axis=0)
        sums = lax.dot_general(flat, w_ref[...], NT, preferred_element_type=F32)
        for n in range(nx):
            for group in range(groups):
                at = (n * groups + group) * rows
                block = pack_lanes(sums[at : at + rows].astype(BF))
                out_ref[(me ^ n) * groups + group] = block

    (down,) = run(
        "project_down", project_down, [((ny, packed, 128), BF)], (*blocks, w_down.T)
    )
    down = exchange(down, "gy")

    def down_sum(parts_ref, down_ref, sums_ref):
        down = unpack_lanes(jnp.sum(parts_ref[...].astype(F32), axis=0), rows)
        down_ref[...] = down
        sums_ref[...] = jnp.broadcast_to(row_sum(down * down), (rows, PAGE))

    down, sums = run(
        "down_sum", down_sum, [((rows, width), F32), ((rows, PAGE), F32)], (down,)
    )
    sums = trade([sums] * nx, "gx")

    def finish(*refs):
        down_ref, mixed_ref, gain_ref, out_ref = refs[nx:]
        square = sum(r[...] for r in refs[:nx])[:, 0:1]
        scale = lax.rsqrt(square / D + EPSILON)
        out = mixed_ref[...] + down_ref[...] * scale * (1.0 + gain_ref[3:4])
        out_ref[...] = out.reshape(beams, steps, width).astype(BF)

    (out,) = run("finish", finish, [(inputs.shape, BF)], (*sums, down, mixed, norm_gains))
    return out


def body_general(
    inputs,
    cache_pool,
    lengths,
    block_table,
    parents,
    norm_gains,
    w_query,
    w_key,
    w_value,
    w_out,
    w_gate,
    w_up,
    w_down,
):
    beams, steps, width = inputs.shape
    nx, ny = lax.axis_size("gx"), lax.axis_size("gy")
    rows = beams * steps
    part = rows // nx
    head_part = w_out.shape[0]
    hidden_part = w_gate.shape[1]
    query_part, key_part = w_query.shape[1], w_key.shape[1]
    columns = query_part + 2 * key_part
    share = columns // nx
    x_own = inputs.reshape(rows, width)
    me = lax.axis_index("gx")

    x_all = exchange(jnp.broadcast_to(x_own[None], (ny, rows, width)), "gy")
    flat = (x_all.astype(F32) * (1.0 + norm_gains[0:1])).astype(BF).reshape(ny * rows, width)
    sums = [jnp.dot(flat, w, preferred_element_type=F32) for w in (w_query, w_key, w_value)]
    sums = jnp.concatenate(sums, axis=1).reshape(ny, rows, nx, share)
    received = exchange_all(sums.transpose(2, 0, 1, 3).astype(BF))
    shares = jnp.sum(received.astype(F32), axis=0).astype(BF)
    every = lax.all_gather(shares, "gx", axis=0)
    every = every.transpose(2, 1, 0, 3).reshape(rows, ny, columns)
    q = every[..., :query_part].reshape(rows, HEADS, 2, HALF).transpose(2, 1, 0, 3)
    k, v = (
        every[..., start : start + key_part].reshape(rows, 2 * KV_HEADS, HALF).transpose(1, 0, 2)
        for start in (query_part, query_part + key_part)
    )
    shares = jnp.concatenate([q, k[None], v[None]], axis=0)
    square = lax.psum(row_sum(jnp.square(x_own.astype(F32))), "gx")
    high = lax.reduce_precision(square, 8, 7)
    squares = jnp.where(jnp.arange(HALF) < HALF // 2, high, square - high).astype(BF)[None]
    cos, sin = rope_tables(lengths, rows, steps)

    def attention(*refs):
        g_ref, square_ref, tables, pool_ref = refs[0], refs[1], refs[2:6], refs[6]
        out_ref, keys_ref, sems = refs[7:]

        def store(head, num, den):
            den = high_low(den, PAGE)
            for rep in range(REPS):
                here = slice(rep * rows, (rep + 1) * rows)
                out_ref[REPS * head + rep, :, 0:HEAD_DIM] = num[here].astype(BF)
                out_ref[REPS * head + rep, :, HEAD_DIM:] = den[here].astype(BF)

        attend(
            lambda share, which: g_ref[share, which],
            square_ref[...],
            tables,
            pool_ref,
            (keys_ref, sems),
            store,
        )

    tables = make_tables(block_table, lengths, parents, cache_pool.shape[1], rows, steps)
    (terms,) = run(
        "attention",
        attention,
        [((HEADS, rows, WIDE), BF)],
        (shares, squares, cos, sin, *tables, cache_pool),
        scratch=key_scratch(cache_pool),
        limit=24,
        specs={6: IN_HBM},
    )
    num = terms[..., :HEAD_DIM].transpose(1, 0, 2).reshape(nx, part, ny, head_part)
    den = terms[..., HEAD_DIM :: PAGE // 2].transpose(1, 0, 2)
    den = jnp.repeat(den, ny // HEADS, axis=1).reshape(nx, part, ny, 2)
    terms = exchange_all(jnp.concatenate([num, den], axis=-1).transpose(0, 2, 1, 3))

    w_wide = lax.all_gather(w_out, "gx", axis=1, tiled=True)
    x_wide = lax.all_gather(x_own, "gx", axis=1, tiled=True)
    x_rows = lax.dynamic_slice_in_dim(x_wide, me * part, part, 0).astype(F32)
    gains = 1.0 + lax.all_gather(norm_gains, "gx", axis=1, tiled=True)

    def scaled(v, gain):
        return v * lax.rsqrt(row_sum(v * v) / D + EPSILON) * gain

    terms = jnp.sum(terms.astype(F32), axis=0)
    den = terms[..., head_part : head_part + 1] + terms[..., -1:]
    attended = (terms[..., :head_part] / den).reshape(ny * part, head_part).astype(BF)
    attn = jnp.dot(attended, w_wide, preferred_element_type=F32).astype(BF)
    attn = exchange(attn.reshape(ny, part, D), "gy").astype(F32).sum(axis=0)
    mixed = x_rows + scaled(attn, gains[1])
    ff_input = scaled(mixed, gains[2]).astype(BF)
    ff_input = ff_input.reshape(part, nx, width).transpose(1, 0, 2)[:, None]
    ff_input = exchange_all(jnp.broadcast_to(ff_input, (nx, ny, part, width)))

    flat = ff_input.reshape(-1, width)
    both = [jnp.dot(flat, w, preferred_element_type=F32).astype(BF) for w in (w_gate, w_up)]
    both = jnp.stack(both, axis=1).reshape(nx, ny * part, 2, hidden_part)
    both = jnp.sum(exchange(both, "gx").astype(F32), axis=0)
    hidden = (jax.nn.gelu(both[:, 0], approximate=True) * both[:, 1]).astype(BF)
    hidden = lax.all_gather(hidden, "gx", axis=0, tiled=True)
    down = jnp.dot(hidden, w_down, preferred_element_type=F32).astype(BF)
    down = exchange_all(down.reshape(nx, ny, part, width)).astype(F32).sum(axis=1)
    down = down.transpose(1, 0, 2).reshape(part, D)
    out = (mixed + scaled(down, gains[3])).astype(BF)
    out = exchange(out.reshape(part, nx, width).transpose(1, 0, 2), "gx")
    return out.reshape(beams, steps, width)


def solution(mesh):
    sizes = dict(mesh.shape)
    fits = sizes["gx"] == 4 and sizes["gy"] == HEADS
    return jax.shard_map(
        body_permutes if fits else body_general,
        mesh=mesh,
        in_specs=(
            P("gy", None, "gx"),
            P(None, "gx", "gy", None),
            P("gy"),
            P("gy", None),
            P(None, "gy"),
            P(None, "gx"),
            P("gx", "gy"),
            P("gx", "gy"),
            P("gx", "gy"),
            P("gy", "gx"),
            P("gx", "gy"),
            P("gx", "gy"),
            P("gy", "gx"),
        ),
        out_specs=P("gy", None, "gx"),
        check_vma=False,
    )
```

```python
import jax
import jax.numpy as jnp
from jax import lax
from jax.experimental import pallas as pl
from jax.experimental.pallas import tpu as pltpu
from jax.sharding import PartitionSpec as P

D = 2304
HEADS = 8
KV_HEADS = 4
HEAD_DIM = 256
HALF = HEAD_DIM // 2
WINDOW = 4096
PAGE = 128
BEAM = 8
EPSILON = 1e-06
SOFT_CAP = 50.0
ROPE_BASE = 10000.0
REPS = HEADS // KV_HEADS
WIDE = HEAD_DIM + PAGE
HALF_PAGE = PAGE // 2
BF = jnp.bfloat16
F32 = jnp.float32
MIB = 1024 * 1024
NT = (((1,), (1,)), ((), ()))
IN_HBM = pl.BlockSpec(memory_space=pltpu.HBM)
IN_SMEM = pl.BlockSpec(memory_space=pltpu.SMEM)


def run(name, kernel, outs, args, scratch=(), limit=16, specs=None, micros=0):
    cost = pl.CostEstimate(flops=micros * 10**9, bytes_accessed=0, transcendentals=0)
    specs = specs or {}
    vmem = pl.BlockSpec(memory_space=pltpu.VMEM)
    return pl.pallas_call(
        kernel,
        out_shape=[jax.ShapeDtypeStruct(s, d) for s, d in outs],
        in_specs=[specs.get(n, vmem) for n in range(len(args))],
        scratch_shapes=scratch,
        compiler_params=pltpu.CompilerParams(vmem_limit_bytes=limit * MIB),
        cost_estimate=cost if micros else None,
        name=name,
    )(*args)


def exchange(values, axes):
    return lax.all_to_all(values, axes, split_axis=0, concat_axis=0, tiled=True)


def exchange_all(values):
    nx, ny = values.shape[:2]
    flat = values.reshape((nx * ny,) + values.shape[2:])
    return exchange(flat, ("gx", "gy")).reshape(values.shape)


def permute(values, axis, m):
    count = lax.axis_size(axis)
    return lax.ppermute(values, axis, [(i, i ^ m) for i in range(count)])


def trade(blocks, axis):
    return [blocks[0]] + [permute(blocks[m], axis, m) for m in range(1, len(blocks))]


def gather_gx(values):
    across = permute(values, "gx", 2)
    return [values, permute(values, "gx", 1), across, permute(across, "gx", 1)]


def weight_of(scores):
    return jnp.exp(SOFT_CAP * jnp.tanh(scores * (1.0 / SOFT_CAP)))


def high_low(column, lanes):
    shape = column.shape[:-1] + (lanes,)
    high = column.astype(BF).astype(F32)
    lane = lax.broadcasted_iota(jnp.int32, shape, len(shape) - 1)
    return jnp.where(lane < lanes // 2, high, column - high)


def pack_lanes(v):
    rows, width = v.shape
    whole = width // 128 * 128
    tiles = [v[:, c : c + 128] for c in range(0, whole, 128)]
    last = jnp.concatenate([v[: rows // 2, whole:], v[rows // 2 :, whole:]], axis=1)
    return jnp.concatenate(tiles + [last], axis=0)


def unpack_lanes(v, rows):
    whole = v.shape[0] // rows * rows
    tiles = [v[r : r + rows] for r in range(0, whole, rows)]
    last = jnp.concatenate([v[whole:, :64], v[whole:, 64:]], axis=0)
    return jnp.concatenate(tiles + [last], axis=1)


def row_sum(v):
    return jnp.sum(v, axis=-1, keepdims=True)


def make_tables(table, lengths, parents, slots, rows, steps):
    def tables(table_ref, length_ref, parents_ref, cached_ref, own_ref, page_ref):
        first_owner = lax.axis_index("gx") * slots
        length = length_ref[0]
        first_page = jnp.maximum(length - WINDOW + 1, 0) // PAGE
        for slot in range(slots + 1):
            page_ref[slot] = -1
        for j in range(table_ref.shape[1]):
            slot = table_ref[0, j] - first_owner
            page_ref[jnp.where((slot >= 0) & (slot < slots), slot, slots)] = j
        step = lax.broadcasted_iota(jnp.int32, (8, PAGE), 0) % steps
        lane = lax.broadcasted_iota(jnp.int32, (8, PAGE), 1)
        for slot in range(slots):
            page = page_ref[slot]
            position = lane + jnp.where(page >= 0, (first_page + page) * PAGE, 2**30)
            seen = (position < length) & (position >= length + step - (WINDOW - 1))
            cached_ref[:, slot * PAGE : (slot + 1) * PAGE] = jnp.where(seen, 1.0, 0.0)

        shape = (REPS * rows, rows)
        row = lax.broadcasted_iota(jnp.int32, shape, 0) % rows
        column = lax.broadcasted_iota(jnp.int32, shape, 1)
        row_step, column_step, column_beam = row % steps, column % steps, column // steps
        current = row // steps
        visible = jnp.zeros(shape, jnp.bool_)
        for j in range(steps - 1, -1, -1):
            if j < steps - 1:
                parent = jnp.zeros(shape, jnp.int32)
                for beam in range(BEAM):
                    parent = jnp.where(current == beam, parents_ref[j, beam], parent)
                current = jnp.where(row_step > j, parent, current)
            visible = visible | ((column_step == j) & (row_step >= j) & (column_beam == current))
        visible = visible & (lax.axis_index("gx") == 0)
        own_ref[...] = jnp.where(visible, 1.0, 0.0)

    return run(
        "tables",
        tables,
        [((8, slots * PAGE), F32), ((REPS * rows, rows), F32)],
        (table, lengths, parents),
        scratch=[pltpu.SMEM((slots + 1,), jnp.int32)],
        specs={0: IN_SMEM, 1: IN_SMEM, 2: IN_SMEM},
    )


def attend(shares, squares, tables, pool_ref, kept, store):
    cos_ref, sin_ref, cached_ref, own_ref = tables
    keys_ref, sems = kept
    slots = pool_ref.shape[1]
    rows = cos_ref.shape[0]
    copies = []
    for head in range(KV_HEADS):
        here = pool_ref.at[:, :, :, head * HEAD_DIM : (head + 1) * HEAD_DIM]
        copies.append(pltpu.make_async_copy(here, keys_ref.at[head], sems.at[head]))
        copies[-1].start()
    square = jnp.sum(squares.astype(F32), axis=0)
    square = square[:, 0:1] + square[:, HALF // 2 : HALF // 2 + 1]
    scale = lax.rsqrt(square / D + EPSILON)
    cos, sin = cos_ref[...] * scale, sin_ref[...] * scale
    cached, own = cached_ref[...], own_ref[...]

    def rotated(u, w):
        u, w = u.astype(F32), w.astype(F32)
        return u * cos - w * sin, w * cos + u * sin

    for head in range(KV_HEADS):
        query = []
        for rep in range(REPS):
            u, w = rotated(shares(0, REPS * head + rep), shares(1, REPS * head + rep))
            query.append(jnp.concatenate([u, w], axis=1) * HEAD_DIM ** (-0.5))
        query = jnp.concatenate(query, axis=0).astype(BF)
        first, second = 2 * head, 2 * head + 1
        key_step = rotated(shares(2, first), shares(2, second))
        key_step = jnp.concatenate(key_step, axis=1).astype(BF)
        value_step = [shares(3, n).astype(F32) * scale for n in (first, second)]
        value_step = jnp.concatenate(value_step, axis=1).astype(BF)

        scores = lax.dot_general(query, key_step, NT, preferred_element_type=F32)
        weights = weight_of(scores) * own
        den = row_sum(weights)
        num = jnp.dot(weights.astype(BF), value_step, preferred_element_type=F32)

        copies[head].wait()
        keys = keys_ref[head, 0].reshape(slots * PAGE, HEAD_DIM)
        values = keys_ref[head, 1].reshape(slots * PAGE, HEAD_DIM)
        scores = lax.dot_general(query, keys, NT, preferred_element_type=F32)
        weights = weight_of(scores).reshape(REPS * rows // 8, 8, slots * PAGE) * cached[None]
        weights = weights.reshape(REPS * rows, slots * PAGE)
        den = den + row_sum(weights)
        num = num + jnp.dot(weights.astype(BF), values, preferred_element_type=F32)
        store(head, num, den)


def key_scratch(pool):
    return [
        pltpu.VMEM((KV_HEADS, 2) + pool.shape[1:3] + (HEAD_DIM,), BF),
        pltpu.SemaphoreType.DMA((KV_HEADS,)),
    ]


def rope_tables(lengths, rows, steps):
    positions = lengths[0] + jnp.arange(rows, dtype=jnp.int32) % steps
    inverse_freq = ROPE_BASE ** (-jnp.arange(HALF, dtype=F32) * 2.0 / HEAD_DIM)
    angles = positions[:, None].astype(F32) * inverse_freq
    return jnp.cos(angles), jnp.sin(angles)


def body_permutes(
    inputs,
    cache_pool,
    lengths,
    block_table,
    parents,
    norm_gains,
    w_query,
    w_key,
    w_value,
    w_out,
    w_gate,
    w_up,
    w_down,
):
    beams, steps, width = inputs.shape
    nx, ny = lax.axis_size("gx"), lax.axis_size("gy")
    rows = beams * steps
    half = rows // 2
    all_rows = ny * rows
    share_rows = all_rows // nx
    hidden = w_gate.shape[1]
    packed = rows * width // 128

    def my(axis):
        return lax.axis_index(axis)

    def spread(x_ref, own_ref, out_ref):
        own = x_ref[...].astype(F32).reshape(rows, width).astype(BF)
        own_ref[...] = own
        own = pack_lanes(own)
        for m in range(ny):
            out_ref[m] = own

    x_own, x_all = run(
        "spread", spread, [((rows, width), BF), ((ny, packed, 128), BF)], (inputs,), micros=12
    )
    w_own = w_out.T
    x_all, w_split = lax.optimization_barrier((x_all, w_own))
    x_all = exchange(x_all, "gy")

    w_blocks = {0: w_own, 1: permute(w_own, "gy", 1), 2: permute(w_own, "gy", 2)}
    w_first = permute(w_split[: width // 2], "gy", 4)

    def project(x_ref, gain_ref, q_ref, k_ref, v_ref, z0_ref, z2_ref, z13_ref, held):
        gain = 1.0 + gain_ref[0:1]
        flat = [
            (unpack_lanes(x_ref[m], rows).astype(F32) * gain).astype(BF) for m in range(ny)
        ]
        flat = jnp.concatenate(flat, axis=0)
        query = jnp.dot(flat, q_ref[...], preferred_element_type=F32).astype(BF)
        held[0], held[1] = query[:, :HALF], query[:, HALF:]
        held[2] = jnp.dot(flat, k_ref[...], preferred_element_type=F32).astype(BF)
        held[3] = jnp.dot(flat, v_ref[...], preferred_element_type=F32).astype(BF)
        me = my("gx")
        z0_ref[...], z2_ref[...] = held[me], held[me ^ 2]
        z13_ref[0], z13_ref[1] = held[me ^ 1], held[me ^ 3]

    shape = (all_rows, HALF)
    z0, z2, z13 = run(
        "project",
        project,
        [(shape, BF), (shape, BF), ((2,) + shape, BF)],
        (x_all, norm_gains, w_query, w_key, w_value),
        scratch=[
            pltpu.VMEM((nx,) + shape, BF),
        ],
    )
    z13 = permute(z13, "gx", 1)

    def pair_sum(z_ref, from_pair_ref, out_ref):
        total = z_ref[...].astype(F32) + from_pair_ref[1].astype(F32)
        out_ref[...] = total.astype(BF)

    (z2,) = run("pair_sum", pair_sum, [(shape, BF)], (z2, z13))
    late, _ = lax.optimization_barrier((lengths, z2))
    cos, sin = rope_tables(late, rows, steps)
    z2 = permute(z2, "gx", 2)
    early = w_split[width // 2 :], w_blocks[2], w_blocks[1], w_first
    early, _ = lax.optimization_barrier((early, cos))
    w_second = permute(early[0], "gy", 4)
    w_blocks[3] = permute(early[1], "gy", 1)

    def share_sum(z0_ref, z13_ref, z2_ref, out_ref):
        total = z0_ref[...].astype(F32) + z13_ref[0].astype(F32) + z2_ref[...].astype(F32)
        out_ref[...] = total.reshape(ny, rows, HALF).astype(BF)

    (shares,) = run("share_sum", share_sum, [((ny, rows, HALF), BF)], (z0, z13, z2))
    shares, *late = lax.optimization_barrier((shares, block_table, lengths, parents))
    tables = make_tables(*late, cache_pool.shape[1], rows, steps)
    shares = exchange(shares, "gy")
    beside = tables, w_first, w_second, w_blocks[3]
    shares, (tables, *_) = lax.optimization_barrier((shares, beside))

    def pack_shares(share_ref, x_ref, out_ref):
        x = x_ref[...].astype(F32)
        out_ref[0:ny] = share_ref[...]
        out_ref[ny] = high_low(row_sum(x * x), HALF).astype(BF)

    (shares,) = run(
        "pack_shares", pack_shares, [((ny + 1, rows, HALF), BF)], (shares, x_own), micros=5
    )
    shares = gather_gx(shares)
    w_blocks[4] = jnp.concatenate([w_first, w_second], axis=0)
    w_late, _ = lax.optimization_barrier((w_blocks[4], shares[1]))
    w_blocks[6] = permute(w_late, "gy", 2)
    w_blocks[5] = permute(w_late, "gy", 1)

    def attention(*refs):
        a_refs, tables, pool_ref, outs = refs[:nx], refs[nx : nx + 4], refs[nx + 4], refs[nx + 5 :]
        own_ref, pair_ref, keys_ref, sems, held, num_held, den_held = outs
        me = my("gx")
        core = me & 1
        for n, ref in enumerate(a_refs):
            held[me ^ n] = ref[...]
        den_held[...] = jnp.zeros(den_held.shape, F32)
        lane = lax.broadcasted_iota(jnp.int32, (2, half, PAGE), 2)

        def store(head, num, den):
            num_held[head] = num.reshape(REPS, 2, half, HEAD_DIM)
            den = high_low(den, PAGE).reshape(REPS, 2, half, PAGE)
            for rep in range(REPS):
                at = REPS * head + rep
                den_held[...] = jnp.where(lane % HALF_PAGE == at, den[rep], den_held[...])
                for n, out in enumerate((own_ref, pair_ref)):
                    for tile in range(2):
                        here = num_held[head, rep, core ^ n, :, tile * PAGE : (tile + 1) * PAGE]
                        out[2 * at + tile] = here.astype(BF)

        attend(
            lambda share, which: held[share, which],
            held[:, ny],
            tables,
            pool_ref,
            (keys_ref, sems),
            store,
        )
        for n, out in enumerate((own_ref, pair_ref)):
            out[2 * HEADS] = den_held[core ^ n].astype(BF)

    shape = (2 * HEADS + 1, half, PAGE)
    own, pair = run(
        "attention",
        attention,
        [(shape, BF), (shape, BF)],
        (*shares, cos, sin, *tables, cache_pool),
        scratch=key_scratch(cache_pool)
        + [
            pltpu.VMEM((nx,) + shares[0].shape, BF),
            pltpu.VMEM((KV_HEADS, REPS, 2, half, HEAD_DIM), F32),
            pltpu.VMEM((2, half, PAGE), F32),
        ],
        limit=24,
        specs={nx + 4: IN_HBM},
        micros=8,
    )
    pair = permute(pair, "gx", 1)

    def pair_terms(own_ref, pair_ref, out_ref):
        total = own_ref[...].astype(F32) + pair_ref[...].astype(F32)
        out_ref[0 : 2 * HEADS] = total[0 : 2 * HEADS].astype(BF)
        den = total[2 * HEADS]
        den = den[:, :HALF_PAGE] + den[:, HALF_PAGE:]
        high = den.astype(BF).astype(F32)
        out_ref[2 * HEADS] = jnp.concatenate([high, den - high], axis=1).astype(BF)

    (own,) = run("pair_terms", pair_terms, [(shape, BF)], (own, pair))
    across = permute(own, "gx", 2)

    w_late, _ = lax.optimization_barrier(((w_blocks[6], w_blocks[5]), own))
    w_blocks[7] = permute(w_late[0], "gy", 1)

    def divide(own_ref, across_ref, out_ref):
        total = own_ref[...].astype(F32) + across_ref[...].astype(F32)
        den = total[2 * HEADS]
        den = den[:, :HALF_PAGE] + den[:, HALF_PAGE:]
        for head in range(HEADS):
            scale = 1.0 / den[:, head : head + 1]
            for tile in range(2):
                at = 2 * head + tile
                out_ref[at] = (total[at] * scale).astype(BF)

    (attended,) = run(
        "divide", divide, [((2 * HEADS, half, PAGE), BF)], (own, across), micros=4
    )
    others = permute(attended, "gx", 1)

    def project_out(own_ref, other_ref, x_ref, gain_ref, *refs):
        w_refs, (attn_ref, sums_ref, held) = refs[:ny], refs[ny:]
        core = my("gx") & 1
        held[core], held[1 - core] = own_ref[...], other_ref[...]
        me = my("gy")
        attn = jnp.zeros((rows, width), F32)
        for m, w_ref in enumerate(w_refs):
            at = 2 * (me ^ m)
            flat = [jnp.concatenate([held[n, at], held[n, at + 1]], axis=1) for n in range(2)]
            flat = jnp.concatenate(flat, axis=0)
            attn = attn + lax.dot_general(flat, w_ref[...], NT, preferred_element_type=F32)
        attn_ref[...] = attn
        x = x_ref[...].astype(F32)
        scaled = attn * (1.0 + gain_ref[1:2])
        lane = lax.broadcasted_iota(jnp.int32, (rows, PAGE), 1)
        sums = jnp.zeros((rows, PAGE), F32)
        for n, terms in enumerate((attn * attn, scaled * scaled, x * scaled, x * x)):
            sums = jnp.where(lane == n, row_sum(terms), sums)
        sums_ref[...] = sums

    attn, sums = run(
        "project_out",
        project_out,
        [((rows, width), F32), ((rows, PAGE), F32)],
        (attended, others, x_own, norm_gains, *[w_blocks[m] for m in range(ny)]),
        scratch=[pltpu.VMEM((2, 2 * HEADS, half, PAGE), BF)],
    )
    sums = trade([sums] * nx, "gx")

    def mix(*refs):
        attn_ref, x_ref, gain_ref, mixed_ref, ff_ref = refs[nx:]
        total = sum(r[...] for r in refs[:nx])
        plain, scaled, cross, square = (total[:, n : n + 1] for n in range(4))
        scale = lax.rsqrt(plain / D + EPSILON)
        mixed = x_ref[...].astype(F32) + attn_ref[...] * scale * (1.0 + gain_ref[1:2])
        square = jnp.maximum(square + 2.0 * scale * cross + scale * scale * scaled, 0.0)
        mixed_ref[...] = mixed
        scale = lax.rsqrt(square / D + EPSILON)
        ff_input = (mixed * scale * (1.0 + gain_ref[2:3])).astype(BF)
        ff_input = pack_lanes(ff_input)
        for m in range(ny):
            ff_ref[m] = ff_input

    mixed, ff_input = run(
        "mix",
        mix,
        [((rows, width), F32), ((ny, packed, 128), BF)],
        (*sums, attn, x_own, norm_gains),
    )
    ff_input = exchange(ff_input, "gy")

    groups = ny // nx

    cut = (hidden // 128 + 1) // 2 * 128
    column_parts = (0, cut), (cut, hidden)

    def gate_up(start, end):
        def kernel(ff_ref, gate_ref, up_ref, z0_ref, z2_ref, z13_ref):
            me = my("gx")
            flat = [
                unpack_lanes(ff_ref[(me ^ n) * groups + group], rows)
                for n in range(nx)
                for group in range(groups)
            ]
            flat = jnp.concatenate(flat, axis=0)
            for n, w_ref in enumerate((gate_ref, up_ref)):
                sums = jnp.dot(flat, w_ref[:, start:end], preferred_element_type=F32).astype(BF)
                here = pl.ds(n * (end - start), end - start)
                for p, out in enumerate((z0_ref, z13_ref.at[0], z2_ref, z13_ref.at[1])):
                    out[:, here] = sums[p * share_rows : (p + 1) * share_rows]

        shape = (share_rows, 2 * (end - start))
        return run(
            "gate_up",
            kernel,
            [(shape, BF), (shape, BF), ((2,) + shape, BF)],
            (ff_input, w_gate, w_up),
            limit=24,
        )

    def activate(z0_ref, z13_ref, z2_ref, out_ref):
        total = z0_ref[...].astype(F32) + z13_ref[0].astype(F32) + z2_ref[...].astype(F32)
        count = total.shape[1] // 2
        gate, up = total[:, :count], total[:, count:]
        out_ref[...] = (jax.nn.gelu(gate, approximate=True) * up).astype(BF)

    parts = [gate_up(*columns) for columns in column_parts]
    blocks = []
    for z0, z2, z13 in parts:
        shape = z0.shape
        z13 = permute(z13, "gx", 1)
        (z2,) = run("pair_sum_ff", pair_sum, [(shape, BF)], (z2, z13))
        z2 = permute(z2, "gx", 2)
        shape = (share_rows, shape[1] // 2)
        blocks += gather_gx(run("activate", activate, [(shape, BF)], (z0, z13, z2))[0])

    def project_down(*refs):
        w_ref, out_ref = refs[2 * nx :]
        me = my("gx")
        flat = [
            jnp.concatenate([refs[n][...], refs[nx + n][...]], axis=1) for n in range(nx)
        ]
        flat = jnp.concatenate(flat, axis=0)
        sums = lax.dot_general(flat, w_ref[...], NT, preferred_element_type=F32)
        for n in range(nx):
            for group in range(groups):
                at = (n * groups + group) * rows
                block = pack_lanes(sums[at : at + rows].astype(BF))
                out_ref[(me ^ n) * groups + group] = block

    (down,) = run(
        "project_down", project_down, [((ny, packed, 128), BF)], (*blocks, w_down.T)
    )
    down = exchange(down, "gy")

    def down_sum(parts_ref, down_ref, sums_ref):
        down = unpack_lanes(jnp.sum(parts_ref[...].astype(F32), axis=0), rows)
        down_ref[...] = down
        sums_ref[...] = jnp.broadcast_to(row_sum(down * down), (rows, PAGE))

    down, sums = run(
        "down_sum", down_sum, [((rows, width), F32), ((rows, PAGE), F32)], (down,)
    )
    sums = trade([sums] * nx, "gx")

    def finish(*refs):
        down_ref, mixed_ref, gain_ref, out_ref = refs[nx:]
        square = sum(r[...] for r in refs[:nx])[:, 0:1]
        scale = lax.rsqrt(square / D + EPSILON)
        out = mixed_ref[...] + down_ref[...] * scale * (1.0 + gain_ref[3:4])
        out_ref[...] = out.reshape(beams, steps, width).astype(BF)

    (out,) = run("finish", finish, [(inputs.shape, BF)], (*sums, down, mixed, norm_gains))
    return out


def body_general(
    inputs,
    cache_pool,
    lengths,
    block_table,
    parents,
    norm_gains,
    w_query,
    w_key,
    w_value,
    w_out,
    w_gate,
    w_up,
    w_down,
):
    beams, steps, width = inputs.shape
    nx, ny = lax.axis_size("gx"), lax.axis_size("gy")
    rows = beams * steps
    part = rows // nx
    head_part = w_out.shape[0]
    hidden_part = w_gate.shape[1]
    query_part, key_part = w_query.shape[1], w_key.shape[1]
    columns = query_part + 2 * key_part
    share = columns // nx
    x_own = inputs.reshape(rows, width)
    me = lax.axis_index("gx")

    x_all = exchange(jnp.broadcast_to(x_own[None], (ny, rows, width)), "gy")
    flat = (x_all.astype(F32) * (1.0 + norm_gains[0:1])).astype(BF).reshape(ny * rows, width)
    sums = [jnp.dot(flat, w, preferred_element_type=F32) for w in (w_query, w_key, w_value)]
    sums = jnp.concatenate(sums, axis=1).reshape(ny, rows, nx, share)
    received = exchange_all(sums.transpose(2, 0, 1, 3).astype(BF))
    shares = jnp.sum(received.astype(F32), axis=0).astype(BF)
    every = lax.all_gather(shares, "gx", axis=0)
    every = every.transpose(2, 1, 0, 3).reshape(rows, ny, columns)
    q = every[..., :query_part].reshape(rows, HEADS, 2, HALF).transpose(2, 1, 0, 3)
    k, v = (
        every[..., start : start + key_part].reshape(rows, 2 * KV_HEADS, HALF).transpose(1, 0, 2)
        for start in (query_part, query_part + key_part)
    )
    shares = jnp.concatenate([q, k[None], v[None]], axis=0)
    square = lax.psum(row_sum(jnp.square(x_own.astype(F32))), "gx")
    high = lax.reduce_precision(square, 8, 7)
    squares = jnp.where(jnp.arange(HALF) < HALF // 2, high, square - high).astype(BF)[None]
    cos, sin = rope_tables(lengths, rows, steps)

    def attention(*refs):
        g_ref, square_ref, tables, pool_ref = refs[0], refs[1], refs[2:6], refs[6]
        out_ref, keys_ref, sems = refs[7:]

        def store(head, num, den):
            den = high_low(den, PAGE)
            for rep in range(REPS):
                here = slice(rep * rows, (rep + 1) * rows)
                out_ref[REPS * head + rep, :, 0:HEAD_DIM] = num[here].astype(BF)
                out_ref[REPS * head + rep, :, HEAD_DIM:] = den[here].astype(BF)

        attend(
            lambda share, which: g_ref[share, which],
            square_ref[...],
            tables,
            pool_ref,
            (keys_ref, sems),
            store,
        )

    tables = make_tables(block_table, lengths, parents, cache_pool.shape[1], rows, steps)
    (terms,) = run(
        "attention",
        attention,
        [((HEADS, rows, WIDE), BF)],
        (shares, squares, cos, sin, *tables, cache_pool),
        scratch=key_scratch(cache_pool),
        limit=24,
        specs={6: IN_HBM},
    )
    num = terms[..., :HEAD_DIM].transpose(1, 0, 2).reshape(nx, part, ny, head_part)
    den = terms[..., HEAD_DIM :: PAGE // 2].transpose(1, 0, 2)
    den = jnp.repeat(den, ny // HEADS, axis=1).reshape(nx, part, ny, 2)
    terms = exchange_all(jnp.concatenate([num, den], axis=-1).transpose(0, 2, 1, 3))

    w_wide = lax.all_gather(w_out, "gx", axis=1, tiled=True)
    x_wide = lax.all_gather(x_own, "gx", axis=1, tiled=True)
    x_rows = lax.dynamic_slice_in_dim(x_wide, me * part, part, 0).astype(F32)
    gains = 1.0 + lax.all_gather(norm_gains, "gx", axis=1, tiled=True)

    def scaled(v, gain):
        return v * lax.rsqrt(row_sum(v * v) / D + EPSILON) * gain

    terms = jnp.sum(terms.astype(F32), axis=0)
    den = terms[..., head_part : head_part + 1] + terms[..., -1:]
    attended = (terms[..., :head_part] / den).reshape(ny * part, head_part).astype(BF)
    attn = jnp.dot(attended, w_wide, preferred_element_type=F32).astype(BF)
    attn = exchange(attn.reshape(ny, part, D), "gy").astype(F32).sum(axis=0)
    mixed = x_rows + scaled(attn, gains[1])
    ff_input = scaled(mixed, gains[2]).astype(BF)
    ff_input = ff_input.reshape(part, nx, width).transpose(1, 0, 2)[:, None]
    ff_input = exchange_all(jnp.broadcast_to(ff_input, (nx, ny, part, width)))

    flat = ff_input.reshape(-1, width)
    both = [jnp.dot(flat, w, preferred_element_type=F32).astype(BF) for w in (w_gate, w_up)]
    both = jnp.stack(both, axis=1).reshape(nx, ny * part, 2, hidden_part)
    both = jnp.sum(exchange(both, "gx").astype(F32), axis=0)
    hidden = (jax.nn.gelu(both[:, 0], approximate=True) * both[:, 1]).astype(BF)
    hidden = lax.all_gather(hidden, "gx", axis=0, tiled=True)
    down = jnp.dot(hidden, w_down, preferred_element_type=F32).astype(BF)
    down = exchange_all(down.reshape(nx, ny, part, width)).astype(F32).sum(axis=1)
    down = down.transpose(1, 0, 2).reshape(part, D)
    out = (mixed + scaled(down, gains[3])).astype(BF)
    out = exchange(out.reshape(part, nx, width).transpose(1, 0, 2), "gx")
    return out.reshape(beams, steps, width)


def solution(mesh):
    sizes = dict(mesh.shape)
    fits = sizes["gx"] == 4 and sizes["gy"] == HEADS
    return jax.shard_map(
        body_permutes if fits else body_general,
        mesh=mesh,
        in_specs=(
            P("gy", None, "gx"),
            P(None, "gx", "gy", None),
            P("gy"),
            P("gy", None),
            P(None, "gy"),
            P(None, "gx"),
            P("gx", "gy"),
            P("gx", "gy"),
            P("gx", "gy"),
            P("gy", "gx"),
            P("gx", "gy"),
            P("gx", "gy"),
            P("gy", "gx"),
        ),
        out_specs=P("gy", None, "gx"),
        check_vma=False,
    )
```

```python
import jax
import jax.numpy as jnp
from jax import lax
from jax.experimental import pallas as pl
from jax.experimental.pallas import tpu as pltpu
from jax.sharding import PartitionSpec as P

D = 2304
HEADS = 8
KV_HEADS = 4
HEAD_DIM = 256
HALF = HEAD_DIM // 2
WINDOW = 4096
PAGE = 128
BEAM = 8
EPSILON = 1e-06
SOFT_CAP = 50.0
ROPE_BASE = 10000.0
REPS = HEADS // KV_HEADS
WIDE = HEAD_DIM + PAGE
HALF_PAGE = PAGE // 2
BF = jnp.bfloat16
F32 = jnp.float32
MIB = 1024 * 1024
NT = (((1,), (1,)), ((), ()))
IN_HBM = pl.BlockSpec(memory_space=pltpu.HBM)
IN_SMEM = pl.BlockSpec(memory_space=pltpu.SMEM)


def run(name, kernel, outs, args, scratch=(), limit=16, specs=None, micros=0):
    cost = pl.CostEstimate(flops=micros * 10**9, bytes_accessed=0, transcendentals=0)
    specs = specs or {}
    vmem = pl.BlockSpec(memory_space=pltpu.VMEM)
    return pl.pallas_call(
        kernel,
        out_shape=[jax.ShapeDtypeStruct(s, d) for s, d in outs],
        in_specs=[specs.get(n, vmem) for n in range(len(args))],
        scratch_shapes=scratch,
        compiler_params=pltpu.CompilerParams(vmem_limit_bytes=limit * MIB),
        cost_estimate=cost if micros else None,
        name=name,
    )(*args)


def exchange(values, axes):
    return lax.all_to_all(values, axes, split_axis=0, concat_axis=0, tiled=True)


def exchange_all(values):
    nx, ny = values.shape[:2]
    flat = values.reshape((nx * ny,) + values.shape[2:])
    return exchange(flat, ("gx", "gy")).reshape(values.shape)


def permute(values, axis, m):
    count = lax.axis_size(axis)
    return lax.ppermute(values, axis, [(i, i ^ m) for i in range(count)])


def trade(blocks, axis):
    return [blocks[0]] + [permute(blocks[m], axis, m) for m in range(1, len(blocks))]


def gather_gx(values):
    across = permute(values, "gx", 2)
    return [values, permute(values, "gx", 1), across, permute(across, "gx", 1)]


def weight_of(scores):
    return jnp.exp(SOFT_CAP * jnp.tanh(scores * (1.0 / SOFT_CAP)))


def high_low(column, lanes):
    shape = column.shape[:-1] + (lanes,)
    high = column.astype(BF).astype(F32)
    lane = lax.broadcasted_iota(jnp.int32, shape, len(shape) - 1)
    return jnp.where(lane < lanes // 2, high, column - high)


def pack_lanes(v):
    rows, width = v.shape
    whole = width // 128 * 128
    tiles = [v[:, c : c + 128] for c in range(0, whole, 128)]
    last = jnp.concatenate([v[: rows // 2, whole:], v[rows // 2 :, whole:]], axis=1)
    return jnp.concatenate(tiles + [last], axis=0)


def unpack_lanes(v, rows):
    whole = v.shape[0] // rows * rows
    tiles = [v[r : r + rows] for r in range(0, whole, rows)]
    last = jnp.concatenate([v[whole:, :64], v[whole:, 64:]], axis=0)
    return jnp.concatenate(tiles + [last], axis=1)


def row_sum(v):
    return jnp.sum(v, axis=-1, keepdims=True)


def make_tables(table, lengths, parents, slots, rows, steps):
    def tables(table_ref, length_ref, parents_ref, cached_ref, own_ref, page_ref):
        first_owner = lax.axis_index("gx") * slots
        length = length_ref[0]
        first_page = jnp.maximum(length - WINDOW + 1, 0) // PAGE
        for slot in range(slots + 1):
            page_ref[slot] = -1
        for j in range(table_ref.shape[1]):
            slot = table_ref[0, j] - first_owner
            page_ref[jnp.where((slot >= 0) & (slot < slots), slot, slots)] = j
        step = lax.broadcasted_iota(jnp.int32, (8, PAGE), 0) % steps
        lane = lax.broadcasted_iota(jnp.int32, (8, PAGE), 1)
        for slot in range(slots):
            page = page_ref[slot]
            position = lane + jnp.where(page >= 0, (first_page + page) * PAGE, 2**30)
            seen = (position < length) & (position >= length + step - (WINDOW - 1))
            cached_ref[:, slot * PAGE : (slot + 1) * PAGE] = jnp.where(seen, 1.0, 0.0)

        shape = (REPS * rows, rows)
        row = lax.broadcasted_iota(jnp.int32, shape, 0) % rows
        column = lax.broadcasted_iota(jnp.int32, shape, 1)
        row_step, column_step, column_beam = row % steps, column % steps, column // steps
        current = row // steps
        visible = jnp.zeros(shape, jnp.bool_)
        for j in range(steps - 1, -1, -1):
            if j < steps - 1:
                parent = jnp.zeros(shape, jnp.int32)
                for beam in range(BEAM):
                    parent = jnp.where(current == beam, parents_ref[j, beam], parent)
                current = jnp.where(row_step > j, parent, current)
            visible = visible | ((column_step == j) & (row_step >= j) & (column_beam == current))
        visible = visible & (lax.axis_index("gx") == 0)
        own_ref[...] = jnp.where(visible, 1.0, 0.0)

    return run(
        "tables",
        tables,
        [((8, slots * PAGE), F32), ((REPS * rows, rows), F32)],
        (table, lengths, parents),
        scratch=[pltpu.SMEM((slots + 1,), jnp.int32)],
        specs={0: IN_SMEM, 1: IN_SMEM, 2: IN_SMEM},
    )


def attend(shares, squares, tables, pool_ref, kept, store):
    cos_ref, sin_ref, cached_ref, own_ref = tables
    keys_ref, sems = kept
    slots = pool_ref.shape[1]
    rows = cos_ref.shape[0]
    copies = []
    for head in range(KV_HEADS):
        here = pool_ref.at[:, :, :, head * HEAD_DIM : (head + 1) * HEAD_DIM]
        copies.append(pltpu.make_async_copy(here, keys_ref.at[head], sems.at[head]))
        copies[-1].start()
    square = jnp.sum(squares.astype(F32), axis=0)
    square = square[:, 0:1] + square[:, HALF // 2 : HALF // 2 + 1]
    scale = lax.rsqrt(square / D + EPSILON)
    cos, sin = cos_ref[...] * scale, sin_ref[...] * scale
    cached, own = cached_ref[...], own_ref[...]

    def rotated(u, w):
        u, w = u.astype(F32), w.astype(F32)
        return u * cos - w * sin, w * cos + u * sin

    for head in range(KV_HEADS):
        query = []
        for rep in range(REPS):
            u, w = rotated(shares(0, REPS * head + rep), shares(1, REPS * head + rep))
            query.append(jnp.concatenate([u, w], axis=1) * HEAD_DIM ** (-0.5))
        query = jnp.concatenate(query, axis=0).astype(BF)
        first, second = 2 * head, 2 * head + 1
        key_step = rotated(shares(2, first), shares(2, second))
        key_step = jnp.concatenate(key_step, axis=1).astype(BF)
        value_step = [shares(3, n).astype(F32) * scale for n in (first, second)]
        value_step = jnp.concatenate(value_step, axis=1).astype(BF)

        scores = lax.dot_general(query, key_step, NT, preferred_element_type=F32)
        weights = weight_of(scores) * own
        den = row_sum(weights)
        num = jnp.dot(weights.astype(BF), value_step, preferred_element_type=F32)

        copies[head].wait()
        keys = keys_ref[head, 0].reshape(slots * PAGE, HEAD_DIM)
        values = keys_ref[head, 1].reshape(slots * PAGE, HEAD_DIM)
        scores = lax.dot_general(query, keys, NT, preferred_element_type=F32)
        weights = weight_of(scores).reshape(REPS * rows // 8, 8, slots * PAGE) * cached[None]
        weights = weights.reshape(REPS * rows, slots * PAGE)
        den = den + row_sum(weights)
        num = num + jnp.dot(weights.astype(BF), values, preferred_element_type=F32)
        store(head, num, den)


def key_scratch(pool):
    return [
        pltpu.VMEM((KV_HEADS, 2) + pool.shape[1:3] + (HEAD_DIM,), BF),
        pltpu.SemaphoreType.DMA((KV_HEADS,)),
    ]


def rope_tables(lengths, rows, steps):
    positions = lengths[0] + jnp.arange(rows, dtype=jnp.int32) % steps
    inverse_freq = ROPE_BASE ** (-jnp.arange(HALF, dtype=F32) * 2.0 / HEAD_DIM)
    angles = positions[:, None].astype(F32) * inverse_freq
    return jnp.cos(angles), jnp.sin(angles)


def body_permutes(
    inputs,
    cache_pool,
    lengths,
    block_table,
    parents,
    norm_gains,
    w_query,
    w_key,
    w_value,
    w_out,
    w_gate,
    w_up,
    w_down,
):
    beams, steps, width = inputs.shape
    nx, ny = lax.axis_size("gx"), lax.axis_size("gy")
    rows = beams * steps
    half = rows // 2
    all_rows = ny * rows
    share_rows = all_rows // nx
    hidden = w_gate.shape[1]
    packed = rows * width // 128

    def my(axis):
        return lax.axis_index(axis)

    def spread(x_ref, own_ref, out_ref):
        own = x_ref[...].astype(F32).reshape(rows, width).astype(BF)
        own_ref[...] = own
        own = pack_lanes(own)
        for m in range(ny):
            out_ref[m] = own

    x_own, x_all = run(
        "spread", spread, [((rows, width), BF), ((ny, packed, 128), BF)], (inputs,), micros=12
    )
    w_own = w_out.T
    x_all, w_split = lax.optimization_barrier((x_all, w_own))
    x_all = exchange(x_all, "gy")

    w_blocks = {0: w_own, 1: permute(w_own, "gy", 1), 2: permute(w_own, "gy", 2)}
    w_first = permute(w_split[: width // 2], "gy", 4)
    w_late, _ = lax.optimization_barrier(((w_blocks[1], w_split[width // 2 :]), x_all))
    w_blocks[3] = permute(w_late[0], "gy", 2)
    w_second = permute(w_late[1], "gy", 4)

    def project(x_ref, gain_ref, q_ref, k_ref, v_ref, z0_ref, z2_ref, z13_ref, held):
        gain = 1.0 + gain_ref[0:1]
        flat = [
            (unpack_lanes(x_ref[m], rows).astype(F32) * gain).astype(BF) for m in range(ny)
        ]
        flat = jnp.concatenate(flat, axis=0)
        query = jnp.dot(flat, q_ref[...], preferred_element_type=F32).astype(BF)
        held[0], held[1] = query[:, :HALF], query[:, HALF:]
        held[2] = jnp.dot(flat, k_ref[...], preferred_element_type=F32).astype(BF)
        held[3] = jnp.dot(flat, v_ref[...], preferred_element_type=F32).astype(BF)
        me = my("gx")
        z0_ref[...], z2_ref[...] = held[me], held[me ^ 2]
        z13_ref[0], z13_ref[1] = held[me ^ 1], held[me ^ 3]

    shape = (all_rows, HALF)
    z0, z2, z13 = run(
        "project",
        project,
        [(shape, BF), (shape, BF), ((2,) + shape, BF)],
        (x_all, norm_gains, w_query, w_key, w_value),
        scratch=[
            pltpu.VMEM((nx,) + shape, BF),
        ],
    )
    z13 = permute(z13, "gx", 1)

    def pair_sum(z_ref, from_pair_ref, out_ref):
        total = z_ref[...].astype(F32) + from_pair_ref[1].astype(F32)
        out_ref[...] = total.astype(BF)

    (z2,) = run("pair_sum", pair_sum, [(shape, BF)], (z2, z13))
    z2 = permute(z2, "gx", 2)

    def share_sum(z0_ref, z13_ref, z2_ref, out_ref):
        total = z0_ref[...].astype(F32) + z13_ref[0].astype(F32) + z2_ref[...].astype(F32)
        out_ref[...] = total.reshape(ny, rows, HALF).astype(BF)

    (shares,) = run("share_sum", share_sum, [((ny, rows, HALF), BF)], (z0, z13, z2))
    shares, *late = lax.optimization_barrier((shares, block_table, lengths, parents))
    cos, sin = rope_tables(late[1], rows, steps)
    tables = make_tables(*late, cache_pool.shape[1], rows, steps)
    shares = exchange(shares, "gy")
    beside = tables, cos, sin, w_blocks[2], w_blocks[3], w_first, w_second
    shares, (tables, cos, sin, *_) = lax.optimization_barrier((shares, beside))

    def pack_shares(share_ref, x_ref, out_ref):
        x = x_ref[...].astype(F32)
        out_ref[0:ny] = share_ref[...]
        out_ref[ny] = high_low(row_sum(x * x), HALF).astype(BF)

    (shares,) = run(
        "pack_shares", pack_shares, [((ny + 1, rows, HALF), BF)], (shares, x_own), micros=5
    )
    shares = gather_gx(shares)
    w_blocks[4] = jnp.concatenate([w_first, w_second], axis=0)
    w_late, _ = lax.optimization_barrier((w_blocks[4], shares[2]))
    w_blocks[6] = permute(w_late, "gy", 2)
    w_blocks[5] = permute(w_late, "gy", 1)

    def attention(*refs):
        a_refs, tables, pool_ref, outs = refs[:nx], refs[nx : nx + 4], refs[nx + 4], refs[nx + 5 :]
        own_ref, pair_ref, keys_ref, sems, held, num_held, den_held = outs
        me = my("gx")
        core = me & 1
        for n, ref in enumerate(a_refs):
            held[me ^ n] = ref[...]
        den_held[...] = jnp.zeros(den_held.shape, F32)
        lane = lax.broadcasted_iota(jnp.int32, (2, half, PAGE), 2)

        def store(head, num, den):
            num_held[head] = num.reshape(REPS, 2, half, HEAD_DIM)
            den = high_low(den, PAGE).reshape(REPS, 2, half, PAGE)
            for rep in range(REPS):
                at = REPS * head + rep
                den_held[...] = jnp.where(lane % HALF_PAGE == at, den[rep], den_held[...])
                for n, out in enumerate((own_ref, pair_ref)):
                    for tile in range(2):
                        here = num_held[head, rep, core ^ n, :, tile * PAGE : (tile + 1) * PAGE]
                        out[2 * at + tile] = here.astype(BF)

        attend(
            lambda share, which: held[share, which],
            held[:, ny],
            tables,
            pool_ref,
            (keys_ref, sems),
            store,
        )
        for n, out in enumerate((own_ref, pair_ref)):
            out[2 * HEADS] = den_held[core ^ n].astype(BF)

    shape = (2 * HEADS + 1, half, PAGE)
    own, pair = run(
        "attention",
        attention,
        [(shape, BF), (shape, BF)],
        (*shares, cos, sin, *tables, cache_pool),
        scratch=key_scratch(cache_pool)
        + [
            pltpu.VMEM((nx,) + shares[0].shape, BF),
            pltpu.VMEM((KV_HEADS, REPS, 2, half, HEAD_DIM), F32),
            pltpu.VMEM((2, half, PAGE), F32),
        ],
        limit=24,
        specs={nx + 4: IN_HBM},
    )
    w_late, _ = lax.optimization_barrier((w_blocks, own))
    w_blocks[7] = permute(w_late[6], "gy", 1)
    pair = permute(pair, "gx", 1)

    def pair_terms(own_ref, pair_ref, out_ref):
        total = own_ref[...].astype(F32) + pair_ref[...].astype(F32)
        out_ref[0 : 2 * HEADS] = total[0 : 2 * HEADS].astype(BF)
        den = total[2 * HEADS]
        den = den[:, :HALF_PAGE] + den[:, HALF_PAGE:]
        high = den.astype(BF).astype(F32)
        out_ref[2 * HEADS] = jnp.concatenate([high, den - high], axis=1).astype(BF)

    (own,) = run("pair_terms", pair_terms, [(shape, BF)], (own, pair))
    across = permute(own, "gx", 2)

    def divide(own_ref, across_ref, out_ref):
        total = own_ref[...].astype(F32) + across_ref[...].astype(F32)
        den = total[2 * HEADS]
        den = den[:, :HALF_PAGE] + den[:, HALF_PAGE:]
        for head in range(HEADS):
            scale = 1.0 / den[:, head : head + 1]
            for tile in range(2):
                at = 2 * head + tile
                out_ref[at] = (total[at] * scale).astype(BF)

    (attended,) = run("divide", divide, [((2 * HEADS, half, PAGE), BF)], (own, across))
    others = permute(attended, "gx", 1)

    def project_out(own_ref, other_ref, x_ref, gain_ref, *refs):
        w_refs, (attn_ref, sums_ref, held) = refs[:ny], refs[ny:]
        core = my("gx") & 1
        held[core], held[1 - core] = own_ref[...], other_ref[...]
        me = my("gy")
        attn = jnp.zeros((rows, width), F32)
        for m, w_ref in enumerate(w_refs):
            at = 2 * (me ^ m)
            flat = [jnp.concatenate([held[n, at], held[n, at + 1]], axis=1) for n in range(2)]
            flat = jnp.concatenate(flat, axis=0)
            attn = attn + lax.dot_general(flat, w_ref[...], NT, preferred_element_type=F32)
        attn_ref[...] = attn
        x = x_ref[...].astype(F32)
        scaled = attn * (1.0 + gain_ref[1:2])
        lane = lax.broadcasted_iota(jnp.int32, (rows, PAGE), 1)
        sums = jnp.zeros((rows, PAGE), F32)
        for n, terms in enumerate((attn * attn, scaled * scaled, x * scaled, x * x)):
            sums = jnp.where(lane == n, row_sum(terms), sums)
        sums_ref[...] = sums

    attn, sums = run(
        "project_out",
        project_out,
        [((rows, width), F32), ((rows, PAGE), F32)],
        (attended, others, x_own, norm_gains, *[w_blocks[m] for m in range(ny)]),
        scratch=[pltpu.VMEM((2, 2 * HEADS, half, PAGE), BF)],
    )
    sums = trade([sums] * nx, "gx")

    def mix(*refs):
        attn_ref, x_ref, gain_ref, mixed_ref, ff_ref = refs[nx:]
        total = sum(r[...] for r in refs[:nx])
        plain, scaled, cross, square = (total[:, n : n + 1] for n in range(4))
        scale = lax.rsqrt(plain / D + EPSILON)
        mixed = x_ref[...].astype(F32) + attn_ref[...] * scale * (1.0 + gain_ref[1:2])
        square = jnp.maximum(square + 2.0 * scale * cross + scale * scale * scaled, 0.0)
        mixed_ref[...] = mixed
        scale = lax.rsqrt(square / D + EPSILON)
        ff_input = (mixed * scale * (1.0 + gain_ref[2:3])).astype(BF)
        ff_input = pack_lanes(ff_input)
        for m in range(ny):
            ff_ref[m] = ff_input

    mixed, ff_input = run(
        "mix",
        mix,
        [((rows, width), F32), ((ny, packed, 128), BF)],
        (*sums, attn, x_own, norm_gains),
    )
    ff_input = exchange(ff_input, "gy")

    groups = ny // nx

    cut = (hidden // 128 + 1) // 2 * 128
    column_parts = (0, cut), (cut, hidden)

    def gate_up(start, end):
        def kernel(ff_ref, gate_ref, up_ref, z0_ref, z2_ref, z13_ref):
            me = my("gx")
            flat = [
                unpack_lanes(ff_ref[(me ^ n) * groups + group], rows)
                for n in range(nx)
                for group in range(groups)
            ]
            flat = jnp.concatenate(flat, axis=0)
            for n, w_ref in enumerate((gate_ref, up_ref)):
                sums = jnp.dot(flat, w_ref[:, start:end], preferred_element_type=F32).astype(BF)
                here = pl.ds(n * (end - start), end - start)
                for p, out in enumerate((z0_ref, z13_ref.at[0], z2_ref, z13_ref.at[1])):
                    out[:, here] = sums[p * share_rows : (p + 1) * share_rows]

        shape = (share_rows, 2 * (end - start))
        return run(
            "gate_up",
            kernel,
            [(shape, BF), (shape, BF), ((2,) + shape, BF)],
            (ff_input, w_gate, w_up),
            limit=24,
        )

    def activate(z0_ref, z13_ref, z2_ref, out_ref):
        total = z0_ref[...].astype(F32) + z13_ref[0].astype(F32) + z2_ref[...].astype(F32)
        count = total.shape[1] // 2
        gate, up = total[:, :count], total[:, count:]
        out_ref[...] = (jax.nn.gelu(gate, approximate=True) * up).astype(BF)

    parts = [gate_up(*columns) for columns in column_parts]
    blocks = []
    for z0, z2, z13 in parts:
        shape = z0.shape
        z13 = permute(z13, "gx", 1)
        (z2,) = run("pair_sum_ff", pair_sum, [(shape, BF)], (z2, z13))
        z2 = permute(z2, "gx", 2)
        shape = (share_rows, shape[1] // 2)
        blocks += gather_gx(run("activate", activate, [(shape, BF)], (z0, z13, z2))[0])

    def project_down(*refs):
        w_ref, out_ref = refs[2 * nx :]
        me = my("gx")
        flat = [
            jnp.concatenate([refs[n][...], refs[nx + n][...]], axis=1) for n in range(nx)
        ]
        flat = jnp.concatenate(flat, axis=0)
        sums = lax.dot_general(flat, w_ref[...], NT, preferred_element_type=F32)
        for n in range(nx):
            for group in range(groups):
                at = (n * groups + group) * rows
                block = pack_lanes(sums[at : at + rows].astype(BF))
                out_ref[(me ^ n) * groups + group] = block

    (down,) = run(
        "project_down", project_down, [((ny, packed, 128), BF)], (*blocks, w_down.T)
    )
    down = exchange(down, "gy")

    def down_sum(parts_ref, down_ref, sums_ref):
        down = unpack_lanes(jnp.sum(parts_ref[...].astype(F32), axis=0), rows)
        down_ref[...] = down
        sums_ref[...] = jnp.broadcast_to(row_sum(down * down), (rows, PAGE))

    down, sums = run(
        "down_sum", down_sum, [((rows, width), F32), ((rows, PAGE), F32)], (down,)
    )
    sums = trade([sums] * nx, "gx")

    def finish(*refs):
        down_ref, mixed_ref, gain_ref, out_ref = refs[nx:]
        square = sum(r[...] for r in refs[:nx])[:, 0:1]
        scale = lax.rsqrt(square / D + EPSILON)
        out = mixed_ref[...] + down_ref[...] * scale * (1.0 + gain_ref[3:4])
        out_ref[...] = out.reshape(beams, steps, width).astype(BF)

    (out,) = run("finish", finish, [(inputs.shape, BF)], (*sums, down, mixed, norm_gains))
    return out


def body_general(
    inputs,
    cache_pool,
    lengths,
    block_table,
    parents,
    norm_gains,
    w_query,
    w_key,
    w_value,
    w_out,
    w_gate,
    w_up,
    w_down,
):
    beams, steps, width = inputs.shape
    nx, ny = lax.axis_size("gx"), lax.axis_size("gy")
    rows = beams * steps
    part = rows // nx
    head_part = w_out.shape[0]
    hidden_part = w_gate.shape[1]
    query_part, key_part = w_query.shape[1], w_key.shape[1]
    columns = query_part + 2 * key_part
    share = columns // nx
    x_own = inputs.reshape(rows, width)
    me = lax.axis_index("gx")

    x_all = exchange(jnp.broadcast_to(x_own[None], (ny, rows, width)), "gy")
    flat = (x_all.astype(F32) * (1.0 + norm_gains[0:1])).astype(BF).reshape(ny * rows, width)
    sums = [jnp.dot(flat, w, preferred_element_type=F32) for w in (w_query, w_key, w_value)]
    sums = jnp.concatenate(sums, axis=1).reshape(ny, rows, nx, share)
    received = exchange_all(sums.transpose(2, 0, 1, 3).astype(BF))
    shares = jnp.sum(received.astype(F32), axis=0).astype(BF)
    every = lax.all_gather(shares, "gx", axis=0)
    every = every.transpose(2, 1, 0, 3).reshape(rows, ny, columns)
    q = every[..., :query_part].reshape(rows, HEADS, 2, HALF).transpose(2, 1, 0, 3)
    k, v = (
        every[..., start : start + key_part].reshape(rows, 2 * KV_HEADS, HALF).transpose(1, 0, 2)
        for start in (query_part, query_part + key_part)
    )
    shares = jnp.concatenate([q, k[None], v[None]], axis=0)
    square = lax.psum(row_sum(jnp.square(x_own.astype(F32))), "gx")
    high = lax.reduce_precision(square, 8, 7)
    squares = jnp.where(jnp.arange(HALF) < HALF // 2, high, square - high).astype(BF)[None]
    cos, sin = rope_tables(lengths, rows, steps)

    def attention(*refs):
        g_ref, square_ref, tables, pool_ref = refs[0], refs[1], refs[2:6], refs[6]
        out_ref, keys_ref, sems = refs[7:]

        def store(head, num, den):
            den = high_low(den, PAGE)
            for rep in range(REPS):
                here = slice(rep * rows, (rep + 1) * rows)
                out_ref[REPS * head + rep, :, 0:HEAD_DIM] = num[here].astype(BF)
                out_ref[REPS * head + rep, :, HEAD_DIM:] = den[here].astype(BF)

        attend(
            lambda share, which: g_ref[share, which],
            square_ref[...],
            tables,
            pool_ref,
            (keys_ref, sems),
            store,
        )

    tables = make_tables(block_table, lengths, parents, cache_pool.shape[1], rows, steps)
    (terms,) = run(
        "attention",
        attention,
        [((HEADS, rows, WIDE), BF)],
        (shares, squares, cos, sin, *tables, cache_pool),
        scratch=key_scratch(cache_pool),
        limit=24,
        specs={6: IN_HBM},
    )
    num = terms[..., :HEAD_DIM].transpose(1, 0, 2).reshape(nx, part, ny, head_part)
    den = terms[..., HEAD_DIM :: PAGE // 2].transpose(1, 0, 2)
    den = jnp.repeat(den, ny // HEADS, axis=1).reshape(nx, part, ny, 2)
    terms = exchange_all(jnp.concatenate([num, den], axis=-1).transpose(0, 2, 1, 3))

    w_wide = lax.all_gather(w_out, "gx", axis=1, tiled=True)
    x_wide = lax.all_gather(x_own, "gx", axis=1, tiled=True)
    x_rows = lax.dynamic_slice_in_dim(x_wide, me * part, part, 0).astype(F32)
    gains = 1.0 + lax.all_gather(norm_gains, "gx", axis=1, tiled=True)

    def scaled(v, gain):
        return v * lax.rsqrt(row_sum(v * v) / D + EPSILON) * gain

    terms = jnp.sum(terms.astype(F32), axis=0)
    den = terms[..., head_part : head_part + 1] + terms[..., -1:]
    attended = (terms[..., :head_part] / den).reshape(ny * part, head_part).astype(BF)
    attn = jnp.dot(attended, w_wide, preferred_element_type=F32).astype(BF)
    attn = exchange(attn.reshape(ny, part, D), "gy").astype(F32).sum(axis=0)
    mixed = x_rows + scaled(attn, gains[1])
    ff_input = scaled(mixed, gains[2]).astype(BF)
    ff_input = ff_input.reshape(part, nx, width).transpose(1, 0, 2)[:, None]
    ff_input = exchange_all(jnp.broadcast_to(ff_input, (nx, ny, part, width)))

    flat = ff_input.reshape(-1, width)
    both = [jnp.dot(flat, w, preferred_element_type=F32).astype(BF) for w in (w_gate, w_up)]
    both = jnp.stack(both, axis=1).reshape(nx, ny * part, 2, hidden_part)
    both = jnp.sum(exchange(both, "gx").astype(F32), axis=0)
    hidden = (jax.nn.gelu(both[:, 0], approximate=True) * both[:, 1]).astype(BF)
    hidden = lax.all_gather(hidden, "gx", axis=0, tiled=True)
    down = jnp.dot(hidden, w_down, preferred_element_type=F32).astype(BF)
    down = exchange_all(down.reshape(nx, ny, part, width)).astype(F32).sum(axis=1)
    down = down.transpose(1, 0, 2).reshape(part, D)
    out = (mixed + scaled(down, gains[3])).astype(BF)
    out = exchange(out.reshape(part, nx, width).transpose(1, 0, 2), "gx")
    return out.reshape(beams, steps, width)


def solution(mesh):
    sizes = dict(mesh.shape)
    fits = sizes["gx"] == 4 and sizes["gy"] == HEADS
    return jax.shard_map(
        body_permutes if fits else body_general,
        mesh=mesh,
        in_specs=(
            P("gy", None, "gx"),
            P(None, "gx", "gy", None),
            P("gy"),
            P("gy", None),
            P(None, "gy"),
            P(None, "gx"),
            P("gx", "gy"),
            P("gx", "gy"),
            P("gx", "gy"),
            P("gy", "gx"),
            P("gx", "gy"),
            P("gx", "gy"),
            P("gy", "gx"),
        ),
        out_specs=P("gy", None, "gx"),
        check_vma=False,
    )
```

```python
import jax
import jax.numpy as jnp
from jax import lax
from jax.experimental import pallas as pl
from jax.experimental.pallas import tpu as pltpu
from jax.sharding import PartitionSpec as P

D = 2304
HEADS = 8
KV_HEADS = 4
HEAD_DIM = 256
HALF = HEAD_DIM // 2
WINDOW = 4096
PAGE = 128
BEAM = 8
EPSILON = 1e-06
SOFT_CAP = 50.0
ROPE_BASE = 10000.0
REPS = HEADS // KV_HEADS
WIDE = HEAD_DIM + PAGE
HALF_PAGE = PAGE // 2
BF = jnp.bfloat16
F32 = jnp.float32
MIB = 1024 * 1024
NT = (((1,), (1,)), ((), ()))
IN_HBM = pl.BlockSpec(memory_space=pltpu.HBM)
IN_SMEM = pl.BlockSpec(memory_space=pltpu.SMEM)


def run(name, kernel, outs, args, scratch=(), limit=16, specs=None, micros=0):
    cost = pl.CostEstimate(flops=micros * 10**9, bytes_accessed=0, transcendentals=0)
    specs = specs or {}
    vmem = pl.BlockSpec(memory_space=pltpu.VMEM)
    return pl.pallas_call(
        kernel,
        out_shape=[jax.ShapeDtypeStruct(s, d) for s, d in outs],
        in_specs=[specs.get(n, vmem) for n in range(len(args))],
        scratch_shapes=scratch,
        compiler_params=pltpu.CompilerParams(vmem_limit_bytes=limit * MIB),
        cost_estimate=cost if micros else None,
        name=name,
    )(*args)


def exchange(values, axes):
    return lax.all_to_all(values, axes, split_axis=0, concat_axis=0, tiled=True)


def exchange_all(values):
    nx, ny = values.shape[:2]
    flat = values.reshape((nx * ny,) + values.shape[2:])
    return exchange(flat, ("gx", "gy")).reshape(values.shape)


def permute(values, axis, m):
    count = lax.axis_size(axis)
    return lax.ppermute(values, axis, [(i, i ^ m) for i in range(count)])


def trade(blocks, axis):
    return [blocks[0]] + [permute(blocks[m], axis, m) for m in range(1, len(blocks))]


def gather_gx(values):
    across = permute(values, "gx", 2)
    return [values, permute(values, "gx", 1), across, permute(across, "gx", 1)]


def weight_of(scores):
    return jnp.exp(SOFT_CAP * jnp.tanh(scores * (1.0 / SOFT_CAP)))


def high_low(column, lanes):
    shape = column.shape[:-1] + (lanes,)
    high = column.astype(BF).astype(F32)
    lane = lax.broadcasted_iota(jnp.int32, shape, len(shape) - 1)
    return jnp.where(lane < lanes // 2, high, column - high)


def pack_lanes(v):
    rows, width = v.shape
    whole = width // 128 * 128
    tiles = [v[:, c : c + 128] for c in range(0, whole, 128)]
    last = jnp.concatenate([v[: rows // 2, whole:], v[rows // 2 :, whole:]], axis=1)
    return jnp.concatenate(tiles + [last], axis=0)


def unpack_lanes(v, rows):
    whole = v.shape[0] // rows * rows
    tiles = [v[r : r + rows] for r in range(0, whole, rows)]
    last = jnp.concatenate([v[whole:, :64], v[whole:, 64:]], axis=0)
    return jnp.concatenate(tiles + [last], axis=1)


def row_sum(v):
    return jnp.sum(v, axis=-1, keepdims=True)


def make_tables(table, lengths, parents, slots, rows, steps):
    def tables(table_ref, length_ref, parents_ref, cached_ref, own_ref, page_ref):
        first_owner = lax.axis_index("gx") * slots
        length = length_ref[0]
        first_page = jnp.maximum(length - WINDOW + 1, 0) // PAGE
        for slot in range(slots + 1):
            page_ref[slot] = -1
        for j in range(table_ref.shape[1]):
            slot = table_ref[0, j] - first_owner
            page_ref[jnp.where((slot >= 0) & (slot < slots), slot, slots)] = j
        step = lax.broadcasted_iota(jnp.int32, (8, PAGE), 0) % steps
        lane = lax.broadcasted_iota(jnp.int32, (8, PAGE), 1)
        for slot in range(slots):
            page = page_ref[slot]
            position = lane + jnp.where(page >= 0, (first_page + page) * PAGE, 2**30)
            seen = (position < length) & (position >= length + step - (WINDOW - 1))
            cached_ref[:, slot * PAGE : (slot + 1) * PAGE] = jnp.where(seen, 1.0, 0.0)

        shape = (REPS * rows, rows)
        row = lax.broadcasted_iota(jnp.int32, shape, 0) % rows
        column = lax.broadcasted_iota(jnp.int32, shape, 1)
        row_step, column_step, column_beam = row % steps, column % steps, column // steps
        current = row // steps
        visible = jnp.zeros(shape, jnp.bool_)
        for j in range(steps - 1, -1, -1):
            if j < steps - 1:
                parent = jnp.zeros(shape, jnp.int32)
                for beam in range(BEAM):
                    parent = jnp.where(current == beam, parents_ref[j, beam], parent)
                current = jnp.where(row_step > j, parent, current)
            visible = visible | ((column_step == j) & (row_step >= j) & (column_beam == current))
        visible = visible & (lax.axis_index("gx") == 0)
        own_ref[...] = jnp.where(visible, 1.0, 0.0)

    return run(
        "tables",
        tables,
        [((8, slots * PAGE), F32), ((REPS * rows, rows), F32)],
        (table, lengths, parents),
        scratch=[pltpu.SMEM((slots + 1,), jnp.int32)],
        specs={0: IN_SMEM, 1: IN_SMEM, 2: IN_SMEM},
        micros=5,
    )


def attend(shares, squares, tables, pool_ref, kept, store):
    cos_ref, sin_ref, cached_ref, own_ref = tables
    keys_ref, sems = kept
    slots = pool_ref.shape[1]
    rows = cos_ref.shape[0]
    copies = []
    for head in range(KV_HEADS):
        here = pool_ref.at[:, :, :, head * HEAD_DIM : (head + 1) * HEAD_DIM]
        copies.append(pltpu.make_async_copy(here, keys_ref.at[head], sems.at[head]))
        copies[-1].start()
    square = jnp.sum(squares.astype(F32), axis=0)
    square = square[:, 0:1] + square[:, HALF // 2 : HALF // 2 + 1]
    scale = lax.rsqrt(square / D + EPSILON)
    cos, sin = cos_ref[...] * scale, sin_ref[...] * scale
    cached, own = cached_ref[...], own_ref[...]

    def rotated(u, w):
        u, w = u.astype(F32), w.astype(F32)
        return u * cos - w * sin, w * cos + u * sin

    for head in range(KV_HEADS):
        query = []
        for rep in range(REPS):
            u, w = rotated(shares(0, REPS * head + rep), shares(1, REPS * head + rep))
            query.append(jnp.concatenate([u, w], axis=1) * HEAD_DIM ** (-0.5))
        query = jnp.concatenate(query, axis=0).astype(BF)
        first, second = 2 * head, 2 * head + 1
        key_step = rotated(shares(2, first), shares(2, second))
        key_step = jnp.concatenate(key_step, axis=1).astype(BF)
        value_step = [shares(3, n).astype(F32) * scale for n in (first, second)]
        value_step = jnp.concatenate(value_step, axis=1).astype(BF)

        scores = lax.dot_general(query, key_step, NT, preferred_element_type=F32)
        weights = weight_of(scores) * own
        den = row_sum(weights)
        num = jnp.dot(weights.astype(BF), value_step, preferred_element_type=F32)

        copies[head].wait()
        keys = keys_ref[head, 0].reshape(slots * PAGE, HEAD_DIM)
        values = keys_ref[head, 1].reshape(slots * PAGE, HEAD_DIM)
        scores = lax.dot_general(query, keys, NT, preferred_element_type=F32)
        weights = weight_of(scores).reshape(REPS * rows // 8, 8, slots * PAGE) * cached[None]
        weights = weights.reshape(REPS * rows, slots * PAGE)
        den = den + row_sum(weights)
        num = num + jnp.dot(weights.astype(BF), values, preferred_element_type=F32)
        store(head, num, den)


def key_scratch(pool):
    return [
        pltpu.VMEM((KV_HEADS, 2) + pool.shape[1:3] + (HEAD_DIM,), BF),
        pltpu.SemaphoreType.DMA((KV_HEADS,)),
    ]


def rope_tables(lengths, rows, steps):
    positions = lengths[0] + jnp.arange(rows, dtype=jnp.int32) % steps
    inverse_freq = ROPE_BASE ** (-jnp.arange(HALF, dtype=F32) * 2.0 / HEAD_DIM)
    angles = positions[:, None].astype(F32) * inverse_freq
    return jnp.cos(angles), jnp.sin(angles)


def body_permutes(
    inputs,
    cache_pool,
    lengths,
    block_table,
    parents,
    norm_gains,
    w_query,
    w_key,
    w_value,
    w_out,
    w_gate,
    w_up,
    w_down,
):
    beams, steps, width = inputs.shape
    nx, ny = lax.axis_size("gx"), lax.axis_size("gy")
    rows = beams * steps
    half = rows // 2
    all_rows = ny * rows
    share_rows = all_rows // nx
    hidden = w_gate.shape[1]
    packed = rows * width // 128

    def my(axis):
        return lax.axis_index(axis)

    def spread(x_ref, own_ref, out_ref):
        own = x_ref[...].astype(F32).reshape(rows, width).astype(BF)
        own_ref[...] = own
        own = pack_lanes(own)
        for m in range(ny):
            out_ref[m] = own

    x_own, x_all = run(
        "spread", spread, [((rows, width), BF), ((ny, packed, 128), BF)], (inputs,), micros=12
    )
    w_own = w_out.T
    x_all, w_split = lax.optimization_barrier((x_all, w_own))
    x_all = exchange(x_all, "gy")

    w_blocks = {0: w_own, 1: permute(w_own, "gy", 1), 2: permute(w_own, "gy", 2)}
    w_first = permute(w_split[: width // 2], "gy", 4)
    w_late, _ = lax.optimization_barrier(((w_blocks[1], w_split[width // 2 :]), x_all))
    w_blocks[3] = permute(w_late[0], "gy", 2)
    w_second = permute(w_late[1], "gy", 4)

    def project(x_ref, gain_ref, q_ref, k_ref, v_ref, z0_ref, z2_ref, z13_ref, held):
        gain = 1.0 + gain_ref[0:1]
        flat = [
            (unpack_lanes(x_ref[m], rows).astype(F32) * gain).astype(BF) for m in range(ny)
        ]
        flat = jnp.concatenate(flat, axis=0)
        query = jnp.dot(flat, q_ref[...], preferred_element_type=F32).astype(BF)
        held[0], held[1] = query[:, :HALF], query[:, HALF:]
        held[2] = jnp.dot(flat, k_ref[...], preferred_element_type=F32).astype(BF)
        held[3] = jnp.dot(flat, v_ref[...], preferred_element_type=F32).astype(BF)
        me = my("gx")
        z0_ref[...], z2_ref[...] = held[me], held[me ^ 2]
        z13_ref[0], z13_ref[1] = held[me ^ 1], held[me ^ 3]

    shape = (all_rows, HALF)
    z0, z2, z13 = run(
        "project",
        project,
        [(shape, BF), (shape, BF), ((2,) + shape, BF)],
        (x_all, norm_gains, w_query, w_key, w_value),
        scratch=[
            pltpu.VMEM((nx,) + shape, BF),
        ],
    )
    z13 = permute(z13, "gx", 1)

    def pair_sum(z_ref, from_pair_ref, out_ref):
        total = z_ref[...].astype(F32) + from_pair_ref[1].astype(F32)
        out_ref[...] = total.astype(BF)

    (z2,) = run("pair_sum", pair_sum, [(shape, BF)], (z2, z13))
    z2 = permute(z2, "gx", 2)

    def share_sum(z0_ref, z13_ref, z2_ref, out_ref):
        total = z0_ref[...].astype(F32) + z13_ref[0].astype(F32) + z2_ref[...].astype(F32)
        out_ref[...] = total.reshape(ny, rows, HALF).astype(BF)

    (shares,) = run("share_sum", share_sum, [((ny, rows, HALF), BF)], (z0, z13, z2))
    late = block_table, lengths, parents
    late, _ = lax.optimization_barrier((late, (shares, w_blocks[2], w_blocks[3])))
    cos, sin = rope_tables(late[1], rows, steps)
    tables = make_tables(*late, cache_pool.shape[1], rows, steps)
    w_blocks[4] = jnp.concatenate([w_first, w_second], axis=0)
    late, _ = lax.optimization_barrier((w_blocks[4], tables))
    w_blocks[6] = permute(late, "gy", 2)
    w_blocks[5] = permute(late, "gy", 1)
    shares = exchange(shares, "gy")
    shares, tables, cos, sin = lax.optimization_barrier((shares, tables, cos, sin))

    def pack_shares(share_ref, x_ref, out_ref):
        x = x_ref[...].astype(F32)
        out_ref[0:ny] = share_ref[...]
        out_ref[ny] = high_low(row_sum(x * x), HALF).astype(BF)

    (shares,) = run("pack_shares", pack_shares, [((ny + 1, rows, HALF), BF)], (shares, x_own))
    near, across = permute(shares, "gx", 1), permute(shares, "gx", 2)
    across, _ = lax.optimization_barrier((across, (w_blocks[6], w_blocks[5])))
    shares = [shares, near, across, permute(across, "gx", 1)]
    late, _ = lax.optimization_barrier((w_blocks[6], near))
    w_blocks[7] = permute(late, "gy", 1)

    def attention(*refs):
        a_refs, tables, pool_ref, outs = refs[:nx], refs[nx : nx + 4], refs[nx + 4], refs[nx + 5 :]
        own_ref, pair_ref, keys_ref, sems, held, num_held, den_held = outs
        me = my("gx")
        core = me & 1
        for n, ref in enumerate(a_refs):
            held[me ^ n] = ref[...]
        den_held[...] = jnp.zeros(den_held.shape, F32)
        lane = lax.broadcasted_iota(jnp.int32, (2, half, PAGE), 2)

        def store(head, num, den):
            num_held[head] = num.reshape(REPS, 2, half, HEAD_DIM)
            den = high_low(den, PAGE).reshape(REPS, 2, half, PAGE)
            for rep in range(REPS):
                at = REPS * head + rep
                den_held[...] = jnp.where(lane % HALF_PAGE == at, den[rep], den_held[...])
                for n, out in enumerate((own_ref, pair_ref)):
                    for tile in range(2):
                        here = num_held[head, rep, core ^ n, :, tile * PAGE : (tile + 1) * PAGE]
                        out[2 * at + tile] = here.astype(BF)

        attend(
            lambda share, which: held[share, which],
            held[:, ny],
            tables,
            pool_ref,
            (keys_ref, sems),
            store,
        )
        for n, out in enumerate((own_ref, pair_ref)):
            out[2 * HEADS] = den_held[core ^ n].astype(BF)

    shape = (2 * HEADS + 1, half, PAGE)
    own, pair = run(
        "attention",
        attention,
        [(shape, BF), (shape, BF)],
        (*shares, cos, sin, *tables, cache_pool),
        scratch=key_scratch(cache_pool)
        + [
            pltpu.VMEM((nx,) + shares[0].shape, BF),
            pltpu.VMEM((KV_HEADS, REPS, 2, half, HEAD_DIM), F32),
            pltpu.VMEM((2, half, PAGE), F32),
        ],
        limit=24,
        specs={nx + 4: IN_HBM},
    )
    pair = permute(pair, "gx", 1)

    def pair_terms(own_ref, pair_ref, out_ref):
        total = own_ref[...].astype(F32) + pair_ref[...].astype(F32)
        out_ref[0 : 2 * HEADS] = total[0 : 2 * HEADS].astype(BF)
        den = total[2 * HEADS]
        den = den[:, :HALF_PAGE] + den[:, HALF_PAGE:]
        high = den.astype(BF).astype(F32)
        out_ref[2 * HEADS] = jnp.concatenate([high, den - high], axis=1).astype(BF)

    (own,) = run("pair_terms", pair_terms, [(shape, BF)], (own, pair))
    across = permute(own, "gx", 2)
    across, _ = lax.optimization_barrier((across, w_blocks[7]))

    def divide(own_ref, across_ref, out_ref):
        total = own_ref[...].astype(F32) + across_ref[...].astype(F32)
        den = total[2 * HEADS]
        den = den[:, :HALF_PAGE] + den[:, HALF_PAGE:]
        for head in range(HEADS):
            scale = 1.0 / den[:, head : head + 1]
            for tile in range(2):
                at = 2 * head + tile
                out_ref[at] = (total[at] * scale).astype(BF)

    (attended,) = run("divide", divide, [((2 * HEADS, half, PAGE), BF)], (own, across))
    others = permute(attended, "gx", 1)

    def project_out(own_ref, other_ref, x_ref, gain_ref, *refs):
        w_refs, (attn_ref, sums_ref, held) = refs[:ny], refs[ny:]
        core = my("gx") & 1
        held[core], held[1 - core] = own_ref[...], other_ref[...]
        me = my("gy")
        attn = jnp.zeros((rows, width), F32)
        for m, w_ref in enumerate(w_refs):
            at = 2 * (me ^ m)
            flat = [jnp.concatenate([held[n, at], held[n, at + 1]], axis=1) for n in range(2)]
            flat = jnp.concatenate(flat, axis=0)
            attn = attn + lax.dot_general(flat, w_ref[...], NT, preferred_element_type=F32)
        attn_ref[...] = attn
        x = x_ref[...].astype(F32)
        scaled = attn * (1.0 + gain_ref[1:2])
        lane = lax.broadcasted_iota(jnp.int32, (rows, PAGE), 1)
        sums = jnp.zeros((rows, PAGE), F32)
        for n, terms in enumerate((attn * attn, scaled * scaled, x * scaled, x * x)):
            sums = jnp.where(lane == n, row_sum(terms), sums)
        sums_ref[...] = sums

    attn, sums = run(
        "project_out",
        project_out,
        [((rows, width), F32), ((rows, PAGE), F32)],
        (attended, others, x_own, norm_gains, *[w_blocks[m] for m in range(ny)]),
        scratch=[pltpu.VMEM((2, 2 * HEADS, half, PAGE), BF)],
    )
    sums = trade([sums] * nx, "gx")

    def mix(*refs):
        attn_ref, x_ref, gain_ref, mixed_ref, ff_ref = refs[nx:]
        total = sum(r[...] for r in refs[:nx])
        plain, scaled, cross, square = (total[:, n : n + 1] for n in range(4))
        scale = lax.rsqrt(plain / D + EPSILON)
        mixed = x_ref[...].astype(F32) + attn_ref[...] * scale * (1.0 + gain_ref[1:2])
        square = jnp.maximum(square + 2.0 * scale * cross + scale * scale * scaled, 0.0)
        mixed_ref[...] = mixed
        scale = lax.rsqrt(square / D + EPSILON)
        ff_input = (mixed * scale * (1.0 + gain_ref[2:3])).astype(BF)
        ff_input = pack_lanes(ff_input)
        for m in range(ny):
            ff_ref[m] = ff_input

    mixed, ff_input = run(
        "mix",
        mix,
        [((rows, width), F32), ((ny, packed, 128), BF)],
        (*sums, attn, x_own, norm_gains),
    )
    ff_input = exchange(ff_input, "gy")

    groups = ny // nx

    cut = (hidden // 128 + 1) // 2 * 128
    column_parts = (0, cut), (cut, hidden)

    def gate_up(start, end):
        def kernel(ff_ref, gate_ref, up_ref, z0_ref, z2_ref, z13_ref):
            me = my("gx")
            flat = [
                unpack_lanes(ff_ref[(me ^ n) * groups + group], rows)
                for n in range(nx)
                for group in range(groups)
            ]
            flat = jnp.concatenate(flat, axis=0)
            for n, w_ref in enumerate((gate_ref, up_ref)):
                sums = jnp.dot(flat, w_ref[:, start:end], preferred_element_type=F32).astype(BF)
                here = pl.ds(n * (end - start), end - start)
                for p, out in enumerate((z0_ref, z13_ref.at[0], z2_ref, z13_ref.at[1])):
                    out[:, here] = sums[p * share_rows : (p + 1) * share_rows]

        shape = (share_rows, 2 * (end - start))
        return run(
            "gate_up",
            kernel,
            [(shape, BF), (shape, BF), ((2,) + shape, BF)],
            (ff_input, w_gate, w_up),
            limit=24,
        )

    def activate(z0_ref, z13_ref, z2_ref, out_ref):
        total = z0_ref[...].astype(F32) + z13_ref[0].astype(F32) + z2_ref[...].astype(F32)
        count = total.shape[1] // 2
        gate, up = total[:, :count], total[:, count:]
        out_ref[...] = (jax.nn.gelu(gate, approximate=True) * up).astype(BF)

    parts = [gate_up(*columns) for columns in column_parts]
    blocks = []
    for z0, z2, z13 in parts:
        shape = z0.shape
        z13 = permute(z13, "gx", 1)
        (z2,) = run("pair_sum_ff", pair_sum, [(shape, BF)], (z2, z13))
        z2 = permute(z2, "gx", 2)
        shape = (share_rows, shape[1] // 2)
        blocks += gather_gx(run("activate", activate, [(shape, BF)], (z0, z13, z2))[0])

    def project_down(*refs):
        w_ref, out_ref = refs[2 * nx :]
        me = my("gx")
        flat = [
            jnp.concatenate([refs[n][...], refs[nx + n][...]], axis=1) for n in range(nx)
        ]
        flat = jnp.concatenate(flat, axis=0)
        sums = lax.dot_general(flat, w_ref[...], NT, preferred_element_type=F32)
        for n in range(nx):
            for group in range(groups):
                at = (n * groups + group) * rows
                block = pack_lanes(sums[at : at + rows].astype(BF))
                out_ref[(me ^ n) * groups + group] = block

    (down,) = run(
        "project_down", project_down, [((ny, packed, 128), BF)], (*blocks, w_down.T)
    )
    down = exchange(down, "gy")

    def down_sum(parts_ref, down_ref, sums_ref):
        down = unpack_lanes(jnp.sum(parts_ref[...].astype(F32), axis=0), rows)
        down_ref[...] = down
        sums_ref[...] = jnp.broadcast_to(row_sum(down * down), (rows, PAGE))

    down, sums = run(
        "down_sum", down_sum, [((rows, width), F32), ((rows, PAGE), F32)], (down,)
    )
    sums = trade([sums] * nx, "gx")

    def finish(*refs):
        down_ref, mixed_ref, gain_ref, out_ref = refs[nx:]
        square = sum(r[...] for r in refs[:nx])[:, 0:1]
        scale = lax.rsqrt(square / D + EPSILON)
        out = mixed_ref[...] + down_ref[...] * scale * (1.0 + gain_ref[3:4])
        out_ref[...] = out.reshape(beams, steps, width).astype(BF)

    (out,) = run("finish", finish, [(inputs.shape, BF)], (*sums, down, mixed, norm_gains))
    return out


def body_general(
    inputs,
    cache_pool,
    lengths,
    block_table,
    parents,
    norm_gains,
    w_query,
    w_key,
    w_value,
    w_out,
    w_gate,
    w_up,
    w_down,
):
    beams, steps, width = inputs.shape
    nx, ny = lax.axis_size("gx"), lax.axis_size("gy")
    rows = beams * steps
    part = rows // nx
    head_part = w_out.shape[0]
    hidden_part = w_gate.shape[1]
    query_part, key_part = w_query.shape[1], w_key.shape[1]
    columns = query_part + 2 * key_part
    share = columns // nx
    x_own = inputs.reshape(rows, width)
    me = lax.axis_index("gx")

    x_all = exchange(jnp.broadcast_to(x_own[None], (ny, rows, width)), "gy")
    flat = (x_all.astype(F32) * (1.0 + norm_gains[0:1])).astype(BF).reshape(ny * rows, width)
    sums = [jnp.dot(flat, w, preferred_element_type=F32) for w in (w_query, w_key, w_value)]
    sums = jnp.concatenate(sums, axis=1).reshape(ny, rows, nx, share)
    received = exchange_all(sums.transpose(2, 0, 1, 3).astype(BF))
    shares = jnp.sum(received.astype(F32), axis=0).astype(BF)
    every = lax.all_gather(shares, "gx", axis=0)
    every = every.transpose(2, 1, 0, 3).reshape(rows, ny, columns)
    q = every[..., :query_part].reshape(rows, HEADS, 2, HALF).transpose(2, 1, 0, 3)
    k, v = (
        every[..., start : start + key_part].reshape(rows, 2 * KV_HEADS, HALF).transpose(1, 0, 2)
        for start in (query_part, query_part + key_part)
    )
    shares = jnp.concatenate([q, k[None], v[None]], axis=0)
    square = lax.psum(row_sum(jnp.square(x_own.astype(F32))), "gx")
    high = lax.reduce_precision(square, 8, 7)
    squares = jnp.where(jnp.arange(HALF) < HALF // 2, high, square - high).astype(BF)[None]
    cos, sin = rope_tables(lengths, rows, steps)

    def attention(*refs):
        g_ref, square_ref, tables, pool_ref = refs[0], refs[1], refs[2:6], refs[6]
        out_ref, keys_ref, sems = refs[7:]

        def store(head, num, den):
            den = high_low(den, PAGE)
            for rep in range(REPS):
                here = slice(rep * rows, (rep + 1) * rows)
                out_ref[REPS * head + rep, :, 0:HEAD_DIM] = num[here].astype(BF)
                out_ref[REPS * head + rep, :, HEAD_DIM:] = den[here].astype(BF)

        attend(
            lambda share, which: g_ref[share, which],
            square_ref[...],
            tables,
            pool_ref,
            (keys_ref, sems),
            store,
        )

    tables = make_tables(block_table, lengths, parents, cache_pool.shape[1], rows, steps)
    (terms,) = run(
        "attention",
        attention,
        [((HEADS, rows, WIDE), BF)],
        (shares, squares, cos, sin, *tables, cache_pool),
        scratch=key_scratch(cache_pool),
        limit=24,
        specs={6: IN_HBM},
    )
    num = terms[..., :HEAD_DIM].transpose(1, 0, 2).reshape(nx, part, ny, head_part)
    den = terms[..., HEAD_DIM :: PAGE // 2].transpose(1, 0, 2)
    den = jnp.repeat(den, ny // HEADS, axis=1).reshape(nx, part, ny, 2)
    terms = exchange_all(jnp.concatenate([num, den], axis=-1).transpose(0, 2, 1, 3))

    w_wide = lax.all_gather(w_out, "gx", axis=1, tiled=True)
    x_wide = lax.all_gather(x_own, "gx", axis=1, tiled=True)
    x_rows = lax.dynamic_slice_in_dim(x_wide, me * part, part, 0).astype(F32)
    gains = 1.0 + lax.all_gather(norm_gains, "gx", axis=1, tiled=True)

    def scaled(v, gain):
        return v * lax.rsqrt(row_sum(v * v) / D + EPSILON) * gain

    terms = jnp.sum(terms.astype(F32), axis=0)
    den = terms[..., head_part : head_part + 1] + terms[..., -1:]
    attended = (terms[..., :head_part] / den).reshape(ny * part, head_part).astype(BF)
    attn = jnp.dot(attended, w_wide, preferred_element_type=F32).astype(BF)
    attn = exchange(attn.reshape(ny, part, D), "gy").astype(F32).sum(axis=0)
    mixed = x_rows + scaled(attn, gains[1])
    ff_input = scaled(mixed, gains[2]).astype(BF)
    ff_input = ff_input.reshape(part, nx, width).transpose(1, 0, 2)[:, None]
    ff_input = exchange_all(jnp.broadcast_to(ff_input, (nx, ny, part, width)))

    flat = ff_input.reshape(-1, width)
    both = [jnp.dot(flat, w, preferred_element_type=F32).astype(BF) for w in (w_gate, w_up)]
    both = jnp.stack(both, axis=1).reshape(nx, ny * part, 2, hidden_part)
    both = jnp.sum(exchange(both, "gx").astype(F32), axis=0)
    hidden = (jax.nn.gelu(both[:, 0], approximate=True) * both[:, 1]).astype(BF)
    hidden = lax.all_gather(hidden, "gx", axis=0, tiled=True)
    down = jnp.dot(hidden, w_down, preferred_element_type=F32).astype(BF)
    down = exchange_all(down.reshape(nx, ny, part, width)).astype(F32).sum(axis=1)
    down = down.transpose(1, 0, 2).reshape(part, D)
    out = (mixed + scaled(down, gains[3])).astype(BF)
    out = exchange(out.reshape(part, nx, width).transpose(1, 0, 2), "gx")
    return out.reshape(beams, steps, width)


def solution(mesh):
    sizes = dict(mesh.shape)
    fits = sizes["gx"] == 4 and sizes["gy"] == HEADS
    return jax.shard_map(
        body_permutes if fits else body_general,
        mesh=mesh,
        in_specs=(
            P("gy", None, "gx"),
            P(None, "gx", "gy", None),
            P("gy"),
            P("gy", None),
            P(None, "gy"),
            P(None, "gx"),
            P("gx", "gy"),
            P("gx", "gy"),
            P("gx", "gy"),
            P("gy", "gx"),
            P("gx", "gy"),
            P("gx", "gy"),
            P("gy", "gx"),
        ),
        out_specs=P("gy", None, "gx"),
        check_vma=False,
    )
```

```python
import jax
import jax.numpy as jnp
from jax import lax
from jax.experimental import pallas as pl
from jax.experimental.pallas import tpu as pltpu
from jax.sharding import PartitionSpec as P

D = 2304
HEADS = 8
KV_HEADS = 4
HEAD_DIM = 256
HALF = HEAD_DIM // 2
WINDOW = 4096
PAGE = 128
BEAM = 8
EPSILON = 1e-06
SOFT_CAP = 50.0
ROPE_BASE = 10000.0
REPS = HEADS // KV_HEADS
WIDE = HEAD_DIM + PAGE
HALF_PAGE = PAGE // 2
BF = jnp.bfloat16
F32 = jnp.float32
MIB = 1024 * 1024
NT = (((1,), (1,)), ((), ()))
IN_HBM = pl.BlockSpec(memory_space=pltpu.HBM)
IN_SMEM = pl.BlockSpec(memory_space=pltpu.SMEM)


def run(name, kernel, outs, args, scratch=(), limit=16, specs=None, micros=0):
    cost = pl.CostEstimate(flops=micros * 10**9, bytes_accessed=0, transcendentals=0)
    specs = specs or {}
    vmem = pl.BlockSpec(memory_space=pltpu.VMEM)
    return pl.pallas_call(
        kernel,
        out_shape=[jax.ShapeDtypeStruct(s, d) for s, d in outs],
        in_specs=[specs.get(n, vmem) for n in range(len(args))],
        scratch_shapes=scratch,
        compiler_params=pltpu.CompilerParams(vmem_limit_bytes=limit * MIB),
        cost_estimate=cost if micros else None,
        name=name,
    )(*args)


def exchange(values, axes):
    return lax.all_to_all(values, axes, split_axis=0, concat_axis=0, tiled=True)


def exchange_all(values):
    nx, ny = values.shape[:2]
    flat = values.reshape((nx * ny,) + values.shape[2:])
    return exchange(flat, ("gx", "gy")).reshape(values.shape)


def permute(values, axis, m):
    count = lax.axis_size(axis)
    return lax.ppermute(values, axis, [(i, i ^ m) for i in range(count)])


def trade(blocks, axis):
    return [blocks[0]] + [permute(blocks[m], axis, m) for m in range(1, len(blocks))]


def gather_gx(values):
    across = permute(values, "gx", 2)
    return [values, permute(values, "gx", 1), across, permute(across, "gx", 1)]


def weight_of(scores):
    return jnp.exp(SOFT_CAP * jnp.tanh(scores * (1.0 / SOFT_CAP)))


def high_low(column, lanes):
    shape = column.shape[:-1] + (lanes,)
    high = column.astype(BF).astype(F32)
    lane = lax.broadcasted_iota(jnp.int32, shape, len(shape) - 1)
    return jnp.where(lane < lanes // 2, high, column - high)


def pack_lanes(v):
    rows, width = v.shape
    whole = width // 128 * 128
    tiles = [v[:, c : c + 128] for c in range(0, whole, 128)]
    last = jnp.concatenate([v[: rows // 2, whole:], v[rows // 2 :, whole:]], axis=1)
    return jnp.concatenate(tiles + [last], axis=0)


def unpack_lanes(v, rows):
    whole = v.shape[0] // rows * rows
    tiles = [v[r : r + rows] for r in range(0, whole, rows)]
    last = jnp.concatenate([v[whole:, :64], v[whole:, 64:]], axis=0)
    return jnp.concatenate(tiles + [last], axis=1)


def row_sum(v):
    return jnp.sum(v, axis=-1, keepdims=True)


def make_tables(table, lengths, parents, slots, rows, steps):
    def tables(table_ref, length_ref, parents_ref, cached_ref, own_ref, page_ref):
        first_owner = lax.axis_index("gx") * slots
        length = length_ref[0]
        first_page = jnp.maximum(length - WINDOW + 1, 0) // PAGE
        for slot in range(slots + 1):
            page_ref[slot] = -1
        for j in range(table_ref.shape[1]):
            slot = table_ref[0, j] - first_owner
            page_ref[jnp.where((slot >= 0) & (slot < slots), slot, slots)] = j
        step = lax.broadcasted_iota(jnp.int32, (8, PAGE), 0) % steps
        lane = lax.broadcasted_iota(jnp.int32, (8, PAGE), 1)
        for slot in range(slots):
            page = page_ref[slot]
            position = lane + jnp.where(page >= 0, (first_page + page) * PAGE, 2**30)
            seen = (position < length) & (position >= length + step - (WINDOW - 1))
            cached_ref[:, slot * PAGE : (slot + 1) * PAGE] = jnp.where(seen, 1.0, 0.0)

        shape = (REPS * rows, rows)
        row = lax.broadcasted_iota(jnp.int32, shape, 0) % rows
        column = lax.broadcasted_iota(jnp.int32, shape, 1)
        row_step, column_step, column_beam = row % steps, column % steps, column // steps
        current = row // steps
        visible = jnp.zeros(shape, jnp.bool_)
        for j in range(steps - 1, -1, -1):
            if j < steps - 1:
                parent = jnp.zeros(shape, jnp.int32)
                for beam in range(BEAM):
                    parent = jnp.where(current == beam, parents_ref[j, beam], parent)
                current = jnp.where(row_step > j, parent, current)
            visible = visible | ((column_step == j) & (row_step >= j) & (column_beam == current))
        visible = visible & (lax.axis_index("gx") == 0)
        own_ref[...] = jnp.where(visible, 1.0, 0.0)

    return run(
        "tables",
        tables,
        [((8, slots * PAGE), F32), ((REPS * rows, rows), F32)],
        (table, lengths, parents),
        scratch=[pltpu.SMEM((slots + 1,), jnp.int32)],
        specs={0: IN_SMEM, 1: IN_SMEM, 2: IN_SMEM},
    )


def by_head(pool):
    def kernel(pool_ref, out_ref, sems):
        copies = []
        for head in range(KV_HEADS):
            here = pool_ref.at[:, :, :, head * HEAD_DIM : (head + 1) * HEAD_DIM]
            copies.append(pltpu.make_async_copy(here, out_ref.at[head], sems.at[head]))
            copies[-1].start()
        for copy in copies:
            copy.wait()

    shape = (KV_HEADS,) + pool.shape[:3] + (HEAD_DIM,)
    return run(
        "by_head",
        kernel,
        [(shape, BF)],
        (pool,),
        scratch=[pltpu.SemaphoreType.DMA((KV_HEADS,))],
        specs={0: IN_HBM},
        micros=3,
    )[0]


def attend(shares, squares, tables, keys_ref, store):
    cos_ref, sin_ref, cached_ref, own_ref = tables
    slots = keys_ref.shape[2]
    rows = cos_ref.shape[0]
    square = jnp.sum(squares.astype(F32), axis=0)
    square = square[:, 0:1] + square[:, HALF // 2 : HALF // 2 + 1]
    scale = lax.rsqrt(square / D + EPSILON)
    cos, sin = cos_ref[...] * scale, sin_ref[...] * scale
    cached, own = cached_ref[...], own_ref[...]

    def rotated(u, w):
        u, w = u.astype(F32), w.astype(F32)
        return u * cos - w * sin, w * cos + u * sin

    for head in range(KV_HEADS):
        query = []
        for rep in range(REPS):
            u, w = rotated(shares(0, REPS * head + rep), shares(1, REPS * head + rep))
            query.append(jnp.concatenate([u, w], axis=1) * HEAD_DIM ** (-0.5))
        query = jnp.concatenate(query, axis=0).astype(BF)
        first, second = 2 * head, 2 * head + 1
        key_step = rotated(shares(2, first), shares(2, second))
        key_step = jnp.concatenate(key_step, axis=1).astype(BF)
        value_step = [shares(3, n).astype(F32) * scale for n in (first, second)]
        value_step = jnp.concatenate(value_step, axis=1).astype(BF)

        scores = lax.dot_general(query, key_step, NT, preferred_element_type=F32)
        weights = weight_of(scores) * own
        den = row_sum(weights)
        num = jnp.dot(weights.astype(BF), value_step, preferred_element_type=F32)

        keys = keys_ref[head, 0].reshape(slots * PAGE, HEAD_DIM)
        values = keys_ref[head, 1].reshape(slots * PAGE, HEAD_DIM)
        scores = lax.dot_general(query, keys, NT, preferred_element_type=F32)
        weights = weight_of(scores).reshape(REPS * rows // 8, 8, slots * PAGE) * cached[None]
        weights = weights.reshape(REPS * rows, slots * PAGE)
        den = den + row_sum(weights)
        num = num + jnp.dot(weights.astype(BF), values, preferred_element_type=F32)
        store(head, num, den)


def rope_tables(lengths, rows, steps):
    positions = lengths[0] + jnp.arange(rows, dtype=jnp.int32) % steps
    inverse_freq = ROPE_BASE ** (-jnp.arange(HALF, dtype=F32) * 2.0 / HEAD_DIM)
    angles = positions[:, None].astype(F32) * inverse_freq
    return jnp.cos(angles), jnp.sin(angles)


def body_permutes(
    inputs,
    cache_pool,
    lengths,
    block_table,
    parents,
    norm_gains,
    w_query,
    w_key,
    w_value,
    w_out,
    w_gate,
    w_up,
    w_down,
):
    beams, steps, width = inputs.shape
    nx, ny = lax.axis_size("gx"), lax.axis_size("gy")
    rows = beams * steps
    half = rows // 2
    all_rows = ny * rows
    share_rows = all_rows // nx
    hidden = w_gate.shape[1]
    packed = rows * width // 128

    def my(axis):
        return lax.axis_index(axis)

    def spread(x_ref, own_ref, out_ref):
        own = x_ref[...].astype(F32).reshape(rows, width).astype(BF)
        own_ref[...] = own
        own = pack_lanes(own)
        for m in range(ny):
            out_ref[m] = own

    x_own, x_all = run(
        "spread", spread, [((rows, width), BF), ((ny, packed, 128), BF)], (inputs,), micros=12
    )
    w_own = w_out.T
    x_all, w_split = lax.optimization_barrier((x_all, w_own))
    x_all = exchange(x_all, "gy")
    x_all, keys = lax.optimization_barrier((x_all, by_head(cache_pool)))

    w_blocks = {0: w_own, 1: permute(w_own, "gy", 1), 2: permute(w_own, "gy", 2)}
    w_first = permute(w_split[: width // 2], "gy", 4)
    w_late, _ = lax.optimization_barrier(((w_blocks[1], w_split[width // 2 :]), x_all))
    w_blocks[3] = permute(w_late[0], "gy", 2)
    w_second = permute(w_late[1], "gy", 4)

    def project(x_ref, gain_ref, q_ref, k_ref, v_ref, z0_ref, z2_ref, z13_ref, held):
        gain = 1.0 + gain_ref[0:1]
        flat = [
            (unpack_lanes(x_ref[m], rows).astype(F32) * gain).astype(BF) for m in range(ny)
        ]
        flat = jnp.concatenate(flat, axis=0)
        query = jnp.dot(flat, q_ref[...], preferred_element_type=F32).astype(BF)
        held[0], held[1] = query[:, :HALF], query[:, HALF:]
        held[2] = jnp.dot(flat, k_ref[...], preferred_element_type=F32).astype(BF)
        held[3] = jnp.dot(flat, v_ref[...], preferred_element_type=F32).astype(BF)
        me = my("gx")
        z0_ref[...], z2_ref[...] = held[me], held[me ^ 2]
        z13_ref[0], z13_ref[1] = held[me ^ 1], held[me ^ 3]

    shape = (all_rows, HALF)
    z0, z2, z13 = run(
        "project",
        project,
        [(shape, BF), (shape, BF), ((2,) + shape, BF)],
        (x_all, norm_gains, w_query, w_key, w_value),
        scratch=[
            pltpu.VMEM((nx,) + shape, BF),
        ],
    )
    z13 = permute(z13, "gx", 1)

    def pair_sum(z_ref, from_pair_ref, out_ref):
        total = z_ref[...].astype(F32) + from_pair_ref[1].astype(F32)
        out_ref[...] = total.astype(BF)

    (z2,) = run("pair_sum", pair_sum, [(shape, BF)], (z2, z13))
    z2 = permute(z2, "gx", 2)

    def share_sum(z0_ref, z13_ref, z2_ref, out_ref):
        total = z0_ref[...].astype(F32) + z13_ref[0].astype(F32) + z2_ref[...].astype(F32)
        out_ref[...] = total.reshape(ny, rows, HALF).astype(BF)

    (shares,) = run("share_sum", share_sum, [((ny, rows, HALF), BF)], (z0, z13, z2))
    late = block_table, lengths, parents
    late, _ = lax.optimization_barrier((late, (shares, w_blocks[2], w_blocks[3])))
    cos, sin = rope_tables(late[1], rows, steps)
    tables = make_tables(*late, cache_pool.shape[1], rows, steps)
    halves, _ = lax.optimization_barrier(((w_first, w_second), tables))
    w_blocks[4] = jnp.concatenate(halves, axis=0)
    late = w_blocks[4]
    w_blocks[6] = permute(late, "gy", 2)
    w_blocks[5] = permute(late, "gy", 1)
    shares = exchange(shares, "gy")
    shares, tables, cos, sin = lax.optimization_barrier((shares, tables, cos, sin))

    def pack_shares(share_ref, x_ref, out_ref):
        x = x_ref[...].astype(F32)
        out_ref[0:ny] = share_ref[...]
        out_ref[ny] = high_low(row_sum(x * x), HALF).astype(BF)

    (shares,) = run("pack_shares", pack_shares, [((ny + 1, rows, HALF), BF)], (shares, x_own))
    near, across = permute(shares, "gx", 1), permute(shares, "gx", 2)
    across, _ = lax.optimization_barrier((across, (w_blocks[6], w_blocks[5])))
    shares = [shares, near, across, permute(across, "gx", 1)]
    late, _ = lax.optimization_barrier((w_blocks[6], near))
    w_blocks[7] = permute(late, "gy", 1)

    def attention(*refs):
        a_refs, tables, keys_ref, outs = refs[:nx], refs[nx : nx + 4], refs[nx + 4], refs[nx + 5 :]
        own_ref, pair_ref, held, num_held, den_held = outs
        me = my("gx")
        core = me & 1
        for n, ref in enumerate(a_refs):
            held[me ^ n] = ref[...]
        den_held[...] = jnp.zeros(den_held.shape, F32)
        lane = lax.broadcasted_iota(jnp.int32, (2, half, PAGE), 2)

        def store(head, num, den):
            num_held[head] = num.reshape(REPS, 2, half, HEAD_DIM)
            den = high_low(den, PAGE).reshape(REPS, 2, half, PAGE)
            for rep in range(REPS):
                at = REPS * head + rep
                den_held[...] = jnp.where(lane % HALF_PAGE == at, den[rep], den_held[...])
                for n, out in enumerate((own_ref, pair_ref)):
                    for tile in range(2):
                        here = num_held[head, rep, core ^ n, :, tile * PAGE : (tile + 1) * PAGE]
                        out[2 * at + tile] = here.astype(BF)

        attend(
            lambda share, which: held[share, which],
            held[:, ny],
            tables,
            keys_ref,
            store,
        )
        for n, out in enumerate((own_ref, pair_ref)):
            out[2 * HEADS] = den_held[core ^ n].astype(BF)

    shape = (2 * HEADS + 1, half, PAGE)
    own, pair = run(
        "attention",
        attention,
        [(shape, BF), (shape, BF)],
        (*shares, cos, sin, *tables, keys),
        scratch=[
            pltpu.VMEM((nx,) + shares[0].shape, BF),
            pltpu.VMEM((KV_HEADS, REPS, 2, half, HEAD_DIM), F32),
            pltpu.VMEM((2, half, PAGE), F32),
        ],
        limit=24,
        micros=8,
    )
    pair = permute(pair, "gx", 1)

    def pair_terms(own_ref, pair_ref, out_ref):
        total = own_ref[...].astype(F32) + pair_ref[...].astype(F32)
        out_ref[0 : 2 * HEADS] = total[0 : 2 * HEADS].astype(BF)
        den = total[2 * HEADS]
        den = den[:, :HALF_PAGE] + den[:, HALF_PAGE:]
        high = den.astype(BF).astype(F32)
        out_ref[2 * HEADS] = jnp.concatenate([high, den - high], axis=1).astype(BF)

    (own,) = run("pair_terms", pair_terms, [(shape, BF)], (own, pair))
    across = permute(own, "gx", 2)
    across, _ = lax.optimization_barrier((across, w_blocks[7]))

    def divide(own_ref, across_ref, out_ref):
        total = own_ref[...].astype(F32) + across_ref[...].astype(F32)
        den = total[2 * HEADS]
        den = den[:, :HALF_PAGE] + den[:, HALF_PAGE:]
        for head in range(HEADS):
            scale = 1.0 / den[:, head : head + 1]
            for tile in range(2):
                at = 2 * head + tile
                out_ref[at] = (total[at] * scale).astype(BF)

    (attended,) = run("divide", divide, [((2 * HEADS, half, PAGE), BF)], (own, across))
    others = permute(attended, "gx", 1)

    def project_out(own_ref, other_ref, x_ref, gain_ref, *refs):
        w_refs, (attn_ref, sums_ref, held) = refs[:ny], refs[ny:]
        core = my("gx") & 1
        held[core], held[1 - core] = own_ref[...], other_ref[...]
        me = my("gy")
        attn = jnp.zeros((rows, width), F32)
        for m, w_ref in enumerate(w_refs):
            at = 2 * (me ^ m)
            flat = [jnp.concatenate([held[n, at], held[n, at + 1]], axis=1) for n in range(2)]
            flat = jnp.concatenate(flat, axis=0)
            attn = attn + lax.dot_general(flat, w_ref[...], NT, preferred_element_type=F32)
        attn_ref[...] = attn
        x = x_ref[...].astype(F32)
        scaled = attn * (1.0 + gain_ref[1:2])
        lane = lax.broadcasted_iota(jnp.int32, (rows, PAGE), 1)
        sums = jnp.zeros((rows, PAGE), F32)
        for n, terms in enumerate((attn * attn, scaled * scaled, x * scaled, x * x)):
            sums = jnp.where(lane == n, row_sum(terms), sums)
        sums_ref[...] = sums

    attn, sums = run(
        "project_out",
        project_out,
        [((rows, width), F32), ((rows, PAGE), F32)],
        (attended, others, x_own, norm_gains, *[w_blocks[m] for m in range(ny)]),
        scratch=[pltpu.VMEM((2, 2 * HEADS, half, PAGE), BF)],
    )
    sums = trade([sums] * nx, "gx")

    def mix(*refs):
        attn_ref, x_ref, gain_ref, mixed_ref, ff_ref = refs[nx:]
        total = sum(r[...] for r in refs[:nx])
        plain, scaled, cross, square = (total[:, n : n + 1] for n in range(4))
        scale = lax.rsqrt(plain / D + EPSILON)
        mixed = x_ref[...].astype(F32) + attn_ref[...] * scale * (1.0 + gain_ref[1:2])
        square = jnp.maximum(square + 2.0 * scale * cross + scale * scale * scaled, 0.0)
        mixed_ref[...] = mixed
        scale = lax.rsqrt(square / D + EPSILON)
        ff_input = (mixed * scale * (1.0 + gain_ref[2:3])).astype(BF)
        ff_input = pack_lanes(ff_input)
        for m in range(ny):
            ff_ref[m] = ff_input

    mixed, ff_input = run(
        "mix",
        mix,
        [((rows, width), F32), ((ny, packed, 128), BF)],
        (*sums, attn, x_own, norm_gains),
    )
    ff_input = exchange(ff_input, "gy")

    groups = ny // nx

    cut = (hidden // 128 + 1) // 2 * 128
    column_parts = (0, cut), (cut, hidden)

    def gate_up(start, end):
        def kernel(ff_ref, gate_ref, up_ref, z0_ref, z2_ref, z13_ref):
            me = my("gx")
            flat = [
                unpack_lanes(ff_ref[(me ^ n) * groups + group], rows)
                for n in range(nx)
                for group in range(groups)
            ]
            flat = jnp.concatenate(flat, axis=0)
            for n, w_ref in enumerate((gate_ref, up_ref)):
                sums = jnp.dot(flat, w_ref[:, start:end], preferred_element_type=F32).astype(BF)
                here = pl.ds(n * (end - start), end - start)
                for p, out in enumerate((z0_ref, z13_ref.at[0], z2_ref, z13_ref.at[1])):
                    out[:, here] = sums[p * share_rows : (p + 1) * share_rows]

        shape = (share_rows, 2 * (end - start))
        return run(
            "gate_up",
            kernel,
            [(shape, BF), (shape, BF), ((2,) + shape, BF)],
            (ff_input, w_gate, w_up),
            limit=24,
        )

    def activate(z0_ref, z13_ref, z2_ref, out_ref):
        total = z0_ref[...].astype(F32) + z13_ref[0].astype(F32) + z2_ref[...].astype(F32)
        count = total.shape[1] // 2
        gate, up = total[:, :count], total[:, count:]
        out_ref[...] = (jax.nn.gelu(gate, approximate=True) * up).astype(BF)

    parts = [gate_up(*columns) for columns in column_parts]
    blocks = []
    for z0, z2, z13 in parts:
        shape = z0.shape
        z13 = permute(z13, "gx", 1)
        (z2,) = run("pair_sum_ff", pair_sum, [(shape, BF)], (z2, z13))
        z2 = permute(z2, "gx", 2)
        shape = (share_rows, shape[1] // 2)
        blocks += gather_gx(run("activate", activate, [(shape, BF)], (z0, z13, z2))[0])

    def project_down(*refs):
        w_ref, out_ref = refs[2 * nx :]
        me = my("gx")
        flat = [
            jnp.concatenate([refs[n][...], refs[nx + n][...]], axis=1) for n in range(nx)
        ]
        flat = jnp.concatenate(flat, axis=0)
        sums = lax.dot_general(flat, w_ref[...], NT, preferred_element_type=F32)
        for n in range(nx):
            for group in range(groups):
                at = (n * groups + group) * rows
                block = pack_lanes(sums[at : at + rows].astype(BF))
                out_ref[(me ^ n) * groups + group] = block

    (down,) = run(
        "project_down", project_down, [((ny, packed, 128), BF)], (*blocks, w_down.T)
    )
    down = exchange(down, "gy")

    def down_sum(parts_ref, down_ref, sums_ref):
        down = unpack_lanes(jnp.sum(parts_ref[...].astype(F32), axis=0), rows)
        down_ref[...] = down
        sums_ref[...] = jnp.broadcast_to(row_sum(down * down), (rows, PAGE))

    down, sums = run(
        "down_sum", down_sum, [((rows, width), F32), ((rows, PAGE), F32)], (down,)
    )
    sums = trade([sums] * nx, "gx")

    def finish(*refs):
        down_ref, mixed_ref, gain_ref, out_ref = refs[nx:]
        square = sum(r[...] for r in refs[:nx])[:, 0:1]
        scale = lax.rsqrt(square / D + EPSILON)
        out = mixed_ref[...] + down_ref[...] * scale * (1.0 + gain_ref[3:4])
        out_ref[...] = out.reshape(beams, steps, width).astype(BF)

    (out,) = run("finish", finish, [(inputs.shape, BF)], (*sums, down, mixed, norm_gains))
    return out


def body_general(
    inputs,
    cache_pool,
    lengths,
    block_table,
    parents,
    norm_gains,
    w_query,
    w_key,
    w_value,
    w_out,
    w_gate,
    w_up,
    w_down,
):
    beams, steps, width = inputs.shape
    nx, ny = lax.axis_size("gx"), lax.axis_size("gy")
    rows = beams * steps
    part = rows // nx
    head_part = w_out.shape[0]
    hidden_part = w_gate.shape[1]
    query_part, key_part = w_query.shape[1], w_key.shape[1]
    columns = query_part + 2 * key_part
    share = columns // nx
    x_own = inputs.reshape(rows, width)
    me = lax.axis_index("gx")

    x_all = exchange(jnp.broadcast_to(x_own[None], (ny, rows, width)), "gy")
    flat = (x_all.astype(F32) * (1.0 + norm_gains[0:1])).astype(BF).reshape(ny * rows, width)
    sums = [jnp.dot(flat, w, preferred_element_type=F32) for w in (w_query, w_key, w_value)]
    sums = jnp.concatenate(sums, axis=1).reshape(ny, rows, nx, share)
    received = exchange_all(sums.transpose(2, 0, 1, 3).astype(BF))
    shares = jnp.sum(received.astype(F32), axis=0).astype(BF)
    every = lax.all_gather(shares, "gx", axis=0)
    every = every.transpose(2, 1, 0, 3).reshape(rows, ny, columns)
    q = every[..., :query_part].reshape(rows, HEADS, 2, HALF).transpose(2, 1, 0, 3)
    k, v = (
        every[..., start : start + key_part].reshape(rows, 2 * KV_HEADS, HALF).transpose(1, 0, 2)
        for start in (query_part, query_part + key_part)
    )
    shares = jnp.concatenate([q, k[None], v[None]], axis=0)
    square = lax.psum(row_sum(jnp.square(x_own.astype(F32))), "gx")
    high = lax.reduce_precision(square, 8, 7)
    squares = jnp.where(jnp.arange(HALF) < HALF // 2, high, square - high).astype(BF)[None]
    cos, sin = rope_tables(lengths, rows, steps)

    def attention(*refs):
        g_ref, square_ref, tables, keys_ref, out_ref = refs[0], refs[1], refs[2:6], *refs[6:]

        def store(head, num, den):
            den = high_low(den, PAGE)
            for rep in range(REPS):
                here = slice(rep * rows, (rep + 1) * rows)
                out_ref[REPS * head + rep, :, 0:HEAD_DIM] = num[here].astype(BF)
                out_ref[REPS * head + rep, :, HEAD_DIM:] = den[here].astype(BF)

        attend(
            lambda share, which: g_ref[share, which],
            square_ref[...],
            tables,
            keys_ref,
            store,
        )

    tables = make_tables(block_table, lengths, parents, cache_pool.shape[1], rows, steps)
    (terms,) = run(
        "attention",
        attention,
        [((HEADS, rows, WIDE), BF)],
        (shares, squares, cos, sin, *tables, by_head(cache_pool)),
        limit=24,
    )
    num = terms[..., :HEAD_DIM].transpose(1, 0, 2).reshape(nx, part, ny, head_part)
    den = terms[..., HEAD_DIM :: PAGE // 2].transpose(1, 0, 2)
    den = jnp.repeat(den, ny // HEADS, axis=1).reshape(nx, part, ny, 2)
    terms = exchange_all(jnp.concatenate([num, den], axis=-1).transpose(0, 2, 1, 3))

    w_wide = lax.all_gather(w_out, "gx", axis=1, tiled=True)
    x_wide = lax.all_gather(x_own, "gx", axis=1, tiled=True)
    x_rows = lax.dynamic_slice_in_dim(x_wide, me * part, part, 0).astype(F32)
    gains = 1.0 + lax.all_gather(norm_gains, "gx", axis=1, tiled=True)

    def scaled(v, gain):
        return v * lax.rsqrt(row_sum(v * v) / D + EPSILON) * gain

    terms = jnp.sum(terms.astype(F32), axis=0)
    den = terms[..., head_part : head_part + 1] + terms[..., -1:]
    attended = (terms[..., :head_part] / den).reshape(ny * part, head_part).astype(BF)
    attn = jnp.dot(attended, w_wide, preferred_element_type=F32).astype(BF)
    attn = exchange(attn.reshape(ny, part, D), "gy").astype(F32).sum(axis=0)
    mixed = x_rows + scaled(attn, gains[1])
    ff_input = scaled(mixed, gains[2]).astype(BF)
    ff_input = ff_input.reshape(part, nx, width).transpose(1, 0, 2)[:, None]
    ff_input = exchange_all(jnp.broadcast_to(ff_input, (nx, ny, part, width)))

    flat = ff_input.reshape(-1, width)
    both = [jnp.dot(flat, w, preferred_element_type=F32).astype(BF) for w in (w_gate, w_up)]
    both = jnp.stack(both, axis=1).reshape(nx, ny * part, 2, hidden_part)
    both = jnp.sum(exchange(both, "gx").astype(F32), axis=0)
    hidden = (jax.nn.gelu(both[:, 0], approximate=True) * both[:, 1]).astype(BF)
    hidden = lax.all_gather(hidden, "gx", axis=0, tiled=True)
    down = jnp.dot(hidden, w_down, preferred_element_type=F32).astype(BF)
    down = exchange_all(down.reshape(nx, ny, part, width)).astype(F32).sum(axis=1)
    down = down.transpose(1, 0, 2).reshape(part, D)
    out = (mixed + scaled(down, gains[3])).astype(BF)
    out = exchange(out.reshape(part, nx, width).transpose(1, 0, 2), "gx")
    return out.reshape(beams, steps, width)


def solution(mesh):
    sizes = dict(mesh.shape)
    fits = sizes["gx"] == 4 and sizes["gy"] == HEADS
    return jax.shard_map(
        body_permutes if fits else body_general,
        mesh=mesh,
        in_specs=(
            P("gy", None, "gx"),
            P(None, "gx", "gy", None),
            P("gy"),
            P("gy", None),
            P(None, "gy"),
            P(None, "gx"),
            P("gx", "gy"),
            P("gx", "gy"),
            P("gx", "gy"),
            P("gy", "gx"),
            P("gx", "gy"),
            P("gx", "gy"),
            P("gy", "gx"),
        ),
        out_specs=P("gy", None, "gx"),
        check_vma=False,
    )
```

```python
import jax
import jax.numpy as jnp
from jax import lax
from jax.experimental import pallas as pl
from jax.experimental.pallas import tpu as pltpu
from jax.sharding import PartitionSpec as P

D = 2304
HEADS = 8
KV_HEADS = 4
HEAD_DIM = 256
HALF = HEAD_DIM // 2
WINDOW = 4096
PAGE = 128
BEAM = 8
EPSILON = 1e-06
SOFT_CAP = 50.0
ROPE_BASE = 10000.0
REPS = HEADS // KV_HEADS
WIDE = HEAD_DIM + PAGE
HALF_PAGE = PAGE // 2
BF = jnp.bfloat16
F32 = jnp.float32
MIB = 1024 * 1024
NT = (((1,), (1,)), ((), ()))
IN_SMEM = pl.BlockSpec(memory_space=pltpu.SMEM)


def run(name, kernel, outs, args, scratch=(), limit=16, specs=None, micros=0):
    cost = pl.CostEstimate(flops=micros * 10**9, bytes_accessed=0, transcendentals=0)
    specs = specs or {}
    vmem = pl.BlockSpec(memory_space=pltpu.VMEM)
    return pl.pallas_call(
        kernel,
        out_shape=[jax.ShapeDtypeStruct(s, d) for s, d in outs],
        in_specs=[specs.get(n, vmem) for n in range(len(args))],
        scratch_shapes=scratch,
        compiler_params=pltpu.CompilerParams(vmem_limit_bytes=limit * MIB),
        cost_estimate=cost if micros else None,
        name=name,
    )(*args)


def exchange(values, axes):
    return lax.all_to_all(values, axes, split_axis=0, concat_axis=0, tiled=True)


def exchange_all(values):
    nx, ny = values.shape[:2]
    flat = values.reshape((nx * ny,) + values.shape[2:])
    return exchange(flat, ("gx", "gy")).reshape(values.shape)


def permute(values, axis, m):
    count = lax.axis_size(axis)
    return lax.ppermute(values, axis, [(i, i ^ m) for i in range(count)])


def trade(blocks, axis):
    return [blocks[0]] + [permute(blocks[m], axis, m) for m in range(1, len(blocks))]


def gather_gx(values):
    across = permute(values, "gx", 2)
    return [values, permute(values, "gx", 1), across, permute(across, "gx", 1)]


def weight_of(scores):
    return jnp.exp(SOFT_CAP * jnp.tanh(scores * (1.0 / SOFT_CAP)))


def high_low(column, lanes):
    shape = column.shape[:-1] + (lanes,)
    high = column.astype(BF).astype(F32)
    lane = lax.broadcasted_iota(jnp.int32, shape, len(shape) - 1)
    return jnp.where(lane < lanes // 2, high, column - high)


def pack_lanes(v):
    rows, width = v.shape
    whole = width // 128 * 128
    tiles = [v[:, c : c + 128] for c in range(0, whole, 128)]
    last = jnp.concatenate([v[: rows // 2, whole:], v[rows // 2 :, whole:]], axis=1)
    return jnp.concatenate(tiles + [last], axis=0)


def unpack_lanes(v, rows):
    whole = v.shape[0] // rows * rows
    tiles = [v[r : r + rows] for r in range(0, whole, rows)]
    last = jnp.concatenate([v[whole:, :64], v[whole:, 64:]], axis=0)
    return jnp.concatenate(tiles + [last], axis=1)


def row_sum(v):
    return jnp.sum(v, axis=-1, keepdims=True)


def make_tables(table, lengths, parents, slots, rows, steps):
    def tables(table_ref, length_ref, parents_ref, cached_ref, own_ref, page_ref):
        first_owner = lax.axis_index("gx") * slots
        length = length_ref[0]
        first_page = jnp.maximum(length - WINDOW + 1, 0) // PAGE
        for slot in range(slots + 1):
            page_ref[slot] = -1
        for j in range(table_ref.shape[1]):
            slot = table_ref[0, j] - first_owner
            page_ref[jnp.where((slot >= 0) & (slot < slots), slot, slots)] = j
        step = lax.broadcasted_iota(jnp.int32, (8, PAGE), 0) % steps
        lane = lax.broadcasted_iota(jnp.int32, (8, PAGE), 1)
        for slot in range(slots):
            page = page_ref[slot]
            position = lane + jnp.where(page >= 0, (first_page + page) * PAGE, 2**30)
            seen = (position < length) & (position >= length + step - (WINDOW - 1))
            cached_ref[:, slot * PAGE : (slot + 1) * PAGE] = jnp.where(seen, 1.0, 0.0)

        shape = (REPS * rows, rows)
        row = lax.broadcasted_iota(jnp.int32, shape, 0) % rows
        column = lax.broadcasted_iota(jnp.int32, shape, 1)
        row_step, column_step, column_beam = row % steps, column % steps, column // steps
        current = row // steps
        visible = jnp.zeros(shape, jnp.bool_)
        for j in range(steps - 1, -1, -1):
            if j < steps - 1:
                parent = jnp.zeros(shape, jnp.int32)
                for beam in range(BEAM):
                    parent = jnp.where(current == beam, parents_ref[j, beam], parent)
                current = jnp.where(row_step > j, parent, current)
            visible = visible | ((column_step == j) & (row_step >= j) & (column_beam == current))
        visible = visible & (lax.axis_index("gx") == 0)
        own_ref[...] = jnp.where(visible, 1.0, 0.0)

    return run(
        "tables",
        tables,
        [((8, slots * PAGE), F32), ((REPS * rows, rows), F32)],
        (table, lengths, parents),
        scratch=[pltpu.SMEM((slots + 1,), jnp.int32)],
        specs={0: IN_SMEM, 1: IN_SMEM, 2: IN_SMEM},
    )


def attend(shares, squares, tables, pool_ref, store):
    cos_ref, sin_ref, cached_ref, own_ref = tables
    slots = pool_ref.shape[1]
    rows = cos_ref.shape[0]
    square = jnp.sum(squares.astype(F32), axis=0)
    square = square[:, 0:1] + square[:, HALF // 2 : HALF // 2 + 1]
    scale = lax.rsqrt(square / D + EPSILON)
    cos, sin = cos_ref[...] * scale, sin_ref[...] * scale
    cached, own = cached_ref[...], own_ref[...]

    def rotated(u, w):
        u, w = u.astype(F32), w.astype(F32)
        return u * cos - w * sin, w * cos + u * sin

    for head in range(KV_HEADS):
        query = []
        for rep in range(REPS):
            u, w = rotated(shares(0, REPS * head + rep), shares(1, REPS * head + rep))
            query.append(jnp.concatenate([u, w], axis=1) * HEAD_DIM ** (-0.5))
        query = jnp.concatenate(query, axis=0).astype(BF)
        first, second = 2 * head, 2 * head + 1
        key_step = rotated(shares(2, first), shares(2, second))
        key_step = jnp.concatenate(key_step, axis=1).astype(BF)
        value_step = [shares(3, n).astype(F32) * scale for n in (first, second)]
        value_step = jnp.concatenate(value_step, axis=1).astype(BF)

        scores = lax.dot_general(query, key_step, NT, preferred_element_type=F32)
        weights = weight_of(scores) * own
        den = row_sum(weights)
        num = jnp.dot(weights.astype(BF), value_step, preferred_element_type=F32)

        here = slice(head * HEAD_DIM, (head + 1) * HEAD_DIM)
        keys = pool_ref[0, :, :, here].reshape(slots * PAGE, HEAD_DIM)
        values = pool_ref[1, :, :, here].reshape(slots * PAGE, HEAD_DIM)
        scores = lax.dot_general(query, keys, NT, preferred_element_type=F32)
        weights = weight_of(scores).reshape(REPS * rows // 8, 8, slots * PAGE) * cached[None]
        weights = weights.reshape(REPS * rows, slots * PAGE)
        den = den + row_sum(weights)
        num = num + jnp.dot(weights.astype(BF), values, preferred_element_type=F32)
        store(head, num, den)


def rope_tables(lengths, rows, steps):
    positions = lengths[0] + jnp.arange(rows, dtype=jnp.int32) % steps
    inverse_freq = ROPE_BASE ** (-jnp.arange(HALF, dtype=F32) * 2.0 / HEAD_DIM)
    angles = positions[:, None].astype(F32) * inverse_freq
    return jnp.cos(angles), jnp.sin(angles)


def body_permutes(
    inputs,
    cache_pool,
    lengths,
    block_table,
    parents,
    norm_gains,
    w_query,
    w_key,
    w_value,
    w_out,
    w_gate,
    w_up,
    w_down,
):
    beams, steps, width = inputs.shape
    nx, ny = lax.axis_size("gx"), lax.axis_size("gy")
    rows = beams * steps
    half = rows // 2
    all_rows = ny * rows
    share_rows = all_rows // nx
    hidden = w_gate.shape[1]
    packed = rows * width // 128

    def my(axis):
        return lax.axis_index(axis)

    def spread(x_ref, own_ref, out_ref):
        own = x_ref[...].astype(F32).reshape(rows, width).astype(BF)
        own_ref[...] = own
        own = pack_lanes(own)
        for m in range(ny):
            out_ref[m] = own

    x_own, x_all = run(
        "spread", spread, [((rows, width), BF), ((ny, packed, 128), BF)], (inputs,), micros=12
    )
    w_own = w_out.T
    x_all, w_split = lax.optimization_barrier((x_all, w_own))
    x_all = exchange(x_all, "gy")

    w_blocks = {0: w_own, 1: permute(w_own, "gy", 1), 2: permute(w_own, "gy", 2)}
    w_first = permute(w_split[: width // 2], "gy", 4)
    w_late, _ = lax.optimization_barrier(((w_blocks[1], w_split[width // 2 :]), x_all))
    w_blocks[3] = permute(w_late[0], "gy", 2)
    w_second = permute(w_late[1], "gy", 4)

    def project(x_ref, gain_ref, q_ref, k_ref, v_ref, z0_ref, z2_ref, z13_ref, held):
        gain = 1.0 + gain_ref[0:1]
        flat = [
            (unpack_lanes(x_ref[m], rows).astype(F32) * gain).astype(BF) for m in range(ny)
        ]
        flat = jnp.concatenate(flat, axis=0)
        query = jnp.dot(flat, q_ref[...], preferred_element_type=F32).astype(BF)
        held[0], held[1] = query[:, :HALF], query[:, HALF:]
        held[2] = jnp.dot(flat, k_ref[...], preferred_element_type=F32).astype(BF)
        held[3] = jnp.dot(flat, v_ref[...], preferred_element_type=F32).astype(BF)
        me = my("gx")
        z0_ref[...], z2_ref[...] = held[me], held[me ^ 2]
        z13_ref[0], z13_ref[1] = held[me ^ 1], held[me ^ 3]

    shape = (all_rows, HALF)
    z0, z2, z13 = run(
        "project",
        project,
        [(shape, BF), (shape, BF), ((2,) + shape, BF)],
        (x_all, norm_gains, w_query, w_key, w_value),
        scratch=[
            pltpu.VMEM((nx,) + shape, BF),
        ],
    )
    z13 = permute(z13, "gx", 1)

    def pair_sum(z_ref, from_pair_ref, out_ref):
        total = z_ref[...].astype(F32) + from_pair_ref[1].astype(F32)
        out_ref[...] = total.astype(BF)

    (z2,) = run("pair_sum", pair_sum, [(shape, BF)], (z2, z13))
    z2 = permute(z2, "gx", 2)

    def share_sum(z0_ref, z13_ref, z2_ref, out_ref):
        total = z0_ref[...].astype(F32) + z13_ref[0].astype(F32) + z2_ref[...].astype(F32)
        out_ref[...] = total.reshape(ny, rows, HALF).astype(BF)

    (shares,) = run("share_sum", share_sum, [((ny, rows, HALF), BF)], (z0, z13, z2))
    shares, *late = lax.optimization_barrier((shares, block_table, lengths, parents))
    cos, sin = rope_tables(late[1], rows, steps)
    tables = make_tables(*late, cache_pool.shape[1], rows, steps)
    halves, _ = lax.optimization_barrier(((w_first, w_second), tables))
    w_blocks[4] = jnp.concatenate(halves, axis=0)
    w_blocks[6] = permute(w_blocks[4], "gy", 2)
    w_blocks[5] = permute(w_blocks[4], "gy", 1)
    shares = exchange(shares, "gy")
    beside = tables, cos, sin, w_blocks[2], w_blocks[3], w_blocks[4]
    shares, (tables, cos, sin, *_) = lax.optimization_barrier((shares, beside))

    def pack_shares(share_ref, x_ref, out_ref):
        x = x_ref[...].astype(F32)
        out_ref[0:ny] = share_ref[...]
        out_ref[ny] = high_low(row_sum(x * x), HALF).astype(BF)

    (shares,) = run(
        "pack_shares", pack_shares, [((ny + 1, rows, HALF), BF)], (shares, x_own), micros=5
    )
    shares = gather_gx(shares)

    def attention(*refs):
        a_refs, tables, pool_ref, outs = refs[:nx], refs[nx : nx + 4], refs[nx + 4], refs[nx + 5 :]
        own_ref, pair_ref, held, num_held, den_held = outs
        me = my("gx")
        core = me & 1
        for n, ref in enumerate(a_refs):
            held[me ^ n] = ref[...]
        den_held[...] = jnp.zeros(den_held.shape, F32)
        lane = lax.broadcasted_iota(jnp.int32, (2, half, PAGE), 2)

        def store(head, num, den):
            num_held[head] = num.reshape(REPS, 2, half, HEAD_DIM)
            den = high_low(den, PAGE).reshape(REPS, 2, half, PAGE)
            for rep in range(REPS):
                at = REPS * head + rep
                den_held[...] = jnp.where(lane % HALF_PAGE == at, den[rep], den_held[...])
                for n, out in enumerate((own_ref, pair_ref)):
                    for tile in range(2):
                        here = num_held[head, rep, core ^ n, :, tile * PAGE : (tile + 1) * PAGE]
                        out[2 * at + tile] = here.astype(BF)

        attend(
            lambda share, which: held[share, which],
            held[:, ny],
            tables,
            pool_ref,
            store,
        )
        for n, out in enumerate((own_ref, pair_ref)):
            out[2 * HEADS] = den_held[core ^ n].astype(BF)

    shape = (2 * HEADS + 1, half, PAGE)
    own, pair = run(
        "attention",
        attention,
        [(shape, BF), (shape, BF)],
        (*shares, cos, sin, *tables, cache_pool),
        scratch=[
            pltpu.VMEM((nx,) + shares[0].shape, BF),
            pltpu.VMEM((KV_HEADS, REPS, 2, half, HEAD_DIM), F32),
            pltpu.VMEM((2, half, PAGE), F32),
        ],
        limit=24,
    )
    w_late, _ = lax.optimization_barrier((w_blocks, own))
    w_blocks[7] = permute(w_late[6], "gy", 1)
    pair = permute(pair, "gx", 1)

    def pair_terms(own_ref, pair_ref, out_ref):
        total = own_ref[...].astype(F32) + pair_ref[...].astype(F32)
        out_ref[0 : 2 * HEADS] = total[0 : 2 * HEADS].astype(BF)
        den = total[2 * HEADS]
        den = den[:, :HALF_PAGE] + den[:, HALF_PAGE:]
        high = den.astype(BF).astype(F32)
        out_ref[2 * HEADS] = jnp.concatenate([high, den - high], axis=1).astype(BF)

    (own,) = run("pair_terms", pair_terms, [(shape, BF)], (own, pair))
    across = permute(own, "gx", 2)

    def divide(own_ref, across_ref, out_ref):
        total = own_ref[...].astype(F32) + across_ref[...].astype(F32)
        den = total[2 * HEADS]
        den = den[:, :HALF_PAGE] + den[:, HALF_PAGE:]
        for head in range(HEADS):
            scale = 1.0 / den[:, head : head + 1]
            for tile in range(2):
                at = 2 * head + tile
                out_ref[at] = (total[at] * scale).astype(BF)

    (attended,) = run("divide", divide, [((2 * HEADS, half, PAGE), BF)], (own, across))
    others = permute(attended, "gx", 1)

    def project_out(own_ref, other_ref, x_ref, gain_ref, *refs):
        w_refs, (attn_ref, sums_ref, held) = refs[:ny], refs[ny:]
        core = my("gx") & 1
        held[core], held[1 - core] = own_ref[...], other_ref[...]
        me = my("gy")
        attn = jnp.zeros((rows, width), F32)
        for m, w_ref in enumerate(w_refs):
            at = 2 * (me ^ m)
            flat = [jnp.concatenate([held[n, at], held[n, at + 1]], axis=1) for n in range(2)]
            flat = jnp.concatenate(flat, axis=0)
            attn = attn + lax.dot_general(flat, w_ref[...], NT, preferred_element_type=F32)
        attn_ref[...] = attn
        x = x_ref[...].astype(F32)
        scaled = attn * (1.0 + gain_ref[1:2])
        lane = lax.broadcasted_iota(jnp.int32, (rows, PAGE), 1)
        sums = jnp.zeros((rows, PAGE), F32)
        for n, terms in enumerate((attn * attn, scaled * scaled, x * scaled, x * x)):
            sums = jnp.where(lane == n, row_sum(terms), sums)
        sums_ref[...] = sums

    attn, sums = run(
        "project_out",
        project_out,
        [((rows, width), F32), ((rows, PAGE), F32)],
        (attended, others, x_own, norm_gains, *[w_blocks[m] for m in range(ny)]),
        scratch=[pltpu.VMEM((2, 2 * HEADS, half, PAGE), BF)],
    )
    sums = trade([sums] * nx, "gx")

    def mix(*refs):
        attn_ref, x_ref, gain_ref, mixed_ref, ff_ref = refs[nx:]
        total = sum(r[...] for r in refs[:nx])
        plain, scaled, cross, square = (total[:, n : n + 1] for n in range(4))
        scale = lax.rsqrt(plain / D + EPSILON)
        mixed = x_ref[...].astype(F32) + attn_ref[...] * scale * (1.0 + gain_ref[1:2])
        square = jnp.maximum(square + 2.0 * scale * cross + scale * scale * scaled, 0.0)
        mixed_ref[...] = mixed
        scale = lax.rsqrt(square / D + EPSILON)
        ff_input = (mixed * scale * (1.0 + gain_ref[2:3])).astype(BF)
        ff_input = pack_lanes(ff_input)
        for m in range(ny):
            ff_ref[m] = ff_input

    mixed, ff_input = run(
        "mix",
        mix,
        [((rows, width), F32), ((ny, packed, 128), BF)],
        (*sums, attn, x_own, norm_gains),
    )
    ff_input = exchange(ff_input, "gy")

    groups = ny // nx

    cut = (hidden // 128 + 1) // 2 * 128
    column_parts = (0, cut), (cut, hidden)

    def gate_up(start, end):
        def kernel(ff_ref, gate_ref, up_ref, z0_ref, z2_ref, z13_ref):
            me = my("gx")
            flat = [
                unpack_lanes(ff_ref[(me ^ n) * groups + group], rows)
                for n in range(nx)
                for group in range(groups)
            ]
            flat = jnp.concatenate(flat, axis=0)
            for n, w_ref in enumerate((gate_ref, up_ref)):
                sums = jnp.dot(flat, w_ref[:, start:end], preferred_element_type=F32).astype(BF)
                here = pl.ds(n * (end - start), end - start)
                for p, out in enumerate((z0_ref, z13_ref.at[0], z2_ref, z13_ref.at[1])):
                    out[:, here] = sums[p * share_rows : (p + 1) * share_rows]

        shape = (share_rows, 2 * (end - start))
        return run(
            "gate_up",
            kernel,
            [(shape, BF), (shape, BF), ((2,) + shape, BF)],
            (ff_input, w_gate, w_up),
            limit=24,
        )

    def activate(z0_ref, z13_ref, z2_ref, out_ref):
        total = z0_ref[...].astype(F32) + z13_ref[0].astype(F32) + z2_ref[...].astype(F32)
        count = total.shape[1] // 2
        gate, up = total[:, :count], total[:, count:]
        out_ref[...] = (jax.nn.gelu(gate, approximate=True) * up).astype(BF)

    parts = [gate_up(*columns) for columns in column_parts]
    blocks = []
    for z0, z2, z13 in parts:
        shape = z0.shape
        z13 = permute(z13, "gx", 1)
        (z2,) = run("pair_sum_ff", pair_sum, [(shape, BF)], (z2, z13))
        z2 = permute(z2, "gx", 2)
        shape = (share_rows, shape[1] // 2)
        blocks += gather_gx(run("activate", activate, [(shape, BF)], (z0, z13, z2))[0])

    def project_down(*refs):
        w_ref, out_ref = refs[2 * nx :]
        me = my("gx")
        flat = [
            jnp.concatenate([refs[n][...], refs[nx + n][...]], axis=1) for n in range(nx)
        ]
        flat = jnp.concatenate(flat, axis=0)
        sums = lax.dot_general(flat, w_ref[...], NT, preferred_element_type=F32)
        for n in range(nx):
            for group in range(groups):
                at = (n * groups + group) * rows
                block = pack_lanes(sums[at : at + rows].astype(BF))
                out_ref[(me ^ n) * groups + group] = block

    (down,) = run(
        "project_down", project_down, [((ny, packed, 128), BF)], (*blocks, w_down.T)
    )
    down = exchange(down, "gy")

    def down_sum(parts_ref, down_ref, sums_ref):
        down = unpack_lanes(jnp.sum(parts_ref[...].astype(F32), axis=0), rows)
        down_ref[...] = down
        sums_ref[...] = jnp.broadcast_to(row_sum(down * down), (rows, PAGE))

    down, sums = run(
        "down_sum", down_sum, [((rows, width), F32), ((rows, PAGE), F32)], (down,)
    )
    sums = trade([sums] * nx, "gx")

    def finish(*refs):
        down_ref, mixed_ref, gain_ref, out_ref = refs[nx:]
        square = sum(r[...] for r in refs[:nx])[:, 0:1]
        scale = lax.rsqrt(square / D + EPSILON)
        out = mixed_ref[...] + down_ref[...] * scale * (1.0 + gain_ref[3:4])
        out_ref[...] = out.reshape(beams, steps, width).astype(BF)

    (out,) = run("finish", finish, [(inputs.shape, BF)], (*sums, down, mixed, norm_gains))
    return out


def body_general(
    inputs,
    cache_pool,
    lengths,
    block_table,
    parents,
    norm_gains,
    w_query,
    w_key,
    w_value,
    w_out,
    w_gate,
    w_up,
    w_down,
):
    beams, steps, width = inputs.shape
    nx, ny = lax.axis_size("gx"), lax.axis_size("gy")
    rows = beams * steps
    part = rows // nx
    head_part = w_out.shape[0]
    hidden_part = w_gate.shape[1]
    query_part, key_part = w_query.shape[1], w_key.shape[1]
    columns = query_part + 2 * key_part
    share = columns // nx
    x_own = inputs.reshape(rows, width)
    me = lax.axis_index("gx")

    x_all = exchange(jnp.broadcast_to(x_own[None], (ny, rows, width)), "gy")
    flat = (x_all.astype(F32) * (1.0 + norm_gains[0:1])).astype(BF).reshape(ny * rows, width)
    sums = [jnp.dot(flat, w, preferred_element_type=F32) for w in (w_query, w_key, w_value)]
    sums = jnp.concatenate(sums, axis=1).reshape(ny, rows, nx, share)
    received = exchange_all(sums.transpose(2, 0, 1, 3).astype(BF))
    shares = jnp.sum(received.astype(F32), axis=0).astype(BF)
    every = lax.all_gather(shares, "gx", axis=0)
    every = every.transpose(2, 1, 0, 3).reshape(rows, ny, columns)
    q = every[..., :query_part].reshape(rows, HEADS, 2, HALF).transpose(2, 1, 0, 3)
    k, v = (
        every[..., start : start + key_part].reshape(rows, 2 * KV_HEADS, HALF).transpose(1, 0, 2)
        for start in (query_part, query_part + key_part)
    )
    shares = jnp.concatenate([q, k[None], v[None]], axis=0)
    square = lax.psum(row_sum(jnp.square(x_own.astype(F32))), "gx")
    high = lax.reduce_precision(square, 8, 7)
    squares = jnp.where(jnp.arange(HALF) < HALF // 2, high, square - high).astype(BF)[None]
    cos, sin = rope_tables(lengths, rows, steps)

    def attention(*refs):
        g_ref, square_ref, tables, pool_ref, out_ref = refs[0], refs[1], refs[2:6], *refs[6:]

        def store(head, num, den):
            den = high_low(den, PAGE)
            for rep in range(REPS):
                here = slice(rep * rows, (rep + 1) * rows)
                out_ref[REPS * head + rep, :, 0:HEAD_DIM] = num[here].astype(BF)
                out_ref[REPS * head + rep, :, HEAD_DIM:] = den[here].astype(BF)

        attend(
            lambda share, which: g_ref[share, which],
            square_ref[...],
            tables,
            pool_ref,
            store,
        )

    tables = make_tables(block_table, lengths, parents, cache_pool.shape[1], rows, steps)
    (terms,) = run(
        "attention",
        attention,
        [((HEADS, rows, WIDE), BF)],
        (shares, squares, cos, sin, *tables, cache_pool),
        limit=24,
    )
    num = terms[..., :HEAD_DIM].transpose(1, 0, 2).reshape(nx, part, ny, head_part)
    den = terms[..., HEAD_DIM :: PAGE // 2].transpose(1, 0, 2)
    den = jnp.repeat(den, ny // HEADS, axis=1).reshape(nx, part, ny, 2)
    terms = exchange_all(jnp.concatenate([num, den], axis=-1).transpose(0, 2, 1, 3))

    w_wide = lax.all_gather(w_out, "gx", axis=1, tiled=True)
    x_wide = lax.all_gather(x_own, "gx", axis=1, tiled=True)
    x_rows = lax.dynamic_slice_in_dim(x_wide, me * part, part, 0).astype(F32)
    gains = 1.0 + lax.all_gather(norm_gains, "gx", axis=1, tiled=True)

    def scaled(v, gain):
        return v * lax.rsqrt(row_sum(v * v) / D + EPSILON) * gain

    terms = jnp.sum(terms.astype(F32), axis=0)
    den = terms[..., head_part : head_part + 1] + terms[..., -1:]
    attended = (terms[..., :head_part] / den).reshape(ny * part, head_part).astype(BF)
    attn = jnp.dot(attended, w_wide, preferred_element_type=F32).astype(BF)
    attn = exchange(attn.reshape(ny, part, D), "gy").astype(F32).sum(axis=0)
    mixed = x_rows + scaled(attn, gains[1])
    ff_input = scaled(mixed, gains[2]).astype(BF)
    ff_input = ff_input.reshape(part, nx, width).transpose(1, 0, 2)[:, None]
    ff_input = exchange_all(jnp.broadcast_to(ff_input, (nx, ny, part, width)))

    flat = ff_input.reshape(-1, width)
    both = [jnp.dot(flat, w, preferred_element_type=F32).astype(BF) for w in (w_gate, w_up)]
    both = jnp.stack(both, axis=1).reshape(nx, ny * part, 2, hidden_part)
    both = jnp.sum(exchange(both, "gx").astype(F32), axis=0)
    hidden = (jax.nn.gelu(both[:, 0], approximate=True) * both[:, 1]).astype(BF)
    hidden = lax.all_gather(hidden, "gx", axis=0, tiled=True)
    down = jnp.dot(hidden, w_down, preferred_element_type=F32).astype(BF)
    down = exchange_all(down.reshape(nx, ny, part, width)).astype(F32).sum(axis=1)
    down = down.transpose(1, 0, 2).reshape(part, D)
    out = (mixed + scaled(down, gains[3])).astype(BF)
    out = exchange(out.reshape(part, nx, width).transpose(1, 0, 2), "gx")
    return out.reshape(beams, steps, width)


def solution(mesh):
    sizes = dict(mesh.shape)
    fits = sizes["gx"] == 4 and sizes["gy"] == HEADS
    return jax.shard_map(
        body_permutes if fits else body_general,
        mesh=mesh,
        in_specs=(
            P("gy", None, "gx"),
            P(None, "gx", "gy", None),
            P("gy"),
            P("gy", None),
            P(None, "gy"),
            P(None, "gx"),
            P("gx", "gy"),
            P("gx", "gy"),
            P("gx", "gy"),
            P("gy", "gx"),
            P("gx", "gy"),
            P("gx", "gy"),
            P("gy", "gx"),
        ),
        out_specs=P("gy", None, "gx"),
        check_vma=False,
    )
```

```python
import jax
import jax.numpy as jnp
from jax import lax
from jax.experimental import pallas as pl
from jax.experimental.pallas import tpu as pltpu
from jax.sharding import PartitionSpec as P

D = 2304
HEADS = 8
KV_HEADS = 4
HEAD_DIM = 256
HALF = HEAD_DIM // 2
WINDOW = 4096
PAGE = 128
BEAM = 8
EPSILON = 1e-06
SOFT_CAP = 50.0
ROPE_BASE = 10000.0
REPS = HEADS // KV_HEADS
WIDE = HEAD_DIM + PAGE
HALF_PAGE = PAGE // 2
BF = jnp.bfloat16
F32 = jnp.float32
MIB = 1024 * 1024
NT = (((1,), (1,)), ((), ()))
IN_SMEM = pl.BlockSpec(memory_space=pltpu.SMEM)


def run(name, kernel, outs, args, scratch=(), limit=16, specs=None, micros=0):
    cost = pl.CostEstimate(flops=micros * 10**9, bytes_accessed=0, transcendentals=0)
    specs = specs or {}
    vmem = pl.BlockSpec(memory_space=pltpu.VMEM)
    return pl.pallas_call(
        kernel,
        out_shape=[jax.ShapeDtypeStruct(s, d) for s, d in outs],
        in_specs=[specs.get(n, vmem) for n in range(len(args))],
        scratch_shapes=scratch,
        compiler_params=pltpu.CompilerParams(vmem_limit_bytes=limit * MIB),
        cost_estimate=cost if micros else None,
        name=name,
    )(*args)


def exchange(values, axes):
    return lax.all_to_all(values, axes, split_axis=0, concat_axis=0, tiled=True)


def exchange_all(values):
    nx, ny = values.shape[:2]
    flat = values.reshape((nx * ny,) + values.shape[2:])
    return exchange(flat, ("gx", "gy")).reshape(values.shape)


def permute(values, axis, m):
    count = lax.axis_size(axis)
    return lax.ppermute(values, axis, [(i, i ^ m) for i in range(count)])


def trade(blocks, axis):
    return [blocks[0]] + [permute(blocks[m], axis, m) for m in range(1, len(blocks))]


def gather_gx(values):
    across = permute(values, "gx", 2)
    return [values, permute(values, "gx", 1), across, permute(across, "gx", 1)]


def weight_of(scores):
    return jnp.exp(SOFT_CAP * jnp.tanh(scores * (1.0 / SOFT_CAP)))


def high_low(column, lanes):
    shape = column.shape[:-1] + (lanes,)
    high = column.astype(BF).astype(F32)
    lane = lax.broadcasted_iota(jnp.int32, shape, len(shape) - 1)
    return jnp.where(lane < lanes // 2, high, column - high)


def pack_lanes(v):
    rows, width = v.shape
    whole = width // 128 * 128
    tiles = [v[:, c : c + 128] for c in range(0, whole, 128)]
    last = jnp.concatenate([v[: rows // 2, whole:], v[rows // 2 :, whole:]], axis=1)
    return jnp.concatenate(tiles + [last], axis=0)


def unpack_lanes(v, rows):
    whole = v.shape[0] // rows * rows
    tiles = [v[r : r + rows] for r in range(0, whole, rows)]
    last = jnp.concatenate([v[whole:, :64], v[whole:, 64:]], axis=0)
    return jnp.concatenate(tiles + [last], axis=1)


def row_sum(v):
    return jnp.sum(v, axis=-1, keepdims=True)


def make_tables(table, lengths, parents, slots, rows, steps):
    def tables(table_ref, length_ref, parents_ref, cached_ref, own_ref, page_ref):
        first_owner = lax.axis_index("gx") * slots
        length = length_ref[0]
        first_page = jnp.maximum(length - WINDOW + 1, 0) // PAGE
        for slot in range(slots + 1):
            page_ref[slot] = -1
        for j in range(table_ref.shape[1]):
            slot = table_ref[0, j] - first_owner
            page_ref[jnp.where((slot >= 0) & (slot < slots), slot, slots)] = j
        step = lax.broadcasted_iota(jnp.int32, (8, PAGE), 0) % steps
        lane = lax.broadcasted_iota(jnp.int32, (8, PAGE), 1)
        for slot in range(slots):
            page = page_ref[slot]
            position = lane + jnp.where(page >= 0, (first_page + page) * PAGE, 2**30)
            seen = (position < length) & (position >= length + step - (WINDOW - 1))
            cached_ref[:, slot * PAGE : (slot + 1) * PAGE] = jnp.where(seen, 1.0, 0.0)

        shape = (REPS * rows, rows)
        row = lax.broadcasted_iota(jnp.int32, shape, 0) % rows
        column = lax.broadcasted_iota(jnp.int32, shape, 1)
        row_step, column_step, column_beam = row % steps, column % steps, column // steps
        current = row // steps
        visible = jnp.zeros(shape, jnp.bool_)
        for j in range(steps - 1, -1, -1):
            if j < steps - 1:
                parent = jnp.zeros(shape, jnp.int32)
                for beam in range(BEAM):
                    parent = jnp.where(current == beam, parents_ref[j, beam], parent)
                current = jnp.where(row_step > j, parent, current)
            visible = visible | ((column_step == j) & (row_step >= j) & (column_beam == current))
        visible = visible & (lax.axis_index("gx") == 0)
        own_ref[...] = jnp.where(visible, 1.0, 0.0)

    return run(
        "tables",
        tables,
        [((8, slots * PAGE), F32), ((REPS * rows, rows), F32)],
        (table, lengths, parents),
        scratch=[pltpu.SMEM((slots + 1,), jnp.int32)],
        specs={0: IN_SMEM, 1: IN_SMEM, 2: IN_SMEM},
    )


def attend(shares, squares, tables, pool_ref, store):
    cos_ref, sin_ref, cached_ref, own_ref = tables
    slots = pool_ref.shape[1]
    rows = cos_ref.shape[0]
    square = jnp.sum(squares.astype(F32), axis=0)
    square = square[:, 0:1] + square[:, HALF // 2 : HALF // 2 + 1]
    scale = lax.rsqrt(square / D + EPSILON)
    cos, sin = cos_ref[...] * scale, sin_ref[...] * scale
    cached, own = cached_ref[...], own_ref[...]

    def rotated(u, w):
        u, w = u.astype(F32), w.astype(F32)
        return u * cos - w * sin, w * cos + u * sin

    for head in range(KV_HEADS):
        query = []
        for rep in range(REPS):
            u, w = rotated(shares(0, REPS * head + rep), shares(1, REPS * head + rep))
            query.append(jnp.concatenate([u, w], axis=1) * HEAD_DIM ** (-0.5))
        query = jnp.concatenate(query, axis=0).astype(BF)
        first, second = 2 * head, 2 * head + 1
        key_step = rotated(shares(2, first), shares(2, second))
        key_step = jnp.concatenate(key_step, axis=1).astype(BF)
        value_step = [shares(3, n).astype(F32) * scale for n in (first, second)]
        value_step = jnp.concatenate(value_step, axis=1).astype(BF)

        scores = lax.dot_general(query, key_step, NT, preferred_element_type=F32)
        weights = weight_of(scores) * own
        den = row_sum(weights)
        num = jnp.dot(weights.astype(BF), value_step, preferred_element_type=F32)

        here = slice(head * HEAD_DIM, (head + 1) * HEAD_DIM)
        keys = pool_ref[0, :, :, here].reshape(slots * PAGE, HEAD_DIM)
        values = pool_ref[1, :, :, here].reshape(slots * PAGE, HEAD_DIM)
        scores = lax.dot_general(query, keys, NT, preferred_element_type=F32)
        weights = weight_of(scores).reshape(REPS * rows // 8, 8, slots * PAGE) * cached[None]
        weights = weights.reshape(REPS * rows, slots * PAGE)
        den = den + row_sum(weights)
        num = num + jnp.dot(weights.astype(BF), values, preferred_element_type=F32)
        store(head, num, den)


def rope_tables(lengths, rows, steps):
    positions = lengths[0] + jnp.arange(rows, dtype=jnp.int32) % steps
    inverse_freq = ROPE_BASE ** (-jnp.arange(HALF, dtype=F32) * 2.0 / HEAD_DIM)
    angles = positions[:, None].astype(F32) * inverse_freq
    return jnp.cos(angles), jnp.sin(angles)


def body_permutes(
    inputs,
    cache_pool,
    lengths,
    block_table,
    parents,
    norm_gains,
    w_query,
    w_key,
    w_value,
    w_out,
    w_gate,
    w_up,
    w_down,
):
    beams, steps, width = inputs.shape
    nx, ny = lax.axis_size("gx"), lax.axis_size("gy")
    rows = beams * steps
    half = rows // 2
    all_rows = ny * rows
    share_rows = all_rows // nx
    hidden = w_gate.shape[1]
    packed = rows * width // 128

    def my(axis):
        return lax.axis_index(axis)

    def spread(x_ref, own_ref, out_ref):
        own = x_ref[...].astype(F32).reshape(rows, width).astype(BF)
        own_ref[...] = own
        own = pack_lanes(own)
        for m in range(ny):
            out_ref[m] = own

    x_own, x_all = run(
        "spread", spread, [((rows, width), BF), ((ny, packed, 128), BF)], (inputs,), micros=12
    )
    w_own = w_out.T
    x_all, w_split = lax.optimization_barrier((x_all, w_own))
    x_all = exchange(x_all, "gy")

    w_blocks = {0: w_own, 1: permute(w_own, "gy", 1), 2: permute(w_own, "gy", 2)}
    w_first = permute(w_split[: width // 2], "gy", 4)
    w_late, _ = lax.optimization_barrier(((w_blocks[1], w_split[width // 2 :]), x_all))
    w_blocks[3] = permute(w_late[0], "gy", 2)
    w_second = permute(w_late[1], "gy", 4)

    def project(x_ref, gain_ref, q_ref, k_ref, v_ref, z0_ref, z2_ref, z13_ref, held):
        gain = 1.0 + gain_ref[0:1]
        flat = [
            (unpack_lanes(x_ref[m], rows).astype(F32) * gain).astype(BF) for m in range(ny)
        ]
        flat = jnp.concatenate(flat, axis=0)
        query = jnp.dot(flat, q_ref[...], preferred_element_type=F32).astype(BF)
        held[0], held[1] = query[:, :HALF], query[:, HALF:]
        held[2] = jnp.dot(flat, k_ref[...], preferred_element_type=F32).astype(BF)
        held[3] = jnp.dot(flat, v_ref[...], preferred_element_type=F32).astype(BF)
        me = my("gx")
        z0_ref[...], z2_ref[...] = held[me], held[me ^ 2]
        z13_ref[0], z13_ref[1] = held[me ^ 1], held[me ^ 3]

    shape = (all_rows, HALF)
    z0, z2, z13 = run(
        "project",
        project,
        [(shape, BF), (shape, BF), ((2,) + shape, BF)],
        (x_all, norm_gains, w_query, w_key, w_value),
        scratch=[
            pltpu.VMEM((nx,) + shape, BF),
        ],
    )
    z13 = permute(z13, "gx", 1)

    def pair_sum(z_ref, from_pair_ref, out_ref):
        total = z_ref[...].astype(F32) + from_pair_ref[1].astype(F32)
        out_ref[...] = total.astype(BF)

    (z2,) = run("pair_sum", pair_sum, [(shape, BF)], (z2, z13))
    z2 = permute(z2, "gx", 2)

    def share_sum(z0_ref, z13_ref, z2_ref, out_ref):
        total = z0_ref[...].astype(F32) + z13_ref[0].astype(F32) + z2_ref[...].astype(F32)
        out_ref[...] = total.reshape(ny, rows, HALF).astype(BF)

    (shares,) = run("share_sum", share_sum, [((ny, rows, HALF), BF)], (z0, z13, z2))
    shares, *late = lax.optimization_barrier((shares, block_table, lengths, parents))
    cos, sin = rope_tables(late[1], rows, steps)
    tables = make_tables(*late, cache_pool.shape[1], rows, steps)
    shares = exchange(shares, "gy")
    beside = tables, cos, sin, w_blocks[2], w_blocks[3], w_first, w_second
    shares, (tables, cos, sin, *_) = lax.optimization_barrier((shares, beside))

    def pack_shares(share_ref, x_ref, out_ref):
        x = x_ref[...].astype(F32)
        out_ref[0:ny] = share_ref[...]
        out_ref[ny] = high_low(row_sum(x * x), HALF).astype(BF)

    (shares,) = run(
        "pack_shares", pack_shares, [((ny + 1, rows, HALF), BF)], (shares, x_own), micros=5
    )
    shares = gather_gx(shares)
    w_blocks[4] = jnp.concatenate([w_first, w_second], axis=0)
    w_late, _ = lax.optimization_barrier((w_blocks[4], shares[2]))
    w_blocks[6] = permute(w_late, "gy", 2)
    w_blocks[5] = permute(w_late, "gy", 1)

    def attention(*refs):
        a_refs, tables, pool_ref, outs = refs[:nx], refs[nx : nx + 4], refs[nx + 4], refs[nx + 5 :]
        own_ref, pair_ref, held, num_held, den_held = outs
        me = my("gx")
        core = me & 1
        for n, ref in enumerate(a_refs):
            held[me ^ n] = ref[...]
        den_held[...] = jnp.zeros(den_held.shape, F32)
        lane = lax.broadcasted_iota(jnp.int32, (2, half, PAGE), 2)

        def store(head, num, den):
            num_held[head] = num.reshape(REPS, 2, half, HEAD_DIM)
            den = high_low(den, PAGE).reshape(REPS, 2, half, PAGE)
            for rep in range(REPS):
                at = REPS * head + rep
                den_held[...] = jnp.where(lane % HALF_PAGE == at, den[rep], den_held[...])
                for n, out in enumerate((own_ref, pair_ref)):
                    for tile in range(2):
                        here = num_held[head, rep, core ^ n, :, tile * PAGE : (tile + 1) * PAGE]
                        out[2 * at + tile] = here.astype(BF)

        attend(
            lambda share, which: held[share, which],
            held[:, ny],
            tables,
            pool_ref,
            store,
        )
        for n, out in enumerate((own_ref, pair_ref)):
            out[2 * HEADS] = den_held[core ^ n].astype(BF)

    shape = (2 * HEADS + 1, half, PAGE)
    own, pair = run(
        "attention",
        attention,
        [(shape, BF), (shape, BF)],
        (*shares, cos, sin, *tables, cache_pool),
        scratch=[
            pltpu.VMEM((nx,) + shares[0].shape, BF),
            pltpu.VMEM((KV_HEADS, REPS, 2, half, HEAD_DIM), F32),
            pltpu.VMEM((2, half, PAGE), F32),
        ],
        limit=24,
    )
    w_late, _ = lax.optimization_barrier((w_blocks, own))
    w_blocks[7] = permute(w_late[6], "gy", 1)
    pair = permute(pair, "gx", 1)

    def pair_terms(own_ref, pair_ref, out_ref):
        total = own_ref[...].astype(F32) + pair_ref[...].astype(F32)
        out_ref[0 : 2 * HEADS] = total[0 : 2 * HEADS].astype(BF)
        den = total[2 * HEADS]
        den = den[:, :HALF_PAGE] + den[:, HALF_PAGE:]
        high = den.astype(BF).astype(F32)
        out_ref[2 * HEADS] = jnp.concatenate([high, den - high], axis=1).astype(BF)

    (own,) = run("pair_terms", pair_terms, [(shape, BF)], (own, pair))
    across = permute(own, "gx", 2)

    def divide(own_ref, across_ref, out_ref):
        total = own_ref[...].astype(F32) + across_ref[...].astype(F32)
        den = total[2 * HEADS]
        den = den[:, :HALF_PAGE] + den[:, HALF_PAGE:]
        for head in range(HEADS):
            scale = 1.0 / den[:, head : head + 1]
            for tile in range(2):
                at = 2 * head + tile
                out_ref[at] = (total[at] * scale).astype(BF)

    (attended,) = run("divide", divide, [((2 * HEADS, half, PAGE), BF)], (own, across))
    others = permute(attended, "gx", 1)

    def project_out(own_ref, other_ref, x_ref, gain_ref, *refs):
        w_refs, (attn_ref, sums_ref, held) = refs[:ny], refs[ny:]
        core = my("gx") & 1
        held[core], held[1 - core] = own_ref[...], other_ref[...]
        me = my("gy")
        attn = jnp.zeros((rows, width), F32)
        for m, w_ref in enumerate(w_refs):
            at = 2 * (me ^ m)
            flat = [jnp.concatenate([held[n, at], held[n, at + 1]], axis=1) for n in range(2)]
            flat = jnp.concatenate(flat, axis=0)
            attn = attn + lax.dot_general(flat, w_ref[...], NT, preferred_element_type=F32)
        attn_ref[...] = attn
        x = x_ref[...].astype(F32)
        scaled = attn * (1.0 + gain_ref[1:2])
        lane = lax.broadcasted_iota(jnp.int32, (rows, PAGE), 1)
        sums = jnp.zeros((rows, PAGE), F32)
        for n, terms in enumerate((attn * attn, scaled * scaled, x * scaled, x * x)):
            sums = jnp.where(lane == n, row_sum(terms), sums)
        sums_ref[...] = sums

    attn, sums = run(
        "project_out",
        project_out,
        [((rows, width), F32), ((rows, PAGE), F32)],
        (attended, others, x_own, norm_gains, *[w_blocks[m] for m in range(ny)]),
        scratch=[pltpu.VMEM((2, 2 * HEADS, half, PAGE), BF)],
    )
    sums = trade([sums] * nx, "gx")

    def mix(*refs):
        attn_ref, x_ref, gain_ref, mixed_ref, ff_ref = refs[nx:]
        total = sum(r[...] for r in refs[:nx])
        plain, scaled, cross, square = (total[:, n : n + 1] for n in range(4))
        scale = lax.rsqrt(plain / D + EPSILON)
        mixed = x_ref[...].astype(F32) + attn_ref[...] * scale * (1.0 + gain_ref[1:2])
        square = jnp.maximum(square + 2.0 * scale * cross + scale * scale * scaled, 0.0)
        mixed_ref[...] = mixed
        scale = lax.rsqrt(square / D + EPSILON)
        ff_input = (mixed * scale * (1.0 + gain_ref[2:3])).astype(BF)
        ff_input = pack_lanes(ff_input)
        for m in range(ny):
            ff_ref[m] = ff_input

    mixed, ff_input = run(
        "mix",
        mix,
        [((rows, width), F32), ((ny, packed, 128), BF)],
        (*sums, attn, x_own, norm_gains),
    )
    ff_input = exchange(ff_input, "gy")

    groups = ny // nx

    cut = hidden // 384 * 256
    column_parts = (0, cut), (cut, hidden)

    def gate_up(start, end):
        def kernel(ff_ref, gate_ref, up_ref, z0_ref, z2_ref, z13_ref):
            me = my("gx")
            flat = [
                unpack_lanes(ff_ref[(me ^ n) * groups + group], rows)
                for n in range(nx)
                for group in range(groups)
            ]
            flat = jnp.concatenate(flat, axis=0)
            for n, w_ref in enumerate((gate_ref, up_ref)):
                sums = jnp.dot(flat, w_ref[:, start:end], preferred_element_type=F32).astype(BF)
                here = pl.ds(n * (end - start), end - start)
                for p, out in enumerate((z0_ref, z13_ref.at[0], z2_ref, z13_ref.at[1])):
                    out[:, here] = sums[p * share_rows : (p + 1) * share_rows]

        shape = (share_rows, 2 * (end - start))
        return run(
            "gate_up",
            kernel,
            [(shape, BF), (shape, BF), ((2,) + shape, BF)],
            (ff_input, w_gate, w_up),
            limit=24,
        )

    def activate(z0_ref, z13_ref, z2_ref, out_ref):
        total = z0_ref[...].astype(F32) + z13_ref[0].astype(F32) + z2_ref[...].astype(F32)
        count = total.shape[1] // 2
        gate, up = total[:, :count], total[:, count:]
        out_ref[...] = (jax.nn.gelu(gate, approximate=True) * up).astype(BF)

    parts = [gate_up(*columns) for columns in column_parts]
    blocks = []
    for z0, z2, z13 in parts:
        shape = z0.shape
        z13 = permute(z13, "gx", 1)
        (z2,) = run("pair_sum_ff", pair_sum, [(shape, BF)], (z2, z13))
        z2 = permute(z2, "gx", 2)
        shape = (share_rows, shape[1] // 2)
        blocks += gather_gx(run("activate", activate, [(shape, BF)], (z0, z13, z2))[0])

    def project_down(*refs):
        w_ref, out_ref = refs[2 * nx :]
        me = my("gx")
        flat = [
            jnp.concatenate([refs[n][...], refs[nx + n][...]], axis=1) for n in range(nx)
        ]
        flat = jnp.concatenate(flat, axis=0)
        sums = lax.dot_general(flat, w_ref[...], NT, preferred_element_type=F32)
        for n in range(nx):
            for group in range(groups):
                at = (n * groups + group) * rows
                block = pack_lanes(sums[at : at + rows].astype(BF))
                out_ref[(me ^ n) * groups + group] = block

    (down,) = run(
        "project_down", project_down, [((ny, packed, 128), BF)], (*blocks, w_down.T)
    )
    down = exchange(down, "gy")

    def down_sum(parts_ref, down_ref, sums_ref):
        down = unpack_lanes(jnp.sum(parts_ref[...].astype(F32), axis=0), rows)
        down_ref[...] = down
        sums_ref[...] = jnp.broadcast_to(row_sum(down * down), (rows, PAGE))

    down, sums = run(
        "down_sum", down_sum, [((rows, width), F32), ((rows, PAGE), F32)], (down,)
    )
    sums = trade([sums] * nx, "gx")

    def finish(*refs):
        down_ref, mixed_ref, gain_ref, out_ref = refs[nx:]
        square = sum(r[...] for r in refs[:nx])[:, 0:1]
        scale = lax.rsqrt(square / D + EPSILON)
        out = mixed_ref[...] + down_ref[...] * scale * (1.0 + gain_ref[3:4])
        out_ref[...] = out.reshape(beams, steps, width).astype(BF)

    (out,) = run("finish", finish, [(inputs.shape, BF)], (*sums, down, mixed, norm_gains))
    return out


def body_general(
    inputs,
    cache_pool,
    lengths,
    block_table,
    parents,
    norm_gains,
    w_query,
    w_key,
    w_value,
    w_out,
    w_gate,
    w_up,
    w_down,
):
    beams, steps, width = inputs.shape
    nx, ny = lax.axis_size("gx"), lax.axis_size("gy")
    rows = beams * steps
    part = rows // nx
    head_part = w_out.shape[0]
    hidden_part = w_gate.shape[1]
    query_part, key_part = w_query.shape[1], w_key.shape[1]
    columns = query_part + 2 * key_part
    share = columns // nx
    x_own = inputs.reshape(rows, width)
    me = lax.axis_index("gx")

    x_all = exchange(jnp.broadcast_to(x_own[None], (ny, rows, width)), "gy")
    flat = (x_all.astype(F32) * (1.0 + norm_gains[0:1])).astype(BF).reshape(ny * rows, width)
    sums = [jnp.dot(flat, w, preferred_element_type=F32) for w in (w_query, w_key, w_value)]
    sums = jnp.concatenate(sums, axis=1).reshape(ny, rows, nx, share)
    received = exchange_all(sums.transpose(2, 0, 1, 3).astype(BF))
    shares = jnp.sum(received.astype(F32), axis=0).astype(BF)
    every = lax.all_gather(shares, "gx", axis=0)
    every = every.transpose(2, 1, 0, 3).reshape(rows, ny, columns)
    q = every[..., :query_part].reshape(rows, HEADS, 2, HALF).transpose(2, 1, 0, 3)
    k, v = (
        every[..., start : start + key_part].reshape(rows, 2 * KV_HEADS, HALF).transpose(1, 0, 2)
        for start in (query_part, query_part + key_part)
    )
    shares = jnp.concatenate([q, k[None], v[None]], axis=0)
    square = lax.psum(row_sum(jnp.square(x_own.astype(F32))), "gx")
    high = lax.reduce_precision(square, 8, 7)
    squares = jnp.where(jnp.arange(HALF) < HALF // 2, high, square - high).astype(BF)[None]
    cos, sin = rope_tables(lengths, rows, steps)

    def attention(*refs):
        g_ref, square_ref, tables, pool_ref, out_ref = refs[0], refs[1], refs[2:6], *refs[6:]

        def store(head, num, den):
            den = high_low(den, PAGE)
            for rep in range(REPS):
                here = slice(rep * rows, (rep + 1) * rows)
                out_ref[REPS * head + rep, :, 0:HEAD_DIM] = num[here].astype(BF)
                out_ref[REPS * head + rep, :, HEAD_DIM:] = den[here].astype(BF)

        attend(
            lambda share, which: g_ref[share, which],
            square_ref[...],
            tables,
            pool_ref,
            store,
        )

    tables = make_tables(block_table, lengths, parents, cache_pool.shape[1], rows, steps)
    (terms,) = run(
        "attention",
        attention,
        [((HEADS, rows, WIDE), BF)],
        (shares, squares, cos, sin, *tables, cache_pool),
        limit=24,
    )
    num = terms[..., :HEAD_DIM].transpose(1, 0, 2).reshape(nx, part, ny, head_part)
    den = terms[..., HEAD_DIM :: PAGE // 2].transpose(1, 0, 2)
    den = jnp.repeat(den, ny // HEADS, axis=1).reshape(nx, part, ny, 2)
    terms = exchange_all(jnp.concatenate([num, den], axis=-1).transpose(0, 2, 1, 3))

    w_wide = lax.all_gather(w_out, "gx", axis=1, tiled=True)
    x_wide = lax.all_gather(x_own, "gx", axis=1, tiled=True)
    x_rows = lax.dynamic_slice_in_dim(x_wide, me * part, part, 0).astype(F32)
    gains = 1.0 + lax.all_gather(norm_gains, "gx", axis=1, tiled=True)

    def scaled(v, gain):
        return v * lax.rsqrt(row_sum(v * v) / D + EPSILON) * gain

    terms = jnp.sum(terms.astype(F32), axis=0)
    den = terms[..., head_part : head_part + 1] + terms[..., -1:]
    attended = (terms[..., :head_part] / den).reshape(ny * part, head_part).astype(BF)
    attn = jnp.dot(attended, w_wide, preferred_element_type=F32).astype(BF)
    attn = exchange(attn.reshape(ny, part, D), "gy").astype(F32).sum(axis=0)
    mixed = x_rows + scaled(attn, gains[1])
    ff_input = scaled(mixed, gains[2]).astype(BF)
    ff_input = ff_input.reshape(part, nx, width).transpose(1, 0, 2)[:, None]
    ff_input = exchange_all(jnp.broadcast_to(ff_input, (nx, ny, part, width)))

    flat = ff_input.reshape(-1, width)
    both = [jnp.dot(flat, w, preferred_element_type=F32).astype(BF) for w in (w_gate, w_up)]
    both = jnp.stack(both, axis=1).reshape(nx, ny * part, 2, hidden_part)
    both = jnp.sum(exchange(both, "gx").astype(F32), axis=0)
    hidden = (jax.nn.gelu(both[:, 0], approximate=True) * both[:, 1]).astype(BF)
    hidden = lax.all_gather(hidden, "gx", axis=0, tiled=True)
    down = jnp.dot(hidden, w_down, preferred_element_type=F32).astype(BF)
    down = exchange_all(down.reshape(nx, ny, part, width)).astype(F32).sum(axis=1)
    down = down.transpose(1, 0, 2).reshape(part, D)
    out = (mixed + scaled(down, gains[3])).astype(BF)
    out = exchange(out.reshape(part, nx, width).transpose(1, 0, 2), "gx")
    return out.reshape(beams, steps, width)


def solution(mesh):
    sizes = dict(mesh.shape)
    fits = sizes["gx"] == 4 and sizes["gy"] == HEADS
    return jax.shard_map(
        body_permutes if fits else body_general,
        mesh=mesh,
        in_specs=(
            P("gy", None, "gx"),
            P(None, "gx", "gy", None),
            P("gy"),
            P("gy", None),
            P(None, "gy"),
            P(None, "gx"),
            P("gx", "gy"),
            P("gx", "gy"),
            P("gx", "gy"),
            P("gy", "gx"),
            P("gx", "gy"),
            P("gx", "gy"),
            P("gy", "gx"),
        ),
        out_specs=P("gy", None, "gx"),
        check_vma=False,
    )
```

```python
import jax
import jax.numpy as jnp
from jax import lax
from jax.experimental import pallas as pl
from jax.experimental.pallas import tpu as pltpu
from jax.sharding import PartitionSpec as P

D = 2304
HEADS = 8
KV_HEADS = 4
HEAD_DIM = 256
HALF = HEAD_DIM // 2
WINDOW = 4096
PAGE = 128
BEAM = 8
EPSILON = 1e-06
SOFT_CAP = 50.0
ROPE_BASE = 10000.0
REPS = HEADS // KV_HEADS
WIDE = HEAD_DIM + PAGE
HALF_PAGE = PAGE // 2
BF = jnp.bfloat16
F32 = jnp.float32
MIB = 1024 * 1024
NT = (((1,), (1,)), ((), ()))
IN_SMEM = pl.BlockSpec(memory_space=pltpu.SMEM)


def run(name, kernel, outs, args, scratch=(), limit=16, specs=None, micros=0):
    cost = pl.CostEstimate(flops=micros * 10**9, bytes_accessed=0, transcendentals=0)
    specs = specs or {}
    vmem = pl.BlockSpec(memory_space=pltpu.VMEM)
    return pl.pallas_call(
        kernel,
        out_shape=[jax.ShapeDtypeStruct(s, d) for s, d in outs],
        in_specs=[specs.get(n, vmem) for n in range(len(args))],
        scratch_shapes=scratch,
        compiler_params=pltpu.CompilerParams(vmem_limit_bytes=limit * MIB),
        cost_estimate=cost if micros else None,
        name=name,
    )(*args)


def exchange(values, axes):
    return lax.all_to_all(values, axes, split_axis=0, concat_axis=0, tiled=True)


def exchange_all(values):
    nx, ny = values.shape[:2]
    flat = values.reshape((nx * ny,) + values.shape[2:])
    return exchange(flat, ("gx", "gy")).reshape(values.shape)


def permute(values, axis, m):
    count = lax.axis_size(axis)
    return lax.ppermute(values, axis, [(i, i ^ m) for i in range(count)])


def trade(blocks, axis):
    return [blocks[0]] + [permute(blocks[m], axis, m) for m in range(1, len(blocks))]


def gather_gx(values):
    across = permute(values, "gx", 2)
    return [values, permute(values, "gx", 1), across, permute(across, "gx", 1)]


def weight_of(scores):
    return jnp.exp(SOFT_CAP * jnp.tanh(scores * (1.0 / SOFT_CAP)))


def high_low(column, lanes):
    shape = column.shape[:-1] + (lanes,)
    high = column.astype(BF).astype(F32)
    lane = lax.broadcasted_iota(jnp.int32, shape, len(shape) - 1)
    return jnp.where(lane < lanes // 2, high, column - high)


def pack_lanes(v):
    rows, width = v.shape
    whole = width // 128 * 128
    tiles = [v[:, c : c + 128] for c in range(0, whole, 128)]
    last = jnp.concatenate([v[: rows // 2, whole:], v[rows // 2 :, whole:]], axis=1)
    return jnp.concatenate(tiles + [last], axis=0)


def unpack_lanes(v, rows):
    whole = v.shape[0] // rows * rows
    tiles = [v[r : r + rows] for r in range(0, whole, rows)]
    last = jnp.concatenate([v[whole:, :64], v[whole:, 64:]], axis=0)
    return jnp.concatenate(tiles + [last], axis=1)


def row_sum(v):
    return jnp.sum(v, axis=-1, keepdims=True)


def make_tables(table, lengths, parents, slots, rows, steps):
    def tables(table_ref, length_ref, parents_ref, cached_ref, own_ref, page_ref):
        first_owner = lax.axis_index("gx") * slots
        length = length_ref[0]
        first_page = jnp.maximum(length - WINDOW + 1, 0) // PAGE
        for slot in range(slots + 1):
            page_ref[slot] = -1
        for j in range(table_ref.shape[1]):
            slot = table_ref[0, j] - first_owner
            page_ref[jnp.where((slot >= 0) & (slot < slots), slot, slots)] = j
        step = lax.broadcasted_iota(jnp.int32, (8, PAGE), 0) % steps
        lane = lax.broadcasted_iota(jnp.int32, (8, PAGE), 1)
        for slot in range(slots):
            page = page_ref[slot]
            position = lane + jnp.where(page >= 0, (first_page + page) * PAGE, 2**30)
            seen = (position < length) & (position >= length + step - (WINDOW - 1))
            cached_ref[:, slot * PAGE : (slot + 1) * PAGE] = jnp.where(seen, 1.0, 0.0)

        shape = (REPS * rows, rows)
        row = lax.broadcasted_iota(jnp.int32, shape, 0) % rows
        column = lax.broadcasted_iota(jnp.int32, shape, 1)
        row_step, column_step, column_beam = row % steps, column % steps, column // steps
        current = row // steps
        visible = jnp.zeros(shape, jnp.bool_)
        for j in range(steps - 1, -1, -1):
            if j < steps - 1:
                parent = jnp.zeros(shape, jnp.int32)
                for beam in range(BEAM):
                    parent = jnp.where(current == beam, parents_ref[j, beam], parent)
                current = jnp.where(row_step > j, parent, current)
            visible = visible | ((column_step == j) & (row_step >= j) & (column_beam == current))
        visible = visible & (lax.axis_index("gx") == 0)
        own_ref[...] = jnp.where(visible, 1.0, 0.0)

    return run(
        "tables",
        tables,
        [((8, slots * PAGE), F32), ((REPS * rows, rows), F32)],
        (table, lengths, parents),
        scratch=[pltpu.SMEM((slots + 1,), jnp.int32)],
        specs={0: IN_SMEM, 1: IN_SMEM, 2: IN_SMEM},
        micros=3,
    )


def attend(shares, squares, tables, pool_ref, store):
    cos_ref, sin_ref, cached_ref, own_ref = tables
    slots = pool_ref.shape[1]
    rows = cos_ref.shape[0]
    square = jnp.sum(squares.astype(F32), axis=0)
    square = square[:, 0:1] + square[:, HALF // 2 : HALF // 2 + 1]
    scale = lax.rsqrt(square / D + EPSILON)
    cos, sin = cos_ref[...] * scale, sin_ref[...] * scale
    cached, own = cached_ref[...], own_ref[...]

    def rotated(u, w):
        u, w = u.astype(F32), w.astype(F32)
        return u * cos - w * sin, w * cos + u * sin

    for head in range(KV_HEADS):
        query = []
        for rep in range(REPS):
            u, w = rotated(shares(0, REPS * head + rep), shares(1, REPS * head + rep))
            query.append(jnp.concatenate([u, w], axis=1) * HEAD_DIM ** (-0.5))
        query = jnp.concatenate(query, axis=0).astype(BF)
        first, second = 2 * head, 2 * head + 1
        key_step = rotated(shares(2, first), shares(2, second))
        key_step = jnp.concatenate(key_step, axis=1).astype(BF)
        value_step = [shares(3, n).astype(F32) * scale for n in (first, second)]
        value_step = jnp.concatenate(value_step, axis=1).astype(BF)

        scores = lax.dot_general(query, key_step, NT, preferred_element_type=F32)
        weights = weight_of(scores) * own
        den = row_sum(weights)
        num = jnp.dot(weights.astype(BF), value_step, preferred_element_type=F32)

        here = slice(head * HEAD_DIM, (head + 1) * HEAD_DIM)
        keys = pool_ref[0, :, :, here].reshape(slots * PAGE, HEAD_DIM)
        values = pool_ref[1, :, :, here].reshape(slots * PAGE, HEAD_DIM)
        scores = lax.dot_general(query, keys, NT, preferred_element_type=F32)
        weights = weight_of(scores).reshape(REPS * rows // 8, 8, slots * PAGE) * cached[None]
        weights = weights.reshape(REPS * rows, slots * PAGE)
        den = den + row_sum(weights)
        num = num + jnp.dot(weights.astype(BF), values, preferred_element_type=F32)
        store(head, num, den)


def rope_tables(lengths, rows, steps):
    positions = lengths[0] + jnp.arange(rows, dtype=jnp.int32) % steps
    inverse_freq = ROPE_BASE ** (-jnp.arange(HALF, dtype=F32) * 2.0 / HEAD_DIM)
    angles = positions[:, None].astype(F32) * inverse_freq
    return jnp.cos(angles), jnp.sin(angles)


def body_permutes(
    inputs,
    cache_pool,
    lengths,
    block_table,
    parents,
    norm_gains,
    w_query,
    w_key,
    w_value,
    w_out,
    w_gate,
    w_up,
    w_down,
):
    beams, steps, width = inputs.shape
    nx, ny = lax.axis_size("gx"), lax.axis_size("gy")
    rows = beams * steps
    half = rows // 2
    all_rows = ny * rows
    share_rows = all_rows // nx
    hidden = w_gate.shape[1]
    packed = rows * width // 128

    def my(axis):
        return lax.axis_index(axis)

    def spread(x_ref, own_ref, out_ref):
        own = x_ref[...].astype(F32).reshape(rows, width).astype(BF)
        own_ref[...] = own
        own = pack_lanes(own)
        for m in range(ny):
            out_ref[m] = own

    x_own, x_all = run(
        "spread", spread, [((rows, width), BF), ((ny, packed, 128), BF)], (inputs,), micros=12
    )
    w_own = w_out.T
    x_all, *late = lax.optimization_barrier((x_all, block_table, lengths, parents))
    tables = make_tables(*late, cache_pool.shape[1], rows, steps)
    x_all = exchange(x_all, "gy")
    x_all, tables = lax.optimization_barrier((x_all, tables))

    w_blocks = {0: w_own, 1: permute(w_own, "gy", 1), 2: permute(w_own, "gy", 2)}
    w_first = permute(w_own[: width // 2], "gy", 4)
    w_late, _ = lax.optimization_barrier(((w_blocks[1], w_own[width // 2 :]), x_all))
    w_blocks[3] = permute(w_late[0], "gy", 2)
    w_second = permute(w_late[1], "gy", 4)

    def project(x_ref, gain_ref, q_ref, k_ref, v_ref, z0_ref, z2_ref, z13_ref, held):
        gain = 1.0 + gain_ref[0:1]
        flat = [
            (unpack_lanes(x_ref[m], rows).astype(F32) * gain).astype(BF) for m in range(ny)
        ]
        flat = jnp.concatenate(flat, axis=0)
        query = jnp.dot(flat, q_ref[...], preferred_element_type=F32).astype(BF)
        held[0], held[1] = query[:, :HALF], query[:, HALF:]
        held[2] = jnp.dot(flat, k_ref[...], preferred_element_type=F32).astype(BF)
        held[3] = jnp.dot(flat, v_ref[...], preferred_element_type=F32).astype(BF)
        me = my("gx")
        z0_ref[...], z2_ref[...] = held[me], held[me ^ 2]
        z13_ref[0], z13_ref[1] = held[me ^ 1], held[me ^ 3]

    shape = (all_rows, HALF)
    z0, z2, z13 = run(
        "project",
        project,
        [(shape, BF), (shape, BF), ((2,) + shape, BF)],
        (x_all, norm_gains, w_query, w_key, w_value),
        scratch=[
            pltpu.VMEM((nx,) + shape, BF),
        ],
    )
    z13 = permute(z13, "gx", 1)

    def pair_sum(z_ref, from_pair_ref, out_ref):
        total = z_ref[...].astype(F32) + from_pair_ref[1].astype(F32)
        out_ref[...] = total.astype(BF)

    (z2,) = run("pair_sum", pair_sum, [(shape, BF)], (z2, z13))
    z2 = permute(z2, "gx", 2)

    def share_sum(z0_ref, z13_ref, z2_ref, out_ref):
        total = z0_ref[...].astype(F32) + z13_ref[0].astype(F32) + z2_ref[...].astype(F32)
        out_ref[...] = total.reshape(ny, rows, HALF).astype(BF)

    (shares,) = run("share_sum", share_sum, [((ny, rows, HALF), BF)], (z0, z13, z2))
    shares, late = lax.optimization_barrier((shares, lengths))
    cos, sin = rope_tables(late, rows, steps)
    halves, _ = lax.optimization_barrier(((w_first, w_second), shares))
    w_blocks[4] = jnp.concatenate(halves, axis=0)
    w_blocks[6] = permute(w_blocks[4], "gy", 2)
    w_blocks[5] = permute(w_blocks[4], "gy", 1)
    shares = exchange(shares, "gy")
    beside = cos, sin, w_blocks[2], w_blocks[3], w_blocks[4]
    shares, (cos, sin, *_) = lax.optimization_barrier((shares, beside))

    def pack_shares(share_ref, x_ref, out_ref):
        x = x_ref[...].astype(F32)
        out_ref[0:ny] = share_ref[...]
        out_ref[ny] = high_low(row_sum(x * x), HALF).astype(BF)

    (shares,) = run(
        "pack_shares", pack_shares, [((ny + 1, rows, HALF), BF)], (shares, x_own), micros=5
    )
    shares = gather_gx(shares)

    def attention(*refs):
        a_refs, tables, pool_ref, outs = refs[:nx], refs[nx : nx + 4], refs[nx + 4], refs[nx + 5 :]
        own_ref, pair_ref, held, num_held, den_held = outs
        me = my("gx")
        core = me & 1
        for n, ref in enumerate(a_refs):
            held[me ^ n] = ref[...]
        den_held[...] = jnp.zeros(den_held.shape, F32)
        lane = lax.broadcasted_iota(jnp.int32, (2, half, PAGE), 2)

        def store(head, num, den):
            num_held[head] = num.reshape(REPS, 2, half, HEAD_DIM)
            den = high_low(den, PAGE).reshape(REPS, 2, half, PAGE)
            for rep in range(REPS):
                at = REPS * head + rep
                den_held[...] = jnp.where(lane % HALF_PAGE == at, den[rep], den_held[...])
                for n, out in enumerate((own_ref, pair_ref)):
                    for tile in range(2):
                        here = num_held[head, rep, core ^ n, :, tile * PAGE : (tile + 1) * PAGE]
                        out[2 * at + tile] = here.astype(BF)

        attend(
            lambda share, which: held[share, which],
            held[:, ny],
            tables,
            pool_ref,
            store,
        )
        for n, out in enumerate((own_ref, pair_ref)):
            out[2 * HEADS] = den_held[core ^ n].astype(BF)

    shape = (2 * HEADS + 1, half, PAGE)
    own, pair = run(
        "attention",
        attention,
        [(shape, BF), (shape, BF)],
        (*shares, cos, sin, *tables, cache_pool),
        scratch=[
            pltpu.VMEM((nx,) + shares[0].shape, BF),
            pltpu.VMEM((KV_HEADS, REPS, 2, half, HEAD_DIM), F32),
            pltpu.VMEM((2, half, PAGE), F32),
        ],
        limit=24,
    )
    w_late, _ = lax.optimization_barrier((w_blocks, own))
    w_blocks[7] = permute(w_late[6], "gy", 1)
    pair = permute(pair, "gx", 1)

    def pair_terms(own_ref, pair_ref, out_ref):
        total = own_ref[...].astype(F32) + pair_ref[...].astype(F32)
        out_ref[0 : 2 * HEADS] = total[0 : 2 * HEADS].astype(BF)
        den = total[2 * HEADS]
        den = den[:, :HALF_PAGE] + den[:, HALF_PAGE:]
        high = den.astype(BF).astype(F32)
        out_ref[2 * HEADS] = jnp.concatenate([high, den - high], axis=1).astype(BF)

    (own,) = run("pair_terms", pair_terms, [(shape, BF)], (own, pair))
    across = permute(own, "gx", 2)

    def divide(own_ref, across_ref, out_ref):
        total = own_ref[...].astype(F32) + across_ref[...].astype(F32)
        den = total[2 * HEADS]
        den = den[:, :HALF_PAGE] + den[:, HALF_PAGE:]
        for head in range(HEADS):
            scale = 1.0 / den[:, head : head + 1]
            for tile in range(2):
                at = 2 * head + tile
                out_ref[at] = (total[at] * scale).astype(BF)

    (attended,) = run("divide", divide, [((2 * HEADS, half, PAGE), BF)], (own, across))
    others = permute(attended, "gx", 1)

    def project_out(own_ref, other_ref, x_ref, gain_ref, *refs):
        w_refs, (attn_ref, sums_ref, held) = refs[:ny], refs[ny:]
        core = my("gx") & 1
        held[core], held[1 - core] = own_ref[...], other_ref[...]
        me = my("gy")
        attn = jnp.zeros((rows, width), F32)
        for m, w_ref in enumerate(w_refs):
            at = 2 * (me ^ m)
            flat = [jnp.concatenate([held[n, at], held[n, at + 1]], axis=1) for n in range(2)]
            flat = jnp.concatenate(flat, axis=0)
            attn = attn + lax.dot_general(flat, w_ref[...], NT, preferred_element_type=F32)
        attn_ref[...] = attn
        x = x_ref[...].astype(F32)
        scaled = attn * (1.0 + gain_ref[1:2])
        lane = lax.broadcasted_iota(jnp.int32, (rows, PAGE), 1)
        sums = jnp.zeros((rows, PAGE), F32)
        for n, terms in enumerate((attn * attn, scaled * scaled, x * scaled, x * x)):
            sums = jnp.where(lane == n, row_sum(terms), sums)
        sums_ref[...] = sums

    attn, sums = run(
        "project_out",
        project_out,
        [((rows, width), F32), ((rows, PAGE), F32)],
        (attended, others, x_own, norm_gains, *[w_blocks[m] for m in range(ny)]),
        scratch=[pltpu.VMEM((2, 2 * HEADS, half, PAGE), BF)],
    )
    sums = trade([sums] * nx, "gx")

    def mix(*refs):
        attn_ref, x_ref, gain_ref, mixed_ref, ff_ref = refs[nx:]
        total = sum(r[...] for r in refs[:nx])
        plain, scaled, cross, square = (total[:, n : n + 1] for n in range(4))
        scale = lax.rsqrt(plain / D + EPSILON)
        mixed = x_ref[...].astype(F32) + attn_ref[...] * scale * (1.0 + gain_ref[1:2])
        square = jnp.maximum(square + 2.0 * scale * cross + scale * scale * scaled, 0.0)
        mixed_ref[...] = mixed
        scale = lax.rsqrt(square / D + EPSILON)
        ff_input = (mixed * scale * (1.0 + gain_ref[2:3])).astype(BF)
        ff_input = pack_lanes(ff_input)
        for m in range(ny):
            ff_ref[m] = ff_input

    mixed, ff_input = run(
        "mix",
        mix,
        [((rows, width), F32), ((ny, packed, 128), BF)],
        (*sums, attn, x_own, norm_gains),
    )
    ff_input = exchange(ff_input, "gy")

    groups = ny // nx

    cut = hidden // 384 * 256
    column_parts = (0, cut), (cut, hidden)

    def gate_up(start, end):
        def kernel(ff_ref, gate_ref, up_ref, z0_ref, z2_ref, z13_ref):
            me = my("gx")
            flat = [
                unpack_lanes(ff_ref[(me ^ n) * groups + group], rows)
                for n in range(nx)
                for group in range(groups)
            ]
            flat = jnp.concatenate(flat, axis=0)
            for n, w_ref in enumerate((gate_ref, up_ref)):
                sums = jnp.dot(flat, w_ref[:, start:end], preferred_element_type=F32).astype(BF)
                here = pl.ds(n * (end - start), end - start)
                for p, out in enumerate((z0_ref, z13_ref.at[0], z2_ref, z13_ref.at[1])):
                    out[:, here] = sums[p * share_rows : (p + 1) * share_rows]

        shape = (share_rows, 2 * (end - start))
        return run(
            "gate_up",
            kernel,
            [(shape, BF), (shape, BF), ((2,) + shape, BF)],
            (ff_input, w_gate, w_up),
            limit=24,
        )

    def activate(z0_ref, z13_ref, z2_ref, out_ref):
        total = z0_ref[...].astype(F32) + z13_ref[0].astype(F32) + z2_ref[...].astype(F32)
        count = total.shape[1] // 2
        gate, up = total[:, :count], total[:, count:]
        out_ref[...] = (jax.nn.gelu(gate, approximate=True) * up).astype(BF)

    parts = [gate_up(*columns) for columns in column_parts]
    blocks = []
    for z0, z2, z13 in parts:
        shape = z0.shape
        z13 = permute(z13, "gx", 1)
        (z2,) = run("pair_sum_ff", pair_sum, [(shape, BF)], (z2, z13))
        z2 = permute(z2, "gx", 2)
        shape = (share_rows, shape[1] // 2)
        blocks += gather_gx(run("activate", activate, [(shape, BF)], (z0, z13, z2))[0])

    def project_down(*refs):
        w_ref, out_ref = refs[2 * nx :]
        me = my("gx")
        flat = [
            jnp.concatenate([refs[n][...], refs[nx + n][...]], axis=1) for n in range(nx)
        ]
        flat = jnp.concatenate(flat, axis=0)
        sums = lax.dot_general(flat, w_ref[...], NT, preferred_element_type=F32)
        for n in range(nx):
            for group in range(groups):
                at = (n * groups + group) * rows
                block = pack_lanes(sums[at : at + rows].astype(BF))
                out_ref[(me ^ n) * groups + group] = block

    (down,) = run(
        "project_down", project_down, [((ny, packed, 128), BF)], (*blocks, w_down.T)
    )
    down = exchange(down, "gy")

    def down_sum(parts_ref, down_ref, sums_ref):
        down = unpack_lanes(jnp.sum(parts_ref[...].astype(F32), axis=0), rows)
        down_ref[...] = down
        sums_ref[...] = jnp.broadcast_to(row_sum(down * down), (rows, PAGE))

    down, sums = run(
        "down_sum", down_sum, [((rows, width), F32), ((rows, PAGE), F32)], (down,)
    )
    sums = trade([sums] * nx, "gx")

    def finish(*refs):
        down_ref, mixed_ref, gain_ref, out_ref = refs[nx:]
        square = sum(r[...] for r in refs[:nx])[:, 0:1]
        scale = lax.rsqrt(square / D + EPSILON)
        out = mixed_ref[...] + down_ref[...] * scale * (1.0 + gain_ref[3:4])
        out_ref[...] = out.reshape(beams, steps, width).astype(BF)

    (out,) = run("finish", finish, [(inputs.shape, BF)], (*sums, down, mixed, norm_gains))
    return out


def body_general(
    inputs,
    cache_pool,
    lengths,
    block_table,
    parents,
    norm_gains,
    w_query,
    w_key,
    w_value,
    w_out,
    w_gate,
    w_up,
    w_down,
):
    beams, steps, width = inputs.shape
    nx, ny = lax.axis_size("gx"), lax.axis_size("gy")
    rows = beams * steps
    part = rows // nx
    head_part = w_out.shape[0]
    hidden_part = w_gate.shape[1]
    query_part, key_part = w_query.shape[1], w_key.shape[1]
    columns = query_part + 2 * key_part
    share = columns // nx
    x_own = inputs.reshape(rows, width)
    me = lax.axis_index("gx")

    x_all = exchange(jnp.broadcast_to(x_own[None], (ny, rows, width)), "gy")
    flat = (x_all.astype(F32) * (1.0 + norm_gains[0:1])).astype(BF).reshape(ny * rows, width)
    sums = [jnp.dot(flat, w, preferred_element_type=F32) for w in (w_query, w_key, w_value)]
    sums = jnp.concatenate(sums, axis=1).reshape(ny, rows, nx, share)
    received = exchange_all(sums.transpose(2, 0, 1, 3).astype(BF))
    shares = jnp.sum(received.astype(F32), axis=0).astype(BF)
    every = lax.all_gather(shares, "gx", axis=0)
    every = every.transpose(2, 1, 0, 3).reshape(rows, ny, columns)
    q = every[..., :query_part].reshape(rows, HEADS, 2, HALF).transpose(2, 1, 0, 3)
    k, v = (
        every[..., start : start + key_part].reshape(rows, 2 * KV_HEADS, HALF).transpose(1, 0, 2)
        for start in (query_part, query_part + key_part)
    )
    shares = jnp.concatenate([q, k[None], v[None]], axis=0)
    square = lax.psum(row_sum(jnp.square(x_own.astype(F32))), "gx")
    high = lax.reduce_precision(square, 8, 7)
    squares = jnp.where(jnp.arange(HALF) < HALF // 2, high, square - high).astype(BF)[None]
    cos, sin = rope_tables(lengths, rows, steps)

    def attention(*refs):
        g_ref, square_ref, tables, pool_ref, out_ref = refs[0], refs[1], refs[2:6], *refs[6:]

        def store(head, num, den):
            den = high_low(den, PAGE)
            for rep in range(REPS):
                here = slice(rep * rows, (rep + 1) * rows)
                out_ref[REPS * head + rep, :, 0:HEAD_DIM] = num[here].astype(BF)
                out_ref[REPS * head + rep, :, HEAD_DIM:] = den[here].astype(BF)

        attend(
            lambda share, which: g_ref[share, which],
            square_ref[...],
            tables,
            pool_ref,
            store,
        )

    tables = make_tables(block_table, lengths, parents, cache_pool.shape[1], rows, steps)
    (terms,) = run(
        "attention",
        attention,
        [((HEADS, rows, WIDE), BF)],
        (shares, squares, cos, sin, *tables, cache_pool),
        limit=24,
    )
    num = terms[..., :HEAD_DIM].transpose(1, 0, 2).reshape(nx, part, ny, head_part)
    den = terms[..., HEAD_DIM :: PAGE // 2].transpose(1, 0, 2)
    den = jnp.repeat(den, ny // HEADS, axis=1).reshape(nx, part, ny, 2)
    terms = exchange_all(jnp.concatenate([num, den], axis=-1).transpose(0, 2, 1, 3))

    w_wide = lax.all_gather(w_out, "gx", axis=1, tiled=True)
    x_wide = lax.all_gather(x_own, "gx", axis=1, tiled=True)
    x_rows = lax.dynamic_slice_in_dim(x_wide, me * part, part, 0).astype(F32)
    gains = 1.0 + lax.all_gather(norm_gains, "gx", axis=1, tiled=True)

    def scaled(v, gain):
        return v * lax.rsqrt(row_sum(v * v) / D + EPSILON) * gain

    terms = jnp.sum(terms.astype(F32), axis=0)
    den = terms[..., head_part : head_part + 1] + terms[..., -1:]
    attended = (terms[..., :head_part] / den).reshape(ny * part, head_part).astype(BF)
    attn = jnp.dot(attended, w_wide, preferred_element_type=F32).astype(BF)
    attn = exchange(attn.reshape(ny, part, D), "gy").astype(F32).sum(axis=0)
    mixed = x_rows + scaled(attn, gains[1])
    ff_input = scaled(mixed, gains[2]).astype(BF)
    ff_input = ff_input.reshape(part, nx, width).transpose(1, 0, 2)[:, None]
    ff_input = exchange_all(jnp.broadcast_to(ff_input, (nx, ny, part, width)))

    flat = ff_input.reshape(-1, width)
    both = [jnp.dot(flat, w, preferred_element_type=F32).astype(BF) for w in (w_gate, w_up)]
    both = jnp.stack(both, axis=1).reshape(nx, ny * part, 2, hidden_part)
    both = jnp.sum(exchange(both, "gx").astype(F32), axis=0)
    hidden = (jax.nn.gelu(both[:, 0], approximate=True) * both[:, 1]).astype(BF)
    hidden = lax.all_gather(hidden, "gx", axis=0, tiled=True)
    down = jnp.dot(hidden, w_down, preferred_element_type=F32).astype(BF)
    down = exchange_all(down.reshape(nx, ny, part, width)).astype(F32).sum(axis=1)
    down = down.transpose(1, 0, 2).reshape(part, D)
    out = (mixed + scaled(down, gains[3])).astype(BF)
    out = exchange(out.reshape(part, nx, width).transpose(1, 0, 2), "gx")
    return out.reshape(beams, steps, width)


def solution(mesh):
    sizes = dict(mesh.shape)
    fits = sizes["gx"] == 4 and sizes["gy"] == HEADS
    return jax.shard_map(
        body_permutes if fits else body_general,
        mesh=mesh,
        in_specs=(
            P("gy", None, "gx"),
            P(None, "gx", "gy", None),
            P("gy"),
            P("gy", None),
            P(None, "gy"),
            P(None, "gx"),
            P("gx", "gy"),
            P("gx", "gy"),
            P("gx", "gy"),
            P("gy", "gx"),
            P("gx", "gy"),
            P("gx", "gy"),
            P("gy", "gx"),
        ),
        out_specs=P("gy", None, "gx"),
        check_vma=False,
    )
```

```python
import jax
import jax.numpy as jnp
from jax import lax
from jax.experimental import pallas as pl
from jax.experimental.pallas import tpu as pltpu
from jax.sharding import PartitionSpec as P

D = 2304
HEADS = 8
KV_HEADS = 4
HEAD_DIM = 256
HALF = HEAD_DIM // 2
WINDOW = 4096
PAGE = 128
BEAM = 8
EPSILON = 1e-06
SOFT_CAP = 50.0
ROPE_BASE = 10000.0
REPS = HEADS // KV_HEADS
WIDE = HEAD_DIM + PAGE
HALF_PAGE = PAGE // 2
BF = jnp.bfloat16
F32 = jnp.float32
MIB = 1024 * 1024
NT = (((1,), (1,)), ((), ()))
IN_SMEM = pl.BlockSpec(memory_space=pltpu.SMEM)


def run(name, kernel, outs, args, scratch=(), limit=16, specs=None, micros=0):
    cost = pl.CostEstimate(flops=micros * 10**9, bytes_accessed=0, transcendentals=0)
    specs = specs or {}
    vmem = pl.BlockSpec(memory_space=pltpu.VMEM)
    return pl.pallas_call(
        kernel,
        out_shape=[jax.ShapeDtypeStruct(s, d) for s, d in outs],
        in_specs=[specs.get(n, vmem) for n in range(len(args))],
        scratch_shapes=scratch,
        compiler_params=pltpu.CompilerParams(vmem_limit_bytes=limit * MIB),
        cost_estimate=cost if micros else None,
        name=name,
    )(*args)


def exchange(values, axes):
    return lax.all_to_all(values, axes, split_axis=0, concat_axis=0, tiled=True)


def exchange_all(values):
    nx, ny = values.shape[:2]
    flat = values.reshape((nx * ny,) + values.shape[2:])
    return exchange(flat, ("gx", "gy")).reshape(values.shape)


def permute(values, axis, m):
    count = lax.axis_size(axis)
    return lax.ppermute(values, axis, [(i, i ^ m) for i in range(count)])


def trade(blocks, axis):
    return [blocks[0]] + [permute(blocks[m], axis, m) for m in range(1, len(blocks))]


def gather_gx(values):
    across = permute(values, "gx", 2)
    return [values, permute(values, "gx", 1), across, permute(across, "gx", 1)]


def weight_of(scores):
    return jnp.exp(SOFT_CAP * jnp.tanh(scores * (1.0 / SOFT_CAP)))


def high_low(column, lanes):
    shape = column.shape[:-1] + (lanes,)
    high = column.astype(BF).astype(F32)
    lane = lax.broadcasted_iota(jnp.int32, shape, len(shape) - 1)
    return jnp.where(lane < lanes // 2, high, column - high)


def pack_lanes(v):
    rows, width = v.shape
    whole = width // 128 * 128
    tiles = [v[:, c : c + 128] for c in range(0, whole, 128)]
    last = jnp.concatenate([v[: rows // 2, whole:], v[rows // 2 :, whole:]], axis=1)
    return jnp.concatenate(tiles + [last], axis=0)


def unpack_lanes(v, rows):
    whole = v.shape[0] // rows * rows
    tiles = [v[r : r + rows] for r in range(0, whole, rows)]
    last = jnp.concatenate([v[whole:, :64], v[whole:, 64:]], axis=0)
    return jnp.concatenate(tiles + [last], axis=1)


def row_sum(v):
    return jnp.sum(v, axis=-1, keepdims=True)


def make_tables(table, lengths, parents, slots, rows, steps):
    def tables(table_ref, length_ref, parents_ref, cached_ref, own_ref, page_ref):
        first_owner = lax.axis_index("gx") * slots
        length = length_ref[0]
        first_page = jnp.maximum(length - WINDOW + 1, 0) // PAGE
        for slot in range(slots + 1):
            page_ref[slot] = -1
        for j in range(table_ref.shape[1]):
            slot = table_ref[0, j] - first_owner
            page_ref[jnp.where((slot >= 0) & (slot < slots), slot, slots)] = j
        step = lax.broadcasted_iota(jnp.int32, (8, PAGE), 0) % steps
        lane = lax.broadcasted_iota(jnp.int32, (8, PAGE), 1)
        for slot in range(slots):
            page = page_ref[slot]
            position = lane + jnp.where(page >= 0, (first_page + page) * PAGE, 2**30)
            seen = (position < length) & (position >= length + step - (WINDOW - 1))
            cached_ref[:, slot * PAGE : (slot + 1) * PAGE] = jnp.where(seen, 1.0, 0.0)

        shape = (REPS * rows, rows)
        row = lax.broadcasted_iota(jnp.int32, shape, 0) % rows
        column = lax.broadcasted_iota(jnp.int32, shape, 1)
        row_step, column_step, column_beam = row % steps, column % steps, column // steps
        current = row // steps
        visible = jnp.zeros(shape, jnp.bool_)
        for j in range(steps - 1, -1, -1):
            if j < steps - 1:
                parent = jnp.zeros(shape, jnp.int32)
                for beam in range(BEAM):
                    parent = jnp.where(current == beam, parents_ref[j, beam], parent)
                current = jnp.where(row_step > j, parent, current)
            visible = visible | ((column_step == j) & (row_step >= j) & (column_beam == current))
        visible = visible & (lax.axis_index("gx") == 0)
        own_ref[...] = jnp.where(visible, 1.0, 0.0)

    return run(
        "tables",
        tables,
        [((8, slots * PAGE), F32), ((REPS * rows, rows), F32)],
        (table, lengths, parents),
        scratch=[pltpu.SMEM((slots + 1,), jnp.int32)],
        specs={0: IN_SMEM, 1: IN_SMEM, 2: IN_SMEM},
    )


def attend(shares, squares, tables, pool_ref, store):
    cos_ref, sin_ref, cached_ref, own_ref = tables
    slots = pool_ref.shape[1]
    rows = cos_ref.shape[0]
    square = jnp.sum(squares.astype(F32), axis=0)
    square = square[:, 0:1] + square[:, HALF // 2 : HALF // 2 + 1]
    scale = lax.rsqrt(square / D + EPSILON)
    cos, sin = cos_ref[...] * scale, sin_ref[...] * scale
    cached, own = cached_ref[...], own_ref[...]

    def rotated(u, w):
        u, w = u.astype(F32), w.astype(F32)
        return u * cos - w * sin, w * cos + u * sin

    for head in range(KV_HEADS):
        query = []
        for rep in range(REPS):
            u, w = rotated(shares(0, REPS * head + rep), shares(1, REPS * head + rep))
            query.append(jnp.concatenate([u, w], axis=1) * HEAD_DIM ** (-0.5))
        query = jnp.concatenate(query, axis=0).astype(BF)
        first, second = 2 * head, 2 * head + 1
        key_step = rotated(shares(2, first), shares(2, second))
        key_step = jnp.concatenate(key_step, axis=1).astype(BF)
        value_step = [shares(3, n).astype(F32) * scale for n in (first, second)]
        value_step = jnp.concatenate(value_step, axis=1).astype(BF)

        scores = lax.dot_general(query, key_step, NT, preferred_element_type=F32)
        weights = weight_of(scores) * own
        den = row_sum(weights)
        num = jnp.dot(weights.astype(BF), value_step, preferred_element_type=F32)

        here = slice(head * HEAD_DIM, (head + 1) * HEAD_DIM)
        keys = pool_ref[0, :, :, here].reshape(slots * PAGE, HEAD_DIM)
        values = pool_ref[1, :, :, here].reshape(slots * PAGE, HEAD_DIM)
        scores = lax.dot_general(query, keys, NT, preferred_element_type=F32)
        weights = weight_of(scores).reshape(REPS * rows // 8, 8, slots * PAGE) * cached[None]
        weights = weights.reshape(REPS * rows, slots * PAGE)
        den = den + row_sum(weights)
        num = num + jnp.dot(weights.astype(BF), values, preferred_element_type=F32)
        store(head, num, den)


def rope_tables(lengths, rows, steps):
    positions = lengths[0] + jnp.arange(rows, dtype=jnp.int32) % steps
    inverse_freq = ROPE_BASE ** (-jnp.arange(HALF, dtype=F32) * 2.0 / HEAD_DIM)
    angles = positions[:, None].astype(F32) * inverse_freq
    return jnp.cos(angles), jnp.sin(angles)


def body_permutes(
    inputs,
    cache_pool,
    lengths,
    block_table,
    parents,
    norm_gains,
    w_query,
    w_key,
    w_value,
    w_out,
    w_gate,
    w_up,
    w_down,
):
    beams, steps, width = inputs.shape
    nx, ny = lax.axis_size("gx"), lax.axis_size("gy")
    rows = beams * steps
    half = rows // 2
    all_rows = ny * rows
    share_rows = all_rows // nx
    hidden = w_gate.shape[1]
    packed = rows * width // 128

    def my(axis):
        return lax.axis_index(axis)

    def spread(x_ref, own_ref, out_ref):
        own = x_ref[...].astype(F32).reshape(rows, width).astype(BF)
        own_ref[...] = own
        own = pack_lanes(own)
        for m in range(ny):
            out_ref[m] = own

    x_own, x_all = run(
        "spread", spread, [((rows, width), BF), ((ny, packed, 128), BF)], (inputs,), micros=12
    )
    w_own = w_out.T
    x_all, w_split = lax.optimization_barrier((x_all, w_own))
    x_all = exchange(x_all, "gy")

    w_blocks = {0: w_own, 1: permute(w_own, "gy", 1), 2: permute(w_own, "gy", 2)}
    w_first = permute(w_split[: width // 2], "gy", 4)
    w_late, _ = lax.optimization_barrier(((w_blocks[1], w_split[width // 2 :]), x_all))
    w_blocks[3] = permute(w_late[0], "gy", 2)
    w_second = permute(w_late[1], "gy", 4)

    def project(x_ref, gain_ref, q_ref, k_ref, v_ref, z0_ref, z2_ref, z13_ref, held):
        gain = 1.0 + gain_ref[0:1]
        flat = [
            (unpack_lanes(x_ref[m], rows).astype(F32) * gain).astype(BF) for m in range(ny)
        ]
        flat = jnp.concatenate(flat, axis=0)
        query = jnp.dot(flat, q_ref[...], preferred_element_type=F32).astype(BF)
        held[0], held[1] = query[:, :HALF], query[:, HALF:]
        held[2] = jnp.dot(flat, k_ref[...], preferred_element_type=F32).astype(BF)
        held[3] = jnp.dot(flat, v_ref[...], preferred_element_type=F32).astype(BF)
        me = my("gx")
        z0_ref[...], z2_ref[...] = held[me], held[me ^ 2]
        z13_ref[0], z13_ref[1] = held[me ^ 1], held[me ^ 3]

    shape = (all_rows, HALF)
    z0, z2, z13 = run(
        "project",
        project,
        [(shape, BF), (shape, BF), ((2,) + shape, BF)],
        (x_all, norm_gains, w_query, w_key, w_value),
        scratch=[
            pltpu.VMEM((nx,) + shape, BF),
        ],
    )
    z13 = permute(z13, "gx", 1)

    def pair_sum(z_ref, from_pair_ref, out_ref):
        total = z_ref[...].astype(F32) + from_pair_ref[1].astype(F32)
        out_ref[...] = total.astype(BF)

    (z2,) = run("pair_sum", pair_sum, [(shape, BF)], (z2, z13))
    z2 = permute(z2, "gx", 2)

    def share_sum(z0_ref, z13_ref, z2_ref, out_ref):
        total = z0_ref[...].astype(F32) + z13_ref[0].astype(F32) + z2_ref[...].astype(F32)
        out_ref[...] = total.reshape(ny, rows, HALF).astype(BF)

    (shares,) = run("share_sum", share_sum, [((ny, rows, HALF), BF)], (z0, z13, z2))
    shares, *late = lax.optimization_barrier((shares, block_table, lengths, parents))
    cos, sin = rope_tables(late[1], rows, steps)
    tables = make_tables(*late, cache_pool.shape[1], rows, steps)
    halves, _ = lax.optimization_barrier(((w_first, w_second), shares))
    w_blocks[4] = jnp.concatenate(halves, axis=0)
    w_blocks[6] = permute(w_blocks[4], "gy", 2)
    w_blocks[5] = permute(w_blocks[4], "gy", 1)
    shares = exchange(shares, "gy")
    beside = tables, cos, sin, w_blocks[2], w_blocks[3], w_blocks[4]
    shares, (tables, cos, sin, *_) = lax.optimization_barrier((shares, beside))

    def pack_shares(share_ref, x_ref, out_ref):
        x = x_ref[...].astype(F32)
        out_ref[0:ny] = share_ref[...]
        out_ref[ny] = high_low(row_sum(x * x), HALF).astype(BF)

    (shares,) = run(
        "pack_shares", pack_shares, [((ny + 1, rows, HALF), BF)], (shares, x_own), micros=5
    )
    shares = gather_gx(shares)

    def attention(*refs):
        a_refs, tables, pool_ref, outs = refs[:nx], refs[nx : nx + 4], refs[nx + 4], refs[nx + 5 :]
        own_ref, pair_ref, held, num_held, den_held = outs
        me = my("gx")
        core = me & 1
        for n, ref in enumerate(a_refs):
            held[me ^ n] = ref[...]
        den_held[...] = jnp.zeros(den_held.shape, F32)
        lane = lax.broadcasted_iota(jnp.int32, (2, half, PAGE), 2)

        def store(head, num, den):
            num_held[head] = num.reshape(REPS, 2, half, HEAD_DIM)
            den = high_low(den, PAGE).reshape(REPS, 2, half, PAGE)
            for rep in range(REPS):
                at = REPS * head + rep
                den_held[...] = jnp.where(lane % HALF_PAGE == at, den[rep], den_held[...])
                for n, out in enumerate((own_ref, pair_ref)):
                    for tile in range(2):
                        here = num_held[head, rep, core ^ n, :, tile * PAGE : (tile + 1) * PAGE]
                        out[2 * at + tile] = here.astype(BF)

        attend(
            lambda share, which: held[share, which],
            held[:, ny],
            tables,
            pool_ref,
            store,
        )
        for n, out in enumerate((own_ref, pair_ref)):
            out[2 * HEADS] = den_held[core ^ n].astype(BF)

    shape = (2 * HEADS + 1, half, PAGE)
    own, pair = run(
        "attention",
        attention,
        [(shape, BF), (shape, BF)],
        (*shares, cos, sin, *tables, cache_pool),
        scratch=[
            pltpu.VMEM((nx,) + shares[0].shape, BF),
            pltpu.VMEM((KV_HEADS, REPS, 2, half, HEAD_DIM), F32),
            pltpu.VMEM((2, half, PAGE), F32),
        ],
        limit=24,
    )
    w_late, _ = lax.optimization_barrier((w_blocks, own))
    w_blocks[7] = permute(w_late[6], "gy", 1)
    pair = permute(pair, "gx", 1)

    def pair_terms(own_ref, pair_ref, out_ref):
        total = own_ref[...].astype(F32) + pair_ref[...].astype(F32)
        out_ref[0 : 2 * HEADS] = total[0 : 2 * HEADS].astype(BF)
        den = total[2 * HEADS]
        den = den[:, :HALF_PAGE] + den[:, HALF_PAGE:]
        high = den.astype(BF).astype(F32)
        out_ref[2 * HEADS] = jnp.concatenate([high, den - high], axis=1).astype(BF)

    (own,) = run("pair_terms", pair_terms, [(shape, BF)], (own, pair))
    across = permute(own, "gx", 2)

    def divide(own_ref, across_ref, out_ref):
        total = own_ref[...].astype(F32) + across_ref[...].astype(F32)
        den = total[2 * HEADS]
        den = den[:, :HALF_PAGE] + den[:, HALF_PAGE:]
        for head in range(HEADS):
            scale = 1.0 / den[:, head : head + 1]
            for tile in range(2):
                at = 2 * head + tile
                out_ref[at] = (total[at] * scale).astype(BF)

    (attended,) = run("divide", divide, [((2 * HEADS, half, PAGE), BF)], (own, across))
    others = permute(attended, "gx", 1)

    def project_out(own_ref, other_ref, x_ref, gain_ref, *refs):
        w_refs, (attn_ref, sums_ref, held) = refs[:ny], refs[ny:]
        core = my("gx") & 1
        held[core], held[1 - core] = own_ref[...], other_ref[...]
        me = my("gy")
        attn = jnp.zeros((rows, width), F32)
        for m, w_ref in enumerate(w_refs):
            at = 2 * (me ^ m)
            flat = [jnp.concatenate([held[n, at], held[n, at + 1]], axis=1) for n in range(2)]
            flat = jnp.concatenate(flat, axis=0)
            attn = attn + lax.dot_general(flat, w_ref[...], NT, preferred_element_type=F32)
        attn_ref[...] = attn
        x = x_ref[...].astype(F32)
        scaled = attn * (1.0 + gain_ref[1:2])
        lane = lax.broadcasted_iota(jnp.int32, (rows, PAGE), 1)
        sums = jnp.zeros((rows, PAGE), F32)
        for n, terms in enumerate((attn * attn, scaled * scaled, x * scaled, x * x)):
            sums = jnp.where(lane == n, row_sum(terms), sums)
        sums_ref[...] = sums

    attn, sums = run(
        "project_out",
        project_out,
        [((rows, width), F32), ((rows, PAGE), F32)],
        (attended, others, x_own, norm_gains, *[w_blocks[m] for m in range(ny)]),
        scratch=[pltpu.VMEM((2, 2 * HEADS, half, PAGE), BF)],
    )
    sums = trade([sums] * nx, "gx")

    def mix(*refs):
        attn_ref, x_ref, gain_ref, mixed_ref, ff_ref = refs[nx:]
        total = sum(r[...] for r in refs[:nx])
        plain, scaled, cross, square = (total[:, n : n + 1] for n in range(4))
        scale = lax.rsqrt(plain / D + EPSILON)
        mixed = x_ref[...].astype(F32) + attn_ref[...] * scale * (1.0 + gain_ref[1:2])
        square = jnp.maximum(square + 2.0 * scale * cross + scale * scale * scaled, 0.0)
        mixed_ref[...] = mixed
        scale = lax.rsqrt(square / D + EPSILON)
        ff_input = (mixed * scale * (1.0 + gain_ref[2:3])).astype(BF)
        ff_input = pack_lanes(ff_input)
        for m in range(ny):
            ff_ref[m] = ff_input

    mixed, ff_input = run(
        "mix",
        mix,
        [((rows, width), F32), ((ny, packed, 128), BF)],
        (*sums, attn, x_own, norm_gains),
    )
    ff_input = exchange(ff_input, "gy")

    groups = ny // nx

    cut = hidden // 384 * 256
    column_parts = (0, cut), (cut, hidden)

    def gate_up(start, end):
        def kernel(ff_ref, gate_ref, up_ref, z0_ref, z2_ref, z13_ref):
            me = my("gx")
            flat = [
                unpack_lanes(ff_ref[(me ^ n) * groups + group], rows)
                for n in range(nx)
                for group in range(groups)
            ]
            flat = jnp.concatenate(flat, axis=0)
            for n, w_ref in enumerate((gate_ref, up_ref)):
                sums = jnp.dot(flat, w_ref[:, start:end], preferred_element_type=F32).astype(BF)
                here = pl.ds(n * (end - start), end - start)
                for p, out in enumerate((z0_ref, z13_ref.at[0], z2_ref, z13_ref.at[1])):
                    out[:, here] = sums[p * share_rows : (p + 1) * share_rows]

        shape = (share_rows, 2 * (end - start))
        return run(
            "gate_up",
            kernel,
            [(shape, BF), (shape, BF), ((2,) + shape, BF)],
            (ff_input, w_gate, w_up),
            limit=24,
        )

    def activate(z0_ref, z13_ref, z2_ref, out_ref):
        total = z0_ref[...].astype(F32) + z13_ref[0].astype(F32) + z2_ref[...].astype(F32)
        count = total.shape[1] // 2
        gate, up = total[:, :count], total[:, count:]
        out_ref[...] = (jax.nn.gelu(gate, approximate=True) * up).astype(BF)

    parts = [gate_up(*columns) for columns in column_parts]
    blocks = []
    for z0, z2, z13 in parts:
        shape = z0.shape
        z13 = permute(z13, "gx", 1)
        (z2,) = run("pair_sum_ff", pair_sum, [(shape, BF)], (z2, z13))
        z2 = permute(z2, "gx", 2)
        shape = (share_rows, shape[1] // 2)
        blocks += gather_gx(run("activate", activate, [(shape, BF)], (z0, z13, z2))[0])

    def project_down(*refs):
        w_ref, out_ref = refs[2 * nx :]
        me = my("gx")
        flat = [
            jnp.concatenate([refs[n][...], refs[nx + n][...]], axis=1) for n in range(nx)
        ]
        flat = jnp.concatenate(flat, axis=0)
        sums = lax.dot_general(flat, w_ref[...], NT, preferred_element_type=F32)
        for n in range(nx):
            for group in range(groups):
                at = (n * groups + group) * rows
                block = pack_lanes(sums[at : at + rows].astype(BF))
                out_ref[(me ^ n) * groups + group] = block

    (down,) = run(
        "project_down", project_down, [((ny, packed, 128), BF)], (*blocks, w_down.T)
    )
    down = exchange(down, "gy")

    def down_sum(parts_ref, down_ref, sums_ref):
        down = unpack_lanes(jnp.sum(parts_ref[...].astype(F32), axis=0), rows)
        down_ref[...] = down
        sums_ref[...] = jnp.broadcast_to(row_sum(down * down), (rows, PAGE))

    down, sums = run(
        "down_sum", down_sum, [((rows, width), F32), ((rows, PAGE), F32)], (down,)
    )
    sums = trade([sums] * nx, "gx")

    def finish(*refs):
        down_ref, mixed_ref, gain_ref, out_ref = refs[nx:]
        square = sum(r[...] for r in refs[:nx])[:, 0:1]
        scale = lax.rsqrt(square / D + EPSILON)
        out = mixed_ref[...] + down_ref[...] * scale * (1.0 + gain_ref[3:4])
        out_ref[...] = out.reshape(beams, steps, width).astype(BF)

    (out,) = run("finish", finish, [(inputs.shape, BF)], (*sums, down, mixed, norm_gains))
    return out


def body_general(
    inputs,
    cache_pool,
    lengths,
    block_table,
    parents,
    norm_gains,
    w_query,
    w_key,
    w_value,
    w_out,
    w_gate,
    w_up,
    w_down,
):
    beams, steps, width = inputs.shape
    nx, ny = lax.axis_size("gx"), lax.axis_size("gy")
    rows = beams * steps
    part = rows // nx
    head_part = w_out.shape[0]
    hidden_part = w_gate.shape[1]
    query_part, key_part = w_query.shape[1], w_key.shape[1]
    columns = query_part + 2 * key_part
    share = columns // nx
    x_own = inputs.reshape(rows, width)
    me = lax.axis_index("gx")

    x_all = exchange(jnp.broadcast_to(x_own[None], (ny, rows, width)), "gy")
    flat = (x_all.astype(F32) * (1.0 + norm_gains[0:1])).astype(BF).reshape(ny * rows, width)
    sums = [jnp.dot(flat, w, preferred_element_type=F32) for w in (w_query, w_key, w_value)]
    sums = jnp.concatenate(sums, axis=1).reshape(ny, rows, nx, share)
    received = exchange_all(sums.transpose(2, 0, 1, 3).astype(BF))
    shares = jnp.sum(received.astype(F32), axis=0).astype(BF)
    every = lax.all_gather(shares, "gx", axis=0)
    every = every.transpose(2, 1, 0, 3).reshape(rows, ny, columns)
    q = every[..., :query_part].reshape(rows, HEADS, 2, HALF).transpose(2, 1, 0, 3)
    k, v = (
        every[..., start : start + key_part].reshape(rows, 2 * KV_HEADS, HALF).transpose(1, 0, 2)
        for start in (query_part, query_part + key_part)
    )
    shares = jnp.concatenate([q, k[None], v[None]], axis=0)
    square = lax.psum(row_sum(jnp.square(x_own.astype(F32))), "gx")
    high = lax.reduce_precision(square, 8, 7)
    squares = jnp.where(jnp.arange(HALF) < HALF // 2, high, square - high).astype(BF)[None]
    cos, sin = rope_tables(lengths, rows, steps)

    def attention(*refs):
        g_ref, square_ref, tables, pool_ref, out_ref = refs[0], refs[1], refs[2:6], *refs[6:]

        def store(head, num, den):
            den = high_low(den, PAGE)
            for rep in range(REPS):
                here = slice(rep * rows, (rep + 1) * rows)
                out_ref[REPS * head + rep, :, 0:HEAD_DIM] = num[here].astype(BF)
                out_ref[REPS * head + rep, :, HEAD_DIM:] = den[here].astype(BF)

        attend(
            lambda share, which: g_ref[share, which],
            square_ref[...],
            tables,
            pool_ref,
            store,
        )

    tables = make_tables(block_table, lengths, parents, cache_pool.shape[1], rows, steps)
    (terms,) = run(
        "attention",
        attention,
        [((HEADS, rows, WIDE), BF)],
        (shares, squares, cos, sin, *tables, cache_pool),
        limit=24,
    )
    num = terms[..., :HEAD_DIM].transpose(1, 0, 2).reshape(nx, part, ny, head_part)
    den = terms[..., HEAD_DIM :: PAGE // 2].transpose(1, 0, 2)
    den = jnp.repeat(den, ny // HEADS, axis=1).reshape(nx, part, ny, 2)
    terms = exchange_all(jnp.concatenate([num, den], axis=-1).transpose(0, 2, 1, 3))

    w_wide = lax.all_gather(w_out, "gx", axis=1, tiled=True)
    x_wide = lax.all_gather(x_own, "gx", axis=1, tiled=True)
    x_rows = lax.dynamic_slice_in_dim(x_wide, me * part, part, 0).astype(F32)
    gains = 1.0 + lax.all_gather(norm_gains, "gx", axis=1, tiled=True)

    def scaled(v, gain):
        return v * lax.rsqrt(row_sum(v * v) / D + EPSILON) * gain

    terms = jnp.sum(terms.astype(F32), axis=0)
    den = terms[..., head_part : head_part + 1] + terms[..., -1:]
    attended = (terms[..., :head_part] / den).reshape(ny * part, head_part).astype(BF)
    attn = jnp.dot(attended, w_wide, preferred_element_type=F32).astype(BF)
    attn = exchange(attn.reshape(ny, part, D), "gy").astype(F32).sum(axis=0)
    mixed = x_rows + scaled(attn, gains[1])
    ff_input = scaled(mixed, gains[2]).astype(BF)
    ff_input = ff_input.reshape(part, nx, width).transpose(1, 0, 2)[:, None]
    ff_input = exchange_all(jnp.broadcast_to(ff_input, (nx, ny, part, width)))

    flat = ff_input.reshape(-1, width)
    both = [jnp.dot(flat, w, preferred_element_type=F32).astype(BF) for w in (w_gate, w_up)]
    both = jnp.stack(both, axis=1).reshape(nx, ny * part, 2, hidden_part)
    both = jnp.sum(exchange(both, "gx").astype(F32), axis=0)
    hidden = (jax.nn.gelu(both[:, 0], approximate=True) * both[:, 1]).astype(BF)
    hidden = lax.all_gather(hidden, "gx", axis=0, tiled=True)
    down = jnp.dot(hidden, w_down, preferred_element_type=F32).astype(BF)
    down = exchange_all(down.reshape(nx, ny, part, width)).astype(F32).sum(axis=1)
    down = down.transpose(1, 0, 2).reshape(part, D)
    out = (mixed + scaled(down, gains[3])).astype(BF)
    out = exchange(out.reshape(part, nx, width).transpose(1, 0, 2), "gx")
    return out.reshape(beams, steps, width)


def solution(mesh):
    sizes = dict(mesh.shape)
    fits = sizes["gx"] == 4 and sizes["gy"] == HEADS
    return jax.shard_map(
        body_permutes if fits else body_general,
        mesh=mesh,
        in_specs=(
            P("gy", None, "gx"),
            P(None, "gx", "gy", None),
            P("gy"),
            P("gy", None),
            P(None, "gy"),
            P(None, "gx"),
            P("gx", "gy"),
            P("gx", "gy"),
            P("gx", "gy"),
            P("gy", "gx"),
            P("gx", "gy"),
            P("gx", "gy"),
            P("gy", "gx"),
        ),
        out_specs=P("gy", None, "gx"),
        check_vma=False,
    )
```

```python
import jax
import jax.numpy as jnp
from jax import lax
from jax.experimental import pallas as pl
from jax.experimental.pallas import tpu as pltpu
from jax.sharding import PartitionSpec as P

D = 2304
HEADS = 8
KV_HEADS = 4
HEAD_DIM = 256
HALF = HEAD_DIM // 2
WINDOW = 4096
PAGE = 128
BEAM = 8
EPSILON = 1e-06
SOFT_CAP = 50.0
ROPE_BASE = 10000.0
REPS = HEADS // KV_HEADS
WIDE = HEAD_DIM + PAGE
HALF_PAGE = PAGE // 2
BF = jnp.bfloat16
F32 = jnp.float32
MIB = 1024 * 1024
NT = (((1,), (1,)), ((), ()))
IN_SMEM = pl.BlockSpec(memory_space=pltpu.SMEM)


def run(name, kernel, outs, args, scratch=(), limit=16, specs=None, micros=0):
    cost = pl.CostEstimate(flops=micros * 10**9, bytes_accessed=0, transcendentals=0)
    specs = specs or {}
    vmem = pl.BlockSpec(memory_space=pltpu.VMEM)
    return pl.pallas_call(
        kernel,
        out_shape=[jax.ShapeDtypeStruct(s, d) for s, d in outs],
        in_specs=[specs.get(n, vmem) for n in range(len(args))],
        scratch_shapes=scratch,
        compiler_params=pltpu.CompilerParams(vmem_limit_bytes=limit * MIB),
        cost_estimate=cost if micros else None,
        name=name,
    )(*args)


def exchange(values, axes):
    return lax.all_to_all(values, axes, split_axis=0, concat_axis=0, tiled=True)


def exchange_all(values):
    nx, ny = values.shape[:2]
    flat = values.reshape((nx * ny,) + values.shape[2:])
    return exchange(flat, ("gx", "gy")).reshape(values.shape)


def permute(values, axis, m):
    count = lax.axis_size(axis)
    return lax.ppermute(values, axis, [(i, i ^ m) for i in range(count)])


def gather_gx(values):
    across = permute(values, "gx", 2)
    return [values, permute(values, "gx", 1), across, permute(across, "gx", 1)]


def gx_terms(values):
    def add(a_ref, b_ref, out_ref):
        out_ref[...] = a_ref[...] + b_ref[...]

    (pair,) = run(
        "pair_add", add, [(values.shape, values.dtype)], (values, permute(values, "gx", 1))
    )
    return pair, permute(pair, "gx", 2)


def weight_of(scores):
    return jnp.exp(SOFT_CAP * jnp.tanh(scores * (1.0 / SOFT_CAP)))


def high_low(column, lanes):
    shape = column.shape[:-1] + (lanes,)
    high = column.astype(BF).astype(F32)
    lane = lax.broadcasted_iota(jnp.int32, shape, len(shape) - 1)
    return jnp.where(lane < lanes // 2, high, column - high)


def pack_lanes(v):
    rows, width = v.shape
    whole = width // 128 * 128
    tiles = [v[:, c : c + 128] for c in range(0, whole, 128)]
    last = jnp.concatenate([v[: rows // 2, whole:], v[rows // 2 :, whole:]], axis=1)
    return jnp.concatenate(tiles + [last], axis=0)


def unpack_lanes(v, rows):
    whole = v.shape[0] // rows * rows
    tiles = [v[r : r + rows] for r in range(0, whole, rows)]
    last = jnp.concatenate([v[whole:, :64], v[whole:, 64:]], axis=0)
    return jnp.concatenate(tiles + [last], axis=1)


def row_sum(v):
    return jnp.sum(v, axis=-1, keepdims=True)


def make_tables(table, lengths, parents, slots, rows, steps):
    def tables(table_ref, length_ref, parents_ref, cached_ref, own_ref, page_ref):
        first_owner = lax.axis_index("gx") * slots
        length = length_ref[0]
        first_page = jnp.maximum(length - WINDOW + 1, 0) // PAGE
        for slot in range(slots + 1):
            page_ref[slot] = -1
        for j in range(table_ref.shape[1]):
            slot = table_ref[0, j] - first_owner
            page_ref[jnp.where((slot >= 0) & (slot < slots), slot, slots)] = j
        step = lax.broadcasted_iota(jnp.int32, (8, PAGE), 0) % steps
        lane = lax.broadcasted_iota(jnp.int32, (8, PAGE), 1)
        for slot in range(slots):
            page = page_ref[slot]
            position = lane + jnp.where(page >= 0, (first_page + page) * PAGE, 2**30)
            seen = (position < length) & (position >= length + step - (WINDOW - 1))
            cached_ref[:, slot * PAGE : (slot + 1) * PAGE] = jnp.where(seen, 1.0, 0.0)

        shape = (REPS * rows, rows)
        row = lax.broadcasted_iota(jnp.int32, shape, 0) % rows
        column = lax.broadcasted_iota(jnp.int32, shape, 1)
        row_step, column_step, column_beam = row % steps, column % steps, column // steps
        current = row // steps
        visible = jnp.zeros(shape, jnp.bool_)
        for j in range(steps - 1, -1, -1):
            if j < steps - 1:
                parent = jnp.zeros(shape, jnp.int32)
                for beam in range(BEAM):
                    parent = jnp.where(current == beam, parents_ref[j, beam], parent)
                current = jnp.where(row_step > j, parent, current)
            visible = visible | ((column_step == j) & (row_step >= j) & (column_beam == current))
        visible = visible & (lax.axis_index("gx") == 0)
        own_ref[...] = jnp.where(visible, 1.0, 0.0)

    return run(
        "tables",
        tables,
        [((8, slots * PAGE), F32), ((REPS * rows, rows), F32)],
        (table, lengths, parents),
        scratch=[pltpu.SMEM((slots + 1,), jnp.int32)],
        specs={0: IN_SMEM, 1: IN_SMEM, 2: IN_SMEM},
    )


def attend(shares, squares, tables, pool_ref, store):
    cos_ref, sin_ref, cached_ref, own_ref = tables
    slots = pool_ref.shape[1]
    rows = cos_ref.shape[0]
    square = jnp.sum(squares.astype(F32), axis=0)
    square = square[:, 0:1] + square[:, HALF // 2 : HALF // 2 + 1]
    scale = lax.rsqrt(square / D + EPSILON)
    cos, sin = cos_ref[...] * scale, sin_ref[...] * scale
    cached, own = cached_ref[...], own_ref[...]

    def rotated(u, w):
        u, w = u.astype(F32), w.astype(F32)
        return u * cos - w * sin, w * cos + u * sin

    for head in range(KV_HEADS):
        query = []
        for rep in range(REPS):
            u, w = rotated(shares(0, REPS * head + rep), shares(1, REPS * head + rep))
            query.append(jnp.concatenate([u, w], axis=1) * HEAD_DIM ** (-0.5))
        query = jnp.concatenate(query, axis=0).astype(BF)
        first, second = 2 * head, 2 * head + 1
        key_step = rotated(shares(2, first), shares(2, second))
        key_step = jnp.concatenate(key_step, axis=1).astype(BF)
        value_step = [shares(3, n).astype(F32) * scale for n in (first, second)]
        value_step = jnp.concatenate(value_step, axis=1).astype(BF)

        scores = lax.dot_general(query, key_step, NT, preferred_element_type=F32)
        weights = weight_of(scores) * own
        den = row_sum(weights)
        num = jnp.dot(weights.astype(BF), value_step, preferred_element_type=F32)

        here = slice(head * HEAD_DIM, (head + 1) * HEAD_DIM)
        keys = pool_ref[0, :, :, here].reshape(slots * PAGE, HEAD_DIM)
        values = pool_ref[1, :, :, here].reshape(slots * PAGE, HEAD_DIM)
        scores = lax.dot_general(query, keys, NT, preferred_element_type=F32)
        weights = weight_of(scores).reshape(REPS * rows // 8, 8, slots * PAGE) * cached[None]
        weights = weights.reshape(REPS * rows, slots * PAGE)
        den = den + row_sum(weights)
        num = num + jnp.dot(weights.astype(BF), values, preferred_element_type=F32)
        store(head, num, den)


def rope_tables(lengths, rows, steps):
    positions = lengths[0] + jnp.arange(rows, dtype=jnp.int32) % steps
    inverse_freq = ROPE_BASE ** (-jnp.arange(HALF, dtype=F32) * 2.0 / HEAD_DIM)
    angles = positions[:, None].astype(F32) * inverse_freq
    return jnp.cos(angles), jnp.sin(angles)


def body_permutes(
    inputs,
    cache_pool,
    lengths,
    block_table,
    parents,
    norm_gains,
    w_query,
    w_key,
    w_value,
    w_out,
    w_gate,
    w_up,
    w_down,
):
    beams, steps, width = inputs.shape
    nx, ny = lax.axis_size("gx"), lax.axis_size("gy")
    rows = beams * steps
    half = rows // 2
    all_rows = ny * rows
    share_rows = all_rows // nx
    hidden = w_gate.shape[1]
    packed = rows * width // 128

    def my(axis):
        return lax.axis_index(axis)

    def spread(x_ref, own_ref, out_ref):
        own = x_ref[...].astype(F32).reshape(rows, width).astype(BF)
        own_ref[...] = own
        own = pack_lanes(own)
        for m in range(ny):
            out_ref[m] = own

    x_own, x_all = run(
        "spread", spread, [((rows, width), BF), ((ny, packed, 128), BF)], (inputs,), micros=12
    )
    w_own = w_out.T
    x_all, w_split = lax.optimization_barrier((x_all, w_own))
    x_all = exchange(x_all, "gy")

    w_blocks = {0: w_own, 1: permute(w_own, "gy", 1), 2: permute(w_own, "gy", 2)}
    w_first = permute(w_split[: width // 2], "gy", 4)
    w_late, _ = lax.optimization_barrier(((w_blocks[1], w_split[width // 2 :]), x_all))
    w_blocks[3] = permute(w_late[0], "gy", 2)
    w_second = permute(w_late[1], "gy", 4)

    def project(x_ref, gain_ref, q_ref, k_ref, v_ref, z0_ref, z2_ref, z13_ref, held):
        gain = 1.0 + gain_ref[0:1]
        flat = [
            (unpack_lanes(x_ref[m], rows).astype(F32) * gain).astype(BF) for m in range(ny)
        ]
        flat = jnp.concatenate(flat, axis=0)
        query = jnp.dot(flat, q_ref[...], preferred_element_type=F32).astype(BF)
        held[0], held[1] = query[:, :HALF], query[:, HALF:]
        held[2] = jnp.dot(flat, k_ref[...], preferred_element_type=F32).astype(BF)
        held[3] = jnp.dot(flat, v_ref[...], preferred_element_type=F32).astype(BF)
        me = my("gx")
        z0_ref[...], z2_ref[...] = held[me], held[me ^ 2]
        z13_ref[0], z13_ref[1] = held[me ^ 1], held[me ^ 3]

    shape = (all_rows, HALF)
    z0, z2, z13 = run(
        "project",
        project,
        [(shape, BF), (shape, BF), ((2,) + shape, BF)],
        (x_all, norm_gains, w_query, w_key, w_value),
        scratch=[
            pltpu.VMEM((nx,) + shape, BF),
        ],
    )
    z13 = permute(z13, "gx", 1)

    def pair_sum(z_ref, from_pair_ref, out_ref):
        total = z_ref[...].astype(F32) + from_pair_ref[1].astype(F32)
        out_ref[...] = total.astype(BF)

    (z2,) = run("pair_sum", pair_sum, [(shape, BF)], (z2, z13))
    z2 = permute(z2, "gx", 2)

    def share_sum(z0_ref, z13_ref, z2_ref, out_ref):
        total = z0_ref[...].astype(F32) + z13_ref[0].astype(F32) + z2_ref[...].astype(F32)
        out_ref[...] = total.reshape(ny, rows, HALF).astype(BF)

    (shares,) = run("share_sum", share_sum, [((ny, rows, HALF), BF)], (z0, z13, z2))
    shares, *late = lax.optimization_barrier((shares, block_table, lengths, parents))
    cos, sin = rope_tables(late[1], rows, steps)
    tables = make_tables(*late, cache_pool.shape[1], rows, steps)
    halves, _ = lax.optimization_barrier(((w_first, w_second), shares))
    w_blocks[4] = jnp.concatenate(halves, axis=0)
    w_blocks[6] = permute(w_blocks[4], "gy", 2)
    w_blocks[5] = permute(w_blocks[4], "gy", 1)
    shares = exchange(shares, "gy")
    beside = tables, cos, sin, w_blocks[2], w_blocks[3], w_blocks[4]
    shares, (tables, cos, sin, *_) = lax.optimization_barrier((shares, beside))

    def pack_shares(share_ref, x_ref, out_ref):
        x = x_ref[...].astype(F32)
        out_ref[0:ny] = share_ref[...]
        out_ref[ny] = high_low(row_sum(x * x), HALF).astype(BF)

    (shares,) = run(
        "pack_shares", pack_shares, [((ny + 1, rows, HALF), BF)], (shares, x_own), micros=5
    )
    shares = gather_gx(shares)

    def attention(*refs):
        a_refs, tables, pool_ref, outs = refs[:nx], refs[nx : nx + 4], refs[nx + 4], refs[nx + 5 :]
        own_ref, pair_ref, held, num_held, den_held = outs
        me = my("gx")
        core = me & 1
        for n, ref in enumerate(a_refs):
            held[me ^ n] = ref[...]
        den_held[...] = jnp.zeros(den_held.shape, F32)
        lane = lax.broadcasted_iota(jnp.int32, (2, half, PAGE), 2)

        def store(head, num, den):
            num_held[head] = num.reshape(REPS, 2, half, HEAD_DIM)
            den = high_low(den, PAGE).reshape(REPS, 2, half, PAGE)
            for rep in range(REPS):
                at = REPS * head + rep
                den_held[...] = jnp.where(lane % HALF_PAGE == at, den[rep], den_held[...])
                for n, out in enumerate((own_ref, pair_ref)):
                    for tile in range(2):
                        here = num_held[head, rep, core ^ n, :, tile * PAGE : (tile + 1) * PAGE]
                        out[2 * at + tile] = here.astype(BF)

        attend(
            lambda share, which: held[share, which],
            held[:, ny],
            tables,
            pool_ref,
            store,
        )
        for n, out in enumerate((own_ref, pair_ref)):
            out[2 * HEADS] = den_held[core ^ n].astype(BF)

    shape = (2 * HEADS + 1, half, PAGE)
    own, pair = run(
        "attention",
        attention,
        [(shape, BF), (shape, BF)],
        (*shares, cos, sin, *tables, cache_pool),
        scratch=[
            pltpu.VMEM((nx,) + shares[0].shape, BF),
            pltpu.VMEM((KV_HEADS, REPS, 2, half, HEAD_DIM), F32),
            pltpu.VMEM((2, half, PAGE), F32),
        ],
        limit=24,
    )
    w_late, _ = lax.optimization_barrier((w_blocks, own))
    w_blocks[7] = permute(w_late[6], "gy", 1)
    pair = permute(pair, "gx", 1)

    def pair_terms(own_ref, pair_ref, out_ref):
        total = own_ref[...].astype(F32) + pair_ref[...].astype(F32)
        out_ref[0 : 2 * HEADS] = total[0 : 2 * HEADS].astype(BF)
        den = total[2 * HEADS]
        den = den[:, :HALF_PAGE] + den[:, HALF_PAGE:]
        high = den.astype(BF).astype(F32)
        out_ref[2 * HEADS] = jnp.concatenate([high, den - high], axis=1).astype(BF)

    (own,) = run("pair_terms", pair_terms, [(shape, BF)], (own, pair))
    across = permute(own, "gx", 2)

    def divide(own_ref, across_ref, out_ref):
        total = own_ref[...].astype(F32) + across_ref[...].astype(F32)
        den = total[2 * HEADS]
        den = den[:, :HALF_PAGE] + den[:, HALF_PAGE:]
        for head in range(HEADS):
            scale = 1.0 / den[:, head : head + 1]
            for tile in range(2):
                at = 2 * head + tile
                out_ref[at] = (total[at] * scale).astype(BF)

    (attended,) = run("divide", divide, [((2 * HEADS, half, PAGE), BF)], (own, across))
    others = permute(attended, "gx", 1)

    def project_out(own_ref, other_ref, x_ref, gain_ref, *refs):
        w_refs, (attn_ref, sums_ref, held) = refs[:ny], refs[ny:]
        core = my("gx") & 1
        held[core], held[1 - core] = own_ref[...], other_ref[...]
        me = my("gy")
        attn = jnp.zeros((rows, width), F32)
        for m, w_ref in enumerate(w_refs):
            at = 2 * (me ^ m)
            flat = [jnp.concatenate([held[n, at], held[n, at + 1]], axis=1) for n in range(2)]
            flat = jnp.concatenate(flat, axis=0)
            attn = attn + lax.dot_general(flat, w_ref[...], NT, preferred_element_type=F32)
        attn_ref[...] = attn
        x = x_ref[...].astype(F32)
        scaled = attn * (1.0 + gain_ref[1:2])
        lane = lax.broadcasted_iota(jnp.int32, (rows, PAGE), 1)
        sums = jnp.zeros((rows, PAGE), F32)
        for n, terms in enumerate((attn * attn, scaled * scaled, x * scaled, x * x)):
            sums = jnp.where(lane == n, row_sum(terms), sums)
        sums_ref[...] = sums

    attn, sums = run(
        "project_out",
        project_out,
        [((rows, width), F32), ((rows, PAGE), F32)],
        (attended, others, x_own, norm_gains, *[w_blocks[m] for m in range(ny)]),
        scratch=[pltpu.VMEM((2, 2 * HEADS, half, PAGE), BF)],
    )
    sums = gx_terms(sums)

    def mix(*refs):
        attn_ref, x_ref, gain_ref, mixed_ref, ff_ref = refs[2:]
        total = refs[0][...] + refs[1][...]
        plain, scaled, cross, square = (total[:, n : n + 1] for n in range(4))
        scale = lax.rsqrt(plain / D + EPSILON)
        mixed = x_ref[...].astype(F32) + attn_ref[...] * scale * (1.0 + gain_ref[1:2])
        square = jnp.maximum(square + 2.0 * scale * cross + scale * scale * scaled, 0.0)
        mixed_ref[...] = mixed
        scale = lax.rsqrt(square / D + EPSILON)
        ff_input = (mixed * scale * (1.0 + gain_ref[2:3])).astype(BF)
        ff_input = pack_lanes(ff_input)
        for m in range(ny):
            ff_ref[m] = ff_input

    mixed, ff_input = run(
        "mix",
        mix,
        [((rows, width), F32), ((ny, packed, 128), BF)],
        (*sums, attn, x_own, norm_gains),
    )
    ff_input = exchange(ff_input, "gy")

    groups = ny // nx

    cut = hidden // 384 * 256
    column_parts = (0, cut), (cut, hidden)

    def gate_up(start, end):
        def kernel(ff_ref, gate_ref, up_ref, z0_ref, z2_ref, z13_ref):
            me = my("gx")
            flat = [
                unpack_lanes(ff_ref[(me ^ n) * groups + group], rows)
                for n in range(nx)
                for group in range(groups)
            ]
            flat = jnp.concatenate(flat, axis=0)
            for n, w_ref in enumerate((gate_ref, up_ref)):
                sums = jnp.dot(flat, w_ref[:, start:end], preferred_element_type=F32).astype(BF)
                here = pl.ds(n * (end - start), end - start)
                for p, out in enumerate((z0_ref, z13_ref.at[0], z2_ref, z13_ref.at[1])):
                    out[:, here] = sums[p * share_rows : (p + 1) * share_rows]

        shape = (share_rows, 2 * (end - start))
        return run(
            "gate_up",
            kernel,
            [(shape, BF), (shape, BF), ((2,) + shape, BF)],
            (ff_input, w_gate, w_up),
            limit=24,
        )

    def activate(z0_ref, z13_ref, z2_ref, out_ref):
        total = z0_ref[...].astype(F32) + z13_ref[0].astype(F32) + z2_ref[...].astype(F32)
        count = total.shape[1] // 2
        gate, up = total[:, :count], total[:, count:]
        out_ref[...] = (jax.nn.gelu(gate, approximate=True) * up).astype(BF)

    parts = [gate_up(*columns) for columns in column_parts]
    blocks = []
    for z0, z2, z13 in parts:
        shape = z0.shape
        z13 = permute(z13, "gx", 1)
        (z2,) = run("pair_sum_ff", pair_sum, [(shape, BF)], (z2, z13))
        z2 = permute(z2, "gx", 2)
        shape = (share_rows, shape[1] // 2)
        blocks += gather_gx(run("activate", activate, [(shape, BF)], (z0, z13, z2))[0])

    def project_down(*refs):
        w_ref, out_ref = refs[2 * nx :]
        me = my("gx")
        flat = [
            jnp.concatenate([refs[n][...], refs[nx + n][...]], axis=1) for n in range(nx)
        ]
        flat = jnp.concatenate(flat, axis=0)
        sums = lax.dot_general(flat, w_ref[...], NT, preferred_element_type=F32)
        for n in range(nx):
            for group in range(groups):
                at = (n * groups + group) * rows
                block = pack_lanes(sums[at : at + rows].astype(BF))
                out_ref[(me ^ n) * groups + group] = block

    (down,) = run(
        "project_down", project_down, [((ny, packed, 128), BF)], (*blocks, w_down.T)
    )
    down = exchange(down, "gy")

    def down_sum(parts_ref, down_ref, sums_ref):
        down = unpack_lanes(jnp.sum(parts_ref[...].astype(F32), axis=0), rows)
        down_ref[...] = down
        sums_ref[...] = jnp.broadcast_to(row_sum(down * down), (rows, PAGE))

    down, sums = run(
        "down_sum", down_sum, [((rows, width), F32), ((rows, PAGE), F32)], (down,)
    )
    sums = gx_terms(sums)

    def finish(*refs):
        down_ref, mixed_ref, gain_ref, out_ref = refs[2:]
        square = (refs[0][...] + refs[1][...])[:, 0:1]
        scale = lax.rsqrt(square / D + EPSILON)
        out = mixed_ref[...] + down_ref[...] * scale * (1.0 + gain_ref[3:4])
        out_ref[...] = out.reshape(beams, steps, width).astype(BF)

    (out,) = run("finish", finish, [(inputs.shape, BF)], (*sums, down, mixed, norm_gains))
    return out


def body_general(
    inputs,
    cache_pool,
    lengths,
    block_table,
    parents,
    norm_gains,
    w_query,
    w_key,
    w_value,
    w_out,
    w_gate,
    w_up,
    w_down,
):
    beams, steps, width = inputs.shape
    nx, ny = lax.axis_size("gx"), lax.axis_size("gy")
    rows = beams * steps
    part = rows // nx
    head_part = w_out.shape[0]
    hidden_part = w_gate.shape[1]
    query_part, key_part = w_query.shape[1], w_key.shape[1]
    columns = query_part + 2 * key_part
    share = columns // nx
    x_own = inputs.reshape(rows, width)
    me = lax.axis_index("gx")

    x_all = exchange(jnp.broadcast_to(x_own[None], (ny, rows, width)), "gy")
    flat = (x_all.astype(F32) * (1.0 + norm_gains[0:1])).astype(BF).reshape(ny * rows, width)
    sums = [jnp.dot(flat, w, preferred_element_type=F32) for w in (w_query, w_key, w_value)]
    sums = jnp.concatenate(sums, axis=1).reshape(ny, rows, nx, share)
    received = exchange_all(sums.transpose(2, 0, 1, 3).astype(BF))
    shares = jnp.sum(received.astype(F32), axis=0).astype(BF)
    every = lax.all_gather(shares, "gx", axis=0)
    every = every.transpose(2, 1, 0, 3).reshape(rows, ny, columns)
    q = every[..., :query_part].reshape(rows, HEADS, 2, HALF).transpose(2, 1, 0, 3)
    k, v = (
        every[..., start : start + key_part].reshape(rows, 2 * KV_HEADS, HALF).transpose(1, 0, 2)
        for start in (query_part, query_part + key_part)
    )
    shares = jnp.concatenate([q, k[None], v[None]], axis=0)
    square = lax.psum(row_sum(jnp.square(x_own.astype(F32))), "gx")
    high = lax.reduce_precision(square, 8, 7)
    squares = jnp.where(jnp.arange(HALF) < HALF // 2, high, square - high).astype(BF)[None]
    cos, sin = rope_tables(lengths, rows, steps)

    def attention(*refs):
        g_ref, square_ref, tables, pool_ref, out_ref = refs[0], refs[1], refs[2:6], *refs[6:]

        def store(head, num, den):
            den = high_low(den, PAGE)
            for rep in range(REPS):
                here = slice(rep * rows, (rep + 1) * rows)
                out_ref[REPS * head + rep, :, 0:HEAD_DIM] = num[here].astype(BF)
                out_ref[REPS * head + rep, :, HEAD_DIM:] = den[here].astype(BF)

        attend(
            lambda share, which: g_ref[share, which],
            square_ref[...],
            tables,
            pool_ref,
            store,
        )

    tables = make_tables(block_table, lengths, parents, cache_pool.shape[1], rows, steps)
    (terms,) = run(
        "attention",
        attention,
        [((HEADS, rows, WIDE), BF)],
        (shares, squares, cos, sin, *tables, cache_pool),
        limit=24,
    )
    num = terms[..., :HEAD_DIM].transpose(1, 0, 2).reshape(nx, part, ny, head_part)
    den = terms[..., HEAD_DIM :: PAGE // 2].transpose(1, 0, 2)
    den = jnp.repeat(den, ny // HEADS, axis=1).reshape(nx, part, ny, 2)
    terms = exchange_all(jnp.concatenate([num, den], axis=-1).transpose(0, 2, 1, 3))

    w_wide = lax.all_gather(w_out, "gx", axis=1, tiled=True)
    x_wide = lax.all_gather(x_own, "gx", axis=1, tiled=True)
    x_rows = lax.dynamic_slice_in_dim(x_wide, me * part, part, 0).astype(F32)
    gains = 1.0 + lax.all_gather(norm_gains, "gx", axis=1, tiled=True)

    def scaled(v, gain):
        return v * lax.rsqrt(row_sum(v * v) / D + EPSILON) * gain

    terms = jnp.sum(terms.astype(F32), axis=0)
    den = terms[..., head_part : head_part + 1] + terms[..., -1:]
    attended = (terms[..., :head_part] / den).reshape(ny * part, head_part).astype(BF)
    attn = jnp.dot(attended, w_wide, preferred_element_type=F32).astype(BF)
    attn = exchange(attn.reshape(ny, part, D), "gy").astype(F32).sum(axis=0)
    mixed = x_rows + scaled(attn, gains[1])
    ff_input = scaled(mixed, gains[2]).astype(BF)
    ff_input = ff_input.reshape(part, nx, width).transpose(1, 0, 2)[:, None]
    ff_input = exchange_all(jnp.broadcast_to(ff_input, (nx, ny, part, width)))

    flat = ff_input.reshape(-1, width)
    both = [jnp.dot(flat, w, preferred_element_type=F32).astype(BF) for w in (w_gate, w_up)]
    both = jnp.stack(both, axis=1).reshape(nx, ny * part, 2, hidden_part)
    both = jnp.sum(exchange(both, "gx").astype(F32), axis=0)
    hidden = (jax.nn.gelu(both[:, 0], approximate=True) * both[:, 1]).astype(BF)
    hidden = lax.all_gather(hidden, "gx", axis=0, tiled=True)
    down = jnp.dot(hidden, w_down, preferred_element_type=F32).astype(BF)
    down = exchange_all(down.reshape(nx, ny, part, width)).astype(F32).sum(axis=1)
    down = down.transpose(1, 0, 2).reshape(part, D)
    out = (mixed + scaled(down, gains[3])).astype(BF)
    out = exchange(out.reshape(part, nx, width).transpose(1, 0, 2), "gx")
    return out.reshape(beams, steps, width)


def solution(mesh):
    sizes = dict(mesh.shape)
    fits = sizes["gx"] == 4 and sizes["gy"] == HEADS
    return jax.shard_map(
        body_permutes if fits else body_general,
        mesh=mesh,
        in_specs=(
            P("gy", None, "gx"),
            P(None, "gx", "gy", None),
            P("gy"),
            P("gy", None),
            P(None, "gy"),
            P(None, "gx"),
            P("gx", "gy"),
            P("gx", "gy"),
            P("gx", "gy"),
            P("gy", "gx"),
            P("gx", "gy"),
            P("gx", "gy"),
            P("gy", "gx"),
        ),
        out_specs=P("gy", None, "gx"),
        check_vma=False,
    )
```

```python
import jax
import jax.numpy as jnp
from jax import lax
from jax.experimental import pallas as pl
from jax.experimental.pallas import tpu as pltpu
from jax.sharding import PartitionSpec as P

D = 2304
HEADS = 8
KV_HEADS = 4
HEAD_DIM = 256
HALF = HEAD_DIM // 2
WINDOW = 4096
PAGE = 128
BEAM = 8
EPSILON = 1e-06
SOFT_CAP = 50.0
ROPE_BASE = 10000.0
REPS = HEADS // KV_HEADS
WIDE = HEAD_DIM + PAGE
HALF_PAGE = PAGE // 2
BF = jnp.bfloat16
F32 = jnp.float32
MIB = 1024 * 1024
NT = (((1,), (1,)), ((), ()))
IN_SMEM = pl.BlockSpec(memory_space=pltpu.SMEM)


def run(name, kernel, outs, args, scratch=(), limit=16, specs=None, micros=0):
    cost = pl.CostEstimate(flops=micros * 10**9, bytes_accessed=0, transcendentals=0)
    specs = specs or {}
    vmem = pl.BlockSpec(memory_space=pltpu.VMEM)
    return pl.pallas_call(
        kernel,
        out_shape=[jax.ShapeDtypeStruct(s, d) for s, d in outs],
        in_specs=[specs.get(n, vmem) for n in range(len(args))],
        scratch_shapes=scratch,
        compiler_params=pltpu.CompilerParams(vmem_limit_bytes=limit * MIB),
        cost_estimate=cost if micros else None,
        name=name,
    )(*args)


def exchange(values, axes):
    return lax.all_to_all(values, axes, split_axis=0, concat_axis=0, tiled=True)


def exchange_all(values):
    nx, ny = values.shape[:2]
    flat = values.reshape((nx * ny,) + values.shape[2:])
    return exchange(flat, ("gx", "gy")).reshape(values.shape)


def permute(values, axis, m):
    count = lax.axis_size(axis)
    return lax.ppermute(values, axis, [(i, i ^ m) for i in range(count)])


def trade(blocks, axis):
    return [blocks[0]] + [permute(blocks[m], axis, m) for m in range(1, len(blocks))]


def gather_gx(values):
    across = permute(values, "gx", 2)
    return [values, permute(values, "gx", 1), across, permute(across, "gx", 1)]


def gx_terms(values):
    def add(a_ref, b_ref, out_ref):
        out_ref[...] = a_ref[...] + b_ref[...]

    (pair,) = run(
        "pair_add", add, [(values.shape, values.dtype)], (values, permute(values, "gx", 1))
    )
    return pair, permute(pair, "gx", 2)


def weight_of(scores):
    return jnp.exp(SOFT_CAP * jnp.tanh(scores * (1.0 / SOFT_CAP)))


def high_low(column, lanes):
    shape = column.shape[:-1] + (lanes,)
    high = column.astype(BF).astype(F32)
    lane = lax.broadcasted_iota(jnp.int32, shape, len(shape) - 1)
    return jnp.where(lane < lanes // 2, high, column - high)


def pack_lanes(v):
    rows, width = v.shape
    whole = width // 128 * 128
    tiles = [v[:, c : c + 128] for c in range(0, whole, 128)]
    last = jnp.concatenate([v[: rows // 2, whole:], v[rows // 2 :, whole:]], axis=1)
    return jnp.concatenate(tiles + [last], axis=0)


def unpack_lanes(v, rows):
    whole = v.shape[0] // rows * rows
    tiles = [v[r : r + rows] for r in range(0, whole, rows)]
    last = jnp.concatenate([v[whole:, :64], v[whole:, 64:]], axis=0)
    return jnp.concatenate(tiles + [last], axis=1)


def row_sum(v):
    return jnp.sum(v, axis=-1, keepdims=True)


def make_tables(table, lengths, parents, slots, rows, steps):
    def tables(table_ref, length_ref, parents_ref, cached_ref, own_ref, page_ref):
        first_owner = lax.axis_index("gx") * slots
        length = length_ref[0]
        first_page = jnp.maximum(length - WINDOW + 1, 0) // PAGE
        for slot in range(slots + 1):
            page_ref[slot] = -1
        for j in range(table_ref.shape[1]):
            slot = table_ref[0, j] - first_owner
            page_ref[jnp.where((slot >= 0) & (slot < slots), slot, slots)] = j
        step = lax.broadcasted_iota(jnp.int32, (8, PAGE), 0) % steps
        lane = lax.broadcasted_iota(jnp.int32, (8, PAGE), 1)
        for slot in range(slots):
            page = page_ref[slot]
            position = lane + jnp.where(page >= 0, (first_page + page) * PAGE, 2**30)
            seen = (position < length) & (position >= length + step - (WINDOW - 1))
            cached_ref[:, slot * PAGE : (slot + 1) * PAGE] = jnp.where(seen, 1.0, 0.0)

        shape = (REPS * rows, rows)
        row = lax.broadcasted_iota(jnp.int32, shape, 0) % rows
        column = lax.broadcasted_iota(jnp.int32, shape, 1)
        row_step, column_step, column_beam = row % steps, column % steps, column // steps
        current = row // steps
        visible = jnp.zeros(shape, jnp.bool_)
        for j in range(steps - 1, -1, -1):
            if j < steps - 1:
                parent = jnp.zeros(shape, jnp.int32)
                for beam in range(BEAM):
                    parent = jnp.where(current == beam, parents_ref[j, beam], parent)
                current = jnp.where(row_step > j, parent, current)
            visible = visible | ((column_step == j) & (row_step >= j) & (column_beam == current))
        visible = visible & (lax.axis_index("gx") == 0)
        own_ref[...] = jnp.where(visible, 1.0, 0.0)

    return run(
        "tables",
        tables,
        [((8, slots * PAGE), F32), ((REPS * rows, rows), F32)],
        (table, lengths, parents),
        scratch=[pltpu.SMEM((slots + 1,), jnp.int32)],
        specs={0: IN_SMEM, 1: IN_SMEM, 2: IN_SMEM},
    )


def attend(shares, squares, tables, pool_ref, store):
    cos_ref, sin_ref, cached_ref, own_ref = tables
    slots = pool_ref.shape[1]
    rows = cos_ref.shape[0]
    square = jnp.sum(squares.astype(F32), axis=0)
    square = square[:, 0:1] + square[:, HALF // 2 : HALF // 2 + 1]
    scale = lax.rsqrt(square / D + EPSILON)
    cos, sin = cos_ref[...] * scale, sin_ref[...] * scale
    cached, own = cached_ref[...], own_ref[...]

    def rotated(u, w):
        u, w = u.astype(F32), w.astype(F32)
        return u * cos - w * sin, w * cos + u * sin

    for head in range(KV_HEADS):
        query = []
        for rep in range(REPS):
            u, w = rotated(shares(0, REPS * head + rep), shares(1, REPS * head + rep))
            query.append(jnp.concatenate([u, w], axis=1) * HEAD_DIM ** (-0.5))
        query = jnp.concatenate(query, axis=0).astype(BF)
        first, second = 2 * head, 2 * head + 1
        key_step = rotated(shares(2, first), shares(2, second))
        key_step = jnp.concatenate(key_step, axis=1).astype(BF)
        value_step = [shares(3, n).astype(F32) * scale for n in (first, second)]
        value_step = jnp.concatenate(value_step, axis=1).astype(BF)

        scores = lax.dot_general(query, key_step, NT, preferred_element_type=F32)
        weights = weight_of(scores) * own
        den = row_sum(weights)
        num = jnp.dot(weights.astype(BF), value_step, preferred_element_type=F32)

        here = slice(head * HEAD_DIM, (head + 1) * HEAD_DIM)
        keys = pool_ref[0, :, :, here].reshape(slots * PAGE, HEAD_DIM)
        values = pool_ref[1, :, :, here].reshape(slots * PAGE, HEAD_DIM)
        scores = lax.dot_general(query, keys, NT, preferred_element_type=F32)
        weights = weight_of(scores).reshape(REPS * rows // 8, 8, slots * PAGE) * cached[None]
        weights = weights.reshape(REPS * rows, slots * PAGE)
        den = den + row_sum(weights)
        num = num + jnp.dot(weights.astype(BF), values, preferred_element_type=F32)
        store(head, num, den)


def rope_tables(lengths, rows, steps):
    positions = lengths[0] + jnp.arange(rows, dtype=jnp.int32) % steps
    inverse_freq = ROPE_BASE ** (-jnp.arange(HALF, dtype=F32) * 2.0 / HEAD_DIM)
    angles = positions[:, None].astype(F32) * inverse_freq
    return jnp.cos(angles), jnp.sin(angles)


def body_permutes(
    inputs,
    cache_pool,
    lengths,
    block_table,
    parents,
    norm_gains,
    w_query,
    w_key,
    w_value,
    w_out,
    w_gate,
    w_up,
    w_down,
):
    beams, steps, width = inputs.shape
    nx, ny = lax.axis_size("gx"), lax.axis_size("gy")
    rows = beams * steps
    half = rows // 2
    all_rows = ny * rows
    share_rows = all_rows // nx
    hidden = w_gate.shape[1]
    packed = rows * width // 128

    def my(axis):
        return lax.axis_index(axis)

    def spread(x_ref, own_ref, out_ref):
        own = x_ref[...].astype(F32).reshape(rows, width).astype(BF)
        own_ref[...] = own
        own = pack_lanes(own)
        for m in range(ny):
            out_ref[m] = own

    x_own, x_all = run(
        "spread", spread, [((rows, width), BF), ((ny, packed, 128), BF)], (inputs,), micros=12
    )
    w_own = w_out.T
    x_all, w_split = lax.optimization_barrier((x_all, w_own))
    x_all = exchange(x_all, "gy")

    w_blocks = {0: w_own, 1: permute(w_own, "gy", 1), 2: permute(w_own, "gy", 2)}
    w_first = permute(w_split[: width // 2], "gy", 4)
    w_blocks[3] = permute(w_own, "gy", 3)
    w_late, _ = lax.optimization_barrier((w_split[width // 2 :], x_all))
    w_second = permute(w_late, "gy", 4)

    def project(x_ref, gain_ref, q_ref, k_ref, v_ref, z0_ref, z2_ref, z13_ref, held):
        gain = 1.0 + gain_ref[0:1]
        flat = [
            (unpack_lanes(x_ref[m], rows).astype(F32) * gain).astype(BF) for m in range(ny)
        ]
        flat = jnp.concatenate(flat, axis=0)
        query = jnp.dot(flat, q_ref[...], preferred_element_type=F32).astype(BF)
        held[0], held[1] = query[:, :HALF], query[:, HALF:]
        held[2] = jnp.dot(flat, k_ref[...], preferred_element_type=F32).astype(BF)
        held[3] = jnp.dot(flat, v_ref[...], preferred_element_type=F32).astype(BF)
        me = my("gx")
        z0_ref[...], z2_ref[...] = held[me], held[me ^ 2]
        z13_ref[0], z13_ref[1] = held[me ^ 1], held[me ^ 3]

    shape = (all_rows, HALF)
    z0, z2, z13 = run(
        "project",
        project,
        [(shape, BF), (shape, BF), ((2,) + shape, BF)],
        (x_all, norm_gains, w_query, w_key, w_value),
        scratch=[
            pltpu.VMEM((nx,) + shape, BF),
        ],
    )
    z13 = permute(z13, "gx", 1)

    def pair_sum(z_ref, from_pair_ref, out_ref):
        total = z_ref[...].astype(F32) + from_pair_ref[1].astype(F32)
        out_ref[...] = total.astype(BF)

    (z2,) = run("pair_sum", pair_sum, [(shape, BF)], (z2, z13))
    z2 = permute(z2, "gx", 2)

    def share_sum(z0_ref, z13_ref, z2_ref, out_ref):
        total = z0_ref[...].astype(F32) + z13_ref[0].astype(F32) + z2_ref[...].astype(F32)
        out_ref[...] = total.reshape(ny, rows, HALF).astype(BF)

    (shares,) = run("share_sum", share_sum, [((ny, rows, HALF), BF)], (z0, z13, z2))
    shares, *late = lax.optimization_barrier((shares, block_table, lengths, parents))
    cos, sin = rope_tables(late[1], rows, steps)
    tables = make_tables(*late, cache_pool.shape[1], rows, steps)
    halves, _ = lax.optimization_barrier(((w_first, w_second), shares))
    w_blocks[4] = jnp.concatenate(halves, axis=0)
    w_blocks[6] = permute(w_blocks[4], "gy", 2)
    w_blocks[5] = permute(w_blocks[4], "gy", 1)
    shares = exchange(shares, "gy")
    beside = tables, cos, sin, w_blocks[1], w_blocks[2], w_blocks[3], w_blocks[4]
    shares, (tables, cos, sin, *_) = lax.optimization_barrier((shares, beside))

    def pack_shares(share_ref, x_ref, out_ref):
        x = x_ref[...].astype(F32)
        out_ref[0:ny] = share_ref[...]
        out_ref[ny] = high_low(row_sum(x * x), HALF).astype(BF)

    (shares,) = run(
        "pack_shares", pack_shares, [((ny + 1, rows, HALF), BF)], (shares, x_own), micros=5
    )
    shares = gather_gx(shares)

    def attention(*refs):
        a_refs, tables, pool_ref, outs = refs[:nx], refs[nx : nx + 4], refs[nx + 4], refs[nx + 5 :]
        own_ref, pair_ref, held, num_held, den_held = outs
        me = my("gx")
        core = me & 1
        for n, ref in enumerate(a_refs):
            held[me ^ n] = ref[...]
        den_held[...] = jnp.zeros(den_held.shape, F32)
        lane = lax.broadcasted_iota(jnp.int32, (2, half, PAGE), 2)

        def store(head, num, den):
            num_held[head] = num.reshape(REPS, 2, half, HEAD_DIM)
            den = high_low(den, PAGE).reshape(REPS, 2, half, PAGE)
            for rep in range(REPS):
                at = REPS * head + rep
                den_held[...] = jnp.where(lane % HALF_PAGE == at, den[rep], den_held[...])
                for n, out in enumerate((own_ref, pair_ref)):
                    for tile in range(2):
                        here = num_held[head, rep, core ^ n, :, tile * PAGE : (tile + 1) * PAGE]
                        out[2 * at + tile] = here.astype(BF)

        attend(
            lambda share, which: held[share, which],
            held[:, ny],
            tables,
            pool_ref,
            store,
        )
        for n, out in enumerate((own_ref, pair_ref)):
            out[2 * HEADS] = den_held[core ^ n].astype(BF)

    shape = (2 * HEADS + 1, half, PAGE)
    own, pair = run(
        "attention",
        attention,
        [(shape, BF), (shape, BF)],
        (*shares, cos, sin, *tables, cache_pool),
        scratch=[
            pltpu.VMEM((nx,) + shares[0].shape, BF),
            pltpu.VMEM((KV_HEADS, REPS, 2, half, HEAD_DIM), F32),
            pltpu.VMEM((2, half, PAGE), F32),
        ],
        limit=24,
    )
    w_late, _ = lax.optimization_barrier((w_blocks, own))
    w_blocks[7] = permute(w_late[6], "gy", 1)
    pair = permute(pair, "gx", 1)

    def pair_terms(own_ref, pair_ref, out_ref):
        total = own_ref[...].astype(F32) + pair_ref[...].astype(F32)
        out_ref[0 : 2 * HEADS] = total[0 : 2 * HEADS].astype(BF)
        den = total[2 * HEADS]
        den = den[:, :HALF_PAGE] + den[:, HALF_PAGE:]
        high = den.astype(BF).astype(F32)
        out_ref[2 * HEADS] = jnp.concatenate([high, den - high], axis=1).astype(BF)

    (own,) = run("pair_terms", pair_terms, [(shape, BF)], (own, pair))
    across = permute(own, "gx", 2)

    def divide(own_ref, across_ref, out_ref):
        total = own_ref[...].astype(F32) + across_ref[...].astype(F32)
        den = total[2 * HEADS]
        den = den[:, :HALF_PAGE] + den[:, HALF_PAGE:]
        for head in range(HEADS):
            scale = 1.0 / den[:, head : head + 1]
            for tile in range(2):
                at = 2 * head + tile
                out_ref[at] = (total[at] * scale).astype(BF)

    (attended,) = run("divide", divide, [((2 * HEADS, half, PAGE), BF)], (own, across))
    others = permute(attended, "gx", 1)

    def project_out(own_ref, other_ref, x_ref, gain_ref, *refs):
        w_refs, (attn_ref, sums_ref, held) = refs[:ny], refs[ny:]
        core = my("gx") & 1
        held[core], held[1 - core] = own_ref[...], other_ref[...]
        me = my("gy")
        attn = jnp.zeros((rows, width), F32)
        for m, w_ref in enumerate(w_refs):
            at = 2 * (me ^ m)
            flat = [jnp.concatenate([held[n, at], held[n, at + 1]], axis=1) for n in range(2)]
            flat = jnp.concatenate(flat, axis=0)
            attn = attn + lax.dot_general(flat, w_ref[...], NT, preferred_element_type=F32)
        attn_ref[...] = attn
        x = x_ref[...].astype(F32)
        scaled = attn * (1.0 + gain_ref[1:2])
        lane = lax.broadcasted_iota(jnp.int32, (rows, PAGE), 1)
        sums = jnp.zeros((rows, PAGE), F32)
        for n, terms in enumerate((attn * attn, scaled * scaled, x * scaled, x * x)):
            sums = jnp.where(lane == n, row_sum(terms), sums)
        sums_ref[...] = sums

    attn, sums = run(
        "project_out",
        project_out,
        [((rows, width), F32), ((rows, PAGE), F32)],
        (attended, others, x_own, norm_gains, *[w_blocks[m] for m in range(ny)]),
        scratch=[pltpu.VMEM((2, 2 * HEADS, half, PAGE), BF)],
    )
    sums = gx_terms(sums)

    def mix(*refs):
        attn_ref, x_ref, gain_ref, mixed_ref, ff_ref = refs[2:]
        total = refs[0][...] + refs[1][...]
        plain, scaled, cross, square = (total[:, n : n + 1] for n in range(4))
        scale = lax.rsqrt(plain / D + EPSILON)
        mixed = x_ref[...].astype(F32) + attn_ref[...] * scale * (1.0 + gain_ref[1:2])
        square = jnp.maximum(square + 2.0 * scale * cross + scale * scale * scaled, 0.0)
        mixed_ref[...] = mixed
        scale = lax.rsqrt(square / D + EPSILON)
        ff_input = (mixed * scale * (1.0 + gain_ref[2:3])).astype(BF)
        ff_input = pack_lanes(ff_input)
        for m in range(ny):
            ff_ref[m] = ff_input

    mixed, ff_input = run(
        "mix",
        mix,
        [((rows, width), F32), ((ny, packed, 128), BF)],
        (*sums, attn, x_own, norm_gains),
    )
    ff_input = exchange(ff_input, "gy")

    groups = ny // nx

    cut = hidden // 384 * 256
    column_parts = (0, cut), (cut, hidden)

    def gate_up(start, end):
        def kernel(ff_ref, gate_ref, up_ref, z0_ref, z2_ref, z13_ref):
            me = my("gx")
            flat = [
                unpack_lanes(ff_ref[(me ^ n) * groups + group], rows)
                for n in range(nx)
                for group in range(groups)
            ]
            flat = jnp.concatenate(flat, axis=0)
            for n, w_ref in enumerate((gate_ref, up_ref)):
                sums = jnp.dot(flat, w_ref[:, start:end], preferred_element_type=F32).astype(BF)
                here = pl.ds(n * (end - start), end - start)
                for p, out in enumerate((z0_ref, z13_ref.at[0], z2_ref, z13_ref.at[1])):
                    out[:, here] = sums[p * share_rows : (p + 1) * share_rows]

        shape = (share_rows, 2 * (end - start))
        return run(
            "gate_up",
            kernel,
            [(shape, BF), (shape, BF), ((2,) + shape, BF)],
            (ff_input, w_gate, w_up),
            limit=24,
        )

    def activate(z0_ref, z13_ref, z2_ref, out_ref):
        total = z0_ref[...].astype(F32) + z13_ref[0].astype(F32) + z2_ref[...].astype(F32)
        count = total.shape[1] // 2
        gate, up = total[:, :count], total[:, count:]
        out_ref[...] = (jax.nn.gelu(gate, approximate=True) * up).astype(BF)

    parts = [gate_up(*columns) for columns in column_parts]
    blocks = []
    for z0, z2, z13 in parts:
        shape = z0.shape
        z13 = permute(z13, "gx", 1)
        (z2,) = run("pair_sum_ff", pair_sum, [(shape, BF)], (z2, z13))
        z2 = permute(z2, "gx", 2)
        shape = (share_rows, shape[1] // 2)
        blocks += gather_gx(run("activate", activate, [(shape, BF)], (z0, z13, z2))[0])

    def project_down(*refs):
        w_ref, out_ref = refs[2 * nx :]
        me = my("gx")
        flat = [
            jnp.concatenate([refs[n][...], refs[nx + n][...]], axis=1) for n in range(nx)
        ]
        flat = jnp.concatenate(flat, axis=0)
        sums = lax.dot_general(flat, w_ref[...], NT, preferred_element_type=F32)
        for n in range(nx):
            for group in range(groups):
                at = (n * groups + group) * rows
                block = pack_lanes(sums[at : at + rows].astype(BF))
                out_ref[(me ^ n) * groups + group] = block

    (down,) = run(
        "project_down", project_down, [((ny, packed, 128), BF)], (*blocks, w_down.T)
    )
    down = exchange(down, "gy")

    def down_sum(parts_ref, down_ref, sums_ref):
        down = unpack_lanes(jnp.sum(parts_ref[...].astype(F32), axis=0), rows)
        down_ref[...] = down
        sums_ref[...] = jnp.broadcast_to(row_sum(down * down), (rows, PAGE))

    down, sums = run(
        "down_sum", down_sum, [((rows, width), F32), ((rows, PAGE), F32)], (down,)
    )
    sums = trade([sums] * nx, "gx")

    def finish(*refs):
        down_ref, mixed_ref, gain_ref, out_ref = refs[nx:]
        square = sum(r[...] for r in refs[:nx])[:, 0:1]
        scale = lax.rsqrt(square / D + EPSILON)
        out = mixed_ref[...] + down_ref[...] * scale * (1.0 + gain_ref[3:4])
        out_ref[...] = out.reshape(beams, steps, width).astype(BF)

    (out,) = run("finish", finish, [(inputs.shape, BF)], (*sums, down, mixed, norm_gains))
    return out


def body_general(
    inputs,
    cache_pool,
    lengths,
    block_table,
    parents,
    norm_gains,
    w_query,
    w_key,
    w_value,
    w_out,
    w_gate,
    w_up,
    w_down,
):
    beams, steps, width = inputs.shape
    nx, ny = lax.axis_size("gx"), lax.axis_size("gy")
    rows = beams * steps
    part = rows // nx
    head_part = w_out.shape[0]
    hidden_part = w_gate.shape[1]
    query_part, key_part = w_query.shape[1], w_key.shape[1]
    columns = query_part + 2 * key_part
    share = columns // nx
    x_own = inputs.reshape(rows, width)
    me = lax.axis_index("gx")

    x_all = exchange(jnp.broadcast_to(x_own[None], (ny, rows, width)), "gy")
    flat = (x_all.astype(F32) * (1.0 + norm_gains[0:1])).astype(BF).reshape(ny * rows, width)
    sums = [jnp.dot(flat, w, preferred_element_type=F32) for w in (w_query, w_key, w_value)]
    sums = jnp.concatenate(sums, axis=1).reshape(ny, rows, nx, share)
    received = exchange_all(sums.transpose(2, 0, 1, 3).astype(BF))
    shares = jnp.sum(received.astype(F32), axis=0).astype(BF)
    every = lax.all_gather(shares, "gx", axis=0)
    every = every.transpose(2, 1, 0, 3).reshape(rows, ny, columns)
    q = every[..., :query_part].reshape(rows, HEADS, 2, HALF).transpose(2, 1, 0, 3)
    k, v = (
        every[..., start : start + key_part].reshape(rows, 2 * KV_HEADS, HALF).transpose(1, 0, 2)
        for start in (query_part, query_part + key_part)
    )
    shares = jnp.concatenate([q, k[None], v[None]], axis=0)
    square = lax.psum(row_sum(jnp.square(x_own.astype(F32))), "gx")
    high = lax.reduce_precision(square, 8, 7)
    squares = jnp.where(jnp.arange(HALF) < HALF // 2, high, square - high).astype(BF)[None]
    cos, sin = rope_tables(lengths, rows, steps)

    def attention(*refs):
        g_ref, square_ref, tables, pool_ref, out_ref = refs[0], refs[1], refs[2:6], *refs[6:]

        def store(head, num, den):
            den = high_low(den, PAGE)
            for rep in range(REPS):
                here = slice(rep * rows, (rep + 1) * rows)
                out_ref[REPS * head + rep, :, 0:HEAD_DIM] = num[here].astype(BF)
                out_ref[REPS * head + rep, :, HEAD_DIM:] = den[here].astype(BF)

        attend(
            lambda share, which: g_ref[share, which],
            square_ref[...],
            tables,
            pool_ref,
            store,
        )

    tables = make_tables(block_table, lengths, parents, cache_pool.shape[1], rows, steps)
    (terms,) = run(
        "attention",
        attention,
        [((HEADS, rows, WIDE), BF)],
        (shares, squares, cos, sin, *tables, cache_pool),
        limit=24,
    )
    num = terms[..., :HEAD_DIM].transpose(1, 0, 2).reshape(nx, part, ny, head_part)
    den = terms[..., HEAD_DIM :: PAGE // 2].transpose(1, 0, 2)
    den = jnp.repeat(den, ny // HEADS, axis=1).reshape(nx, part, ny, 2)
    terms = exchange_all(jnp.concatenate([num, den], axis=-1).transpose(0, 2, 1, 3))

    w_wide = lax.all_gather(w_out, "gx", axis=1, tiled=True)
    x_wide = lax.all_gather(x_own, "gx", axis=1, tiled=True)
    x_rows = lax.dynamic_slice_in_dim(x_wide, me * part, part, 0).astype(F32)
    gains = 1.0 + lax.all_gather(norm_gains, "gx", axis=1, tiled=True)

    def scaled(v, gain):
        return v * lax.rsqrt(row_sum(v * v) / D + EPSILON) * gain

    terms = jnp.sum(terms.astype(F32), axis=0)
    den = terms[..., head_part : head_part + 1] + terms[..., -1:]
    attended = (terms[..., :head_part] / den).reshape(ny * part, head_part).astype(BF)
    attn = jnp.dot(attended, w_wide, preferred_element_type=F32).astype(BF)
    attn = exchange(attn.reshape(ny, part, D), "gy").astype(F32).sum(axis=0)
    mixed = x_rows + scaled(attn, gains[1])
    ff_input = scaled(mixed, gains[2]).astype(BF)
    ff_input = ff_input.reshape(part, nx, width).transpose(1, 0, 2)[:, None]
    ff_input = exchange_all(jnp.broadcast_to(ff_input, (nx, ny, part, width)))

    flat = ff_input.reshape(-1, width)
    both = [jnp.dot(flat, w, preferred_element_type=F32).astype(BF) for w in (w_gate, w_up)]
    both = jnp.stack(both, axis=1).reshape(nx, ny * part, 2, hidden_part)
    both = jnp.sum(exchange(both, "gx").astype(F32), axis=0)
    hidden = (jax.nn.gelu(both[:, 0], approximate=True) * both[:, 1]).astype(BF)
    hidden = lax.all_gather(hidden, "gx", axis=0, tiled=True)
    down = jnp.dot(hidden, w_down, preferred_element_type=F32).astype(BF)
    down = exchange_all(down.reshape(nx, ny, part, width)).astype(F32).sum(axis=1)
    down = down.transpose(1, 0, 2).reshape(part, D)
    out = (mixed + scaled(down, gains[3])).astype(BF)
    out = exchange(out.reshape(part, nx, width).transpose(1, 0, 2), "gx")
    return out.reshape(beams, steps, width)


def solution(mesh):
    sizes = dict(mesh.shape)
    fits = sizes["gx"] == 4 and sizes["gy"] == HEADS
    return jax.shard_map(
        body_permutes if fits else body_general,
        mesh=mesh,
        in_specs=(
            P("gy", None, "gx"),
            P(None, "gx", "gy", None),
            P("gy"),
            P("gy", None),
            P(None, "gy"),
            P(None, "gx"),
            P("gx", "gy"),
            P("gx", "gy"),
            P("gx", "gy"),
            P("gy", "gx"),
            P("gx", "gy"),
            P("gx", "gy"),
            P("gy", "gx"),
        ),
        out_specs=P("gy", None, "gx"),
        check_vma=False,
    )
```

```python
import jax
import jax.numpy as jnp
from jax import lax
from jax.experimental import pallas as pl
from jax.experimental.pallas import tpu as pltpu
from jax.sharding import PartitionSpec as P

D = 2304
HEADS = 8
KV_HEADS = 4
HEAD_DIM = 256
HALF = HEAD_DIM // 2
WINDOW = 4096
PAGE = 128
BEAM = 8
EPSILON = 1e-06
SOFT_CAP = 50.0
ROPE_BASE = 10000.0
REPS = HEADS // KV_HEADS
WIDE = HEAD_DIM + PAGE
HALF_PAGE = PAGE // 2
BF = jnp.bfloat16
F32 = jnp.float32
MIB = 1024 * 1024
NT = (((1,), (1,)), ((), ()))
IN_SMEM = pl.BlockSpec(memory_space=pltpu.SMEM)


def run(name, kernel, outs, args, scratch=(), limit=16, specs=None, micros=0):
    cost = pl.CostEstimate(flops=micros * 10**9, bytes_accessed=0, transcendentals=0)
    specs = specs or {}
    vmem = pl.BlockSpec(memory_space=pltpu.VMEM)
    return pl.pallas_call(
        kernel,
        out_shape=[jax.ShapeDtypeStruct(s, d) for s, d in outs],
        in_specs=[specs.get(n, vmem) for n in range(len(args))],
        scratch_shapes=scratch,
        compiler_params=pltpu.CompilerParams(vmem_limit_bytes=limit * MIB),
        cost_estimate=cost if micros else None,
        name=name,
    )(*args)


def exchange(values, axes):
    return lax.all_to_all(values, axes, split_axis=0, concat_axis=0, tiled=True)


def exchange_all(values):
    nx, ny = values.shape[:2]
    flat = values.reshape((nx * ny,) + values.shape[2:])
    return exchange(flat, ("gx", "gy")).reshape(values.shape)


def permute(values, axis, m):
    count = lax.axis_size(axis)
    return lax.ppermute(values, axis, [(i, i ^ m) for i in range(count)])


def trade(blocks, axis):
    return [blocks[0]] + [permute(blocks[m], axis, m) for m in range(1, len(blocks))]


def gather_gx(values):
    across = permute(values, "gx", 2)
    return [values, permute(values, "gx", 1), across, permute(across, "gx", 1)]


def gx_terms(values):
    def add(a_ref, b_ref, out_ref):
        out_ref[...] = a_ref[...] + b_ref[...]

    (pair,) = run(
        "pair_add", add, [(values.shape, values.dtype)], (values, permute(values, "gx", 1))
    )
    return pair, permute(pair, "gx", 2)


def weight_of(scores):
    return jnp.exp(SOFT_CAP * jnp.tanh(scores * (1.0 / SOFT_CAP)))


def high_low(column, lanes):
    shape = column.shape[:-1] + (lanes,)
    high = column.astype(BF).astype(F32)
    lane = lax.broadcasted_iota(jnp.int32, shape, len(shape) - 1)
    return jnp.where(lane < lanes // 2, high, column - high)


def pack_lanes(v):
    rows, width = v.shape
    whole = width // 128 * 128
    tiles = [v[:, c : c + 128] for c in range(0, whole, 128)]
    last = jnp.concatenate([v[: rows // 2, whole:], v[rows // 2 :, whole:]], axis=1)
    return jnp.concatenate(tiles + [last], axis=0)


def unpack_lanes(v, rows):
    whole = v.shape[0] // rows * rows
    tiles = [v[r : r + rows] for r in range(0, whole, rows)]
    last = jnp.concatenate([v[whole:, :64], v[whole:, 64:]], axis=0)
    return jnp.concatenate(tiles + [last], axis=1)


def row_sum(v):
    return jnp.sum(v, axis=-1, keepdims=True)


def make_tables(table, lengths, parents, slots, rows, steps):
    def tables(table_ref, length_ref, parents_ref, cached_ref, own_ref, page_ref):
        first_owner = lax.axis_index("gx") * slots
        length = length_ref[0]
        first_page = jnp.maximum(length - WINDOW + 1, 0) // PAGE
        for slot in range(slots + 1):
            page_ref[slot] = -1
        for j in range(table_ref.shape[1]):
            slot = table_ref[0, j] - first_owner
            page_ref[jnp.where((slot >= 0) & (slot < slots), slot, slots)] = j
        step = lax.broadcasted_iota(jnp.int32, (8, PAGE), 0) % steps
        lane = lax.broadcasted_iota(jnp.int32, (8, PAGE), 1)
        for slot in range(slots):
            page = page_ref[slot]
            position = lane + jnp.where(page >= 0, (first_page + page) * PAGE, 2**30)
            seen = (position < length) & (position >= length + step - (WINDOW - 1))
            cached_ref[:, slot * PAGE : (slot + 1) * PAGE] = jnp.where(seen, 1.0, 0.0)

        shape = (REPS * rows, rows)
        row = lax.broadcasted_iota(jnp.int32, shape, 0) % rows
        column = lax.broadcasted_iota(jnp.int32, shape, 1)
        row_step, column_step, column_beam = row % steps, column % steps, column // steps
        current = row // steps
        visible = jnp.zeros(shape, jnp.bool_)
        for j in range(steps - 1, -1, -1):
            if j < steps - 1:
                parent = jnp.zeros(shape, jnp.int32)
                for beam in range(BEAM):
                    parent = jnp.where(current == beam, parents_ref[j, beam], parent)
                current = jnp.where(row_step > j, parent, current)
            visible = visible | ((column_step == j) & (row_step >= j) & (column_beam == current))
        visible = visible & (lax.axis_index("gx") == 0)
        own_ref[...] = jnp.where(visible, 1.0, 0.0)

    return run(
        "tables",
        tables,
        [((8, slots * PAGE), F32), ((REPS * rows, rows), F32)],
        (table, lengths, parents),
        scratch=[pltpu.SMEM((slots + 1,), jnp.int32)],
        specs={0: IN_SMEM, 1: IN_SMEM, 2: IN_SMEM},
    )


def attend(shares, squares, tables, pool_ref, store):
    cos_ref, sin_ref, cached_ref, own_ref = tables
    slots = pool_ref.shape[1]
    rows = cos_ref.shape[0]
    square = jnp.sum(squares.astype(F32), axis=0)
    square = square[:, 0:1] + square[:, HALF // 2 : HALF // 2 + 1]
    scale = lax.rsqrt(square / D + EPSILON)
    cos, sin = cos_ref[...] * scale, sin_ref[...] * scale
    cached, own = cached_ref[...], own_ref[...]

    def rotated(u, w):
        u, w = u.astype(F32), w.astype(F32)
        return u * cos - w * sin, w * cos + u * sin

    for head in range(KV_HEADS):
        query = []
        for rep in range(REPS):
            u, w = rotated(shares(0, REPS * head + rep), shares(1, REPS * head + rep))
            query.append(jnp.concatenate([u, w], axis=1) * HEAD_DIM ** (-0.5))
        query = jnp.concatenate(query, axis=0).astype(BF)
        first, second = 2 * head, 2 * head + 1
        key_step = rotated(shares(2, first), shares(2, second))
        key_step = jnp.concatenate(key_step, axis=1).astype(BF)
        value_step = [shares(3, n).astype(F32) * scale for n in (first, second)]
        value_step = jnp.concatenate(value_step, axis=1).astype(BF)

        scores = lax.dot_general(query, key_step, NT, preferred_element_type=F32)
        weights = weight_of(scores) * own
        den = row_sum(weights)
        num = jnp.dot(weights.astype(BF), value_step, preferred_element_type=F32)

        here = slice(head * HEAD_DIM, (head + 1) * HEAD_DIM)
        keys = pool_ref[0, :, :, here].reshape(slots * PAGE, HEAD_DIM)
        values = pool_ref[1, :, :, here].reshape(slots * PAGE, HEAD_DIM)
        scores = lax.dot_general(query, keys, NT, preferred_element_type=F32)
        weights = weight_of(scores).reshape(REPS * rows // 8, 8, slots * PAGE) * cached[None]
        weights = weights.reshape(REPS * rows, slots * PAGE)
        den = den + row_sum(weights)
        num = num + jnp.dot(weights.astype(BF), values, preferred_element_type=F32)
        store(head, num, den)


def rope_tables(lengths, rows, steps):
    positions = lengths[0] + jnp.arange(rows, dtype=jnp.int32) % steps
    inverse_freq = ROPE_BASE ** (-jnp.arange(HALF, dtype=F32) * 2.0 / HEAD_DIM)
    angles = positions[:, None].astype(F32) * inverse_freq
    return jnp.cos(angles), jnp.sin(angles)


def body_permutes(
    inputs,
    cache_pool,
    lengths,
    block_table,
    parents,
    norm_gains,
    w_query,
    w_key,
    w_value,
    w_out,
    w_gate,
    w_up,
    w_down,
):
    beams, steps, width = inputs.shape
    nx, ny = lax.axis_size("gx"), lax.axis_size("gy")
    rows = beams * steps
    half = rows // 2
    all_rows = ny * rows
    share_rows = all_rows // nx
    hidden = w_gate.shape[1]
    packed = rows * width // 128

    def my(axis):
        return lax.axis_index(axis)

    def spread(x_ref, own_ref, out_ref):
        own = x_ref[...].astype(F32).reshape(rows, width).astype(BF)
        own_ref[...] = own
        own = pack_lanes(own)
        for m in range(ny):
            out_ref[m] = own

    x_own, x_all = run(
        "spread", spread, [((rows, width), BF), ((ny, packed, 128), BF)], (inputs,), micros=12
    )
    w_own = w_out.T
    x_all, w_split = lax.optimization_barrier((x_all, w_own))
    x_all = exchange(x_all, "gy")

    w_blocks = {0: w_own, 1: permute(w_own, "gy", 1), 2: permute(w_own, "gy", 2)}
    w_first = permute(w_split[: width // 2], "gy", 4)
    w_late, _ = lax.optimization_barrier(((w_blocks[1], w_split[width // 2 :]), x_all))
    w_blocks[3] = permute(w_late[0], "gy", 2)
    w_second = permute(w_late[1], "gy", 4)

    def project(x_ref, gain_ref, q_ref, k_ref, v_ref, z0_ref, z2_ref, z13_ref, held):
        gain = 1.0 + gain_ref[0:1]
        flat = [
            (unpack_lanes(x_ref[m], rows).astype(F32) * gain).astype(BF) for m in range(ny)
        ]
        flat = jnp.concatenate(flat, axis=0)
        query = jnp.dot(flat, q_ref[...], preferred_element_type=F32).astype(BF)
        held[0], held[1] = query[:, :HALF], query[:, HALF:]
        held[2] = jnp.dot(flat, k_ref[...], preferred_element_type=F32).astype(BF)
        held[3] = jnp.dot(flat, v_ref[...], preferred_element_type=F32).astype(BF)
        me = my("gx")
        z0_ref[...], z2_ref[...] = held[me], held[me ^ 2]
        z13_ref[0], z13_ref[1] = held[me ^ 1], held[me ^ 3]

    shape = (all_rows, HALF)
    z0, z2, z13 = run(
        "project",
        project,
        [(shape, BF), (shape, BF), ((2,) + shape, BF)],
        (x_all, norm_gains, w_query, w_key, w_value),
        scratch=[
            pltpu.VMEM((nx,) + shape, BF),
        ],
    )
    z13 = permute(z13, "gx", 1)

    def pair_sum(z_ref, from_pair_ref, out_ref):
        total = z_ref[...].astype(F32) + from_pair_ref[1].astype(F32)
        out_ref[...] = total.astype(BF)

    (z2,) = run("pair_sum", pair_sum, [(shape, BF)], (z2, z13))
    z2 = permute(z2, "gx", 2)

    def share_sum(z0_ref, z13_ref, z2_ref, out_ref):
        total = z0_ref[...].astype(F32) + z13_ref[0].astype(F32) + z2_ref[...].astype(F32)
        out_ref[...] = total.reshape(ny, rows, HALF).astype(BF)

    (shares,) = run("share_sum", share_sum, [((ny, rows, HALF), BF)], (z0, z13, z2))
    shares, *late = lax.optimization_barrier((shares, block_table, lengths, parents))
    cos, sin = rope_tables(late[1], rows, steps)
    tables = make_tables(*late, cache_pool.shape[1], rows, steps)
    halves, _ = lax.optimization_barrier(((w_first, w_second), shares))
    w_blocks[4] = jnp.concatenate(halves, axis=0)
    w_blocks[6] = permute(w_blocks[4], "gy", 2)
    w_blocks[5] = permute(w_blocks[4], "gy", 1)
    shares = exchange(shares, "gy")
    beside = tables, cos, sin, w_blocks[2], w_blocks[3], w_blocks[4]
    shares, (tables, cos, sin, *_) = lax.optimization_barrier((shares, beside))

    def pack_shares(share_ref, x_ref, out_ref):
        x = x_ref[...].astype(F32)
        out_ref[0:ny] = share_ref[...]
        out_ref[ny] = high_low(row_sum(x * x), HALF).astype(BF)

    (shares,) = run(
        "pack_shares", pack_shares, [((ny + 1, rows, HALF), BF)], (shares, x_own), micros=5
    )
    shares = gather_gx(shares)

    def attention(*refs):
        a_refs, tables, pool_ref, outs = refs[:nx], refs[nx : nx + 4], refs[nx + 4], refs[nx + 5 :]
        own_ref, pair_ref, held, num_held, den_held = outs
        me = my("gx")
        core = me & 1
        for n, ref in enumerate(a_refs):
            held[me ^ n] = ref[...]
        den_held[...] = jnp.zeros(den_held.shape, F32)
        lane = lax.broadcasted_iota(jnp.int32, (2, half, PAGE), 2)

        def store(head, num, den):
            num_held[head] = num.reshape(REPS, 2, half, HEAD_DIM)
            den = high_low(den, PAGE).reshape(REPS, 2, half, PAGE)
            for rep in range(REPS):
                at = REPS * head + rep
                den_held[...] = jnp.where(lane % HALF_PAGE == at, den[rep], den_held[...])
                for n, out in enumerate((own_ref, pair_ref)):
                    for tile in range(2):
                        here = num_held[head, rep, core ^ n, :, tile * PAGE : (tile + 1) * PAGE]
                        out[2 * at + tile] = here.astype(BF)

        attend(
            lambda share, which: held[share, which],
            held[:, ny],
            tables,
            pool_ref,
            store,
        )
        for n, out in enumerate((own_ref, pair_ref)):
            out[2 * HEADS] = den_held[core ^ n].astype(BF)

    shape = (2 * HEADS + 1, half, PAGE)
    own, pair = run(
        "attention",
        attention,
        [(shape, BF), (shape, BF)],
        (*shares, cos, sin, *tables, cache_pool),
        scratch=[
            pltpu.VMEM((nx,) + shares[0].shape, BF),
            pltpu.VMEM((KV_HEADS, REPS, 2, half, HEAD_DIM), F32),
            pltpu.VMEM((2, half, PAGE), F32),
        ],
        limit=24,
    )
    w_late, _ = lax.optimization_barrier((w_blocks, own))
    w_blocks[7] = permute(w_late[6], "gy", 1)
    pair = permute(pair, "gx", 1)

    def pair_terms(own_ref, pair_ref, out_ref):
        total = own_ref[...].astype(F32) + pair_ref[...].astype(F32)
        out_ref[0 : 2 * HEADS] = total[0 : 2 * HEADS].astype(BF)
        den = total[2 * HEADS]
        den = den[:, :HALF_PAGE] + den[:, HALF_PAGE:]
        high = den.astype(BF).astype(F32)
        out_ref[2 * HEADS] = jnp.concatenate([high, den - high], axis=1).astype(BF)

    (own,) = run("pair_terms", pair_terms, [(shape, BF)], (own, pair))
    across = permute(own, "gx", 2)

    def divide(own_ref, across_ref, out_ref):
        total = own_ref[...].astype(F32) + across_ref[...].astype(F32)
        den = total[2 * HEADS]
        den = den[:, :HALF_PAGE] + den[:, HALF_PAGE:]
        for head in range(HEADS):
            scale = 1.0 / den[:, head : head + 1]
            for tile in range(2):
                at = 2 * head + tile
                out_ref[at] = (total[at] * scale).astype(BF)

    (attended,) = run("divide", divide, [((2 * HEADS, half, PAGE), BF)], (own, across))
    others = permute(attended, "gx", 1)

    def project_out(own_ref, other_ref, x_ref, gain_ref, *refs):
        w_refs, (attn_ref, sums_ref, held) = refs[:ny], refs[ny:]
        core = my("gx") & 1
        held[core], held[1 - core] = own_ref[...], other_ref[...]
        me = my("gy")
        attn = jnp.zeros((rows, width), F32)
        for m, w_ref in enumerate(w_refs):
            at = 2 * (me ^ m)
            flat = [jnp.concatenate([held[n, at], held[n, at + 1]], axis=1) for n in range(2)]
            flat = jnp.concatenate(flat, axis=0)
            attn = attn + lax.dot_general(flat, w_ref[...], NT, preferred_element_type=F32)
        attn_ref[...] = attn
        x = x_ref[...].astype(F32)
        scaled = attn * (1.0 + gain_ref[1:2])
        lane = lax.broadcasted_iota(jnp.int32, (rows, PAGE), 1)
        sums = jnp.zeros((rows, PAGE), F32)
        for n, terms in enumerate((attn * attn, scaled * scaled, x * scaled, x * x)):
            sums = jnp.where(lane == n, row_sum(terms), sums)
        sums_ref[...] = sums

    attn, sums = run(
        "project_out",
        project_out,
        [((rows, width), F32), ((rows, PAGE), F32)],
        (attended, others, x_own, norm_gains, *[w_blocks[m] for m in range(ny)]),
        scratch=[pltpu.VMEM((2, 2 * HEADS, half, PAGE), BF)],
    )
    sums = gx_terms(sums)

    def mix(*refs):
        attn_ref, x_ref, gain_ref, mixed_ref, ff_ref = refs[2:]
        total = refs[0][...] + refs[1][...]
        plain, scaled, cross, square = (total[:, n : n + 1] for n in range(4))
        scale = lax.rsqrt(plain / D + EPSILON)
        mixed = x_ref[...].astype(F32) + attn_ref[...] * scale * (1.0 + gain_ref[1:2])
        square = jnp.maximum(square + 2.0 * scale * cross + scale * scale * scaled, 0.0)
        mixed_ref[...] = mixed
        scale = lax.rsqrt(square / D + EPSILON)
        ff_input = (mixed * scale * (1.0 + gain_ref[2:3])).astype(BF)
        ff_input = pack_lanes(ff_input)
        for m in range(ny):
            ff_ref[m] = ff_input

    mixed, ff_input = run(
        "mix",
        mix,
        [((rows, width), F32), ((ny, packed, 128), BF)],
        (*sums, attn, x_own, norm_gains),
    )
    ff_input = exchange(ff_input, "gy")

    groups = ny // nx

    cut = hidden // 384 * 256
    column_parts = (0, cut), (cut, hidden)

    def gate_up(start, end):
        def kernel(ff_ref, gate_ref, up_ref, z0_ref, z2_ref, z13_ref):
            me = my("gx")
            flat = [
                unpack_lanes(ff_ref[(me ^ n) * groups + group], rows)
                for n in range(nx)
                for group in range(groups)
            ]
            flat = jnp.concatenate(flat, axis=0)
            for n, w_ref in enumerate((gate_ref, up_ref)):
                sums = jnp.dot(flat, w_ref[:, start:end], preferred_element_type=F32).astype(BF)
                here = pl.ds(n * (end - start), end - start)
                for p, out in enumerate((z0_ref, z13_ref.at[0], z2_ref, z13_ref.at[1])):
                    out[:, here] = sums[p * share_rows : (p + 1) * share_rows]

        shape = (share_rows, 2 * (end - start))
        return run(
            "gate_up",
            kernel,
            [(shape, BF), (shape, BF), ((2,) + shape, BF)],
            (ff_input, w_gate, w_up),
            limit=24,
        )

    def activate(z0_ref, z13_ref, z2_ref, out_ref):
        total = z0_ref[...].astype(F32) + z13_ref[0].astype(F32) + z2_ref[...].astype(F32)
        count = total.shape[1] // 2
        gate, up = total[:, :count], total[:, count:]
        out_ref[...] = (jax.nn.gelu(gate, approximate=True) * up).astype(BF)

    parts = [gate_up(*columns) for columns in column_parts]
    blocks = []
    for z0, z2, z13 in parts:
        shape = z0.shape
        z13 = permute(z13, "gx", 1)
        (z2,) = run("pair_sum_ff", pair_sum, [(shape, BF)], (z2, z13))
        z2 = permute(z2, "gx", 2)
        shape = (share_rows, shape[1] // 2)
        blocks += gather_gx(run("activate", activate, [(shape, BF)], (z0, z13, z2))[0])

    def project_down(*refs):
        w_ref, out_ref = refs[2 * nx :]
        me = my("gx")
        flat = [
            jnp.concatenate([refs[n][...], refs[nx + n][...]], axis=1) for n in range(nx)
        ]
        flat = jnp.concatenate(flat, axis=0)
        sums = lax.dot_general(flat, w_ref[...], NT, preferred_element_type=F32)
        for n in range(nx):
            for group in range(groups):
                at = (n * groups + group) * rows
                block = pack_lanes(sums[at : at + rows].astype(BF))
                out_ref[(me ^ n) * groups + group] = block

    (down,) = run(
        "project_down", project_down, [((ny, packed, 128), BF)], (*blocks, w_down.T)
    )
    down = exchange(down, "gy")

    def down_sum(parts_ref, down_ref, sums_ref):
        down = unpack_lanes(jnp.sum(parts_ref[...].astype(F32), axis=0), rows)
        down_ref[...] = down
        sums_ref[...] = jnp.broadcast_to(row_sum(down * down), (rows, PAGE))

    down, sums = run(
        "down_sum", down_sum, [((rows, width), F32), ((rows, PAGE), F32)], (down,)
    )
    sums = trade([sums] * nx, "gx")

    def finish(*refs):
        down_ref, mixed_ref, gain_ref, out_ref = refs[nx:]
        square = sum(r[...] for r in refs[:nx])[:, 0:1]
        scale = lax.rsqrt(square / D + EPSILON)
        out = mixed_ref[...] + down_ref[...] * scale * (1.0 + gain_ref[3:4])
        out_ref[...] = out.reshape(beams, steps, width).astype(BF)

    (out,) = run("finish", finish, [(inputs.shape, BF)], (*sums, down, mixed, norm_gains))
    return out


def body_general(
    inputs,
    cache_pool,
    lengths,
    block_table,
    parents,
    norm_gains,
    w_query,
    w_key,
    w_value,
    w_out,
    w_gate,
    w_up,
    w_down,
):
    beams, steps, width = inputs.shape
    nx, ny = lax.axis_size("gx"), lax.axis_size("gy")
    rows = beams * steps
    part = rows // nx
    head_part = w_out.shape[0]
    hidden_part = w_gate.shape[1]
    query_part, key_part = w_query.shape[1], w_key.shape[1]
    columns = query_part + 2 * key_part
    share = columns // nx
    x_own = inputs.reshape(rows, width)
    me = lax.axis_index("gx")

    x_all = exchange(jnp.broadcast_to(x_own[None], (ny, rows, width)), "gy")
    flat = (x_all.astype(F32) * (1.0 + norm_gains[0:1])).astype(BF).reshape(ny * rows, width)
    sums = [jnp.dot(flat, w, preferred_element_type=F32) for w in (w_query, w_key, w_value)]
    sums = jnp.concatenate(sums, axis=1).reshape(ny, rows, nx, share)
    received = exchange_all(sums.transpose(2, 0, 1, 3).astype(BF))
    shares = jnp.sum(received.astype(F32), axis=0).astype(BF)
    every = lax.all_gather(shares, "gx", axis=0)
    every = every.transpose(2, 1, 0, 3).reshape(rows, ny, columns)
    q = every[..., :query_part].reshape(rows, HEADS, 2, HALF).transpose(2, 1, 0, 3)
    k, v = (
        every[..., start : start + key_part].reshape(rows, 2 * KV_HEADS, HALF).transpose(1, 0, 2)
        for start in (query_part, query_part + key_part)
    )
    shares = jnp.concatenate([q, k[None], v[None]], axis=0)
    square = lax.psum(row_sum(jnp.square(x_own.astype(F32))), "gx")
    high = lax.reduce_precision(square, 8, 7)
    squares = jnp.where(jnp.arange(HALF) < HALF // 2, high, square - high).astype(BF)[None]
    cos, sin = rope_tables(lengths, rows, steps)

    def attention(*refs):
        g_ref, square_ref, tables, pool_ref, out_ref = refs[0], refs[1], refs[2:6], *refs[6:]

        def store(head, num, den):
            den = high_low(den, PAGE)
            for rep in range(REPS):
                here = slice(rep * rows, (rep + 1) * rows)
                out_ref[REPS * head + rep, :, 0:HEAD_DIM] = num[here].astype(BF)
                out_ref[REPS * head + rep, :, HEAD_DIM:] = den[here].astype(BF)

        attend(
            lambda share, which: g_ref[share, which],
            square_ref[...],
            tables,
            pool_ref,
            store,
        )

    tables = make_tables(block_table, lengths, parents, cache_pool.shape[1], rows, steps)
    (terms,) = run(
        "attention",
        attention,
        [((HEADS, rows, WIDE), BF)],
        (shares, squares, cos, sin, *tables, cache_pool),
        limit=24,
    )
    num = terms[..., :HEAD_DIM].transpose(1, 0, 2).reshape(nx, part, ny, head_part)
    den = terms[..., HEAD_DIM :: PAGE // 2].transpose(1, 0, 2)
    den = jnp.repeat(den, ny // HEADS, axis=1).reshape(nx, part, ny, 2)
    terms = exchange_all(jnp.concatenate([num, den], axis=-1).transpose(0, 2, 1, 3))

    w_wide = lax.all_gather(w_out, "gx", axis=1, tiled=True)
    x_wide = lax.all_gather(x_own, "gx", axis=1, tiled=True)
    x_rows = lax.dynamic_slice_in_dim(x_wide, me * part, part, 0).astype(F32)
    gains = 1.0 + lax.all_gather(norm_gains, "gx", axis=1, tiled=True)

    def scaled(v, gain):
        return v * lax.rsqrt(row_sum(v * v) / D + EPSILON) * gain

    terms = jnp.sum(terms.astype(F32), axis=0)
    den = terms[..., head_part : head_part + 1] + terms[..., -1:]
    attended = (terms[..., :head_part] / den).reshape(ny * part, head_part).astype(BF)
    attn = jnp.dot(attended, w_wide, preferred_element_type=F32).astype(BF)
    attn = exchange(attn.reshape(ny, part, D), "gy").astype(F32).sum(axis=0)
    mixed = x_rows + scaled(attn, gains[1])
    ff_input = scaled(mixed, gains[2]).astype(BF)
    ff_input = ff_input.reshape(part, nx, width).transpose(1, 0, 2)[:, None]
    ff_input = exchange_all(jnp.broadcast_to(ff_input, (nx, ny, part, width)))

    flat = ff_input.reshape(-1, width)
    both = [jnp.dot(flat, w, preferred_element_type=F32).astype(BF) for w in (w_gate, w_up)]
    both = jnp.stack(both, axis=1).reshape(nx, ny * part, 2, hidden_part)
    both = jnp.sum(exchange(both, "gx").astype(F32), axis=0)
    hidden = (jax.nn.gelu(both[:, 0], approximate=True) * both[:, 1]).astype(BF)
    hidden = lax.all_gather(hidden, "gx", axis=0, tiled=True)
    down = jnp.dot(hidden, w_down, preferred_element_type=F32).astype(BF)
    down = exchange_all(down.reshape(nx, ny, part, width)).astype(F32).sum(axis=1)
    down = down.transpose(1, 0, 2).reshape(part, D)
    out = (mixed + scaled(down, gains[3])).astype(BF)
    out = exchange(out.reshape(part, nx, width).transpose(1, 0, 2), "gx")
    return out.reshape(beams, steps, width)


def solution(mesh):
    sizes = dict(mesh.shape)
    fits = sizes["gx"] == 4 and sizes["gy"] == HEADS
    return jax.shard_map(
        body_permutes if fits else body_general,
        mesh=mesh,
        in_specs=(
            P("gy", None, "gx"),
            P(None, "gx", "gy", None),
            P("gy"),
            P("gy", None),
            P(None, "gy"),
            P(None, "gx"),
            P("gx", "gy"),
            P("gx", "gy"),
            P("gx", "gy"),
            P("gy", "gx"),
            P("gx", "gy"),
            P("gx", "gy"),
            P("gy", "gx"),
        ),
        out_specs=P("gy", None, "gx"),
        check_vma=False,
    )
```
